32 devices in a mesh: ctx: 16 (over z, y, x), tp: 2 (over core).
Axes of the slice: x: 2, y: 2, z: 4, core: 2. Of those that a mesh axis runs over, the one named last changes fastest.
Arguments:
- tokens: bfloat16 [2048, 4096], P('ctx'), may hold values from -6 to 6
- weights: bfloat16 [2, 2048, 3, 4096], P('tp', 'ctx'), may hold values from -0.09375 to 0.09375
- residues: float32 [2, 2048, 16], P('tp', 'ctx'), may hold values from -1.5 to 1.5
- decay_rates: float32 [2, 2048, 16], P('tp', 'ctx'), may hold values from 0.00024414062 to 0.03
- cotangent: bfloat16 [4096, 2048], P('tp', 'ctx'), may hold values from -6 to 6
Outputs:
- hyena_out: bfloat16 [4096, 2048], P('tp', 'ctx')
- grad_input: bfloat16 [2048, 4096], P('ctx', 'tp')
- grad_residue: float32 [2, 2048, 16], P('tp', 'ctx')
The draws below stay inside these ranges and needn't reach their ends.
All inputs are finite; a program needn't handle non-finite values.
Results may differ from the reference program's by a relative error of at most 0.018.
Values may be sent and summed in bfloat16 or wider, within the bound.
No kernel may reach another device: no remote copies, remote signals or barrier semaphores. Data moves between devices by JAX's collectives and lax.ppermute only.
A program may use at most 128 MiB of HBM per device.

```python
import math
import jax
import jax.numpy as jnp
from jax import lax

D = 4096
C = 4096
M = 16
L = 2048
C_TP = 2048
N_TP = 2


def levels(key, extent, shards, low, top_value):
    level, own = 1.0, jax.random.fold_in(key, 6)
    for dim, parts in shards:
        draws = jnp.exp(jax.random.uniform(jax.random.fold_in(own, dim), (parts,), jnp.float32, low / len(shards), top_value / len(shards)))
        level = level * jnp.repeat(draws, extent[dim] // parts).reshape([-1 if axis == dim else 1 for axis in range(len(extent))])
    return level


def scatter_about(own_key, extent, width, reach, split=(), held_as=jnp.bfloat16):
    array = width * jax.random.normal(own_key, extent, jnp.float32)
    if split:
        array = array * levels(own_key, extent, split, -0.22, 0.18)
    return jnp.clip(array, -reach, reach).astype(held_as)


def setup_inputs(seed: int = 0) -> dict:
    key_list = jax.random.split(jax.random.key(seed), 6)
    return {
        "tokens": scatter_about(key_list[0], (L, D), 1.0, 6.0, ((0, 16),)),
        "weights": scatter_about(key_list[1], (N_TP, C_TP, 3, D), D ** -0.5, 0.09375, ((0, 2), (1, 16))),
        "residues": scatter_about(key_list[2], (N_TP, C_TP, M), 0.25, 1.5, ((0, 2), (1, 16)), jnp.float32),
        "decay_rates": jnp.clip(jnp.exp(math.log(0.03) - 4.8112082 * jax.random.uniform(key_list[3], (N_TP, C_TP, M), jnp.float32) ** levels(key_list[3], (N_TP, C_TP, M), ((0, 2), (1, 16)), -0.2, 0.2)), 0.00024414062, 0.03),
        "cotangent": scatter_about(key_list[4], (C, L), 1.0, 6.0, ((0, 2), (1, 16))),
    }


def reference(tokens, weights, residues, decay_rates, cotangent):
    flat_weights = weights.reshape(C, 3, D)
    projected = jnp.einsum('ld,cpd->cpl', tokens.astype(jnp.float32), flat_weights.astype(jnp.float32))
    features = projected.astype(jnp.bfloat16)
    query_f = features[:, 0].astype(jnp.float32)
    key_part = features[:, 1].astype(jnp.float32)
    value_part = features[:, 2].astype(jnp.float32)
    gated_in = (key_part * value_part).astype(jnp.bfloat16)
    rate_all = decay_rates.reshape(C, M)
    residue_all = residues.reshape(C, M)
    position = jnp.arange(L, dtype=jnp.float32)

    def mode_basis(mode_index):
        rate_col = rate_all[:, mode_index][:, None]
        return jnp.sqrt(2.0 * rate_col) * jnp.exp(-rate_col * position[None, :])
    taps_full = jnp.zeros((C, L), jnp.float32)
    for mode_index in range(M):
        taps_full = taps_full + residue_all[:, mode_index][:, None] * mode_basis(mode_index)
    padded = 2 * L
    gated_spec = jnp.fft.rfft(gated_in.astype(jnp.float32), n=padded, axis=1)
    taps_spec = jnp.fft.rfft(taps_full, n=padded, axis=1)
    conv_out = jnp.fft.irfft(gated_spec * taps_spec, n=padded, axis=1)[:, :L].astype(jnp.bfloat16)
    hyena_out = (query_f * conv_out.astype(jnp.float32)).astype(jnp.bfloat16)
    slope_in = (cotangent.astype(jnp.float32) * query_f).astype(jnp.bfloat16)
    slope_spec = jnp.fft.rfft(slope_in.astype(jnp.float32), n=padded, axis=1)
    back_in = jnp.fft.irfft(jnp.conj(taps_spec) * slope_spec, n=padded, axis=1)[:, :L].astype(jnp.bfloat16)
    taps_grad = jnp.fft.irfft(jnp.conj(gated_spec) * slope_spec, n=padded, axis=1)[:, :L]
    columns = [lax.optimization_barrier(jnp.sum(taps_grad * mode_basis(mode_index), axis=1)) for mode_index in range(M)]
    grad_residue = (jnp.stack(columns, axis=1) / jnp.sqrt(jnp.float32(L))).reshape(N_TP, C_TP, M)
    back_f = back_in.astype(jnp.float32)
    grad_query = (cotangent.astype(jnp.float32) * conv_out.astype(jnp.float32)).astype(jnp.bfloat16)
    grad_key = (back_f * value_part).astype(jnp.bfloat16)
    grad_value = (back_f * key_part).astype(jnp.bfloat16)
    grad_proj = jnp.stack([grad_query, grad_key, grad_value], axis=1)
    summed = jnp.zeros((L, D), jnp.float32)
    for block_index in range(N_TP):
        first = block_index * C_TP
        partial_value = jnp.einsum('cpl,cpd->ld', grad_proj[first:first + C_TP].astype(jnp.float32), flat_weights[first:first + C_TP].astype(jnp.float32))
        rounded = lax.optimization_barrier(partial_value.astype(jnp.bfloat16))
        summed = summed + rounded.astype(jnp.float32)
    grad_input = summed.astype(jnp.bfloat16)
    return (hyena_out, grad_input, grad_residue)
```

```python
import functools
import math

import jax
import jax.numpy as jnp
from jax import lax
from jax.experimental import pallas as pl
from jax.experimental.pallas import tpu as pltpu
from jax.sharding import PartitionSpec as P


def precise(form, left, right):
    return jnp.einsum(
        form, left, right, precision=lax.Precision.HIGHEST, preferred_element_type=jnp.float32
    )


def tripled(form, left, right):
    return jnp.einsum(
        form, left, right, precision=lax.Precision.HIGH, preferred_element_type=jnp.float32
    )


def angle_table(row_count, col_count, period):
    product = (
        jnp.arange(row_count, dtype=jnp.int32)[:, None]
        * jnp.arange(col_count, dtype=jnp.int32)[None, :]
        % period
    )
    angles = product.astype(jnp.float32) * (2.0 * math.pi / period)
    return (jnp.cos(angles), jnp.sin(angles))


def make_tables(length):
    padded = 2 * length
    outer = math.gcd(padded, 1 << (padded.bit_length() - 1) // 2)
    inner = padded // outer
    cos_outer, sin_outer = angle_table(outer, outer, outer)
    cos_inner, sin_inner = angle_table(inner, inner, inner)
    twist_cos, twist_sin = angle_table(outer, inner, padded)
    return (outer, inner, cos_outer, sin_outer, cos_inner, sin_inner, twist_cos, twist_sin)


def spectrum(signal, tables, product):
    outer, inner, cos_outer, sin_outer, cos_inner, sin_inner, twist_cos, twist_sin = tables
    half_rows = outer // 2
    blocks = signal.reshape(signal.shape[0], half_rows, inner)
    first_re = product("kp,bpq->bkq", cos_outer[:, :half_rows], blocks)
    first_im = -product("kp,bpq->bkq", sin_outer[:, :half_rows], blocks)
    turned_re = first_re * twist_cos + first_im * twist_sin
    turned_im = first_im * twist_cos - first_re * twist_sin
    spec_re = product("bkq,qj->bkj", turned_re, cos_inner) + product(
        "bkq,qj->bkj", turned_im, sin_inner
    )
    spec_im = product("bkq,qj->bkj", turned_im, cos_inner) - product(
        "bkq,qj->bkj", turned_re, sin_inner
    )
    return (spec_re, spec_im)


def signal_of(spec_re, spec_im, tables):
    outer, inner, cos_outer, sin_outer, cos_inner, sin_inner, twist_cos, twist_sin = tables
    half_rows = outer // 2
    back_re = tripled("bkj,jq->bkq", spec_re, cos_inner) - tripled(
        "bkj,jq->bkq", spec_im, sin_inner
    )
    back_im = tripled("bkj,jq->bkq", spec_im, cos_inner) + tripled(
        "bkj,jq->bkq", spec_re, sin_inner
    )
    turned_re = back_re * twist_cos - back_im * twist_sin
    turned_im = back_im * twist_cos + back_re * twist_sin
    values = tripled("pk,bkq->bpq", cos_outer[:half_rows, :], turned_re) - tripled(
        "pk,bkq->bpq", sin_outer[:half_rows, :], turned_im
    )
    return values.reshape(values.shape[0], half_rows * inner) * (1.0 / (outer * inner))


def spec_product(left_re, left_im, right_re, right_im):
    return (left_re * right_re - left_im * right_im, left_re * right_im + left_im * right_re)


def conj_product(left_re, left_im, right_re, right_im):
    return (left_re * right_re + left_im * right_im, left_re * right_im - left_im * right_re)


def filter_basis(residue_loc, rate_loc, length):
    position = jnp.arange(length, dtype=jnp.float32)
    basis_all = jnp.sqrt(2.0 * rate_loc)[:, :, None] * jnp.exp(
        -rate_loc[:, :, None] * position[None, None, :]
    )
    return (basis_all, precise("cm,cmt->ct", residue_loc, basis_all))


def forward_cols(gated_cols, taps_re, taps_im, tables):
    gated_re, gated_im = spectrum(gated_cols.astype(jnp.float32), tables, tripled)
    conv_re, conv_im = spec_product(gated_re, gated_im, taps_re, taps_im)
    conv_cols = signal_of(conv_re, conv_im, tables).astype(jnp.bfloat16)
    return (conv_cols, gated_re, gated_im)


def backward_cols(slope_cols, gated_re, gated_im, taps_re, taps_im, basis_all, tables, length):
    slope_re, slope_im = spectrum(slope_cols.astype(jnp.float32), tables, tripled)
    grad_re, grad_im = conj_product(taps_re, taps_im, slope_re, slope_im)
    back_cols = signal_of(grad_re, grad_im, tables).astype(jnp.bfloat16)
    lag_re, lag_im = conj_product(gated_re, gated_im, slope_re, slope_im)
    taps_grad = signal_of(lag_re, lag_im, tables)
    grad_residue = precise("ct,cmt->cm", taps_grad, basis_all) * (1.0 / math.sqrt(length))
    return (back_cols, grad_residue)


def gather_weights(tokens, weights, residues, decay_rates, cotangent):
    gathered = lax.all_gather(weights, "ctx", axis=1, tiled=True)
    projected = jnp.einsum("xcpd,td->xcpt", gathered, tokens, preferred_element_type=jnp.float32)
    features = projected[0].astype(jnp.bfloat16)
    query_f = features[:, 0].astype(jnp.float32)
    key_part = features[:, 1].astype(jnp.float32)
    value_part = features[:, 2].astype(jnp.float32)
    gated_in = (key_part * value_part).astype(jnp.bfloat16)
    slope_in = (cotangent.astype(jnp.float32) * query_f).astype(jnp.bfloat16)
    length = tokens.shape[0] * lax.axis_size("ctx")
    tables = make_tables(length)
    basis_all, taps_full = filter_basis(residues[0], decay_rates[0], length)
    taps_re, taps_im = spectrum(taps_full, tables, precise)
    gated_cols = lax.all_to_all(gated_in, "ctx", split_axis=0, concat_axis=1, tiled=True)
    conv_cols, gated_re, gated_im = forward_cols(gated_cols, taps_re, taps_im, tables)
    conv_rows = lax.all_to_all(conv_cols, "ctx", split_axis=1, concat_axis=0, tiled=True)
    slope_cols = lax.all_to_all(slope_in, "ctx", split_axis=0, concat_axis=1, tiled=True)
    back_cols, grad_residue = backward_cols(
        slope_cols, gated_re, gated_im, taps_re, taps_im, basis_all, tables, length
    )
    back_rows = lax.all_to_all(back_cols, "ctx", split_axis=1, concat_axis=0, tiled=True)
    conv_f = conv_rows.astype(jnp.float32)
    back_f = back_rows.astype(jnp.float32)
    hyena_out = (query_f * conv_f).astype(jnp.bfloat16)
    grad_query = (cotangent.astype(jnp.float32) * conv_f).astype(jnp.bfloat16)
    grad_key = (back_f * value_part).astype(jnp.bfloat16)
    grad_value = (back_f * key_part).astype(jnp.bfloat16)
    grad_proj = jnp.stack([grad_query, grad_key, grad_value], axis=1)
    partial_value = jnp.einsum(
        "cpt,cpd->td", grad_proj, gathered[0], preferred_element_type=jnp.float32
    )
    grad_input = lax.psum_scatter(
        partial_value.astype(jnp.bfloat16), "tp", scatter_dimension=1, tiled=True
    )
    return (hyena_out, grad_input, grad_residue[None])


GROUP = 4


def rounded(value):
    return value.astype(jnp.bfloat16).astype(jnp.float32)


def earlier_sum(finals, rate, span, back):
    count = finals.shape[0]
    row = lax.broadcasted_iota(jnp.int32, finals.shape, 0)

    def shifted(value, by):
        if back:
            moved = pltpu.roll(value, count - by, 0)
            return jnp.where(row < count - by, moved, 0.0)
        moved = pltpu.roll(value, by, 0)
        return jnp.where(row >= by, moved, 0.0)

    total = shifted(finals, 1)
    by = 1
    while by < count:
        total = total + jnp.exp(rate * (-1.0 * span * by)) * shifted(total, by)
        by *= 2
    return total


def scan_kernel(
    chunks,
    own_ref,
    other_ref,
    cot_ref,
    residue_ref,
    rate_ref,
    hyena_ref,
    proj_ref,
    grad_ref,
    gated_s,
    slope_s,
    conv_s,
    back_s,
):
    length, width = cot_ref.shape
    span = length // chunks
    modes = rate_ref.shape[0]

    def parts(index):
        rows = pl.ds(pl.multiple_of(index * span, span), span)
        feats = own_ref[rows, :] + other_ref[rows, :].astype(jnp.float32)
        feats = rounded(feats)
        cot = cot_ref[rows, :].astype(jnp.float32)
        return rows, feats[:, :width], feats[:, width : 2 * width], feats[:, 2 * width :], cot

    def before(index, _):
        _, query, key, value, cot = parts(index)
        gated_s[pl.ds(index, span, stride=chunks), :] = rounded(key * value)
        slope_s[pl.ds(index, span, stride=chunks), :] = rounded(cot * query)
        return 0

    lax.fori_loop(0, chunks, before, 0)

    def at(step):
        return pl.ds(pl.multiple_of(step * chunks, chunks), chunks)

    zero = jnp.zeros((chunks, width), jnp.float32)
    scale = 1.0 / math.sqrt(length)
    for first in range(0, modes, GROUP):
        count = min(GROUP, modes - first)
        rates = [
            jnp.broadcast_to(rate_ref[m : m + 1, :], (chunks, width))
            for m in range(first, first + count)
        ]
        decays = [jnp.exp(-rate) for rate in rates]
        norms = [jnp.sqrt(2.0 * rate) for rate in rates]
        gains = [
            residue_ref[first + n : first + n + 1, :] * norms[n] for n in range(count)
        ]

        def sums(step, state):
            ahead, behind = state
            gated = gated_s[at(step), :]
            slope = slope_s[at(span - 1 - step), :]
            return (
                tuple(decays[n] * ahead[n] + gated for n in range(count)),
                tuple(decays[n] * behind[n] + slope for n in range(count)),
            )

        ahead, behind = lax.fori_loop(0, span, sums, ((zero,) * count, (zero,) * count), unroll=4)
        ahead = tuple(earlier_sum(ahead[n], rates[n], span, False) for n in range(count))
        behind = tuple(earlier_sum(behind[n], rates[n], span, True) for n in range(count))

        def outs(step, state):
            ahead, behind, grads = state
            other = span - 1 - step
            gated = gated_s[at(step), :]
            slope = slope_s[at(step), :]
            slope_back = slope_s[at(other), :]
            ahead = tuple(decays[n] * ahead[n] + gated for n in range(count))
            behind = tuple(decays[n] * behind[n] + slope_back for n in range(count))
            grads = tuple(grads[n] + slope * ahead[n] for n in range(count))
            conv = sum(gains[n] * ahead[n] for n in range(count))
            back = sum(gains[n] * behind[n] for n in range(count))
            if first:
                conv = conv + conv_s[at(step), :]
                back = back + back_s[at(other), :]
            conv_s[at(step), :] = conv
            back_s[at(other), :] = back
            return ahead, behind, grads

        _, _, grads = lax.fori_loop(0, span, outs, (ahead, behind, (zero,) * count), unroll=2)
        for n in range(count):
            total = jnp.sum(grads[n] * norms[n], axis=0, keepdims=True) * scale
            grad_ref[first + n : first + n + 1, :] = total

    def after(index, _):
        rows, query, key, value, cot = parts(index)
        conv = rounded(conv_s[pl.ds(index, span, stride=chunks), :])
        back = rounded(back_s[pl.ds(index, span, stride=chunks), :])
        hyena_ref[rows, :] = (query * conv).astype(jnp.bfloat16)
        proj_ref[rows, :width] = (cot * conv).astype(jnp.bfloat16)
        proj_ref[rows, width : 2 * width] = (back * value).astype(jnp.bfloat16)
        proj_ref[rows, 2 * width :] = (back * key).astype(jnp.bfloat16)
        return 0

    lax.fori_loop(0, chunks, after, 0)


def scan_all(own, other, cot_cols, residue_rows, rate_rows, chunks):
    length, width = cot_cols.shape
    vmem = pl.BlockSpec(memory_space=pltpu.VMEM)
    return pl.pallas_call(
        functools.partial(scan_kernel, chunks),
        out_shape=(
            jax.ShapeDtypeStruct((length, width), jnp.bfloat16),
            jax.ShapeDtypeStruct((length, 3 * width), jnp.bfloat16),
            jax.ShapeDtypeStruct(rate_rows.shape, jnp.float32),
        ),
        in_specs=[vmem] * 5,
        out_specs=[vmem] * 3,
        scratch_shapes=[pltpu.VMEM((length, width), jnp.float32)] * 4,
        compiler_params=pltpu.CompilerParams(vmem_limit_bytes=40 * 2**20),
        name="modal_scan",
    )(own, other, cot_cols, residue_rows, rate_rows)


def swapped(value):
    return lax.ppermute(value, "tp", [(0, 1), (1, 0)])


def gather_tokens(tokens, weights, residues, decay_rates, cotangent):
    core = lax.axis_index("tp")
    ctx = lax.axis_size("ctx")
    half = tokens.shape[1] // 2
    channels = weights.shape[1]
    rows = weights[0].swapaxes(0, 1).reshape(3 * channels, 2 * half)
    kept = lax.dynamic_slice_in_dim(rows, core * half, half, 1)
    taken = swapped(lax.dynamic_slice_in_dim(rows, (1 - core) * half, half, 1))
    tokens_half = lax.dynamic_slice_in_dim(tokens, core * half, half, 1)
    cot_cols = lax.all_to_all(cotangent.T, "ctx", split_axis=1, concat_axis=0, tiled=True)
    gathered = lax.all_gather(tokens_half, "ctx", axis=0, tiled=True)

    def project(matrix):
        return jnp.einsum("td,rd->tr", gathered, matrix, preferred_element_type=jnp.float32)

    other = swapped(project(taken))
    own = project(kept)
    hyena, proj, grads = scan_all(own, other, cot_cols, residues[0].T, decay_rates[0].T, ctx)
    hyena_out = lax.all_to_all(hyena, "ctx", split_axis=0, concat_axis=1, tiled=True).T
    proj_other = swapped(proj)
    partial_value = jnp.einsum(
        "tr,rd->td",
        jnp.concatenate([proj, proj_other], axis=1),
        jnp.concatenate([kept, taken], axis=0),
        preferred_element_type=jnp.float32,
    )
    grad_input = lax.psum_scatter(
        partial_value.astype(jnp.bfloat16), "ctx", scatter_dimension=0, tiled=True
    )
    return (hyena_out, grad_input, grads.T[None])


def shards(tokens, weights, residues, decay_rates, cotangent):
    ctx, tp = lax.axis_size("ctx"), lax.axis_size("tp")
    if tp == 2 and weights.size * tp > 2 * tokens.size:
        return gather_tokens(tokens, weights, residues, decay_rates, cotangent)
    return gather_weights(tokens, weights, residues, decay_rates, cotangent)


def solution(mesh):
    return jax.shard_map(
        shards,
        mesh=mesh,
        in_specs=(
            P("ctx", None),
            P("tp", "ctx", None, None),
            P("tp", "ctx", None),
            P("tp", "ctx", None),
            P("tp", "ctx"),
        ),
        out_specs=(P("tp", "ctx"), P("ctx", "tp"), P("tp", "ctx", None)),
        check_vma=False,
    )
```

```python
import functools
import math

import jax
import jax.numpy as jnp
from jax import lax
from jax.experimental import pallas as pl
from jax.experimental.pallas import tpu as pltpu
from jax.sharding import PartitionSpec as P


def precise(form, left, right):
    return jnp.einsum(
        form, left, right, precision=lax.Precision.HIGHEST, preferred_element_type=jnp.float32
    )


def tripled(form, left, right):
    return jnp.einsum(
        form, left, right, precision=lax.Precision.HIGH, preferred_element_type=jnp.float32
    )


def angle_table(row_count, col_count, period):
    product = (
        jnp.arange(row_count, dtype=jnp.int32)[:, None]
        * jnp.arange(col_count, dtype=jnp.int32)[None, :]
        % period
    )
    angles = product.astype(jnp.float32) * (2.0 * math.pi / period)
    return (jnp.cos(angles), jnp.sin(angles))


def make_tables(length):
    padded = 2 * length
    outer = math.gcd(padded, 1 << (padded.bit_length() - 1) // 2)
    inner = padded // outer
    cos_outer, sin_outer = angle_table(outer, outer, outer)
    cos_inner, sin_inner = angle_table(inner, inner, inner)
    twist_cos, twist_sin = angle_table(outer, inner, padded)
    return (outer, inner, cos_outer, sin_outer, cos_inner, sin_inner, twist_cos, twist_sin)


def spectrum(signal, tables, product):
    outer, inner, cos_outer, sin_outer, cos_inner, sin_inner, twist_cos, twist_sin = tables
    half_rows = outer // 2
    blocks = signal.reshape(signal.shape[0], half_rows, inner)
    first_re = product("kp,bpq->bkq", cos_outer[:, :half_rows], blocks)
    first_im = -product("kp,bpq->bkq", sin_outer[:, :half_rows], blocks)
    turned_re = first_re * twist_cos + first_im * twist_sin
    turned_im = first_im * twist_cos - first_re * twist_sin
    spec_re = product("bkq,qj->bkj", turned_re, cos_inner) + product(
        "bkq,qj->bkj", turned_im, sin_inner
    )
    spec_im = product("bkq,qj->bkj", turned_im, cos_inner) - product(
        "bkq,qj->bkj", turned_re, sin_inner
    )
    return (spec_re, spec_im)


def signal_of(spec_re, spec_im, tables):
    outer, inner, cos_outer, sin_outer, cos_inner, sin_inner, twist_cos, twist_sin = tables
    half_rows = outer // 2
    back_re = tripled("bkj,jq->bkq", spec_re, cos_inner) - tripled(
        "bkj,jq->bkq", spec_im, sin_inner
    )
    back_im = tripled("bkj,jq->bkq", spec_im, cos_inner) + tripled(
        "bkj,jq->bkq", spec_re, sin_inner
    )
    turned_re = back_re * twist_cos - back_im * twist_sin
    turned_im = back_im * twist_cos + back_re * twist_sin
    values = tripled("pk,bkq->bpq", cos_outer[:half_rows, :], turned_re) - tripled(
        "pk,bkq->bpq", sin_outer[:half_rows, :], turned_im
    )
    return values.reshape(values.shape[0], half_rows * inner) * (1.0 / (outer * inner))


def spec_product(left_re, left_im, right_re, right_im):
    return (left_re * right_re - left_im * right_im, left_re * right_im + left_im * right_re)


def conj_product(left_re, left_im, right_re, right_im):
    return (left_re * right_re + left_im * right_im, left_re * right_im - left_im * right_re)


def filter_basis(residue_loc, rate_loc, length):
    position = jnp.arange(length, dtype=jnp.float32)
    basis_all = jnp.sqrt(2.0 * rate_loc)[:, :, None] * jnp.exp(
        -rate_loc[:, :, None] * position[None, None, :]
    )
    return (basis_all, precise("cm,cmt->ct", residue_loc, basis_all))


def forward_cols(gated_cols, taps_re, taps_im, tables):
    gated_re, gated_im = spectrum(gated_cols.astype(jnp.float32), tables, tripled)
    conv_re, conv_im = spec_product(gated_re, gated_im, taps_re, taps_im)
    conv_cols = signal_of(conv_re, conv_im, tables).astype(jnp.bfloat16)
    return (conv_cols, gated_re, gated_im)


def backward_cols(slope_cols, gated_re, gated_im, taps_re, taps_im, basis_all, tables, length):
    slope_re, slope_im = spectrum(slope_cols.astype(jnp.float32), tables, tripled)
    grad_re, grad_im = conj_product(taps_re, taps_im, slope_re, slope_im)
    back_cols = signal_of(grad_re, grad_im, tables).astype(jnp.bfloat16)
    lag_re, lag_im = conj_product(gated_re, gated_im, slope_re, slope_im)
    taps_grad = signal_of(lag_re, lag_im, tables)
    grad_residue = precise("ct,cmt->cm", taps_grad, basis_all) * (1.0 / math.sqrt(length))
    return (back_cols, grad_residue)


def gather_weights(tokens, weights, residues, decay_rates, cotangent):
    gathered = lax.all_gather(weights, "ctx", axis=1, tiled=True)
    projected = jnp.einsum("xcpd,td->xcpt", gathered, tokens, preferred_element_type=jnp.float32)
    features = projected[0].astype(jnp.bfloat16)
    query_f = features[:, 0].astype(jnp.float32)
    key_part = features[:, 1].astype(jnp.float32)
    value_part = features[:, 2].astype(jnp.float32)
    gated_in = (key_part * value_part).astype(jnp.bfloat16)
    slope_in = (cotangent.astype(jnp.float32) * query_f).astype(jnp.bfloat16)
    length = tokens.shape[0] * lax.axis_size("ctx")
    tables = make_tables(length)
    basis_all, taps_full = filter_basis(residues[0], decay_rates[0], length)
    taps_re, taps_im = spectrum(taps_full, tables, precise)
    gated_cols = lax.all_to_all(gated_in, "ctx", split_axis=0, concat_axis=1, tiled=True)
    conv_cols, gated_re, gated_im = forward_cols(gated_cols, taps_re, taps_im, tables)
    conv_rows = lax.all_to_all(conv_cols, "ctx", split_axis=1, concat_axis=0, tiled=True)
    slope_cols = lax.all_to_all(slope_in, "ctx", split_axis=0, concat_axis=1, tiled=True)
    back_cols, grad_residue = backward_cols(
        slope_cols, gated_re, gated_im, taps_re, taps_im, basis_all, tables, length
    )
    back_rows = lax.all_to_all(back_cols, "ctx", split_axis=1, concat_axis=0, tiled=True)
    conv_f = conv_rows.astype(jnp.float32)
    back_f = back_rows.astype(jnp.float32)
    hyena_out = (query_f * conv_f).astype(jnp.bfloat16)
    grad_query = (cotangent.astype(jnp.float32) * conv_f).astype(jnp.bfloat16)
    grad_key = (back_f * value_part).astype(jnp.bfloat16)
    grad_value = (back_f * key_part).astype(jnp.bfloat16)
    grad_proj = jnp.stack([grad_query, grad_key, grad_value], axis=1)
    partial_value = jnp.einsum(
        "cpt,cpd->td", grad_proj, gathered[0], preferred_element_type=jnp.float32
    )
    grad_input = lax.psum_scatter(
        partial_value.astype(jnp.bfloat16), "tp", scatter_dimension=1, tiled=True
    )
    return (hyena_out, grad_input, grad_residue[None])


GROUP = 4
PLANE = 4


def rounded(value):
    return value.astype(jnp.bfloat16).astype(jnp.float32)


def earlier_sum(finals, rate, span, back):
    count = finals.shape[0]
    row = lax.broadcasted_iota(jnp.int32, finals.shape, 0)

    def shifted(value, by):
        if back:
            moved = pltpu.roll(value, count - by, 0)
            return jnp.where(row < count - by, moved, 0.0)
        moved = pltpu.roll(value, by, 0)
        return jnp.where(row >= by, moved, 0.0)

    total = shifted(finals, 1)
    by = 1
    while by < count:
        total = total + jnp.exp(rate * (-1.0 * span * by)) * shifted(total, by)
        by *= 2
    return total


def scan_kernel(
    groups,
    me_ref,
    cot_ref,
    residue_ref,
    rate_ref,
    *refs,
):
    wide, narrow = refs[: 2 * groups], refs[2 * groups : 4 * groups]
    hyena_ref, grad_ref = refs[4 * groups : 4 * groups + 2]
    proj_refs = refs[4 * groups + 2 : 5 * groups + 2]
    gated_s, slope_s, conv_s, back_s, feats_s = refs[5 * groups + 2 :]
    length, width = cot_ref.shape
    chunks = PLANE * groups
    span = length // chunks
    modes = rate_ref.shape[0]
    me = me_ref[0]
    sizes = [(wide, 0, wide[0].shape[0] // PLANE)]
    sizes.append((narrow, sizes[0][2], narrow[0].shape[0] // PLANE))

    def place(group, member):
        return lax.rem(me // PLANE + group, groups) * PLANE + (member ^ lax.rem(me, PLANE))

    def aligned(start, size):
        return pl.ds(pl.multiple_of(start, size), size)

    for group in range(groups):

        def before(member, _, group=group):
            index = place(group, member)
            for arrays, first, count in sizes:
                rows = aligned(member * count, count)
                feats = arrays[group][rows, :] + arrays[groups + group][rows, :].astype(jnp.float32)
                feats = rounded(feats)
                slot = (group * PLANE + member) * span + first
                feats_s[pl.ds(pl.multiple_of(slot, 16), count), :] = feats
                cot = cot_ref[pl.ds(pl.multiple_of(index * span + first, 16), count), :]
                query, key = feats[:, :width], feats[:, width : 2 * width]
                into = pl.ds(first * chunks + index, count, stride=chunks)
                gated_s[into, :] = rounded(key * feats[:, 2 * width :])
                slope_s[into, :] = rounded(cot.astype(jnp.float32) * query)
            return 0

        lax.fori_loop(0, PLANE, before, 0)

    def at(step):
        return aligned(step * chunks, chunks)

    zero = jnp.zeros((chunks, width), jnp.float32)
    scale = 1.0 / math.sqrt(length)
    for first in range(0, modes, GROUP):
        count = min(GROUP, modes - first)
        rates = [
            jnp.broadcast_to(rate_ref[m : m + 1, :], (chunks, width))
            for m in range(first, first + count)
        ]
        decays = [jnp.exp(-rate) for rate in rates]
        norms = [jnp.sqrt(2.0 * rate) for rate in rates]
        gains = [
            residue_ref[first + n : first + n + 1, :] * norms[n] for n in range(count)
        ]

        def sums(step, state):
            ahead, behind = state
            gated = gated_s[at(step), :]
            slope = slope_s[at(span - 1 - step), :]
            return (
                tuple(decays[n] * ahead[n] + gated for n in range(count)),
                tuple(decays[n] * behind[n] + slope for n in range(count)),
            )

        ahead, behind = lax.fori_loop(0, span, sums, ((zero,) * count, (zero,) * count), unroll=4)
        ahead = tuple(earlier_sum(ahead[n], rates[n], span, False) for n in range(count))
        behind = tuple(earlier_sum(behind[n], rates[n], span, True) for n in range(count))

        def outs(step, state):
            ahead, behind, grads = state
            other = span - 1 - step
            gated = gated_s[at(step), :]
            slope = slope_s[at(step), :]
            slope_back = slope_s[at(other), :]
            ahead = tuple(decays[n] * ahead[n] + gated for n in range(count))
            behind = tuple(decays[n] * behind[n] + slope_back for n in range(count))
            grads = tuple(grads[n] + slope * ahead[n] for n in range(count))
            conv = sum(gains[n] * ahead[n] for n in range(count))
            back = sum(gains[n] * behind[n] for n in range(count))
            if first:
                conv = conv + conv_s[at(step), :]
                back = back + back_s[at(other), :]
            conv_s[at(step), :] = conv
            back_s[at(other), :] = back
            return ahead, behind, grads

        _, _, grads = lax.fori_loop(0, span, outs, (ahead, behind, (zero,) * count), unroll=2)
        for n in range(count):
            total = jnp.sum(grads[n] * norms[n], axis=0, keepdims=True) * scale
            grad_ref[first + n : first + n + 1, :] = total

    for group in range(groups):

        def after(member, _, group=group):
            index = place(group, member)
            feats = feats_s[aligned((group * PLANE + member) * span, span), :]
            query, key, value = feats[:, :width], feats[:, width : 2 * width], feats[:, 2 * width :]
            cot = cot_ref[aligned(index * span, span), :].astype(jnp.float32)
            conv = rounded(conv_s[pl.ds(index, span, stride=chunks), :])
            back = rounded(back_s[pl.ds(index, span, stride=chunks), :])
            hyena_ref[aligned(index * span, span), :] = (query * conv).astype(jnp.bfloat16)
            rows = aligned(member * span, span)
            proj_refs[group][rows, :width] = (cot * conv).astype(jnp.bfloat16)
            proj_refs[group][rows, width : 2 * width] = (back * value).astype(jnp.bfloat16)
            proj_refs[group][rows, 2 * width :] = (back * key).astype(jnp.bfloat16)
            return 0

        lax.fori_loop(0, PLANE, after, 0)


def scan_all(me, cot_cols, residue_rows, rate_rows, wide, narrow):
    groups = len(wide) // 2
    length, width = cot_cols.shape
    vmem = pl.BlockSpec(memory_space=pltpu.VMEM)
    group_rows = length // groups
    outs = pl.pallas_call(
        functools.partial(scan_kernel, groups),
        out_shape=(
            jax.ShapeDtypeStruct((length, width), jnp.bfloat16),
            jax.ShapeDtypeStruct(rate_rows.shape, jnp.float32),
        )
        + (jax.ShapeDtypeStruct((group_rows, 3 * width), jnp.bfloat16),) * groups,
        in_specs=[pl.BlockSpec(memory_space=pltpu.SMEM)] + [vmem] * (3 + 4 * groups),
        out_specs=(vmem,) * (2 + groups),
        scratch_shapes=[pltpu.VMEM((length, width), jnp.float32)] * 4
        + [pltpu.VMEM((length, 3 * width), jnp.float32)],
        compiler_params=pltpu.CompilerParams(vmem_limit_bytes=40 * 2**20),
        name="modal_scan",
    )(me, cot_cols, residue_rows, rate_rows, *wide, *narrow)
    return outs[0], outs[1], outs[2:]


def swapped(value):
    return lax.ppermute(value, "tp", [(0, 1), (1, 0)])


def over_x(value):
    return lax.ppermute(value, "ctx", [(i, i ^ 1) for i in range(lax.axis_size("ctx"))])


def over_y(value):
    return lax.ppermute(value, "ctx", [(i, i ^ 2) for i in range(lax.axis_size("ctx"))])


def up(value):
    count = lax.axis_size("ctx")
    return lax.ppermute(value, "ctx", [(i, (i + PLANE) % count) for i in range(count)])


def down(value):
    count = lax.axis_size("ctx")
    return lax.ppermute(value, "ctx", [((i + PLANE) % count, i) for i in range(count)])


def plane_gather(own):
    half = own.shape[0] // 2
    from_x, from_y = over_x(own), over_y(own)
    across = [over_x(from_y[:half]), over_y(from_x[half:])]
    return jnp.concatenate([own, from_x, from_y] + across, axis=0)


def depth_gather(own):
    half = own.shape[0] // 2
    above, below = down(own), up(own)
    far = jnp.concatenate([up(below[:half]), down(above[half:])], axis=0)
    return [own, above, far, below]


def narrowed(value):
    return value.astype(jnp.bfloat16)


def plane_scatter(term):
    for_y = over_x(narrowed(term(3, 0)))
    for_x = over_y(narrowed(term(3, 1)))
    x_first = over_x(narrowed(term(1, 0)))
    y_second = over_y(narrowed(term(2, 1)))
    x_second = over_x(narrowed(term(1, 1) + for_x.astype(jnp.float32)))
    y_first = over_y(narrowed(term(2, 0) + for_y.astype(jnp.float32)))
    first = term(0, 0) + x_first.astype(jnp.float32) + y_first.astype(jnp.float32)
    second = term(0, 1) + x_second.astype(jnp.float32) + y_second.astype(jnp.float32)
    return first, second


def depth_scatter(term):
    for_above = up(narrowed(term(2, 0)))
    for_below = down(narrowed(term(2, 1)))
    up_second = up(narrowed(term(1, 1)))
    down_first = down(narrowed(term(3, 0)))
    up_first = up(narrowed(term(1, 0) + for_above.astype(jnp.float32)))
    down_second = down(narrowed(term(3, 1) + for_below.astype(jnp.float32)))
    first = term(0, 0) + up_first.astype(jnp.float32) + down_first.astype(jnp.float32)
    second = term(0, 1) + up_second.astype(jnp.float32) + down_second.astype(jnp.float32)
    return first, second


def gather_tokens(tokens, weights, residues, decay_rates, cotangent):
    core = lax.axis_index("tp")
    me = lax.axis_index("ctx").astype(jnp.int32).reshape(1)
    span = tokens.shape[0]
    half = tokens.shape[1] // 2
    channels = weights.shape[1]
    wide_rows = span * 3 // 4
    tokens_half = lax.dynamic_slice_in_dim(tokens, core * half, half, 1)
    narrow_groups = depth_gather(plane_gather(tokens_half[wide_rows:]))
    wide_groups = [plane_gather(part) for part in depth_gather(tokens_half[:wide_rows])]
    rows = weights[0].swapaxes(0, 1).reshape(3 * channels, 2 * half)
    kept = lax.dynamic_slice_in_dim(rows, core * half, half, 1)
    taken = swapped(lax.dynamic_slice_in_dim(rows, (1 - core) * half, half, 1))
    cot_cols = lax.all_to_all(cotangent.T, "ctx", split_axis=1, concat_axis=0, tiled=True)

    def project(part, matrix):
        return jnp.einsum("td,rd->tr", part, matrix, preferred_element_type=jnp.float32)

    def projected(parts):
        other = [swapped(project(part, taken)) for part in parts]
        return [project(part, kept) for part in parts] + other

    hyena, grads, own_proj = scan_all(
        me, cot_cols, residues[0].T, decay_rates[0].T, projected(wide_groups), projected(narrow_groups)
    )
    hyena_out = lax.all_to_all(hyena, "ctx", split_axis=0, concat_axis=1, tiled=True).T
    proj = [jnp.concatenate([part, swapped(part)], axis=1) for part in own_proj]
    matrix = jnp.concatenate([kept, taken], axis=0)
    wide_cols = half * 3 // 4

    def product(left, first, count):
        right = matrix[:, first : first + count]
        return jnp.dot(left, right, preferred_element_type=jnp.float32)

    def wide_plane(group):
        count = wide_cols // 2
        return plane_scatter(
            lambda member, side: product(
                proj[group][member * span : (member + 1) * span], side * count, count
            )
        )

    planes = {group: wide_plane(group) for group in (2, 1, 3, 0)}
    wide_sum = depth_scatter(lambda group, side: planes[group][side])
    count = (half - wide_cols) // 2
    depth = depth_scatter(
        lambda group, side: product(proj[group], wide_cols + side * count, count)
    )
    narrow_sum = plane_scatter(
        lambda member, side: depth[side][member * span : (member + 1) * span]
    )
    grad_input = jnp.concatenate([narrowed(part) for part in wide_sum + narrow_sum], axis=1)
    return (hyena_out, grad_input, grads.T[None])


def shards(tokens, weights, residues, decay_rates, cotangent):
    ctx, tp = lax.axis_size("ctx"), lax.axis_size("tp")
    if ctx == 4 * PLANE and tp == 2 and weights.size * tp > 2 * tokens.size:
        return gather_tokens(tokens, weights, residues, decay_rates, cotangent)
    return gather_weights(tokens, weights, residues, decay_rates, cotangent)


def solution(mesh):
    return jax.shard_map(
        shards,
        mesh=mesh,
        in_specs=(
            P("ctx", None),
            P("tp", "ctx", None, None),
            P("tp", "ctx", None),
            P("tp", "ctx", None),
            P("tp", "ctx"),
        ),
        out_specs=(P("tp", "ctx"), P("ctx", "tp"), P("tp", "ctx", None)),
        check_vma=False,
    )
```

```python
import functools
import math

import jax
import jax.numpy as jnp
from jax import lax
from jax.experimental import pallas as pl
from jax.experimental.pallas import tpu as pltpu
from jax.sharding import PartitionSpec as P


def precise(form, left, right):
    return jnp.einsum(
        form, left, right, precision=lax.Precision.HIGHEST, preferred_element_type=jnp.float32
    )


def tripled(form, left, right):
    return jnp.einsum(
        form, left, right, precision=lax.Precision.HIGH, preferred_element_type=jnp.float32
    )


def angle_table(row_count, col_count, period):
    product = (
        jnp.arange(row_count, dtype=jnp.int32)[:, None]
        * jnp.arange(col_count, dtype=jnp.int32)[None, :]
        % period
    )
    angles = product.astype(jnp.float32) * (2.0 * math.pi / period)
    return (jnp.cos(angles), jnp.sin(angles))


def make_tables(length):
    padded = 2 * length
    outer = math.gcd(padded, 1 << (padded.bit_length() - 1) // 2)
    inner = padded // outer
    cos_outer, sin_outer = angle_table(outer, outer, outer)
    cos_inner, sin_inner = angle_table(inner, inner, inner)
    twist_cos, twist_sin = angle_table(outer, inner, padded)
    return (outer, inner, cos_outer, sin_outer, cos_inner, sin_inner, twist_cos, twist_sin)


def spectrum(signal, tables, product):
    outer, inner, cos_outer, sin_outer, cos_inner, sin_inner, twist_cos, twist_sin = tables
    half_rows = outer // 2
    blocks = signal.reshape(signal.shape[0], half_rows, inner)
    first_re = product("kp,bpq->bkq", cos_outer[:, :half_rows], blocks)
    first_im = -product("kp,bpq->bkq", sin_outer[:, :half_rows], blocks)
    turned_re = first_re * twist_cos + first_im * twist_sin
    turned_im = first_im * twist_cos - first_re * twist_sin
    spec_re = product("bkq,qj->bkj", turned_re, cos_inner) + product(
        "bkq,qj->bkj", turned_im, sin_inner
    )
    spec_im = product("bkq,qj->bkj", turned_im, cos_inner) - product(
        "bkq,qj->bkj", turned_re, sin_inner
    )
    return (spec_re, spec_im)


def signal_of(spec_re, spec_im, tables):
    outer, inner, cos_outer, sin_outer, cos_inner, sin_inner, twist_cos, twist_sin = tables
    half_rows = outer // 2
    back_re = tripled("bkj,jq->bkq", spec_re, cos_inner) - tripled(
        "bkj,jq->bkq", spec_im, sin_inner
    )
    back_im = tripled("bkj,jq->bkq", spec_im, cos_inner) + tripled(
        "bkj,jq->bkq", spec_re, sin_inner
    )
    turned_re = back_re * twist_cos - back_im * twist_sin
    turned_im = back_im * twist_cos + back_re * twist_sin
    values = tripled("pk,bkq->bpq", cos_outer[:half_rows, :], turned_re) - tripled(
        "pk,bkq->bpq", sin_outer[:half_rows, :], turned_im
    )
    return values.reshape(values.shape[0], half_rows * inner) * (1.0 / (outer * inner))


def spec_product(left_re, left_im, right_re, right_im):
    return (left_re * right_re - left_im * right_im, left_re * right_im + left_im * right_re)


def conj_product(left_re, left_im, right_re, right_im):
    return (left_re * right_re + left_im * right_im, left_re * right_im - left_im * right_re)


def filter_basis(residue_loc, rate_loc, length):
    position = jnp.arange(length, dtype=jnp.float32)
    basis_all = jnp.sqrt(2.0 * rate_loc)[:, :, None] * jnp.exp(
        -rate_loc[:, :, None] * position[None, None, :]
    )
    return (basis_all, precise("cm,cmt->ct", residue_loc, basis_all))


def forward_cols(gated_cols, taps_re, taps_im, tables):
    gated_re, gated_im = spectrum(gated_cols.astype(jnp.float32), tables, tripled)
    conv_re, conv_im = spec_product(gated_re, gated_im, taps_re, taps_im)
    conv_cols = signal_of(conv_re, conv_im, tables).astype(jnp.bfloat16)
    return (conv_cols, gated_re, gated_im)


def backward_cols(slope_cols, gated_re, gated_im, taps_re, taps_im, basis_all, tables, length):
    slope_re, slope_im = spectrum(slope_cols.astype(jnp.float32), tables, tripled)
    grad_re, grad_im = conj_product(taps_re, taps_im, slope_re, slope_im)
    back_cols = signal_of(grad_re, grad_im, tables).astype(jnp.bfloat16)
    lag_re, lag_im = conj_product(gated_re, gated_im, slope_re, slope_im)
    taps_grad = signal_of(lag_re, lag_im, tables)
    grad_residue = precise("ct,cmt->cm", taps_grad, basis_all) * (1.0 / math.sqrt(length))
    return (back_cols, grad_residue)


def gather_weights(tokens, weights, residues, decay_rates, cotangent):
    gathered = lax.all_gather(weights, "ctx", axis=1, tiled=True)
    projected = jnp.einsum("xcpd,td->xcpt", gathered, tokens, preferred_element_type=jnp.float32)
    features = projected[0].astype(jnp.bfloat16)
    query_f = features[:, 0].astype(jnp.float32)
    key_part = features[:, 1].astype(jnp.float32)
    value_part = features[:, 2].astype(jnp.float32)
    gated_in = (key_part * value_part).astype(jnp.bfloat16)
    slope_in = (cotangent.astype(jnp.float32) * query_f).astype(jnp.bfloat16)
    length = tokens.shape[0] * lax.axis_size("ctx")
    tables = make_tables(length)
    basis_all, taps_full = filter_basis(residues[0], decay_rates[0], length)
    taps_re, taps_im = spectrum(taps_full, tables, precise)
    gated_cols = lax.all_to_all(gated_in, "ctx", split_axis=0, concat_axis=1, tiled=True)
    conv_cols, gated_re, gated_im = forward_cols(gated_cols, taps_re, taps_im, tables)
    conv_rows = lax.all_to_all(conv_cols, "ctx", split_axis=1, concat_axis=0, tiled=True)
    slope_cols = lax.all_to_all(slope_in, "ctx", split_axis=0, concat_axis=1, tiled=True)
    back_cols, grad_residue = backward_cols(
        slope_cols, gated_re, gated_im, taps_re, taps_im, basis_all, tables, length
    )
    back_rows = lax.all_to_all(back_cols, "ctx", split_axis=1, concat_axis=0, tiled=True)
    conv_f = conv_rows.astype(jnp.float32)
    back_f = back_rows.astype(jnp.float32)
    hyena_out = (query_f * conv_f).astype(jnp.bfloat16)
    grad_query = (cotangent.astype(jnp.float32) * conv_f).astype(jnp.bfloat16)
    grad_key = (back_f * value_part).astype(jnp.bfloat16)
    grad_value = (back_f * key_part).astype(jnp.bfloat16)
    grad_proj = jnp.stack([grad_query, grad_key, grad_value], axis=1)
    partial_value = jnp.einsum(
        "cpt,cpd->td", grad_proj, gathered[0], preferred_element_type=jnp.float32
    )
    grad_input = lax.psum_scatter(
        partial_value.astype(jnp.bfloat16), "tp", scatter_dimension=1, tiled=True
    )
    return (hyena_out, grad_input, grad_residue[None])


GROUP = 4
PLANE = 4


def rounded(value):
    return value.astype(jnp.bfloat16).astype(jnp.float32)


def earlier_sum(finals, rate, span, back):
    count = finals.shape[0]
    row = lax.broadcasted_iota(jnp.int32, finals.shape, 0)

    def shifted(value, by):
        if back:
            moved = pltpu.roll(value, count - by, 0)
            return jnp.where(row < count - by, moved, 0.0)
        moved = pltpu.roll(value, by, 0)
        return jnp.where(row >= by, moved, 0.0)

    total = shifted(finals, 1)
    by = 1
    while by < count:
        total = total + jnp.exp(rate * (-1.0 * span * by)) * shifted(total, by)
        by *= 2
    return total


def scan_kernel(
    groups,
    runs,
    me_ref,
    cot_ref,
    residue_ref,
    rate_ref,
    *refs,
):
    inputs = 1 + max(run[0] for run in runs)
    own, other = refs[:inputs], refs[inputs : 2 * inputs]
    hyena_ref, grad_ref = refs[2 * inputs : 2 * inputs + 2]
    proj_refs = refs[2 * inputs + 2 : 2 * inputs + 2 + groups]
    gated_s, slope_s, conv_s, back_s, feats_s = refs[2 * inputs + 2 + groups :]
    length, width = cot_ref.shape
    chunks = PLANE * groups
    span = length // chunks
    modes = rate_ref.shape[0]
    me = me_ref[0]

    def place(group, member):
        return lax.rem(me // PLANE + group, groups) * PLANE + (member ^ lax.rem(me, PLANE))

    def aligned(start, size):
        return pl.ds(pl.multiple_of(start, size), size)

    for source, offset, group, base, members, count, first in runs:

        def before(step, _, source=source, offset=offset, group=group, base=base, count=count, first=first):
            member = base + step
            index = place(group, member)
            rows = pl.ds(pl.multiple_of(offset + step * count, 32), count)
            feats = rounded(own[source][rows, :] + other[source][rows, :].astype(jnp.float32))
            slot = (group * PLANE + member) * span + first
            feats_s[pl.ds(pl.multiple_of(slot, 32), count), :] = feats
            cot = cot_ref[pl.ds(pl.multiple_of(index * span + first, 32), count), :]
            query, key = feats[:, :width], feats[:, width : 2 * width]
            into = pl.ds(first * chunks + index, count, stride=chunks)
            gated_s[into, :] = rounded(key * feats[:, 2 * width :])
            slope_s[into, :] = rounded(cot.astype(jnp.float32) * query)
            return 0

        lax.fori_loop(0, members, before, 0)

    def at(step):
        return aligned(step * chunks, chunks)

    zero = jnp.zeros((chunks, width), jnp.float32)
    scale = 1.0 / math.sqrt(length)
    for first in range(0, modes, GROUP):
        count = min(GROUP, modes - first)
        rates = [
            jnp.broadcast_to(rate_ref[m : m + 1, :], (chunks, width))
            for m in range(first, first + count)
        ]
        decays = [jnp.exp(-rate) for rate in rates]
        norms = [jnp.sqrt(2.0 * rate) for rate in rates]
        gains = [
            residue_ref[first + n : first + n + 1, :] * norms[n] for n in range(count)
        ]

        def sums(step, state):
            ahead, behind = state
            gated = gated_s[at(step), :]
            slope = slope_s[at(span - 1 - step), :]
            return (
                tuple(decays[n] * ahead[n] + gated for n in range(count)),
                tuple(decays[n] * behind[n] + slope for n in range(count)),
            )

        ahead, behind = lax.fori_loop(0, span, sums, ((zero,) * count, (zero,) * count), unroll=4)
        ahead = tuple(earlier_sum(ahead[n], rates[n], span, False) for n in range(count))
        behind = tuple(earlier_sum(behind[n], rates[n], span, True) for n in range(count))

        def outs(step, state):
            ahead, behind, grads = state
            other = span - 1 - step
            gated = gated_s[at(step), :]
            slope = slope_s[at(step), :]
            slope_back = slope_s[at(other), :]
            ahead = tuple(decays[n] * ahead[n] + gated for n in range(count))
            behind = tuple(decays[n] * behind[n] + slope_back for n in range(count))
            grads = tuple(grads[n] + slope * ahead[n] for n in range(count))
            conv = sum(gains[n] * ahead[n] for n in range(count))
            back = sum(gains[n] * behind[n] for n in range(count))
            if first:
                conv = conv + conv_s[at(step), :]
                back = back + back_s[at(other), :]
            conv_s[at(step), :] = conv
            back_s[at(other), :] = back
            return ahead, behind, grads

        _, _, grads = lax.fori_loop(0, span, outs, (ahead, behind, (zero,) * count), unroll=2)
        for n in range(count):
            total = jnp.sum(grads[n] * norms[n], axis=0, keepdims=True) * scale
            grad_ref[first + n : first + n + 1, :] = total

    for group in range(groups):

        def after(member, _, group=group):
            index = place(group, member)
            feats = feats_s[aligned((group * PLANE + member) * span, span), :]
            query, key, value = feats[:, :width], feats[:, width : 2 * width], feats[:, 2 * width :]
            cot = cot_ref[aligned(index * span, span), :].astype(jnp.float32)
            conv = rounded(conv_s[pl.ds(index, span, stride=chunks), :])
            back = rounded(back_s[pl.ds(index, span, stride=chunks), :])
            hyena_ref[aligned(index * span, span), :] = (query * conv).astype(jnp.bfloat16)
            rows = aligned(member * span, span)
            proj_refs[group][rows, :width] = (cot * conv).astype(jnp.bfloat16)
            proj_refs[group][rows, width : 2 * width] = (back * value).astype(jnp.bfloat16)
            proj_refs[group][rows, 2 * width :] = (back * key).astype(jnp.bfloat16)
            return 0

        lax.fori_loop(0, PLANE, after, 0)


def scan_all(me, cot_cols, residue_rows, rate_rows, groups, runs, own, other):
    length, width = cot_cols.shape
    vmem = pl.BlockSpec(memory_space=pltpu.VMEM)
    outs = pl.pallas_call(
        functools.partial(scan_kernel, groups, runs),
        out_shape=(
            jax.ShapeDtypeStruct((length, width), jnp.bfloat16),
            jax.ShapeDtypeStruct(rate_rows.shape, jnp.float32),
        )
        + (jax.ShapeDtypeStruct((length // groups, 3 * width), jnp.bfloat16),) * groups,
        in_specs=[pl.BlockSpec(memory_space=pltpu.SMEM)] + [vmem] * (3 + 2 * len(own)),
        out_specs=(vmem,) * (2 + groups),
        scratch_shapes=[pltpu.VMEM((length, width), jnp.float32)] * 4
        + [pltpu.VMEM((length, 3 * width), jnp.float32)],
        compiler_params=pltpu.CompilerParams(vmem_limit_bytes=40 * 2**20),
        name="modal_scan",
    )(me, cot_cols, residue_rows, rate_rows, *own, *other)
    return outs[0], outs[1], outs[2:]


def swapped(value):
    return lax.ppermute(value, "tp", [(0, 1), (1, 0)])


def over_x(value):
    return lax.ppermute(value, "ctx", [(i, i ^ 1) for i in range(lax.axis_size("ctx"))])


def over_y(value):
    return lax.ppermute(value, "ctx", [(i, i ^ 2) for i in range(lax.axis_size("ctx"))])


def up(value):
    count = lax.axis_size("ctx")
    return lax.ppermute(value, "ctx", [(i, (i + PLANE) % count) for i in range(count)])


def down(value):
    count = lax.axis_size("ctx")
    return lax.ppermute(value, "ctx", [((i + PLANE) % count, i) for i in range(count)])


def stack(*parts):
    return jnp.concatenate(parts, axis=0)


def beside(*parts):
    return jnp.concatenate(parts, axis=1)


def narrowed(value):
    return value.astype(jnp.bfloat16)


def widened(value):
    return value.astype(jnp.float32)


def gather_groups(tokens):
    span = tokens.shape[0]
    n, m = span * 3 // 4, span // 4
    nh, mh = n // 2, m // 2
    wide, narrow = tokens[:n], tokens[n:]
    wide_1, wide_3 = down(wide), up(wide)
    narrow_x, narrow_y = over_x(narrow), over_y(narrow)
    got_x = over_x(stack(narrow_y[:mh], wide))
    got_y = over_y(stack(narrow_x[mh:], wide))
    wide_0x, wide_0y = got_x[mh:], got_y[mh:]
    plane = stack(narrow, narrow_x, narrow_y, got_x[:mh], got_y[:mh])
    wide_2 = stack(up(wide_3[:nh]), down(wide_1[nh:]))
    got_x = over_x(stack(wide_0y[:nh], wide_3))
    got_y = over_y(stack(wide_0x[nh:], wide_3))
    first = stack(wide, wide_0x, wide_0y, got_x[:nh], got_y[:nh], plane)
    wide_3x, wide_3y = got_x[nh:], got_y[nh:]
    plane_1, plane_3 = down(plane), up(plane)
    got_x = over_x(stack(wide_3y[:nh], wide_1, wide_2))
    got_y = over_y(stack(wide_3x[nh:], wide_1, wide_2))
    second = stack(wide_3, wide_3x, wide_3y, got_x[:nh], got_y[:nh])
    wide_1x, wide_1y = got_x[nh : nh + n], got_y[nh : nh + n]
    wide_2x, wide_2y = got_x[nh + n :], got_y[nh + n :]
    third = stack(wide_1, wide_1x, wide_1y, wide_2, wide_2x, wide_2y)
    fourth = stack(plane_1, plane_3)
    half = plane.shape[0] // 2
    far = (up(plane_3[:half]), down(plane_1[half:]))
    got_x = over_x(stack(wide_1y[:nh], wide_2y[:nh]))
    got_y = over_y(stack(wide_1x[nh:], wide_2x[nh:]))
    fifth = stack(got_x[:nh], got_y[:nh], got_x[nh:], got_y[nh:], *far)
    runs = (
        (0, 0, 0, 0, 4, n, 0),
        (0, 4 * n, 0, 0, 4, m, n),
        (1, 0, 3, 0, 4, n, 0),
        (2, 0, 1, 0, 3, n, 0),
        (2, 3 * n, 2, 0, 3, n, 0),
        (3, 0, 1, 0, 4, m, n),
        (3, 4 * m, 3, 0, 4, m, n),
        (4, 0, 1, 3, 1, n, 0),
        (4, n, 2, 3, 1, n, 0),
        (4, 2 * n, 2, 0, 4, m, n),
    )
    return (first, second, third, fourth, fifth), runs


def scatter_sum(proj, matrix):
    span = proj[0].shape[0] // PLANE
    columns = matrix.shape[1]
    wide, narrow = columns * 3 // 8, columns // 8

    def product(left, first, count):
        right = matrix[:, first : first + count]
        return jnp.dot(left, right, preferred_element_type=jnp.float32)

    def term(group, member, side):
        rows = proj[group][member * span : (member + 1) * span]
        return product(rows, side * wide, wide)

    def low(group, side):
        return product(proj[group], 2 * wide + side * narrow, narrow)

    def to_x(group, across):
        return narrowed(term(group, 1, 0)), narrowed(term(group, 1, 1) + widened(across))

    def to_y(group, across):
        return narrowed(term(group, 2, 0) + widened(across)), narrowed(term(group, 2, 1))

    def kept(group, got_x, got_y):
        return [
            term(group, 0, side)
            + widened(got_x[:, side * wide : (side + 1) * wide])
            + widened(got_y[:, side * wide : (side + 1) * wide])
            for side in (0, 1)
        ]

    low_up = up(narrowed(low(2, 0)))
    low_down = down(narrowed(low(2, 1)))
    got_x = over_x(beside(narrowed(term(2, 3, 0)), narrowed(term(1, 3, 0))))
    got_y = over_y(beside(narrowed(term(2, 3, 1)), narrowed(term(1, 3, 1))))
    got_x, got_y = (
        over_x(
            beside(
                *to_x(2, got_y[:, :wide]), *to_x(1, got_y[:, wide:]), narrowed(term(3, 3, 0))
            )
        ),
        over_y(
            beside(
                *to_y(2, got_x[:, :wide]), *to_y(1, got_x[:, wide:]), narrowed(term(3, 3, 1))
            )
        ),
    )
    low_up, low_down = (
        up(beside(narrowed(low(1, 0) + widened(low_up)), narrowed(low(1, 1)))),
        down(beside(narrowed(low(3, 0)), narrowed(low(3, 1) + widened(low_down)))),
    )
    sum_2 = kept(2, got_x[:, : 2 * wide], got_y[:, : 2 * wide])
    sum_1 = kept(1, got_x[:, 2 * wide : 4 * wide], got_y[:, 2 * wide : 4 * wide])
    wide_up, wide_down = up(narrowed(sum_2[0])), down(narrowed(sum_2[1]))
    got_x, got_y = (
        over_x(beside(*to_x(3, got_y[:, 4 * wide :]), narrowed(term(0, 3, 0)))),
        over_y(beside(*to_y(3, got_x[:, 4 * wide :]), narrowed(term(0, 3, 1)))),
    )
    sum_3 = kept(3, got_x[:, : 2 * wide], got_y[:, : 2 * wide])
    wide_up, wide_down = (
        up(beside(narrowed(sum_1[0] + widened(wide_up)), narrowed(sum_1[1]))),
        down(beside(narrowed(sum_3[0]), narrowed(sum_3[1] + widened(wide_down)))),
    )
    low_sum = [
        low(0, side)
        + widened(low_up[:, side * narrow : (side + 1) * narrow])
        + widened(low_down[:, side * narrow : (side + 1) * narrow])
        for side in (0, 1)
    ]

    def low_term(member, side):
        return low_sum[side][member * span : (member + 1) * span]

    got_x, got_y = (
        over_x(beside(*to_x(0, got_y[:, 2 * wide :]), narrowed(low_term(3, 0)))),
        over_y(beside(*to_y(0, got_x[:, 2 * wide :]), narrowed(low_term(3, 1)))),
    )
    sum_0 = kept(0, got_x[:, : 2 * wide], got_y[:, : 2 * wide])
    across_y, across_x = got_x[:, 2 * wide :], got_y[:, 2 * wide :]
    low_x = over_x(
        beside(narrowed(low_term(1, 0)), narrowed(low_term(1, 1) + widened(across_x)))
    )
    low_y = over_y(
        beside(narrowed(low_term(2, 0) + widened(across_y)), narrowed(low_term(2, 1)))
    )
    outs = [
        sum_0[side]
        + widened(wide_up[:, side * wide : (side + 1) * wide])
        + widened(wide_down[:, side * wide : (side + 1) * wide])
        for side in (0, 1)
    ]
    outs += [
        low_term(0, side)
        + widened(low_x[:, side * narrow : (side + 1) * narrow])
        + widened(low_y[:, side * narrow : (side + 1) * narrow])
        for side in (0, 1)
    ]
    return beside(*[narrowed(part) for part in outs])


def gather_tokens(tokens, weights, residues, decay_rates, cotangent):
    core = lax.axis_index("tp")
    me = lax.axis_index("ctx").astype(jnp.int32).reshape(1)
    half = tokens.shape[1] // 2
    channels = weights.shape[1]
    groups, runs = gather_groups(lax.dynamic_slice_in_dim(tokens, core * half, half, 1))
    rows = weights[0].swapaxes(0, 1).reshape(3 * channels, 2 * half)
    kept = lax.dynamic_slice_in_dim(rows, core * half, half, 1)
    taken = swapped(lax.dynamic_slice_in_dim(rows, (1 - core) * half, half, 1))
    cot_cols = lax.all_to_all(cotangent.T, "ctx", split_axis=1, concat_axis=0, tiled=True)

    def project(part, matrix):
        return jnp.einsum("td,rd->tr", part, matrix, preferred_element_type=jnp.float32)

    other = [swapped(project(part, taken)) for part in groups]
    own = [project(part, kept) for part in groups]
    hyena, grads, proj = scan_all(
        me, cot_cols, residues[0].T, decay_rates[0].T, PLANE, runs, own, other
    )
    hyena_out = lax.all_to_all(hyena, "ctx", split_axis=0, concat_axis=1, tiled=True).T
    proj = [beside(part, swapped(part)) for part in proj]
    grad_input = scatter_sum(proj, stack(kept, taken))
    return (hyena_out, grad_input, grads.T[None])


def shards(tokens, weights, residues, decay_rates, cotangent):
    ctx, tp = lax.axis_size("ctx"), lax.axis_size("tp")
    if ctx == 4 * PLANE and tp == 2 and weights.size * tp > 2 * tokens.size:
        return gather_tokens(tokens, weights, residues, decay_rates, cotangent)
    return gather_weights(tokens, weights, residues, decay_rates, cotangent)


def solution(mesh):
    return jax.shard_map(
        shards,
        mesh=mesh,
        in_specs=(
            P("ctx", None),
            P("tp", "ctx", None, None),
            P("tp", "ctx", None),
            P("tp", "ctx", None),
            P("tp", "ctx"),
        ),
        out_specs=(P("tp", "ctx"), P("ctx", "tp"), P("tp", "ctx", None)),
        check_vma=False,
    )
```

```python
import functools
import math

import jax
import jax.numpy as jnp
from jax import lax
from jax.experimental import pallas as pl
from jax.experimental.pallas import tpu as pltpu
from jax.sharding import PartitionSpec as P


def precise(form, left, right):
    return jnp.einsum(
        form, left, right, precision=lax.Precision.HIGHEST, preferred_element_type=jnp.float32
    )


def tripled(form, left, right):
    return jnp.einsum(
        form, left, right, precision=lax.Precision.HIGH, preferred_element_type=jnp.float32
    )


def angle_table(row_count, col_count, period):
    product = (
        jnp.arange(row_count, dtype=jnp.int32)[:, None]
        * jnp.arange(col_count, dtype=jnp.int32)[None, :]
        % period
    )
    angles = product.astype(jnp.float32) * (2.0 * math.pi / period)
    return (jnp.cos(angles), jnp.sin(angles))


def make_tables(length):
    padded = 2 * length
    outer = math.gcd(padded, 1 << (padded.bit_length() - 1) // 2)
    inner = padded // outer
    cos_outer, sin_outer = angle_table(outer, outer, outer)
    cos_inner, sin_inner = angle_table(inner, inner, inner)
    twist_cos, twist_sin = angle_table(outer, inner, padded)
    return (outer, inner, cos_outer, sin_outer, cos_inner, sin_inner, twist_cos, twist_sin)


def spectrum(signal, tables, product):
    outer, inner, cos_outer, sin_outer, cos_inner, sin_inner, twist_cos, twist_sin = tables
    half_rows = outer // 2
    blocks = signal.reshape(signal.shape[0], half_rows, inner)
    first_re = product("kp,bpq->bkq", cos_outer[:, :half_rows], blocks)
    first_im = -product("kp,bpq->bkq", sin_outer[:, :half_rows], blocks)
    turned_re = first_re * twist_cos + first_im * twist_sin
    turned_im = first_im * twist_cos - first_re * twist_sin
    spec_re = product("bkq,qj->bkj", turned_re, cos_inner) + product(
        "bkq,qj->bkj", turned_im, sin_inner
    )
    spec_im = product("bkq,qj->bkj", turned_im, cos_inner) - product(
        "bkq,qj->bkj", turned_re, sin_inner
    )
    return (spec_re, spec_im)


def signal_of(spec_re, spec_im, tables):
    outer, inner, cos_outer, sin_outer, cos_inner, sin_inner, twist_cos, twist_sin = tables
    half_rows = outer // 2
    back_re = tripled("bkj,jq->bkq", spec_re, cos_inner) - tripled(
        "bkj,jq->bkq", spec_im, sin_inner
    )
    back_im = tripled("bkj,jq->bkq", spec_im, cos_inner) + tripled(
        "bkj,jq->bkq", spec_re, sin_inner
    )
    turned_re = back_re * twist_cos - back_im * twist_sin
    turned_im = back_im * twist_cos + back_re * twist_sin
    values = tripled("pk,bkq->bpq", cos_outer[:half_rows, :], turned_re) - tripled(
        "pk,bkq->bpq", sin_outer[:half_rows, :], turned_im
    )
    return values.reshape(values.shape[0], half_rows * inner) * (1.0 / (outer * inner))


def spec_product(left_re, left_im, right_re, right_im):
    return (left_re * right_re - left_im * right_im, left_re * right_im + left_im * right_re)


def conj_product(left_re, left_im, right_re, right_im):
    return (left_re * right_re + left_im * right_im, left_re * right_im - left_im * right_re)


def filter_basis(residue_loc, rate_loc, length):
    position = jnp.arange(length, dtype=jnp.float32)
    basis_all = jnp.sqrt(2.0 * rate_loc)[:, :, None] * jnp.exp(
        -rate_loc[:, :, None] * position[None, None, :]
    )
    return (basis_all, precise("cm,cmt->ct", residue_loc, basis_all))


def forward_cols(gated_cols, taps_re, taps_im, tables):
    gated_re, gated_im = spectrum(gated_cols.astype(jnp.float32), tables, tripled)
    conv_re, conv_im = spec_product(gated_re, gated_im, taps_re, taps_im)
    conv_cols = signal_of(conv_re, conv_im, tables).astype(jnp.bfloat16)
    return (conv_cols, gated_re, gated_im)


def backward_cols(slope_cols, gated_re, gated_im, taps_re, taps_im, basis_all, tables, length):
    slope_re, slope_im = spectrum(slope_cols.astype(jnp.float32), tables, tripled)
    grad_re, grad_im = conj_product(taps_re, taps_im, slope_re, slope_im)
    back_cols = signal_of(grad_re, grad_im, tables).astype(jnp.bfloat16)
    lag_re, lag_im = conj_product(gated_re, gated_im, slope_re, slope_im)
    taps_grad = signal_of(lag_re, lag_im, tables)
    grad_residue = precise("ct,cmt->cm", taps_grad, basis_all) * (1.0 / math.sqrt(length))
    return (back_cols, grad_residue)


def gather_weights(tokens, weights, residues, decay_rates, cotangent):
    gathered = lax.all_gather(weights, "ctx", axis=1, tiled=True)
    projected = jnp.einsum("xcpd,td->xcpt", gathered, tokens, preferred_element_type=jnp.float32)
    features = projected[0].astype(jnp.bfloat16)
    query_f = features[:, 0].astype(jnp.float32)
    key_part = features[:, 1].astype(jnp.float32)
    value_part = features[:, 2].astype(jnp.float32)
    gated_in = (key_part * value_part).astype(jnp.bfloat16)
    slope_in = (cotangent.astype(jnp.float32) * query_f).astype(jnp.bfloat16)
    length = tokens.shape[0] * lax.axis_size("ctx")
    tables = make_tables(length)
    basis_all, taps_full = filter_basis(residues[0], decay_rates[0], length)
    taps_re, taps_im = spectrum(taps_full, tables, precise)
    gated_cols = lax.all_to_all(gated_in, "ctx", split_axis=0, concat_axis=1, tiled=True)
    conv_cols, gated_re, gated_im = forward_cols(gated_cols, taps_re, taps_im, tables)
    conv_rows = lax.all_to_all(conv_cols, "ctx", split_axis=1, concat_axis=0, tiled=True)
    slope_cols = lax.all_to_all(slope_in, "ctx", split_axis=0, concat_axis=1, tiled=True)
    back_cols, grad_residue = backward_cols(
        slope_cols, gated_re, gated_im, taps_re, taps_im, basis_all, tables, length
    )
    back_rows = lax.all_to_all(back_cols, "ctx", split_axis=1, concat_axis=0, tiled=True)
    conv_f = conv_rows.astype(jnp.float32)
    back_f = back_rows.astype(jnp.float32)
    hyena_out = (query_f * conv_f).astype(jnp.bfloat16)
    grad_query = (cotangent.astype(jnp.float32) * conv_f).astype(jnp.bfloat16)
    grad_key = (back_f * value_part).astype(jnp.bfloat16)
    grad_value = (back_f * key_part).astype(jnp.bfloat16)
    grad_proj = jnp.stack([grad_query, grad_key, grad_value], axis=1)
    partial_value = jnp.einsum(
        "cpt,cpd->td", grad_proj, gathered[0], preferred_element_type=jnp.float32
    )
    grad_input = lax.psum_scatter(
        partial_value.astype(jnp.bfloat16), "tp", scatter_dimension=1, tiled=True
    )
    return (hyena_out, grad_input, grad_residue[None])


GROUP = 4
PLANE = 4


def rounded(value):
    return value.astype(jnp.bfloat16).astype(jnp.float32)


def earlier_sum(finals, rate, span, back):
    count = finals.shape[0]
    row = lax.broadcasted_iota(jnp.int32, finals.shape, 0)

    def shifted(value, by):
        if back:
            moved = pltpu.roll(value, count - by, 0)
            return jnp.where(row < count - by, moved, 0.0)
        moved = pltpu.roll(value, by, 0)
        return jnp.where(row >= by, moved, 0.0)

    total = shifted(finals, 1)
    by = 1
    while by < count:
        total = total + jnp.exp(rate * (-1.0 * span * by)) * shifted(total, by)
        by *= 2
    return total


def scan_kernel(
    groups,
    runs,
    order,
    me_ref,
    cot_ref,
    residue_ref,
    rate_ref,
    *refs,
):
    inputs = 1 + max(run[0] for run in runs)
    own, other = refs[:inputs], refs[inputs : 2 * inputs]
    hyena_ref, grad_ref = refs[2 * inputs : 2 * inputs + 2]
    proj_refs = refs[2 * inputs + 2 : 2 * inputs + 2 + len(order)]
    gated_s, slope_s, conv_s, back_s, feats_s = refs[2 * inputs + 2 + len(order) :]
    length, width = cot_ref.shape
    chunks = PLANE * groups
    span = length // chunks
    modes = rate_ref.shape[0]
    me = me_ref[0]

    def place(group, member):
        return lax.rem(me // PLANE + group, groups) * PLANE + (member ^ lax.rem(me, PLANE))

    def aligned(start, size):
        return pl.ds(pl.multiple_of(start, size), size)

    for source, offset, group, base, members, count, first in runs:

        def before(step, _, source=source, offset=offset, group=group, base=base, count=count, first=first):
            member = base + step
            index = place(group, member)
            rows = pl.ds(pl.multiple_of(offset + step * count, 16), count)
            feats = own[source][rows, 3 * width :] + other[source][rows, :].astype(jnp.float32)
            feats = rounded(feats)
            slot = (group * PLANE + member) * span + first
            feats_s[pl.ds(pl.multiple_of(slot, 16), count), :] = feats
            cot = cot_ref[pl.ds(pl.multiple_of(index * span + first, 16), count), :]
            query, key = feats[:, :width], feats[:, width : 2 * width]
            into = pl.ds(first * chunks + index, count, stride=chunks)
            gated_s[into, :] = rounded(key * feats[:, 2 * width :])
            slope_s[into, :] = rounded(cot.astype(jnp.float32) * query)
            return 0

        lax.fori_loop(0, members, before, 0)

    def at(step):
        return aligned(step * chunks, chunks)

    zero = jnp.zeros((chunks, width), jnp.float32)
    scale = 1.0 / math.sqrt(length)
    for first in range(0, modes, GROUP):
        count = min(GROUP, modes - first)
        rates = [
            jnp.broadcast_to(rate_ref[m : m + 1, :], (chunks, width))
            for m in range(first, first + count)
        ]
        decays = [jnp.exp(-rate) for rate in rates]
        norms = [jnp.sqrt(2.0 * rate) for rate in rates]
        gains = [
            residue_ref[first + n : first + n + 1, :] * norms[n] for n in range(count)
        ]

        def sums(step, state):
            ahead, behind = state
            gated = gated_s[at(step), :]
            slope = slope_s[at(span - 1 - step), :]
            return (
                tuple(decays[n] * ahead[n] + gated for n in range(count)),
                tuple(decays[n] * behind[n] + slope for n in range(count)),
            )

        ahead, behind = lax.fori_loop(0, span, sums, ((zero,) * count, (zero,) * count), unroll=4)
        ahead = tuple(earlier_sum(ahead[n], rates[n], span, False) for n in range(count))
        behind = tuple(earlier_sum(behind[n], rates[n], span, True) for n in range(count))

        def outs(step, state):
            ahead, behind, grads = state
            other = span - 1 - step
            gated = gated_s[at(step), :]
            slope = slope_s[at(step), :]
            slope_back = slope_s[at(other), :]
            ahead = tuple(decays[n] * ahead[n] + gated for n in range(count))
            behind = tuple(decays[n] * behind[n] + slope_back for n in range(count))
            grads = tuple(grads[n] + slope * ahead[n] for n in range(count))
            conv = sum(gains[n] * ahead[n] for n in range(count))
            back = sum(gains[n] * behind[n] for n in range(count))
            if first:
                conv = conv + conv_s[at(step), :]
                back = back + back_s[at(other), :]
            conv_s[at(step), :] = conv
            back_s[at(other), :] = back
            return ahead, behind, grads

        _, _, grads = lax.fori_loop(0, span, outs, (ahead, behind, (zero,) * count), unroll=2)
        for n in range(count):
            total = jnp.sum(grads[n] * norms[n], axis=0, keepdims=True) * scale
            grad_ref[first + n : first + n + 1, :] = total

    for proj_ref, pieces in zip(proj_refs, order):
        start = 0
        for group, base, members in pieces:

            def after(step, _, proj_ref=proj_ref, start=start, group=group, base=base):
                member = base + step
                index = place(group, member)
                feats = feats_s[aligned((group * PLANE + member) * span, span), :]
                query, key = feats[:, :width], feats[:, width : 2 * width]
                cot = cot_ref[aligned(index * span, span), :].astype(jnp.float32)
                conv = rounded(conv_s[pl.ds(index, span, stride=chunks), :])
                back = rounded(back_s[pl.ds(index, span, stride=chunks), :])
                hyena_ref[aligned(index * span, span), :] = narrowed(query * conv)
                rows = aligned(start + step * span, span)
                proj_ref[rows, :width] = narrowed(cot * conv)
                proj_ref[rows, width : 2 * width] = narrowed(back * feats[:, 2 * width :])
                proj_ref[rows, 2 * width :] = narrowed(back * key)
                return 0

            lax.fori_loop(0, members, after, 0)
            start += members * span


def scan_all(me, cot_cols, residue_rows, rate_rows, runs, order, own, other):
    length, width = cot_cols.shape
    span = length // (PLANE * PLANE)
    vmem = pl.BlockSpec(memory_space=pltpu.VMEM)
    outs = pl.pallas_call(
        functools.partial(scan_kernel, PLANE, runs, order),
        out_shape=(
            jax.ShapeDtypeStruct((length, width), jnp.bfloat16),
            jax.ShapeDtypeStruct(rate_rows.shape, jnp.float32),
        )
        + tuple(
            jax.ShapeDtypeStruct((span * sum(piece[2] for piece in pieces), 3 * width), jnp.bfloat16)
            for pieces in order
        ),
        in_specs=[pl.BlockSpec(memory_space=pltpu.SMEM)] + [vmem] * (3 + 2 * len(own)),
        out_specs=(vmem,) * (2 + len(order)),
        scratch_shapes=[pltpu.VMEM((length, width), jnp.float32)] * 4
        + [pltpu.VMEM((length, 3 * width), jnp.float32)],
        compiler_params=pltpu.CompilerParams(vmem_limit_bytes=40 * 2**20),
        name="modal_scan",
    )(me, cot_cols, residue_rows, rate_rows, *own, *other)
    return outs[0], outs[1], outs[2:]


def swapped(value):
    return lax.ppermute(value, "tp", [(0, 1), (1, 0)])


def over_x(value):
    return lax.ppermute(value, "ctx", [(i, i ^ 1) for i in range(lax.axis_size("ctx"))])


def over_y(value):
    return lax.ppermute(value, "ctx", [(i, i ^ 2) for i in range(lax.axis_size("ctx"))])


def up(value):
    count = lax.axis_size("ctx")
    return lax.ppermute(value, "ctx", [(i, (i + PLANE) % count) for i in range(count)])


def down(value):
    count = lax.axis_size("ctx")
    return lax.ppermute(value, "ctx", [((i + PLANE) % count, i) for i in range(count)])


def stack(*parts):
    return jnp.concatenate(parts, axis=0)


def beside(*parts):
    return jnp.concatenate(parts, axis=1)


def narrowed(value):
    return value.astype(jnp.bfloat16)


def widened(value):
    return value.astype(jnp.float32)


def over_plane(for_x, for_y):
    return lax.optimization_barrier((over_x(for_x), over_y(for_y)))


def over_depth(for_above, for_below):
    return lax.optimization_barrier((up(for_above), down(for_below)))


def gather_groups(tokens, matrix, others):
    span = tokens.shape[0]
    n, m = span * 3 // 4, span // 4
    nh, mh = n // 2, m // 2
    wide = tokens[:n]
    own_x, own_y = over_plane(tokens, tokens)
    wide_3, wide_1 = over_depth(wide, wide)
    across_x, across_y = over_plane(
        stack(own_y[:nh], own_y[n : n + mh]), stack(own_x[nh:n], own_x[n + mh :])
    )
    wide_2 = stack(*over_depth(wide_3[:nh], wide_1[nh:]))
    near = stack(wide_3, wide_1)
    near, matrix, others = lax.optimization_barrier((near, matrix, others))
    near_x, near_y = over_plane(near, near)
    plane = stack(tokens[n:], own_x[n:], own_y[n:], across_x[nh:], across_y[nh:])
    plane, wide_2 = lax.optimization_barrier((plane, wide_2))
    plane_3, plane_1 = over_depth(plane, plane)
    far_x, far_y = over_plane(
        stack(near_y[:nh], near_y[n : n + nh], wide_2), stack(near_x[nh:n], near_x[n + nh :], wide_2)
    )
    half = plane.shape[0] // 2
    far = over_depth(plane_3[:half], plane_1[half:])
    last_x, last_y = over_plane(far_y[n : n + nh], far_x[n + nh :])
    parts = (
        stack(tokens, own_x, own_y, across_x, across_y),
        stack(near, near_x, near_y),
        stack(plane_1, plane_3),
        stack(wide_2, far_x, far_y),
        stack(last_x, last_y, *far),
    )
    runs = [
        (0, 0, 0, 0, 3, span, 0),
        (2, 0, 1, 0, 4, m, n),
        (2, 4 * m, 3, 0, 4, m, n),
        (3, 0, 2, 0, 1, n, 0),
        (4, 2 * nh, 2, 0, 4, m, n),
    ]
    for side in range(2):
        runs += [
            (0, 3 * span + side * (nh + mh), 0, 3, 1, nh, side * nh),
            (0, 3 * span + side * (nh + mh) + nh, 0, 3, 1, mh, n + side * mh),
            (3, n + side * 2 * n, 3, 3, 1, nh, side * nh),
            (3, n + side * 2 * n + nh, 1, 3, 1, nh, side * nh),
            (3, n + side * 2 * n + n, 2, 1 + side, 1, n, 0),
            (4, side * nh, 2, 3, 1, nh, side * nh),
        ]
    for member in range(3):
        runs += [(1, member * 2 * n, 3, member, 1, n, 0), (1, member * 2 * n + n, 1, member, 1, n, 0)]
    return parts, tuple(runs), matrix, others


ORDER = (((2, 0, 4), (1, 3, 1)), ((1, 0, 3), (3, 0, 4), (0, 0, 4)))


def scatter_sum(early, later, matrix, hyena):
    span = later.shape[0] // 11
    columns = matrix.shape[1]
    wide, narrow = columns * 3 // 8, columns // 8

    def product(part):
        both = beside(part, swapped(part))
        return narrowed(jnp.dot(both, matrix, preferred_element_type=jnp.float32))

    blocks = {}

    def keep(value, pieces):
        start = 0
        for group, base, members in pieces:
            for member in range(base, base + members):
                blocks[group, member] = value[start : start + span]
                start += span

    early = product(early)
    keep(early, ORDER[0])

    def term(group, member, side):
        return blocks[group, member][:, side * wide : (side + 1) * wide]

    def low(group, side):
        first = 2 * wide + side * narrow
        return stack(*[blocks[group, m][:, first : first + narrow] for m in range(PLANE)])

    def total(*parts):
        return sum(widened(part) for part in parts)

    def to_x(group, across):
        return term(group, 1, 0), narrowed(total(term(group, 1, 1), across))

    def to_y(group, across):
        return narrowed(total(term(group, 2, 0), across)), term(group, 2, 1)

    def kept(group, got_x, got_y):
        return [
            total(
                term(group, 0, side),
                got_x[:, side * wide : (side + 1) * wide],
                got_y[:, side * wide : (side + 1) * wide],
            )
            for side in (0, 1)
        ]

    got_x, got_y = over_plane(
        beside(term(2, 3, 0), term(1, 3, 0)), beside(term(2, 3, 1), term(1, 3, 1))
    )
    low_up, low_down = over_depth(low(2, 0), low(2, 1))
    later, early = lax.optimization_barrier((later, early))
    later, hyena, got_x, got_y = lax.optimization_barrier((product(later), hyena, got_x, got_y))
    keep(later, ORDER[1])
    hyena_out = lax.all_to_all(hyena, "ctx", split_axis=0, concat_axis=1, tiled=True).T
    got_x, got_y = over_plane(
        beside(*to_x(2, got_y[:, :wide]), *to_x(1, got_y[:, wide:]), term(3, 3, 0)),
        beside(*to_y(2, got_x[:, :wide]), *to_y(1, got_x[:, wide:]), term(3, 3, 1)),
    )
    low_up, low_down = over_depth(
        beside(narrowed(total(low(1, 0), low_up)), low(1, 1)),
        beside(low(3, 0), narrowed(total(low(3, 1), low_down))),
    )
    sum_2 = kept(2, got_x[:, : 2 * wide], got_y[:, : 2 * wide])
    sum_1 = kept(1, got_x[:, 2 * wide : 4 * wide], got_y[:, 2 * wide : 4 * wide])
    sum_2, low_up, low_down = lax.optimization_barrier((sum_2, low_up, low_down))
    wide_up, wide_down = over_depth(narrowed(sum_2[0]), narrowed(sum_2[1]))
    got_x, got_y = over_plane(
        beside(*to_x(3, got_y[:, 4 * wide :]), term(0, 3, 0)),
        beside(*to_y(3, got_x[:, 4 * wide :]), term(0, 3, 1)),
    )
    got_x, got_y, wide_up, wide_down = lax.optimization_barrier((got_x, got_y, wide_up, wide_down))
    sum_3 = kept(3, got_x[:, : 2 * wide], got_y[:, : 2 * wide])
    wide_up, wide_down = over_depth(
        beside(narrowed(total(sum_1[0], wide_up)), narrowed(sum_1[1])),
        beside(narrowed(sum_3[0]), narrowed(total(sum_3[1], wide_down))),
    )
    low_sum = [
        total(
            low(0, side),
            low_up[:, side * narrow : (side + 1) * narrow],
            low_down[:, side * narrow : (side + 1) * narrow],
        )
        for side in (0, 1)
    ]

    def low_term(member, side):
        return low_sum[side][member * span : (member + 1) * span]

    got_x, got_y = over_plane(
        beside(*to_x(0, got_y[:, 2 * wide :]), narrowed(low_term(3, 0))),
        beside(*to_y(0, got_x[:, 2 * wide :]), narrowed(low_term(3, 1))),
    )
    sum_0 = kept(0, got_x[:, : 2 * wide], got_y[:, : 2 * wide])
    across_y, across_x = got_x[:, 2 * wide :], got_y[:, 2 * wide :]
    low_x, low_y = over_plane(
        beside(narrowed(low_term(1, 0)), narrowed(total(low_term(1, 1), across_x))),
        beside(narrowed(total(low_term(2, 0), across_y)), narrowed(low_term(2, 1))),
    )
    outs = [
        total(
            sum_0[side],
            wide_up[:, side * wide : (side + 1) * wide],
            wide_down[:, side * wide : (side + 1) * wide],
        )
        for side in (0, 1)
    ]
    outs += [
        total(
            low_term(0, side),
            low_x[:, side * narrow : (side + 1) * narrow],
            low_y[:, side * narrow : (side + 1) * narrow],
        )
        for side in (0, 1)
    ]
    return beside(*[narrowed(part) for part in outs]), hyena_out


def gather_tokens(tokens, weights, residues, decay_rates, cotangent):
    core = lax.axis_index("tp")
    me = lax.axis_index("ctx").astype(jnp.int32).reshape(1)
    half = tokens.shape[1] // 2
    channels = weights.shape[1]
    rows = weights[0].swapaxes(0, 1).reshape(3 * channels, 2 * half)
    kept = lax.dynamic_slice_in_dim(rows, core * half, half, 1)
    taken = swapped(lax.dynamic_slice_in_dim(rows, (1 - core) * half, half, 1))
    cot_cols = lax.all_to_all(cotangent.T, "ctx", split_axis=1, concat_axis=0, tiled=True)
    parts, runs, matrix, cot_cols = gather_groups(
        lax.dynamic_slice_in_dim(tokens, core * half, half, 1), stack(taken, kept), cot_cols
    )
    both = [
        jnp.einsum("td,rd->tr", part, matrix, preferred_element_type=jnp.float32) for part in parts
    ]
    other = [swapped(narrowed(part[:, : 3 * channels])) for part in both]
    hyena, grads, (early, later) = scan_all(
        me, cot_cols, residues[0].T, decay_rates[0].T, runs, ORDER, both, other
    )
    grad_input, hyena_out = scatter_sum(early, later, stack(kept, taken), hyena)
    return (hyena_out, grad_input, grads.T[None])


def shards(tokens, weights, residues, decay_rates, cotangent):
    ctx, tp = lax.axis_size("ctx"), lax.axis_size("tp")
    if ctx == 4 * PLANE and tp == 2 and weights.size * tp > 2 * tokens.size:
        return gather_tokens(tokens, weights, residues, decay_rates, cotangent)
    return gather_weights(tokens, weights, residues, decay_rates, cotangent)


def solution(mesh):
    return jax.shard_map(
        shards,
        mesh=mesh,
        in_specs=(
            P("ctx", None),
            P("tp", "ctx", None, None),
            P("tp", "ctx", None),
            P("tp", "ctx", None),
            P("tp", "ctx"),
        ),
        out_specs=(P("tp", "ctx"), P("ctx", "tp"), P("tp", "ctx", None)),
        check_vma=False,
    )
```

```python
import functools
import math

import jax
import jax.numpy as jnp
from jax import lax
from jax.experimental import pallas as pl
from jax.experimental.pallas import tpu as pltpu
from jax.sharding import PartitionSpec as P


def precise(form, left, right):
    return jnp.einsum(
        form, left, right, precision=lax.Precision.HIGHEST, preferred_element_type=jnp.float32
    )


def tripled(form, left, right):
    return jnp.einsum(
        form, left, right, precision=lax.Precision.HIGH, preferred_element_type=jnp.float32
    )


def angle_table(row_count, col_count, period):
    product = (
        jnp.arange(row_count, dtype=jnp.int32)[:, None]
        * jnp.arange(col_count, dtype=jnp.int32)[None, :]
        % period
    )
    angles = product.astype(jnp.float32) * (2.0 * math.pi / period)
    return (jnp.cos(angles), jnp.sin(angles))


def make_tables(length):
    padded = 2 * length
    outer = math.gcd(padded, 1 << (padded.bit_length() - 1) // 2)
    inner = padded // outer
    cos_outer, sin_outer = angle_table(outer, outer, outer)
    cos_inner, sin_inner = angle_table(inner, inner, inner)
    twist_cos, twist_sin = angle_table(outer, inner, padded)
    return (outer, inner, cos_outer, sin_outer, cos_inner, sin_inner, twist_cos, twist_sin)


def spectrum(signal, tables, product):
    outer, inner, cos_outer, sin_outer, cos_inner, sin_inner, twist_cos, twist_sin = tables
    half_rows = outer // 2
    blocks = signal.reshape(signal.shape[0], half_rows, inner)
    first_re = product("kp,bpq->bkq", cos_outer[:, :half_rows], blocks)
    first_im = -product("kp,bpq->bkq", sin_outer[:, :half_rows], blocks)
    turned_re = first_re * twist_cos + first_im * twist_sin
    turned_im = first_im * twist_cos - first_re * twist_sin
    spec_re = product("bkq,qj->bkj", turned_re, cos_inner) + product(
        "bkq,qj->bkj", turned_im, sin_inner
    )
    spec_im = product("bkq,qj->bkj", turned_im, cos_inner) - product(
        "bkq,qj->bkj", turned_re, sin_inner
    )
    return (spec_re, spec_im)


def signal_of(spec_re, spec_im, tables):
    outer, inner, cos_outer, sin_outer, cos_inner, sin_inner, twist_cos, twist_sin = tables
    half_rows = outer // 2
    back_re = tripled("bkj,jq->bkq", spec_re, cos_inner) - tripled(
        "bkj,jq->bkq", spec_im, sin_inner
    )
    back_im = tripled("bkj,jq->bkq", spec_im, cos_inner) + tripled(
        "bkj,jq->bkq", spec_re, sin_inner
    )
    turned_re = back_re * twist_cos - back_im * twist_sin
    turned_im = back_im * twist_cos + back_re * twist_sin
    values = tripled("pk,bkq->bpq", cos_outer[:half_rows, :], turned_re) - tripled(
        "pk,bkq->bpq", sin_outer[:half_rows, :], turned_im
    )
    return values.reshape(values.shape[0], half_rows * inner) * (1.0 / (outer * inner))


def spec_product(left_re, left_im, right_re, right_im):
    return (left_re * right_re - left_im * right_im, left_re * right_im + left_im * right_re)


def conj_product(left_re, left_im, right_re, right_im):
    return (left_re * right_re + left_im * right_im, left_re * right_im - left_im * right_re)


def filter_basis(residue_loc, rate_loc, length):
    position = jnp.arange(length, dtype=jnp.float32)
    basis_all = jnp.sqrt(2.0 * rate_loc)[:, :, None] * jnp.exp(
        -rate_loc[:, :, None] * position[None, None, :]
    )
    return (basis_all, precise("cm,cmt->ct", residue_loc, basis_all))


def forward_cols(gated_cols, taps_re, taps_im, tables):
    gated_re, gated_im = spectrum(gated_cols.astype(jnp.float32), tables, tripled)
    conv_re, conv_im = spec_product(gated_re, gated_im, taps_re, taps_im)
    conv_cols = signal_of(conv_re, conv_im, tables).astype(jnp.bfloat16)
    return (conv_cols, gated_re, gated_im)


def backward_cols(slope_cols, gated_re, gated_im, taps_re, taps_im, basis_all, tables, length):
    slope_re, slope_im = spectrum(slope_cols.astype(jnp.float32), tables, tripled)
    grad_re, grad_im = conj_product(taps_re, taps_im, slope_re, slope_im)
    back_cols = signal_of(grad_re, grad_im, tables).astype(jnp.bfloat16)
    lag_re, lag_im = conj_product(gated_re, gated_im, slope_re, slope_im)
    taps_grad = signal_of(lag_re, lag_im, tables)
    grad_residue = precise("ct,cmt->cm", taps_grad, basis_all) * (1.0 / math.sqrt(length))
    return (back_cols, grad_residue)


def gather_weights(tokens, weights, residues, decay_rates, cotangent):
    gathered = lax.all_gather(weights, "ctx", axis=1, tiled=True)
    projected = jnp.einsum("xcpd,td->xcpt", gathered, tokens, preferred_element_type=jnp.float32)
    features = projected[0].astype(jnp.bfloat16)
    query_f = features[:, 0].astype(jnp.float32)
    key_part = features[:, 1].astype(jnp.float32)
    value_part = features[:, 2].astype(jnp.float32)
    gated_in = (key_part * value_part).astype(jnp.bfloat16)
    slope_in = (cotangent.astype(jnp.float32) * query_f).astype(jnp.bfloat16)
    length = tokens.shape[0] * lax.axis_size("ctx")
    tables = make_tables(length)
    basis_all, taps_full = filter_basis(residues[0], decay_rates[0], length)
    taps_re, taps_im = spectrum(taps_full, tables, precise)
    gated_cols = lax.all_to_all(gated_in, "ctx", split_axis=0, concat_axis=1, tiled=True)
    conv_cols, gated_re, gated_im = forward_cols(gated_cols, taps_re, taps_im, tables)
    conv_rows = lax.all_to_all(conv_cols, "ctx", split_axis=1, concat_axis=0, tiled=True)
    slope_cols = lax.all_to_all(slope_in, "ctx", split_axis=0, concat_axis=1, tiled=True)
    back_cols, grad_residue = backward_cols(
        slope_cols, gated_re, gated_im, taps_re, taps_im, basis_all, tables, length
    )
    back_rows = lax.all_to_all(back_cols, "ctx", split_axis=1, concat_axis=0, tiled=True)
    conv_f = conv_rows.astype(jnp.float32)
    back_f = back_rows.astype(jnp.float32)
    hyena_out = (query_f * conv_f).astype(jnp.bfloat16)
    grad_query = (cotangent.astype(jnp.float32) * conv_f).astype(jnp.bfloat16)
    grad_key = (back_f * value_part).astype(jnp.bfloat16)
    grad_value = (back_f * key_part).astype(jnp.bfloat16)
    grad_proj = jnp.stack([grad_query, grad_key, grad_value], axis=1)
    partial_value = jnp.einsum(
        "cpt,cpd->td", grad_proj, gathered[0], preferred_element_type=jnp.float32
    )
    grad_input = lax.psum_scatter(
        partial_value.astype(jnp.bfloat16), "tp", scatter_dimension=1, tiled=True
    )
    return (hyena_out, grad_input, grad_residue[None])


GROUP = 4
PLANE = 4


def rounded(value):
    return value.astype(jnp.bfloat16).astype(jnp.float32)


def earlier_sum(finals, rate, span, back):
    count = finals.shape[0]
    row = lax.broadcasted_iota(jnp.int32, finals.shape, 0)

    def shifted(value, by):
        if back:
            moved = pltpu.roll(value, count - by, 0)
            return jnp.where(row < count - by, moved, 0.0)
        moved = pltpu.roll(value, by, 0)
        return jnp.where(row >= by, moved, 0.0)

    total = shifted(finals, 1)
    by = 1
    while by < count:
        total = total + jnp.exp(rate * (-1.0 * span * by)) * shifted(total, by)
        by *= 2
    return total


def scan_kernel(
    groups,
    runs,
    order,
    me_ref,
    residue_ref,
    rate_ref,
    *refs,
):
    inputs = 1 + max(run[0] for run in runs)
    arrays, refs = refs[: 2 * inputs + 1], refs[2 * inputs + 1 :]
    hyena_ref, grad_ref = refs[:2]
    proj_refs, refs = refs[2 : 2 + len(order)], refs[2 + len(order) :]
    gated_s, slope_s, conv_s, back_s, feats_s, arrived = refs[:6]
    held = refs[6:]
    cot_ref, own, other = held[0], held[1 : 1 + inputs], held[1 + inputs :]
    copies = [
        pltpu.make_async_copy(array, here, arrived.at[k])
        for k, (array, here) in enumerate(zip(arrays, held))
    ]
    for copy in copies:
        copy.start()
    length, width = cot_ref.shape
    chunks = PLANE * groups
    span = length // chunks
    modes = rate_ref.shape[0]
    me = me_ref[0]

    def place(group, member):
        return lax.rem(me // PLANE + group, groups) * PLANE + (member ^ lax.rem(me, PLANE))

    def aligned(start, size):
        return pl.ds(pl.multiple_of(start, size), size)

    copies[0].wait()
    waited = set()
    for source, offset, group, base, members, count, first in sorted(runs):
        if source not in waited:
            waited.add(source)
            copies[1 + source].wait()
            copies[1 + inputs + source].wait()

        def before(step, _, source=source, offset=offset, group=group, base=base, count=count, first=first):
            member = base + step
            index = place(group, member)
            rows = pl.ds(pl.multiple_of(offset + step * count, 16), count)
            feats = own[source][rows, :] + other[source][rows, :].astype(jnp.float32)
            feats = rounded(feats)
            slot = (group * PLANE + member) * span + first
            feats_s[pl.ds(pl.multiple_of(slot, 16), count), :] = feats
            cot = cot_ref[pl.ds(pl.multiple_of(index * span + first, 16), count), :]
            query, key = feats[:, :width], feats[:, width : 2 * width]
            into = pl.ds(first * chunks + index, count, stride=chunks)
            gated_s[into, :] = rounded(key * feats[:, 2 * width :])
            slope_s[into, :] = rounded(cot.astype(jnp.float32) * query)
            return 0

        lax.fori_loop(0, members, before, 0)

    def at(step):
        return aligned(step * chunks, chunks)

    zero = jnp.zeros((chunks, width), jnp.float32)
    scale = 1.0 / math.sqrt(length)
    for first in range(0, modes, GROUP):
        count = min(GROUP, modes - first)
        rates = [
            jnp.broadcast_to(rate_ref[m : m + 1, :], (chunks, width))
            for m in range(first, first + count)
        ]
        decays = [jnp.exp(-rate) for rate in rates]
        norms = [jnp.sqrt(2.0 * rate) for rate in rates]
        gains = [
            residue_ref[first + n : first + n + 1, :] * norms[n] for n in range(count)
        ]

        def sums(step, state):
            ahead, behind = state
            gated = gated_s[at(step), :]
            slope = slope_s[at(span - 1 - step), :]
            return (
                tuple(decays[n] * ahead[n] + gated for n in range(count)),
                tuple(decays[n] * behind[n] + slope for n in range(count)),
            )

        ahead, behind = lax.fori_loop(0, span, sums, ((zero,) * count, (zero,) * count), unroll=4)
        ahead = tuple(earlier_sum(ahead[n], rates[n], span, False) for n in range(count))
        behind = tuple(earlier_sum(behind[n], rates[n], span, True) for n in range(count))

        def outs(step, state):
            ahead, behind, grads = state
            other = span - 1 - step
            gated = gated_s[at(step), :]
            slope = slope_s[at(step), :]
            slope_back = slope_s[at(other), :]
            ahead = tuple(decays[n] * ahead[n] + gated for n in range(count))
            behind = tuple(decays[n] * behind[n] + slope_back for n in range(count))
            grads = tuple(grads[n] + slope * ahead[n] for n in range(count))
            conv = sum(gains[n] * ahead[n] for n in range(count))
            back = sum(gains[n] * behind[n] for n in range(count))
            if first:
                conv = conv + conv_s[at(step), :]
                back = back + back_s[at(other), :]
            conv_s[at(step), :] = conv
            back_s[at(other), :] = back
            return ahead, behind, grads

        _, _, grads = lax.fori_loop(0, span, outs, (ahead, behind, (zero,) * count), unroll=2)
        for n in range(count):
            total = jnp.sum(grads[n] * norms[n], axis=0, keepdims=True) * scale
            grad_ref[first + n : first + n + 1, :] = total

    for proj_ref, pieces in zip(proj_refs, order):
        start = 0
        for group, base, members in pieces:

            def after(step, _, proj_ref=proj_ref, start=start, group=group, base=base):
                member = base + step
                index = place(group, member)
                feats = feats_s[aligned((group * PLANE + member) * span, span), :]
                query, key = feats[:, :width], feats[:, width : 2 * width]
                cot = cot_ref[aligned(index * span, span), :].astype(jnp.float32)
                conv = rounded(conv_s[pl.ds(index, span, stride=chunks), :])
                back = rounded(back_s[pl.ds(index, span, stride=chunks), :])
                hyena_ref[aligned(index * span, span), :] = narrowed(query * conv)
                rows = aligned(start + step * span, span)
                proj_ref[rows, :width] = narrowed(cot * conv)
                proj_ref[rows, width : 2 * width] = narrowed(back * feats[:, 2 * width :])
                proj_ref[rows, 2 * width :] = narrowed(back * key)
                return 0

            lax.fori_loop(0, members, after, 0)
            start += members * span


def scan_all(me, cot_cols, residue_rows, rate_rows, runs, order, own, other):
    length, width = cot_cols.shape
    span = length // (PLANE * PLANE)
    vmem = pl.BlockSpec(memory_space=pltpu.VMEM)
    arrays = (cot_cols, *own, *other)
    outs = pl.pallas_call(
        functools.partial(scan_kernel, PLANE, runs, order),
        out_shape=(
            jax.ShapeDtypeStruct((length, width), jnp.bfloat16),
            jax.ShapeDtypeStruct(rate_rows.shape, jnp.float32),
        )
        + tuple(
            jax.ShapeDtypeStruct((span * sum(piece[2] for piece in pieces), 3 * width), jnp.bfloat16)
            for pieces in order
        ),
        in_specs=[pl.BlockSpec(memory_space=pltpu.SMEM), vmem, vmem]
        + [pl.BlockSpec(memory_space=pl.ANY)] * len(arrays),
        out_specs=(vmem,) * (2 + len(order)),
        scratch_shapes=[pltpu.VMEM((length, width), jnp.float32)] * 4
        + [pltpu.VMEM((length, 3 * width), jnp.float32), pltpu.SemaphoreType.DMA((len(arrays),))]
        + [pltpu.VMEM(array.shape, array.dtype) for array in arrays],
        compiler_params=pltpu.CompilerParams(vmem_limit_bytes=40 * 2**20),
        name="modal_scan",
    )(me, residue_rows, rate_rows, *arrays)
    return outs[0], outs[1], outs[2:]


def swapped(value):
    return lax.ppermute(value, "tp", [(0, 1), (1, 0)])


def over_x(value):
    return lax.ppermute(value, "ctx", [(i, i ^ 1) for i in range(lax.axis_size("ctx"))])


def over_y(value):
    return lax.ppermute(value, "ctx", [(i, i ^ 2) for i in range(lax.axis_size("ctx"))])


def up(value):
    count = lax.axis_size("ctx")
    return lax.ppermute(value, "ctx", [(i, (i + PLANE) % count) for i in range(count)])


def down(value):
    count = lax.axis_size("ctx")
    return lax.ppermute(value, "ctx", [((i + PLANE) % count, i) for i in range(count)])


def stack(*parts):
    return jnp.concatenate(parts, axis=0)


def beside(*parts):
    return jnp.concatenate(parts, axis=1)


def narrowed(value):
    return value.astype(jnp.bfloat16)


def widened(value):
    return value.astype(jnp.float32)


def all_ways(for_x, for_y, for_above, for_below):
    return lax.optimization_barrier((over_x(for_x), over_y(for_y), up(for_above), down(for_below)))


def gather_groups(tokens, prepared):
    span = tokens.shape[0]
    n, m = span * 3 // 4, span // 4
    nh, mh = n // 2, m // 2
    wide, narrow = tokens[:n], tokens[n:]
    own_x, own_y, wide_3, wide_1 = all_ways(tokens, tokens, wide, wide)
    own_x, prepared = lax.optimization_barrier((own_x, prepared))
    members = (narrow, own_x[n:], own_y[n:])
    first = (tokens, own_x, own_y, wide_3, wide_1)
    second = all_ways(
        stack(own_y[:nh], own_y[n : n + mh], wide_3, wide_1),
        stack(own_x[nh:n], own_x[n + mh :], wide_3, wide_1),
        stack(wide_3[:nh], *members),
        stack(wide_1[nh:], *members),
    )
    got_x, got_y, below, above = second
    start = nh + mh
    across = (got_x[nh:start], got_y[nh:start])
    wide_2 = (below[:nh], above[:nh])
    third = all_ways(
        stack(got_y[start : start + nh], got_y[start + n : start + n + nh], *wide_2),
        stack(got_x[start + nh : start + n], got_x[start + n + nh :], *wide_2),
        stack(*across, below[nh : 2 * nh]),
        stack(*across, above[2 * nh :]),
    )
    got_x, got_y, below, above = third
    fourth = all_ways(got_y[n : n + nh], got_x[n + nh :], below[:mh], above[mh:m])
    runs = [
        (0, 0, 0, 0, 3, span, 0),
        (0, 3 * span, 3, 0, 1, n, 0),
        (0, 3 * span + n, 1, 0, 1, n, 0),
    ]
    offset = 0
    for side in range(2):
        runs += [
            (1, offset, 0, 3, 1, nh, side * nh),
            (1, offset + nh, 0, 3, 1, mh, n + side * mh),
            (1, offset + start, 3, 1 + side, 1, n, 0),
            (1, offset + start + n, 1, 1 + side, 1, n, 0),
        ]
        offset += start + 2 * n
    for side in range(2):
        runs += [
            (1, offset, 2, 0, 1, nh, side * nh),
            (1, offset + nh, 3 - 2 * side, 0, 3, m, n),
        ]
        offset += nh + 3 * m
    offset = 0
    for side in range(2):
        runs += [
            (2, offset, 3, 3, 1, nh, side * nh),
            (2, offset + nh, 1, 3, 1, nh, side * nh),
            (2, offset + n, 2, 1 + side, 1, n, 0),
        ]
        offset += 2 * n
    runs += [
        (2, offset, 3, 3, 1, m, n),
        (2, offset + m, 2, 0, 1, m, n),
        (2, offset + 2 * m, 2, 1, 1, mh, n),
        (2, offset + 2 * m + mh, 1, 3, 1, m, n),
        (2, offset + 3 * m + mh, 2, 1, 1, mh, n + mh),
        (2, offset + 3 * m + 2 * mh, 2, 2, 1, m, n),
        (3, 0, 2, 3, 1, nh, 0),
        (3, nh, 2, 3, 1, nh, nh),
        (3, n, 2, 3, 1, mh, n),
        (3, n + mh, 2, 3, 1, mh, n + mh),
    ]
    return [stack(*part) for part in (first, second, third, fourth)], tuple(runs), prepared


ORDER = (((2, 0, 4), (1, 3, 1), (3, 3, 1)), ((1, 0, 3), (3, 0, 3), (0, 0, 4)))


def scatter_sum(early, later, matrix, hyena):
    span = early.shape[0] // 6
    columns = matrix.shape[1]
    wide, narrow = columns * 3 // 8, columns // 8
    blocks = {}

    def product(part, other):
        both = beside(part, other)
        return narrowed(jnp.dot(both, matrix, preferred_element_type=jnp.float32))

    def keep(value, pieces):
        start = 0
        for group, base, members in pieces:
            for member in range(base, base + members):
                blocks[group, member] = value[start : start + span]
                start += span

    def term(group, member, side):
        return blocks[group, member][:, side * wide : (side + 1) * wide]

    def low(group, member, side):
        first = 2 * wide + side * narrow
        return blocks[group, member][:, first : first + narrow]

    def total(*parts):
        return sum(widened(part) for part in parts)

    def added(*parts):
        return narrowed(total(*parts))

    def cut(value, *widths):
        parts, start = [], 0
        for width in widths:
            parts.append(value[:, start : start + width])
            start += width
        return parts

    early = product(early, swapped(early))
    keep(early, ORDER[0])
    other = swapped(later)
    across_y, across_x, from_below, from_above = all_ways(
        term(2, 3, 0), term(2, 3, 1), low(2, 3, 0), low(2, 3, 1)
    )
    later, across_x = lax.optimization_barrier((later, across_x))
    got_x, got_y, below, above = all_ways(
        beside(term(2, 1, 0), added(term(2, 1, 1), across_x), term(1, 3, 0), term(3, 3, 0)),
        beside(added(term(2, 2, 0), across_y), term(2, 2, 1), term(1, 3, 1), term(3, 3, 1)),
        beside(
            added(low(1, 3, 0), from_below), low(1, 3, 1), *[low(2, k, 0) for k in range(3)]
        ),
        beside(
            low(3, 3, 0), added(low(3, 3, 1), from_above), *[low(2, k, 1) for k in range(3)]
        ),
    )
    later = product(later, other)
    later, hyena, got_x = lax.optimization_barrier((later, hyena, got_x))
    keep(later, ORDER[1])
    hyena_out = lax.all_to_all(hyena, "ctx", split_axis=0, concat_axis=1, tiled=True).T
    *own_x, across_1y, across_3y = cut(got_x, *[wide] * 4)
    *own_y, across_1x, across_3x = cut(got_y, *[wide] * 4)
    below_0, below_1, *from_below = cut(below, *[narrow] * 5)
    above_0, above_1, *from_above = cut(above, *[narrow] * 5)
    sum_2 = [added(term(2, 0, side), own_x[side], own_y[side]) for side in (0, 1)]
    low_3 = [added(low(0, 3, 0), below_0, above_0), added(low(0, 3, 1), below_1, above_1)]
    for_above, for_below = [], []
    for k in range(3):
        for_above += [added(low(1, k, 0), from_below[k]), low(1, k, 1)]
        for_below += [low(3, k, 0), added(low(3, k, 1), from_above[k])]
    got_x, got_y, below, above = all_ways(
        beside(
            term(1, 1, 0),
            added(term(1, 1, 1), across_1x),
            term(3, 1, 0),
            added(term(3, 1, 1), across_3x),
            term(0, 3, 0),
            low_3[0],
        ),
        beside(
            added(term(1, 2, 0), across_1y),
            term(1, 2, 1),
            added(term(3, 2, 0), across_3y),
            term(3, 2, 1),
            term(0, 3, 1),
            low_3[1],
        ),
        beside(sum_2[0], *for_above),
        beside(sum_2[1], *for_below),
    )
    *own_x, across_y, low_across_y = cut(got_x, *[wide] * 5, narrow)
    *own_y, across_x, low_across_x = cut(got_y, *[wide] * 5, narrow)
    from_below, *low_below = cut(below, wide, *[narrow] * 6)
    from_above, *low_above = cut(above, wide, *[narrow] * 6)
    low_own = [
        [total(low(0, k, side), low_below[2 * k + side], low_above[2 * k + side]) for side in (0, 1)]
        for k in range(3)
    ]
    got_x, got_y, below, above = all_ways(
        beside(
            term(0, 1, 0),
            added(term(0, 1, 1), across_x),
            narrowed(low_own[1][0]),
            added(low_own[1][1], low_across_x),
        ),
        beside(
            added(term(0, 2, 0), across_y),
            term(0, 2, 1),
            added(low_own[2][0], low_across_y),
            narrowed(low_own[2][1]),
        ),
        beside(
            added(term(1, 0, 0), own_x[0], own_y[0], from_below),
            added(term(1, 0, 1), own_x[1], own_y[1]),
        ),
        beside(
            added(term(3, 0, 0), own_x[2], own_y[2]),
            added(term(3, 0, 1), own_x[3], own_y[3], from_above),
        ),
    )
    return (
        beside(
            added(
                blocks[0, 0][:, : 2 * wide], got_x[:, : 2 * wide], got_y[:, : 2 * wide], below, above
            ),
            added(
                beside(*low_own[0]), got_x[:, 2 * wide :], got_y[:, 2 * wide :]
            ),
        ),
        hyena_out,
    )


def gather_tokens(tokens, weights, residues, decay_rates, cotangent):
    core = lax.axis_index("tp")
    me = lax.axis_index("ctx").astype(jnp.int32).reshape(1)
    half = tokens.shape[1] // 2
    channels = weights.shape[1]
    rows = weights[0].swapaxes(0, 1).reshape(3 * channels, 2 * half)
    kept = lax.dynamic_slice_in_dim(rows, core * half, half, 1)
    taken = swapped(lax.dynamic_slice_in_dim(rows, (1 - core) * half, half, 1))
    cot_cols = lax.all_to_all(cotangent.T, "ctx", split_axis=1, concat_axis=0, tiled=True)
    parts, runs, (kept, taken, cot_cols) = gather_groups(
        lax.dynamic_slice_in_dim(tokens, core * half, half, 1), (kept, taken, cot_cols)
    )

    def project(part, matrix):
        return jnp.einsum("td,rd->tr", part, matrix, preferred_element_type=jnp.float32)

    other = [swapped(narrowed(project(part, taken))) for part in parts]
    own = [project(part, kept) for part in parts]
    hyena, grads, (early, later) = scan_all(
        me, cot_cols, residues[0].T, decay_rates[0].T, runs, ORDER, own, other
    )
    grad_input, hyena_out = scatter_sum(early, later, stack(kept, taken), hyena)
    return (hyena_out, grad_input, grads.T[None])


def shards(tokens, weights, residues, decay_rates, cotangent):
    ctx, tp = lax.axis_size("ctx"), lax.axis_size("tp")
    if ctx == 4 * PLANE and tp == 2 and weights.size * tp > 2 * tokens.size:
        return gather_tokens(tokens, weights, residues, decay_rates, cotangent)
    return gather_weights(tokens, weights, residues, decay_rates, cotangent)


def solution(mesh):
    return jax.shard_map(
        shards,
        mesh=mesh,
        in_specs=(
            P("ctx", None),
            P("tp", "ctx", None, None),
            P("tp", "ctx", None),
            P("tp", "ctx", None),
            P("tp", "ctx"),
        ),
        out_specs=(P("tp", "ctx"), P("ctx", "tp"), P("tp", "ctx", None)),
        check_vma=False,
    )
```

```python
import functools
import math

import jax
import jax.numpy as jnp
from jax import lax
from jax.experimental import pallas as pl
from jax.experimental.pallas import tpu as pltpu
from jax.sharding import PartitionSpec as P


def precise(form, left, right):
    return jnp.einsum(
        form, left, right, precision=lax.Precision.HIGHEST, preferred_element_type=jnp.float32
    )


def tripled(form, left, right):
    return jnp.einsum(
        form, left, right, precision=lax.Precision.HIGH, preferred_element_type=jnp.float32
    )


def angle_table(row_count, col_count, period):
    product = (
        jnp.arange(row_count, dtype=jnp.int32)[:, None]
        * jnp.arange(col_count, dtype=jnp.int32)[None, :]
        % period
    )
    angles = product.astype(jnp.float32) * (2.0 * math.pi / period)
    return (jnp.cos(angles), jnp.sin(angles))


def make_tables(length):
    padded = 2 * length
    outer = math.gcd(padded, 1 << (padded.bit_length() - 1) // 2)
    inner = padded // outer
    cos_outer, sin_outer = angle_table(outer, outer, outer)
    cos_inner, sin_inner = angle_table(inner, inner, inner)
    twist_cos, twist_sin = angle_table(outer, inner, padded)
    return (outer, inner, cos_outer, sin_outer, cos_inner, sin_inner, twist_cos, twist_sin)


def spectrum(signal, tables, product):
    outer, inner, cos_outer, sin_outer, cos_inner, sin_inner, twist_cos, twist_sin = tables
    half_rows = outer // 2
    blocks = signal.reshape(signal.shape[0], half_rows, inner)
    first_re = product("kp,bpq->bkq", cos_outer[:, :half_rows], blocks)
    first_im = -product("kp,bpq->bkq", sin_outer[:, :half_rows], blocks)
    turned_re = first_re * twist_cos + first_im * twist_sin
    turned_im = first_im * twist_cos - first_re * twist_sin
    spec_re = product("bkq,qj->bkj", turned_re, cos_inner) + product(
        "bkq,qj->bkj", turned_im, sin_inner
    )
    spec_im = product("bkq,qj->bkj", turned_im, cos_inner) - product(
        "bkq,qj->bkj", turned_re, sin_inner
    )
    return (spec_re, spec_im)


def signal_of(spec_re, spec_im, tables):
    outer, inner, cos_outer, sin_outer, cos_inner, sin_inner, twist_cos, twist_sin = tables
    half_rows = outer // 2
    back_re = tripled("bkj,jq->bkq", spec_re, cos_inner) - tripled(
        "bkj,jq->bkq", spec_im, sin_inner
    )
    back_im = tripled("bkj,jq->bkq", spec_im, cos_inner) + tripled(
        "bkj,jq->bkq", spec_re, sin_inner
    )
    turned_re = back_re * twist_cos - back_im * twist_sin
    turned_im = back_im * twist_cos + back_re * twist_sin
    values = tripled("pk,bkq->bpq", cos_outer[:half_rows, :], turned_re) - tripled(
        "pk,bkq->bpq", sin_outer[:half_rows, :], turned_im
    )
    return values.reshape(values.shape[0], half_rows * inner) * (1.0 / (outer * inner))


def spec_product(left_re, left_im, right_re, right_im):
    return (left_re * right_re - left_im * right_im, left_re * right_im + left_im * right_re)


def conj_product(left_re, left_im, right_re, right_im):
    return (left_re * right_re + left_im * right_im, left_re * right_im - left_im * right_re)


def filter_basis(residue_loc, rate_loc, length):
    position = jnp.arange(length, dtype=jnp.float32)
    basis_all = jnp.sqrt(2.0 * rate_loc)[:, :, None] * jnp.exp(
        -rate_loc[:, :, None] * position[None, None, :]
    )
    return (basis_all, precise("cm,cmt->ct", residue_loc, basis_all))


def forward_cols(gated_cols, taps_re, taps_im, tables):
    gated_re, gated_im = spectrum(gated_cols.astype(jnp.float32), tables, tripled)
    conv_re, conv_im = spec_product(gated_re, gated_im, taps_re, taps_im)
    conv_cols = signal_of(conv_re, conv_im, tables).astype(jnp.bfloat16)
    return (conv_cols, gated_re, gated_im)


def backward_cols(slope_cols, gated_re, gated_im, taps_re, taps_im, basis_all, tables, length):
    slope_re, slope_im = spectrum(slope_cols.astype(jnp.float32), tables, tripled)
    grad_re, grad_im = conj_product(taps_re, taps_im, slope_re, slope_im)
    back_cols = signal_of(grad_re, grad_im, tables).astype(jnp.bfloat16)
    lag_re, lag_im = conj_product(gated_re, gated_im, slope_re, slope_im)
    taps_grad = signal_of(lag_re, lag_im, tables)
    grad_residue = precise("ct,cmt->cm", taps_grad, basis_all) * (1.0 / math.sqrt(length))
    return (back_cols, grad_residue)


def gather_weights(tokens, weights, residues, decay_rates, cotangent):
    gathered = lax.all_gather(weights, "ctx", axis=1, tiled=True)
    projected = jnp.einsum("xcpd,td->xcpt", gathered, tokens, preferred_element_type=jnp.float32)
    features = projected[0].astype(jnp.bfloat16)
    query_f = features[:, 0].astype(jnp.float32)
    key_part = features[:, 1].astype(jnp.float32)
    value_part = features[:, 2].astype(jnp.float32)
    gated_in = (key_part * value_part).astype(jnp.bfloat16)
    slope_in = (cotangent.astype(jnp.float32) * query_f).astype(jnp.bfloat16)
    length = tokens.shape[0] * lax.axis_size("ctx")
    tables = make_tables(length)
    basis_all, taps_full = filter_basis(residues[0], decay_rates[0], length)
    taps_re, taps_im = spectrum(taps_full, tables, precise)
    gated_cols = lax.all_to_all(gated_in, "ctx", split_axis=0, concat_axis=1, tiled=True)
    conv_cols, gated_re, gated_im = forward_cols(gated_cols, taps_re, taps_im, tables)
    conv_rows = lax.all_to_all(conv_cols, "ctx", split_axis=1, concat_axis=0, tiled=True)
    slope_cols = lax.all_to_all(slope_in, "ctx", split_axis=0, concat_axis=1, tiled=True)
    back_cols, grad_residue = backward_cols(
        slope_cols, gated_re, gated_im, taps_re, taps_im, basis_all, tables, length
    )
    back_rows = lax.all_to_all(back_cols, "ctx", split_axis=1, concat_axis=0, tiled=True)
    conv_f = conv_rows.astype(jnp.float32)
    back_f = back_rows.astype(jnp.float32)
    hyena_out = (query_f * conv_f).astype(jnp.bfloat16)
    grad_query = (cotangent.astype(jnp.float32) * conv_f).astype(jnp.bfloat16)
    grad_key = (back_f * value_part).astype(jnp.bfloat16)
    grad_value = (back_f * key_part).astype(jnp.bfloat16)
    grad_proj = jnp.stack([grad_query, grad_key, grad_value], axis=1)
    partial_value = jnp.einsum(
        "cpt,cpd->td", grad_proj, gathered[0], preferred_element_type=jnp.float32
    )
    grad_input = lax.psum_scatter(
        partial_value.astype(jnp.bfloat16), "tp", scatter_dimension=1, tiled=True
    )
    return (hyena_out, grad_input, grad_residue[None])


GROUP = 4
PLANE = 4


def rounded(value):
    return value.astype(jnp.bfloat16).astype(jnp.float32)


def earlier_sum(finals, rate, span, back):
    count = finals.shape[0]
    row = lax.broadcasted_iota(jnp.int32, finals.shape, 0)

    def shifted(value, by):
        if back:
            moved = pltpu.roll(value, count - by, 0)
            return jnp.where(row < count - by, moved, 0.0)
        moved = pltpu.roll(value, by, 0)
        return jnp.where(row >= by, moved, 0.0)

    total = shifted(finals, 1)
    by = 1
    while by < count:
        total = total + jnp.exp(rate * (-1.0 * span * by)) * shifted(total, by)
        by *= 2
    return total


def scan_kernel(
    groups,
    runs,
    order,
    me_ref,
    residue_ref,
    rate_ref,
    *refs,
):
    inputs = 1 + max(run[0] for run in runs)
    arrays, refs = refs[: 2 * inputs + 1], refs[2 * inputs + 1 :]
    hyena_ref, grad_ref = refs[:2]
    proj_refs, refs = refs[2 : 2 + len(order)], refs[2 + len(order) :]
    gated_s, slope_s, conv_s, back_s, feats_s, arrived = refs[:6]
    held = refs[6:]
    cot_ref, own, other = held[0], held[1 : 1 + inputs], held[1 + inputs :]
    copies = [
        pltpu.make_async_copy(array, here, arrived.at[k])
        for k, (array, here) in enumerate(zip(arrays, held))
    ]
    for copy in copies:
        copy.start()
    length, width = cot_ref.shape
    chunks = PLANE * groups
    span = length // chunks
    modes = rate_ref.shape[0]
    me = me_ref[0]

    def place(group, member):
        return lax.rem(me // PLANE + group, groups) * PLANE + (member ^ lax.rem(me, PLANE))

    def aligned(start, size):
        return pl.ds(pl.multiple_of(start, size), size)

    copies[0].wait()
    waited = set()
    for source, offset, group, base, members, count, first in sorted(runs):
        if source not in waited:
            waited.add(source)
            copies[1 + source].wait()
            copies[1 + inputs + source].wait()

        def before(step, _, source=source, offset=offset, group=group, base=base, count=count, first=first):
            member = base + step
            index = place(group, member)
            rows = pl.ds(pl.multiple_of(offset + step * count, 16), count)
            feats = own[source][rows, :] + other[source][rows, :].astype(jnp.float32)
            feats = rounded(feats)
            slot = (group * PLANE + member) * span + first
            feats_s[pl.ds(pl.multiple_of(slot, 16), count), :] = feats
            cot = cot_ref[pl.ds(pl.multiple_of(index * span + first, 16), count), :]
            query, key = feats[:, :width], feats[:, width : 2 * width]
            into = pl.ds(first * chunks + index, count, stride=chunks)
            gated_s[into, :] = rounded(key * feats[:, 2 * width :])
            slope_s[into, :] = rounded(cot.astype(jnp.float32) * query)
            return 0

        lax.fori_loop(0, members, before, 0)

    def at(step):
        return aligned(step * chunks, chunks)

    zero = jnp.zeros((chunks, width), jnp.float32)
    scale = 1.0 / math.sqrt(length)
    for first in range(0, modes, GROUP):
        count = min(GROUP, modes - first)
        rates = [
            jnp.broadcast_to(rate_ref[m : m + 1, :], (chunks, width))
            for m in range(first, first + count)
        ]
        decays = [jnp.exp(-rate) for rate in rates]
        norms = [jnp.sqrt(2.0 * rate) for rate in rates]
        gains = [
            residue_ref[first + n : first + n + 1, :] * norms[n] for n in range(count)
        ]

        def sums(step, state):
            ahead, behind = state
            gated = gated_s[at(step), :]
            slope = slope_s[at(span - 1 - step), :]
            return (
                tuple(decays[n] * ahead[n] + gated for n in range(count)),
                tuple(decays[n] * behind[n] + slope for n in range(count)),
            )

        ahead, behind = lax.fori_loop(0, span, sums, ((zero,) * count, (zero,) * count), unroll=4)
        ahead = tuple(earlier_sum(ahead[n], rates[n], span, False) for n in range(count))
        behind = tuple(earlier_sum(behind[n], rates[n], span, True) for n in range(count))

        def outs(step, state):
            ahead, behind, grads = state
            other = span - 1 - step
            gated = gated_s[at(step), :]
            slope = slope_s[at(step), :]
            slope_back = slope_s[at(other), :]
            ahead = tuple(decays[n] * ahead[n] + gated for n in range(count))
            behind = tuple(decays[n] * behind[n] + slope_back for n in range(count))
            grads = tuple(grads[n] + slope * ahead[n] for n in range(count))
            conv = sum(gains[n] * ahead[n] for n in range(count))
            back = sum(gains[n] * behind[n] for n in range(count))
            if first:
                conv = conv + conv_s[at(step), :]
                back = back + back_s[at(other), :]
            conv_s[at(step), :] = conv
            back_s[at(other), :] = back
            return ahead, behind, grads

        _, _, grads = lax.fori_loop(0, span, outs, (ahead, behind, (zero,) * count), unroll=2)
        for n in range(count):
            total = jnp.sum(grads[n] * norms[n], axis=0, keepdims=True) * scale
            grad_ref[first + n : first + n + 1, :] = total

    for proj_ref, pieces in zip(proj_refs, order):
        start = 0
        for group, base, members in pieces:

            def after(step, _, proj_ref=proj_ref, start=start, group=group, base=base):
                member = base + step
                index = place(group, member)
                feats = feats_s[aligned((group * PLANE + member) * span, span), :]
                query, key = feats[:, :width], feats[:, width : 2 * width]
                cot = cot_ref[aligned(index * span, span), :].astype(jnp.float32)
                conv = rounded(conv_s[pl.ds(index, span, stride=chunks), :])
                back = rounded(back_s[pl.ds(index, span, stride=chunks), :])
                hyena_ref[aligned(index * span, span), :] = narrowed(query * conv)
                rows = aligned(start + step * span, span)
                proj_ref[rows, :width] = narrowed(cot * conv)
                proj_ref[rows, width : 2 * width] = narrowed(back * feats[:, 2 * width :])
                proj_ref[rows, 2 * width :] = narrowed(back * key)
                return 0

            lax.fori_loop(0, members, after, 0)
            start += members * span


def scan_all(me, cot_cols, residue_rows, rate_rows, runs, order, own, other):
    length, width = cot_cols.shape
    span = length // (PLANE * PLANE)
    vmem = pl.BlockSpec(memory_space=pltpu.VMEM)
    arrays = (cot_cols, *own, *other)
    outs = pl.pallas_call(
        functools.partial(scan_kernel, PLANE, runs, order),
        out_shape=(
            jax.ShapeDtypeStruct((length, width), jnp.bfloat16),
            jax.ShapeDtypeStruct(rate_rows.shape, jnp.float32),
        )
        + tuple(
            jax.ShapeDtypeStruct((span * sum(piece[2] for piece in pieces), 3 * width), jnp.bfloat16)
            for pieces in order
        ),
        in_specs=[pl.BlockSpec(memory_space=pltpu.SMEM), vmem, vmem]
        + [pl.BlockSpec(memory_space=pl.ANY)] * len(arrays),
        out_specs=(vmem,) * (2 + len(order)),
        scratch_shapes=[pltpu.VMEM((length, width), jnp.float32)] * 4
        + [pltpu.VMEM((length, 3 * width), jnp.float32), pltpu.SemaphoreType.DMA((len(arrays),))]
        + [pltpu.VMEM(array.shape, array.dtype) for array in arrays],
        compiler_params=pltpu.CompilerParams(vmem_limit_bytes=40 * 2**20),
        name="modal_scan",
    )(me, residue_rows, rate_rows, *arrays)
    return outs[0], outs[1], outs[2:]


def swapped(value):
    return lax.ppermute(value, "tp", [(0, 1), (1, 0)])


def over_x(value):
    return lax.ppermute(value, "ctx", [(i, i ^ 1) for i in range(lax.axis_size("ctx"))])


def over_y(value):
    return lax.ppermute(value, "ctx", [(i, i ^ 2) for i in range(lax.axis_size("ctx"))])


def up(value):
    count = lax.axis_size("ctx")
    return lax.ppermute(value, "ctx", [(i, (i + PLANE) % count) for i in range(count)])


def down(value):
    count = lax.axis_size("ctx")
    return lax.ppermute(value, "ctx", [((i + PLANE) % count, i) for i in range(count)])


def stack(*parts):
    return jnp.concatenate(parts, axis=0)


def beside(*parts):
    return jnp.concatenate(parts, axis=1)


def narrowed(value):
    return value.astype(jnp.bfloat16)


def widened(value):
    return value.astype(jnp.float32)


def halves_kernel(plan, core_ref, array, *refs):
    outs, arrived = refs[:-1], refs[-1]
    half = array.shape[1] // 2
    copies = []
    for k, (out, (count, mine)) in enumerate(zip(outs, plan)):
        side = core_ref[0] if mine else 1 - core_ref[0]
        part = array.at[pl.ds(0, count), pl.ds(pl.multiple_of(side * half, half), half)]
        copies.append(pltpu.make_async_copy(part, out, arrived.at[k]))
    for copy in copies:
        copy.start()
    for copy in copies:
        copy.wait()


def halves(array, *plan):
    half = array.shape[1] // 2
    core = lax.axis_index("tp").astype(jnp.int32).reshape(1)
    moved = sum(2 * count * half for count, _ in plan)
    return pl.pallas_call(
        functools.partial(halves_kernel, plan),
        out_shape=tuple(jax.ShapeDtypeStruct((count, half), jnp.bfloat16) for count, _ in plan),
        in_specs=[pl.BlockSpec(memory_space=pltpu.SMEM), pl.BlockSpec(memory_space=pl.ANY)],
        out_specs=(pl.BlockSpec(memory_space=pltpu.VMEM),) * len(plan),
        scratch_shapes=[pltpu.SemaphoreType.DMA((len(plan),))],
        compiler_params=pltpu.CompilerParams(vmem_limit_bytes=16 * 2**20),
        cost_estimate=pl.CostEstimate(flops=0, bytes_accessed=2 * moved, transcendentals=0),
        name="halves",
    )(core, array)


def assemble_kernel(inputs, plans, *refs):
    arrays, refs = refs[:inputs], refs[inputs:]
    outs, refs = refs[: len(plans)], refs[len(plans) :]
    arrived, held = refs[0], refs[1:]
    started, k, slot = [], 0, 0
    pending = []
    for out, plan in zip(outs, plans):
        for row, col, height, width, sources in plan:
            here = out.at[pl.ds(row, height), pl.ds(col, width)]
            single = len(sources) == 1
            mine = []
            for index, from_row, from_col in sources:
                part = arrays[index].at[pl.ds(from_row, height), pl.ds(from_col, width)]
                into = here if single else held[slot]
                copy = pltpu.make_async_copy(part, into, arrived.at[k])
                copy.start()
                mine.append((copy, into))
                k += 1
                slot += 0 if single else 1
            if single:
                started.append(mine[0][0])
            else:
                pending.append((here, mine))
    for here, mine in pending:
        for copy, _ in mine:
            copy.wait()
        here[...] = narrowed(sum(widened(into[...]) for _, into in mine))
    for copy in started:
        copy.wait()


def assemble(arrays, *plans):
    sources = [(piece, source) for plan in plans for piece in plan for source in piece[4]]
    sums = [piece for piece, _ in sources if len(piece[4]) > 1]
    shapes = [
        (max(p[0] + p[2] for p in plan), max(p[1] + p[3] for p in plan)) for plan in plans
    ]
    moved = sum(2 * rows * cols for rows, cols in shapes)
    return pl.pallas_call(
        functools.partial(assemble_kernel, len(arrays), plans),
        out_shape=tuple(jax.ShapeDtypeStruct(shape, jnp.bfloat16) for shape in shapes),
        in_specs=[pl.BlockSpec(memory_space=pl.ANY)] * len(arrays),
        out_specs=(pl.BlockSpec(memory_space=pltpu.VMEM),) * len(plans),
        scratch_shapes=[pltpu.SemaphoreType.DMA((len(sources),))]
        + [pltpu.VMEM((piece[2], piece[3]), jnp.bfloat16) for piece in sums],
        compiler_params=pltpu.CompilerParams(vmem_limit_bytes=24 * 2**20),
        cost_estimate=pl.CostEstimate(flops=moved, bytes_accessed=4 * moved, transcendentals=0),
        name="assemble",
    )(*arrays)


def rows_of(*parts):
    plan, start = [], 0
    for index, first, count in parts:
        plan.append((start, count, [(index, first, 0)]))
        start += count
    return plan


def full_width(columns, plan):
    return [(row, 0, count, columns, sources) for row, count, sources in plan]


def columns_of(height, *parts):
    plan, start = [], 0
    for width, sources in parts:
        plan.append((0, start, height, width, sources))
        start += width
    return plan


def all_ways(for_x, for_y, for_above, for_below):
    return lax.optimization_barrier((over_x(for_x), over_y(for_y), up(for_above), down(for_below)))


def gather_groups(tokens, matrices, later):
    span = tokens.shape[0]
    n, m = span * 3 // 4, span // 4
    nh, mh = n // 2, m // 2
    columns = tokens.shape[1] // 2

    def put(arrays, *plans):
        return assemble(arrays, *[full_width(columns, rows_of(*plan)) for plan in plans])

    tokens, wide = halves(tokens, (span, True), (n, True))
    own_x, own_y, wide_3, wide_1 = all_ways(tokens, tokens, wide, wide)
    own_x, matrices = lax.optimization_barrier((own_x, matrices))
    first = (tokens, own_x, own_y, wide_3, wide_1)
    members = ((0, n, m), (1, n, m), (2, n, m))
    sent = put(
        first,
        ((2, 0, nh), (2, n, mh), (3, 0, n), (4, 0, n)),
        ((1, nh, nh), (1, n + mh, mh), (3, 0, n), (4, 0, n)),
        ((3, 0, nh), *members),
        ((4, nh, nh), *members),
    )
    second = all_ways(*sent)
    second, later = lax.optimization_barrier((second, later))
    start = nh + mh
    wide_2 = ((2, 0, nh), (3, 0, nh))
    across = ((0, nh, mh), (1, nh, mh))
    third = all_ways(
        *put(
            second,
            ((1, start, nh), (1, start + n, nh), *wide_2),
            ((0, start + nh, nh), (0, start + n + nh, nh), *wide_2),
            (*across, (2, nh, nh)),
            (*across, (3, 2 * nh, nh)),
        )
    )
    fourth = all_ways(
        *put(third, ((1, n, nh),), ((0, n + nh, nh),), ((2, 0, mh),), ((3, mh, mh),))
    )
    runs = [
        (0, 0, 0, 0, 3, span, 0),
        (0, 3 * span, 3, 0, 1, n, 0),
        (0, 3 * span + n, 1, 0, 1, n, 0),
    ]
    offset = 0
    for side in range(2):
        runs += [
            (1, offset, 0, 3, 1, nh, side * nh),
            (1, offset + nh, 0, 3, 1, mh, n + side * mh),
            (1, offset + start, 3, 1 + side, 1, n, 0),
            (1, offset + start + n, 1, 1 + side, 1, n, 0),
        ]
        offset += start + 2 * n
    for side in range(2):
        runs += [
            (1, offset, 2, 0, 1, nh, side * nh),
            (1, offset + nh, 3 - 2 * side, 0, 3, m, n),
        ]
        offset += nh + 3 * m
    offset = 0
    for side in range(2):
        runs += [
            (2, offset, 3, 3, 1, nh, side * nh),
            (2, offset + nh, 1, 3, 1, nh, side * nh),
            (2, offset + n, 2, 1 + side, 1, n, 0),
        ]
        offset += 2 * n
    runs += [
        (2, offset, 3, 3, 1, m, n),
        (2, offset + m, 2, 0, 1, m, n),
        (2, offset + 2 * m, 2, 1, 1, mh, n),
        (2, offset + 2 * m + mh, 1, 3, 1, m, n),
        (2, offset + 3 * m + mh, 2, 1, 1, mh, n + mh),
        (2, offset + 3 * m + 2 * mh, 2, 2, 1, m, n),
        (3, 0, 2, 3, 1, nh, 0),
        (3, nh, 2, 3, 1, nh, nh),
        (3, n, 2, 3, 1, mh, n),
        (3, n + mh, 2, 3, 1, mh, n + mh),
    ]
    return [stack(*part) for part in (first, second, third, fourth)], tuple(runs), matrices, later


ORDER = (((2, 0, 4), (1, 3, 1), (3, 3, 1)), ((1, 0, 3), (3, 0, 3), (0, 0, 4)))


def scatter_sum(early, later, matrix, hyena):
    span = early.shape[0] // 6
    columns = matrix.shape[1]
    wide, narrow = columns * 3 // 8, columns // 8
    places = {}
    for array, pieces in enumerate(ORDER):
        row = 0
        for group, base, members in pieces:
            for member in range(base, base + members):
                places[group, member] = (array, row)
                row += span

    def product(part, other):
        both = beside(part, other)
        return narrowed(jnp.dot(both, matrix, preferred_element_type=jnp.float32))

    def term(group, member, side, *more):
        array, row = places[group, member]
        return (wide, [(array, row, side * wide), *more])

    def low(group, member, side, *more):
        array, row = places[group, member]
        return (narrow, [(array, row, 2 * wide + side * narrow), *more])

    def put(arrays, *plans):
        return assemble(arrays, *[columns_of(span, *plan) for plan in plans])

    early = product(early, swapped(early))
    other = swapped(later)
    first = all_ways(
        *put([early], [term(2, 3, 0)], [term(2, 3, 1)], [low(2, 3, 0)], [low(2, 3, 1)])
    )
    later, first = lax.optimization_barrier((later, first))
    x, y, below, above = range(1, 5)
    second = all_ways(
        *put(
            [early, *first],
            [term(2, 1, 0), term(2, 1, 1, (y, 0, 0)), term(1, 3, 0), term(3, 3, 0)],
            [term(2, 2, 0, (x, 0, 0)), term(2, 2, 1), term(1, 3, 1), term(3, 3, 1)],
            [low(1, 3, 0, (below, 0, 0)), low(1, 3, 1), *[low(2, k, 0) for k in range(3)]],
            [low(3, 3, 0), low(3, 3, 1, (above, 0, 0)), *[low(2, k, 1) for k in range(3)]],
        )
    )
    later = product(later, other)
    later, hyena, second = lax.optimization_barrier((later, hyena, second))
    hyena_out = lax.all_to_all(hyena, "ctx", split_axis=0, concat_axis=1, tiled=True).T
    x, y, below, above = range(2, 6)

    def low_3(side):
        return low(0, 3, side, (below, 0, side * narrow), (above, 0, side * narrow))

    def sum_2(side):
        return term(2, 0, side, (x, 0, side * wide), (y, 0, side * wide))

    for_above, for_below = [], []
    for k in range(3):
        start = (2 + k) * narrow
        for_above += [low(1, k, 0, (below, 0, start)), low(1, k, 1)]
        for_below += [low(3, k, 0), low(3, k, 1, (above, 0, start))]
    third = all_ways(
        *put(
            [early, later, *second],
            [
                term(1, 1, 0),
                term(1, 1, 1, (y, 0, 2 * wide)),
                term(3, 1, 0),
                term(3, 1, 1, (y, 0, 3 * wide)),
                term(0, 3, 0),
                low_3(0),
            ],
            [
                term(1, 2, 0, (x, 0, 2 * wide)),
                term(1, 2, 1),
                term(3, 2, 0, (x, 0, 3 * wide)),
                term(3, 2, 1),
                term(0, 3, 1),
                low_3(1),
            ],
            [sum_2(0), *for_above],
            [sum_2(1), *for_below],
        )
    )

    def low_own(k, side, *more):
        start = wide + (2 * k + side) * narrow
        return low(0, k, side, (below, 0, start), (above, 0, start), *more)

    def own(group, side, *more):
        start = (group - 1 + side) * wide
        return term(group, 0, side, (x, 0, start), (y, 0, start), *more)

    fourth = all_ways(
        *put(
            [early, later, *third],
            [
                term(0, 1, 0),
                term(0, 1, 1, (y, 0, 4 * wide)),
                low_own(1, 0),
                low_own(1, 1, (y, 0, 5 * wide)),
            ],
            [
                term(0, 2, 0, (x, 0, 4 * wide)),
                term(0, 2, 1),
                low_own(2, 0, (x, 0, 5 * wide)),
                low_own(2, 1),
            ],
            [own(1, 0, (below, 0, 0)), own(1, 1)],
            [own(3, 0), own(3, 1, (above, 0, 0))],
        )
    )
    last = range(6, 10)
    (grad_input,) = put(
        [early, later, *third, *fourth],
        [term(0, 0, side, *[(way, 0, side * wide) for way in last]) for side in (0, 1)]
        + [
            low_own(0, side, *[(way, 0, 2 * wide + side * narrow) for way in (6, 7)])
            for side in (0, 1)
        ],
    )
    return grad_input, hyena_out


def gather_tokens(tokens, weights, residues, decay_rates, cotangent):
    me = lax.axis_index("ctx").astype(jnp.int32).reshape(1)
    channels = weights.shape[1]
    rows = weights[0].swapaxes(0, 1).reshape(3 * channels, weights.shape[3])
    kept, given = halves(rows, (3 * channels, True), (3 * channels, False))
    taken = swapped(given)
    parts, runs, (kept, taken), cotangent = gather_groups(tokens, (kept, taken), cotangent)
    cot_cols = lax.all_to_all(cotangent.T, "ctx", split_axis=1, concat_axis=0, tiled=True)

    def project(part, matrix):
        return jnp.einsum("td,rd->tr", part, matrix, preferred_element_type=jnp.float32)

    other = [swapped(narrowed(project(part, taken))) for part in parts]
    own = [project(part, kept) for part in parts]
    hyena, grads, (early, later) = scan_all(
        me, cot_cols, residues[0].T, decay_rates[0].T, runs, ORDER, own, other
    )
    grad_input, hyena_out = scatter_sum(early, later, stack(kept, taken), hyena)
    return (hyena_out, grad_input, grads.T[None])


def shards(tokens, weights, residues, decay_rates, cotangent):
    ctx, tp = lax.axis_size("ctx"), lax.axis_size("tp")
    if ctx == 4 * PLANE and tp == 2 and weights.size * tp > 2 * tokens.size:
        return gather_tokens(tokens, weights, residues, decay_rates, cotangent)
    return gather_weights(tokens, weights, residues, decay_rates, cotangent)


def solution(mesh):
    return jax.shard_map(
        shards,
        mesh=mesh,
        in_specs=(
            P("ctx", None),
            P("tp", "ctx", None, None),
            P("tp", "ctx", None),
            P("tp", "ctx", None),
            P("tp", "ctx"),
        ),
        out_specs=(P("tp", "ctx"), P("ctx", "tp"), P("tp", "ctx", None)),
        check_vma=False,
    )
```

```python
import functools
import math

import jax
import jax.numpy as jnp
from jax import lax
from jax.experimental import pallas as pl
from jax.experimental.pallas import tpu as pltpu
from jax.sharding import PartitionSpec as P


def precise(form, left, right):
    return jnp.einsum(
        form, left, right, precision=lax.Precision.HIGHEST, preferred_element_type=jnp.float32
    )


def tripled(form, left, right):
    return jnp.einsum(
        form, left, right, precision=lax.Precision.HIGH, preferred_element_type=jnp.float32
    )


def angle_table(row_count, col_count, period):
    product = (
        jnp.arange(row_count, dtype=jnp.int32)[:, None]
        * jnp.arange(col_count, dtype=jnp.int32)[None, :]
        % period
    )
    angles = product.astype(jnp.float32) * (2.0 * math.pi / period)
    return (jnp.cos(angles), jnp.sin(angles))


def make_tables(length):
    padded = 2 * length
    outer = math.gcd(padded, 1 << (padded.bit_length() - 1) // 2)
    inner = padded // outer
    cos_outer, sin_outer = angle_table(outer, outer, outer)
    cos_inner, sin_inner = angle_table(inner, inner, inner)
    twist_cos, twist_sin = angle_table(outer, inner, padded)
    return (outer, inner, cos_outer, sin_outer, cos_inner, sin_inner, twist_cos, twist_sin)


def spectrum(signal, tables, product):
    outer, inner, cos_outer, sin_outer, cos_inner, sin_inner, twist_cos, twist_sin = tables
    half_rows = outer // 2
    blocks = signal.reshape(signal.shape[0], half_rows, inner)
    first_re = product("kp,bpq->bkq", cos_outer[:, :half_rows], blocks)
    first_im = -product("kp,bpq->bkq", sin_outer[:, :half_rows], blocks)
    turned_re = first_re * twist_cos + first_im * twist_sin
    turned_im = first_im * twist_cos - first_re * twist_sin
    spec_re = product("bkq,qj->bkj", turned_re, cos_inner) + product(
        "bkq,qj->bkj", turned_im, sin_inner
    )
    spec_im = product("bkq,qj->bkj", turned_im, cos_inner) - product(
        "bkq,qj->bkj", turned_re, sin_inner
    )
    return (spec_re, spec_im)


def signal_of(spec_re, spec_im, tables):
    outer, inner, cos_outer, sin_outer, cos_inner, sin_inner, twist_cos, twist_sin = tables
    half_rows = outer // 2
    back_re = tripled("bkj,jq->bkq", spec_re, cos_inner) - tripled(
        "bkj,jq->bkq", spec_im, sin_inner
    )
    back_im = tripled("bkj,jq->bkq", spec_im, cos_inner) + tripled(
        "bkj,jq->bkq", spec_re, sin_inner
    )
    turned_re = back_re * twist_cos - back_im * twist_sin
    turned_im = back_im * twist_cos + back_re * twist_sin
    values = tripled("pk,bkq->bpq", cos_outer[:half_rows, :], turned_re) - tripled(
        "pk,bkq->bpq", sin_outer[:half_rows, :], turned_im
    )
    return values.reshape(values.shape[0], half_rows * inner) * (1.0 / (outer * inner))


def spec_product(left_re, left_im, right_re, right_im):
    return (left_re * right_re - left_im * right_im, left_re * right_im + left_im * right_re)


def conj_product(left_re, left_im, right_re, right_im):
    return (left_re * right_re + left_im * right_im, left_re * right_im - left_im * right_re)


def filter_basis(residue_loc, rate_loc, length):
    position = jnp.arange(length, dtype=jnp.float32)
    basis_all = jnp.sqrt(2.0 * rate_loc)[:, :, None] * jnp.exp(
        -rate_loc[:, :, None] * position[None, None, :]
    )
    return (basis_all, precise("cm,cmt->ct", residue_loc, basis_all))


def forward_cols(gated_cols, taps_re, taps_im, tables):
    gated_re, gated_im = spectrum(gated_cols.astype(jnp.float32), tables, tripled)
    conv_re, conv_im = spec_product(gated_re, gated_im, taps_re, taps_im)
    conv_cols = signal_of(conv_re, conv_im, tables).astype(jnp.bfloat16)
    return (conv_cols, gated_re, gated_im)


def backward_cols(slope_cols, gated_re, gated_im, taps_re, taps_im, basis_all, tables, length):
    slope_re, slope_im = spectrum(slope_cols.astype(jnp.float32), tables, tripled)
    grad_re, grad_im = conj_product(taps_re, taps_im, slope_re, slope_im)
    back_cols = signal_of(grad_re, grad_im, tables).astype(jnp.bfloat16)
    lag_re, lag_im = conj_product(gated_re, gated_im, slope_re, slope_im)
    taps_grad = signal_of(lag_re, lag_im, tables)
    grad_residue = precise("ct,cmt->cm", taps_grad, basis_all) * (1.0 / math.sqrt(length))
    return (back_cols, grad_residue)


def gather_weights(tokens, weights, residues, decay_rates, cotangent):
    gathered = lax.all_gather(weights, "ctx", axis=1, tiled=True)
    projected = jnp.einsum("xcpd,td->xcpt", gathered, tokens, preferred_element_type=jnp.float32)
    features = projected[0].astype(jnp.bfloat16)
    query_f = features[:, 0].astype(jnp.float32)
    key_part = features[:, 1].astype(jnp.float32)
    value_part = features[:, 2].astype(jnp.float32)
    gated_in = (key_part * value_part).astype(jnp.bfloat16)
    slope_in = (cotangent.astype(jnp.float32) * query_f).astype(jnp.bfloat16)
    length = tokens.shape[0] * lax.axis_size("ctx")
    tables = make_tables(length)
    basis_all, taps_full = filter_basis(residues[0], decay_rates[0], length)
    taps_re, taps_im = spectrum(taps_full, tables, precise)
    gated_cols = lax.all_to_all(gated_in, "ctx", split_axis=0, concat_axis=1, tiled=True)
    conv_cols, gated_re, gated_im = forward_cols(gated_cols, taps_re, taps_im, tables)
    conv_rows = lax.all_to_all(conv_cols, "ctx", split_axis=1, concat_axis=0, tiled=True)
    slope_cols = lax.all_to_all(slope_in, "ctx", split_axis=0, concat_axis=1, tiled=True)
    back_cols, grad_residue = backward_cols(
        slope_cols, gated_re, gated_im, taps_re, taps_im, basis_all, tables, length
    )
    back_rows = lax.all_to_all(back_cols, "ctx", split_axis=1, concat_axis=0, tiled=True)
    conv_f = conv_rows.astype(jnp.float32)
    back_f = back_rows.astype(jnp.float32)
    hyena_out = (query_f * conv_f).astype(jnp.bfloat16)
    grad_query = (cotangent.astype(jnp.float32) * conv_f).astype(jnp.bfloat16)
    grad_key = (back_f * value_part).astype(jnp.bfloat16)
    grad_value = (back_f * key_part).astype(jnp.bfloat16)
    grad_proj = jnp.stack([grad_query, grad_key, grad_value], axis=1)
    partial_value = jnp.einsum(
        "cpt,cpd->td", grad_proj, gathered[0], preferred_element_type=jnp.float32
    )
    grad_input = lax.psum_scatter(
        partial_value.astype(jnp.bfloat16), "tp", scatter_dimension=1, tiled=True
    )
    return (hyena_out, grad_input, grad_residue[None])


GROUP = 4
PLANE = 4
VMEM = 56 * 2**20


def rounded(value):
    return value.astype(jnp.bfloat16).astype(jnp.float32)


def earlier_sum(finals, rate, span, back):
    count = finals.shape[0]
    row = lax.broadcasted_iota(jnp.int32, finals.shape, 0)

    def shifted(value, by):
        if back:
            moved = pltpu.roll(value, count - by, 0)
            return jnp.where(row < count - by, moved, 0.0)
        moved = pltpu.roll(value, by, 0)
        return jnp.where(row >= by, moved, 0.0)

    total = shifted(finals, 1)
    by = 1
    while by < count:
        total = total + jnp.exp(rate * (-1.0 * span * by)) * shifted(total, by)
        by *= 2
    return total


def scan_kernel(
    groups,
    runs,
    order,
    me_ref,
    residue_ref,
    rate_ref,
    *refs,
):
    inputs = 1 + max(run[0] for run in runs)
    arrays, refs = refs[: 2 * inputs + 1], refs[2 * inputs + 1 :]
    hyena_ref, grad_ref = refs[:2]
    proj_refs, refs = refs[2 : 2 + len(order)], refs[2 + len(order) :]
    gated_s, slope_s, conv_s, back_s, feats_s, arrived = refs[:6]
    held = refs[6:]
    cot_ref, own, other = held[0], held[1 : 1 + inputs], held[1 + inputs :]
    copies = [
        pltpu.make_async_copy(array, here, arrived.at[k])
        for k, (array, here) in enumerate(zip(arrays, held))
    ]
    for copy in copies:
        copy.start()
    length, width = cot_ref.shape
    chunks = PLANE * groups
    span = length // chunks
    modes = rate_ref.shape[0]
    me = me_ref[0]

    def place(group, member):
        return lax.rem(me // PLANE + group, groups) * PLANE + (member ^ lax.rem(me, PLANE))

    def aligned(start, size):
        return pl.ds(pl.multiple_of(start, size), size)

    copies[0].wait()
    waited = set()
    for source, offset, group, base, members, count, first in sorted(runs):
        if source not in waited:
            waited.add(source)
            copies[1 + source].wait()
            copies[1 + inputs + source].wait()

        def before(step, _, source=source, offset=offset, group=group, base=base, count=count, first=first):
            member = base + step
            index = place(group, member)
            rows = pl.ds(pl.multiple_of(offset + step * count, 16), count)
            feats = own[source][rows, :] + other[source][rows, :].astype(jnp.float32)
            feats = rounded(feats)
            slot = (group * PLANE + member) * span + first
            feats_s[pl.ds(pl.multiple_of(slot, 16), count), :] = feats
            cot = cot_ref[pl.ds(pl.multiple_of(index * span + first, 16), count), :]
            query, key = feats[:, :width], feats[:, width : 2 * width]
            into = pl.ds(first * chunks + index, count, stride=chunks)
            gated_s[into, :] = rounded(key * feats[:, 2 * width :])
            slope_s[into, :] = rounded(cot.astype(jnp.float32) * query)
            return 0

        lax.fori_loop(0, members, before, 0)

    def at(step):
        return aligned(step * chunks, chunks)

    zero = jnp.zeros((chunks, width), jnp.float32)
    scale = 1.0 / math.sqrt(length)
    for first in range(0, modes, GROUP):
        count = min(GROUP, modes - first)
        rates = [
            jnp.broadcast_to(rate_ref[m : m + 1, :], (chunks, width))
            for m in range(first, first + count)
        ]
        decays = [jnp.exp(-rate) for rate in rates]
        norms = [jnp.sqrt(2.0 * rate) for rate in rates]
        gains = [
            residue_ref[first + n : first + n + 1, :] * norms[n] for n in range(count)
        ]

        def sums(step, state):
            ahead, behind = state
            gated = gated_s[at(step), :]
            slope = slope_s[at(span - 1 - step), :]
            return (
                tuple(decays[n] * ahead[n] + gated for n in range(count)),
                tuple(decays[n] * behind[n] + slope for n in range(count)),
            )

        ahead, behind = lax.fori_loop(0, span, sums, ((zero,) * count, (zero,) * count), unroll=8)
        ahead = tuple(earlier_sum(ahead[n], rates[n], span, False) for n in range(count))
        behind = tuple(earlier_sum(behind[n], rates[n], span, True) for n in range(count))

        def outs(step, state):
            ahead, behind, grads = state
            other = span - 1 - step
            gated = gated_s[at(step), :]
            slope = slope_s[at(step), :]
            slope_back = slope_s[at(other), :]
            ahead = tuple(decays[n] * ahead[n] + gated for n in range(count))
            behind = tuple(decays[n] * behind[n] + slope_back for n in range(count))
            grads = tuple(grads[n] + slope * ahead[n] for n in range(count))
            conv = sum(gains[n] * ahead[n] for n in range(count))
            back = sum(gains[n] * behind[n] for n in range(count))
            if first:
                conv = conv + conv_s[at(step), :]
                back = back + back_s[at(other), :]
            conv_s[at(step), :] = conv
            back_s[at(other), :] = back
            return ahead, behind, grads

        _, _, grads = lax.fori_loop(0, span, outs, (ahead, behind, (zero,) * count), unroll=4)
        for n in range(count):
            total = jnp.sum(grads[n] * norms[n], axis=0, keepdims=True) * scale
            grad_ref[first + n : first + n + 1, :] = total

    for proj_ref, pieces in zip(proj_refs, order):
        start = 0
        for group, base, members in pieces:

            def after(step, _, proj_ref=proj_ref, start=start, group=group, base=base):
                member = base + step
                index = place(group, member)
                feats = feats_s[aligned((group * PLANE + member) * span, span), :]
                query, key = feats[:, :width], feats[:, width : 2 * width]
                cot = cot_ref[aligned(index * span, span), :].astype(jnp.float32)
                conv = rounded(conv_s[pl.ds(index, span, stride=chunks), :])
                back = rounded(back_s[pl.ds(index, span, stride=chunks), :])
                hyena_ref[aligned(index * span, span), :] = narrowed(query * conv)
                rows = aligned(start + step * span, span)
                proj_ref[rows, :width] = narrowed(cot * conv)
                proj_ref[rows, width : 2 * width] = narrowed(back * feats[:, 2 * width :])
                proj_ref[rows, 2 * width :] = narrowed(back * key)
                return 0

            lax.fori_loop(0, members, after, 0)
            start += members * span


def scan_all(me, cot_cols, residue_rows, rate_rows, runs, order, own, other):
    length, width = cot_cols.shape
    span = length // (PLANE * PLANE)
    vmem = pl.BlockSpec(memory_space=pltpu.VMEM)
    arrays = (cot_cols, *own, *other)
    outs = pl.pallas_call(
        functools.partial(scan_kernel, PLANE, runs, order),
        out_shape=(
            jax.ShapeDtypeStruct((length, width), jnp.bfloat16),
            jax.ShapeDtypeStruct(rate_rows.shape, jnp.float32),
        )
        + tuple(
            jax.ShapeDtypeStruct((span * sum(piece[2] for piece in pieces), 3 * width), jnp.bfloat16)
            for pieces in order
        ),
        in_specs=[pl.BlockSpec(memory_space=pltpu.SMEM), vmem, vmem]
        + [pl.BlockSpec(memory_space=pl.ANY)] * len(arrays),
        out_specs=(vmem,) * (2 + len(order)),
        scratch_shapes=[pltpu.VMEM((length, width), jnp.float32)] * 4
        + [pltpu.VMEM((length, 3 * width), jnp.float32), pltpu.SemaphoreType.DMA((len(arrays),))]
        + [pltpu.VMEM(array.shape, array.dtype) for array in arrays],
        compiler_params=pltpu.CompilerParams(vmem_limit_bytes=40 * 2**20),
        name="modal_scan",
    )(me, residue_rows, rate_rows, *arrays)
    return outs[0], outs[1], outs[2:]


def swapped(value):
    return lax.ppermute(value, "tp", [(0, 1), (1, 0)])


def over_x(value):
    return lax.ppermute(value, "ctx", [(i, i ^ 1) for i in range(lax.axis_size("ctx"))])


def over_y(value):
    return lax.ppermute(value, "ctx", [(i, i ^ 2) for i in range(lax.axis_size("ctx"))])


def up(value):
    count = lax.axis_size("ctx")
    return lax.ppermute(value, "ctx", [(i, (i + PLANE) % count) for i in range(count)])


def down(value):
    count = lax.axis_size("ctx")
    return lax.ppermute(value, "ctx", [((i + PLANE) % count, i) for i in range(count)])


def stack(*parts):
    return jnp.concatenate(parts, axis=0)


def beside(*parts):
    return jnp.concatenate(parts, axis=1)


def narrowed(value):
    return value.astype(jnp.bfloat16)


def widened(value):
    return value.astype(jnp.float32)


def halves_kernel(plan, core_ref, array, *refs):
    outs, arrived = refs[:-1], refs[-1]
    half = array.shape[1] // 2
    copies = []
    for k, (out, (count, mine)) in enumerate(zip(outs, plan)):
        side = core_ref[0] if mine else 1 - core_ref[0]
        part = array.at[pl.ds(0, count), pl.ds(pl.multiple_of(side * half, half), half)]
        copies.append(pltpu.make_async_copy(part, out, arrived.at[k]))
    for copy in copies:
        copy.start()
    for copy in copies:
        copy.wait()


def halves(array, *plan):
    half = array.shape[1] // 2
    core = lax.axis_index("tp").astype(jnp.int32).reshape(1)
    moved = sum(2 * count * half for count, _ in plan)
    return pl.pallas_call(
        functools.partial(halves_kernel, plan),
        out_shape=tuple(jax.ShapeDtypeStruct((count, half), jnp.bfloat16) for count, _ in plan),
        in_specs=[pl.BlockSpec(memory_space=pltpu.SMEM), pl.BlockSpec(memory_space=pl.ANY)],
        out_specs=(pl.BlockSpec(memory_space=pl.ANY),) * len(plan),
        scratch_shapes=[pltpu.SemaphoreType.DMA((len(plan),))],
        compiler_params=pltpu.CompilerParams(vmem_limit_bytes=VMEM),
        cost_estimate=pl.CostEstimate(flops=0, bytes_accessed=2 * moved, transcendentals=0),
        name="halves",
    )(core, array)


def assemble_kernel(inputs, plans, *refs):
    arrays, refs = refs[:inputs], refs[inputs:]
    outs, refs = refs[: len(plans)], refs[len(plans) :]
    arrived, held = refs[0], refs[1:]
    started, k, slot = [], 0, 0
    pending = []
    for out, plan in zip(outs, plans):
        for row, col, height, width, sources in plan:
            here = out.at[pl.ds(row, height), pl.ds(col, width)]
            single = len(sources) == 1
            mine = []
            for index, from_row, from_col in sources:
                part = arrays[index].at[pl.ds(from_row, height), pl.ds(from_col, width)]
                into = here if single else held[slot]
                copy = pltpu.make_async_copy(part, into, arrived.at[k])
                copy.start()
                mine.append((copy, into))
                k += 1
                slot += 0 if single else 1
            if single:
                started.append(mine[0][0])
            else:
                pending.append((here, mine))
    for here, mine in pending:
        for copy, _ in mine:
            copy.wait()
        here[...] = narrowed(sum(widened(into[...]) for _, into in mine))
    for copy in started:
        copy.wait()


def assemble(arrays, *plans):
    sources = [(piece, source) for plan in plans for piece in plan for source in piece[4]]
    sums = [piece for piece, _ in sources if len(piece[4]) > 1]
    shapes = [
        (max(p[0] + p[2] for p in plan), max(p[1] + p[3] for p in plan)) for plan in plans
    ]
    moved = sum(2 * rows * cols for rows, cols in shapes)
    return pl.pallas_call(
        functools.partial(assemble_kernel, len(arrays), plans),
        out_shape=tuple(jax.ShapeDtypeStruct(shape, jnp.bfloat16) for shape in shapes),
        in_specs=[pl.BlockSpec(memory_space=pl.ANY)] * len(arrays),
        out_specs=(pl.BlockSpec(memory_space=pltpu.VMEM),) * len(plans),
        scratch_shapes=[pltpu.SemaphoreType.DMA((len(sources),))]
        + [pltpu.VMEM((piece[2], piece[3]), jnp.bfloat16) for piece in sums],
        compiler_params=pltpu.CompilerParams(vmem_limit_bytes=24 * 2**20),
        cost_estimate=pl.CostEstimate(flops=moved, bytes_accessed=4 * moved, transcendentals=0),
        name="assemble",
    )(*arrays)


def rows_of(*parts):
    plan, start = [], 0
    for index, first, count in parts:
        plan.append((start, count, [(index, first, 0)]))
        start += count
    return plan


def full_width(columns, plan):
    return [(row, 0, count, columns, sources) for row, count, sources in plan]


def columns_of(height, *parts):
    plan, start = [], 0
    for width, sources in parts:
        plan.append((0, start, height, width, sources))
        start += width
    return plan


def all_ways(for_x, for_y, for_above, for_below):
    return lax.optimization_barrier((over_x(for_x), over_y(for_y), up(for_above), down(for_below)))


def project(parts, kept, taken):
    rows = stack(*parts)
    own, given = (
        jnp.einsum("td,rd->tr", rows, matrix, preferred_element_type=jnp.float32)
        for matrix in (kept, taken)
    )
    return own, swapped(narrowed(given))


def columns_held(rows):
    return lax.all_to_all(rows.T, "ctx", split_axis=1, concat_axis=0, tiled=True)


def gather_groups(tokens, wide, matrices, later):
    span = tokens.shape[0]
    n, m = span * 3 // 4, span // 4
    nh, mh = n // 2, m // 2
    columns = tokens.shape[1]

    def put(arrays, *plans):
        return assemble(arrays, *[full_width(columns, rows_of(*plan)) for plan in plans])

    own_x, own_y, wide_3, wide_1 = all_ways(tokens, tokens, wide, wide)
    own_x, matrices = lax.optimization_barrier((own_x, matrices))
    first = (tokens, own_x, own_y, wide_3, wide_1)
    members = ((0, n, m), (1, n, m), (2, n, m))
    sent = put(
        first,
        ((2, 0, nh), (2, n, mh), (3, 0, n), (4, 0, n)),
        ((1, nh, nh), (1, n + mh, mh), (3, 0, n), (4, 0, n)),
        ((3, 0, nh), *members),
        ((4, nh, nh), *members),
    )
    sent, later = lax.optimization_barrier((sent, later))
    second, later = lax.optimization_barrier((all_ways(*sent), columns_held(later)))
    start = nh + mh
    wide_2 = ((2, 0, nh), (3, 0, nh))
    across = ((0, nh, mh), (1, nh, mh))
    third = all_ways(
        *put(
            second,
            ((1, start, nh), (1, start + n, nh), *wide_2),
            ((0, start + nh, nh), (0, start + n + nh, nh), *wide_2),
            (*across, (2, nh, nh)),
            (*across, (3, 2 * nh, nh)),
        )
    )
    fourth = all_ways(
        *put(third, ((1, n, nh),), ((0, n + nh, nh),), ((2, 0, mh),), ((3, mh, mh),))
    )
    runs = [
        (0, 0, 0, 0, 3, span, 0),
        (0, 3 * span, 3, 0, 1, n, 0),
        (0, 3 * span + n, 1, 0, 1, n, 0),
    ]
    offset = 0
    for side in range(2):
        runs += [
            (1, offset, 0, 3, 1, nh, side * nh),
            (1, offset + nh, 0, 3, 1, mh, n + side * mh),
            (1, offset + start, 3, 1 + side, 1, n, 0),
            (1, offset + start + n, 1, 1 + side, 1, n, 0),
        ]
        offset += start + 2 * n
    for side in range(2):
        runs += [
            (1, offset, 2, 0, 1, nh, side * nh),
            (1, offset + nh, 3 - 2 * side, 0, 3, m, n),
        ]
        offset += nh + 3 * m
    offset = 0
    for side in range(2):
        runs += [
            (2, offset, 3, 3, 1, nh, side * nh),
            (2, offset + nh, 1, 3, 1, nh, side * nh),
            (2, offset + n, 2, 1 + side, 1, n, 0),
        ]
        offset += 2 * n
    runs += [
        (2, offset, 3, 3, 1, m, n),
        (2, offset + m, 2, 0, 1, m, n),
        (2, offset + 2 * m, 2, 1, 1, mh, n),
        (2, offset + 2 * m + mh, 1, 3, 1, m, n),
        (2, offset + 3 * m + mh, 2, 1, 1, mh, n + mh),
        (2, offset + 3 * m + 2 * mh, 2, 2, 1, m, n),
        (3, 0, 2, 3, 1, nh, 0),
        (3, nh, 2, 3, 1, nh, nh),
        (3, n, 2, 3, 1, mh, n),
        (3, n + mh, 2, 3, 1, mh, n + mh),
    ]
    parts = [project(part, *matrices) for part in (first, second, third, fourth)]
    return parts, tuple(runs), matrices, later


ORDER = (((2, 0, 4), (1, 3, 1), (3, 3, 1)), ((1, 0, 3), (3, 0, 3), (0, 3, 1), (0, 0, 3)))


def scatter_sum(early, later, matrix, hyena):
    span = early.shape[0] // 6
    columns = matrix.shape[1]
    wide, narrow = columns * 3 // 8, columns // 8
    places = {}
    for array, pieces in enumerate((ORDER[0], ORDER[1][:3], ORDER[1][3:])):
        row = 0
        for group, base, members in pieces:
            for member in range(base, base + members):
                places[group, member] = (array, row)
                row += span

    def product(part, other):
        both = beside(part, other)
        return narrowed(jnp.dot(both, matrix, preferred_element_type=jnp.float32))

    def term(group, member, side, *more):
        array, row = places[group, member]
        return (wide, [(array, row, side * wide), *more])

    def low(group, member, side, *more):
        array, row = places[group, member]
        return (narrow, [(array, row, 2 * wide + side * narrow), *more])

    def put(arrays, *plans):
        return assemble(arrays, *[columns_of(span, *plan) for plan in plans])

    early = product(early, swapped(early))
    other = swapped(later)
    first = all_ways(
        *put([early], [term(2, 3, 0)], [term(2, 3, 1)], [low(2, 3, 0)], [low(2, 3, 1)])
    )
    later, first = lax.optimization_barrier((later, first))
    x, y, below, above = range(1, 5)
    second = all_ways(
        *put(
            [early, *first],
            [term(2, 1, 0), term(2, 1, 1, (y, 0, 0)), term(1, 3, 0), term(3, 3, 0)],
            [term(2, 2, 0, (x, 0, 0)), term(2, 2, 1), term(1, 3, 1), term(3, 3, 1)],
            [low(1, 3, 0, (below, 0, 0)), low(1, 3, 1), *[low(2, k, 0) for k in range(3)]],
            [low(3, 3, 0), low(3, 3, 1, (above, 0, 0)), *[low(2, k, 1) for k in range(3)]],
        )
    )
    own = product(later[7 * span :], other[7 * span :])
    later = product(later[: 7 * span], other[: 7 * span])
    later, hyena, second = lax.optimization_barrier((later, hyena, second))
    hyena_out = lax.all_to_all(hyena, "ctx", split_axis=0, concat_axis=1, tiled=True).T
    x, y, below, above = range(2, 6)

    def low_3(side):
        return low(0, 3, side, (below, 0, side * narrow), (above, 0, side * narrow))

    def sum_2(side):
        return term(2, 0, side, (x, 0, side * wide), (y, 0, side * wide))

    for_above, for_below = [], []
    for k in range(3):
        start = (2 + k) * narrow
        for_above += [low(1, k, 0, (below, 0, start)), low(1, k, 1)]
        for_below += [low(3, k, 0), low(3, k, 1, (above, 0, start))]
    third = all_ways(
        *put(
            [early, later, *second],
            [
                term(1, 1, 0),
                term(1, 1, 1, (y, 0, 2 * wide)),
                term(3, 1, 0),
                term(3, 1, 1, (y, 0, 3 * wide)),
                term(0, 3, 0),
                low_3(0),
            ],
            [
                term(1, 2, 0, (x, 0, 2 * wide)),
                term(1, 2, 1),
                term(3, 2, 0, (x, 0, 3 * wide)),
                term(3, 2, 1),
                term(0, 3, 1),
                low_3(1),
            ],
            [sum_2(0), *for_above],
            [sum_2(1), *for_below],
        )
    )

    x, y, below, above = range(3, 7)

    def low_own(k, side, *more):
        start = wide + (2 * k + side) * narrow
        return low(0, k, side, (below, 0, start), (above, 0, start), *more)

    def own_sum(group, side, *more):
        start = (group - 1 + side) * wide
        return term(group, 0, side, (x, 0, start), (y, 0, start), *more)

    fourth = all_ways(
        *put(
            [early, later, own, *third],
            [
                term(0, 1, 0),
                term(0, 1, 1, (y, 0, 4 * wide)),
                low_own(1, 0),
                low_own(1, 1, (y, 0, 5 * wide)),
            ],
            [
                term(0, 2, 0, (x, 0, 4 * wide)),
                term(0, 2, 1),
                low_own(2, 0, (x, 0, 5 * wide)),
                low_own(2, 1),
            ],
            [own_sum(1, 0, (below, 0, 0)), own_sum(1, 1)],
            [own_sum(3, 0), own_sum(3, 1, (above, 0, 0))],
        )
    )
    last = range(7, 11)
    (grad_input,) = put(
        [early, later, own, *third, *fourth],
        [term(0, 0, side, *[(way, 0, side * wide) for way in last]) for side in (0, 1)]
        + [
            low_own(0, side, *[(way, 0, 2 * wide + side * narrow) for way in (7, 8)])
            for side in (0, 1)
        ],
    )
    return grad_input, hyena_out


def gather_tokens(tokens, weights, residues, decay_rates, cotangent):
    me = lax.axis_index("ctx").astype(jnp.int32).reshape(1)
    channels, span = weights.shape[1], tokens.shape[0]
    rows = weights[0].swapaxes(0, 1).reshape(3 * channels, weights.shape[3])
    tokens_half = halves(tokens, (span, True), (span * 3 // 4, True))
    rows, tokens_half = lax.optimization_barrier((rows, tokens_half))
    kept, given = halves(rows, (3 * channels, True), (3 * channels, False))
    taken = swapped(given)
    parts, runs, (kept, taken), cot_cols = gather_groups(*tokens_half, (kept, taken), cotangent)
    own, other = zip(*parts)
    hyena, grads, (early, later) = scan_all(
        me, cot_cols, residues[0].T, decay_rates[0].T, runs, ORDER, own, other
    )
    grad_input, hyena_out = scatter_sum(early, later, stack(kept, taken), hyena)
    return (hyena_out, grad_input, grads.T[None])


def shards(tokens, weights, residues, decay_rates, cotangent):
    ctx, tp = lax.axis_size("ctx"), lax.axis_size("tp")
    if ctx == 4 * PLANE and tp == 2 and weights.size * tp > 2 * tokens.size:
        return gather_tokens(tokens, weights, residues, decay_rates, cotangent)
    return gather_weights(tokens, weights, residues, decay_rates, cotangent)


def solution(mesh):
    return jax.shard_map(
        shards,
        mesh=mesh,
        in_specs=(
            P("ctx", None),
            P("tp", "ctx", None, None),
            P("tp", "ctx", None),
            P("tp", "ctx", None),
            P("tp", "ctx"),
        ),
        out_specs=(P("tp", "ctx"), P("ctx", "tp"), P("tp", "ctx", None)),
        check_vma=False,
    )
```

```python
import functools
import math

import jax
import jax.numpy as jnp
from jax import lax
from jax.experimental import pallas as pl
from jax.experimental.pallas import tpu as pltpu
from jax.sharding import PartitionSpec as P


def precise(form, left, right):
    return jnp.einsum(
        form, left, right, precision=lax.Precision.HIGHEST, preferred_element_type=jnp.float32
    )


def tripled(form, left, right):
    return jnp.einsum(
        form, left, right, precision=lax.Precision.HIGH, preferred_element_type=jnp.float32
    )


def angle_table(row_count, col_count, period):
    product = (
        jnp.arange(row_count, dtype=jnp.int32)[:, None]
        * jnp.arange(col_count, dtype=jnp.int32)[None, :]
        % period
    )
    angles = product.astype(jnp.float32) * (2.0 * math.pi / period)
    return (jnp.cos(angles), jnp.sin(angles))


def make_tables(length):
    padded = 2 * length
    outer = math.gcd(padded, 1 << (padded.bit_length() - 1) // 2)
    inner = padded // outer
    cos_outer, sin_outer = angle_table(outer, outer, outer)
    cos_inner, sin_inner = angle_table(inner, inner, inner)
    twist_cos, twist_sin = angle_table(outer, inner, padded)
    return (outer, inner, cos_outer, sin_outer, cos_inner, sin_inner, twist_cos, twist_sin)


def spectrum(signal, tables, product):
    outer, inner, cos_outer, sin_outer, cos_inner, sin_inner, twist_cos, twist_sin = tables
    half_rows = outer // 2
    blocks = signal.reshape(signal.shape[0], half_rows, inner)
    first_re = product("kp,bpq->bkq", cos_outer[:, :half_rows], blocks)
    first_im = -product("kp,bpq->bkq", sin_outer[:, :half_rows], blocks)
    turned_re = first_re * twist_cos + first_im * twist_sin
    turned_im = first_im * twist_cos - first_re * twist_sin
    spec_re = product("bkq,qj->bkj", turned_re, cos_inner) + product(
        "bkq,qj->bkj", turned_im, sin_inner
    )
    spec_im = product("bkq,qj->bkj", turned_im, cos_inner) - product(
        "bkq,qj->bkj", turned_re, sin_inner
    )
    return (spec_re, spec_im)


def signal_of(spec_re, spec_im, tables):
    outer, inner, cos_outer, sin_outer, cos_inner, sin_inner, twist_cos, twist_sin = tables
    half_rows = outer // 2
    back_re = tripled("bkj,jq->bkq", spec_re, cos_inner) - tripled(
        "bkj,jq->bkq", spec_im, sin_inner
    )
    back_im = tripled("bkj,jq->bkq", spec_im, cos_inner) + tripled(
        "bkj,jq->bkq", spec_re, sin_inner
    )
    turned_re = back_re * twist_cos - back_im * twist_sin
    turned_im = back_im * twist_cos + back_re * twist_sin
    values = tripled("pk,bkq->bpq", cos_outer[:half_rows, :], turned_re) - tripled(
        "pk,bkq->bpq", sin_outer[:half_rows, :], turned_im
    )
    return values.reshape(values.shape[0], half_rows * inner) * (1.0 / (outer * inner))


def spec_product(left_re, left_im, right_re, right_im):
    return (left_re * right_re - left_im * right_im, left_re * right_im + left_im * right_re)


def conj_product(left_re, left_im, right_re, right_im):
    return (left_re * right_re + left_im * right_im, left_re * right_im - left_im * right_re)


def filter_basis(residue_loc, rate_loc, length):
    position = jnp.arange(length, dtype=jnp.float32)
    basis_all = jnp.sqrt(2.0 * rate_loc)[:, :, None] * jnp.exp(
        -rate_loc[:, :, None] * position[None, None, :]
    )
    return (basis_all, precise("cm,cmt->ct", residue_loc, basis_all))


def forward_cols(gated_cols, taps_re, taps_im, tables):
    gated_re, gated_im = spectrum(gated_cols.astype(jnp.float32), tables, tripled)
    conv_re, conv_im = spec_product(gated_re, gated_im, taps_re, taps_im)
    conv_cols = signal_of(conv_re, conv_im, tables).astype(jnp.bfloat16)
    return (conv_cols, gated_re, gated_im)


def backward_cols(slope_cols, gated_re, gated_im, taps_re, taps_im, basis_all, tables, length):
    slope_re, slope_im = spectrum(slope_cols.astype(jnp.float32), tables, tripled)
    grad_re, grad_im = conj_product(taps_re, taps_im, slope_re, slope_im)
    back_cols = signal_of(grad_re, grad_im, tables).astype(jnp.bfloat16)
    lag_re, lag_im = conj_product(gated_re, gated_im, slope_re, slope_im)
    taps_grad = signal_of(lag_re, lag_im, tables)
    grad_residue = precise("ct,cmt->cm", taps_grad, basis_all) * (1.0 / math.sqrt(length))
    return (back_cols, grad_residue)


def gather_weights(tokens, weights, residues, decay_rates, cotangent):
    gathered = lax.all_gather(weights, "ctx", axis=1, tiled=True)
    projected = jnp.einsum("xcpd,td->xcpt", gathered, tokens, preferred_element_type=jnp.float32)
    features = projected[0].astype(jnp.bfloat16)
    query_f = features[:, 0].astype(jnp.float32)
    key_part = features[:, 1].astype(jnp.float32)
    value_part = features[:, 2].astype(jnp.float32)
    gated_in = (key_part * value_part).astype(jnp.bfloat16)
    slope_in = (cotangent.astype(jnp.float32) * query_f).astype(jnp.bfloat16)
    length = tokens.shape[0] * lax.axis_size("ctx")
    tables = make_tables(length)
    basis_all, taps_full = filter_basis(residues[0], decay_rates[0], length)
    taps_re, taps_im = spectrum(taps_full, tables, precise)
    gated_cols = lax.all_to_all(gated_in, "ctx", split_axis=0, concat_axis=1, tiled=True)
    conv_cols, gated_re, gated_im = forward_cols(gated_cols, taps_re, taps_im, tables)
    conv_rows = lax.all_to_all(conv_cols, "ctx", split_axis=1, concat_axis=0, tiled=True)
    slope_cols = lax.all_to_all(slope_in, "ctx", split_axis=0, concat_axis=1, tiled=True)
    back_cols, grad_residue = backward_cols(
        slope_cols, gated_re, gated_im, taps_re, taps_im, basis_all, tables, length
    )
    back_rows = lax.all_to_all(back_cols, "ctx", split_axis=1, concat_axis=0, tiled=True)
    conv_f = conv_rows.astype(jnp.float32)
    back_f = back_rows.astype(jnp.float32)
    hyena_out = (query_f * conv_f).astype(jnp.bfloat16)
    grad_query = (cotangent.astype(jnp.float32) * conv_f).astype(jnp.bfloat16)
    grad_key = (back_f * value_part).astype(jnp.bfloat16)
    grad_value = (back_f * key_part).astype(jnp.bfloat16)
    grad_proj = jnp.stack([grad_query, grad_key, grad_value], axis=1)
    partial_value = jnp.einsum(
        "cpt,cpd->td", grad_proj, gathered[0], preferred_element_type=jnp.float32
    )
    grad_input = lax.psum_scatter(
        partial_value.astype(jnp.bfloat16), "tp", scatter_dimension=1, tiled=True
    )
    return (hyena_out, grad_input, grad_residue[None])


GROUP = 4
PLANE = 4
VMEM = 56 * 2**20


def rounded(value):
    return value.astype(jnp.bfloat16).astype(jnp.float32)


def earlier_sum(finals, rate, span, back):
    count = finals.shape[0]
    row = lax.broadcasted_iota(jnp.int32, finals.shape, 0)

    def shifted(value, by):
        if back:
            moved = pltpu.roll(value, count - by, 0)
            return jnp.where(row < count - by, moved, 0.0)
        moved = pltpu.roll(value, by, 0)
        return jnp.where(row >= by, moved, 0.0)

    total = shifted(finals, 1)
    by = 1
    while by < count:
        total = total + jnp.exp(rate * (-1.0 * span * by)) * shifted(total, by)
        by *= 2
    return total


def scan_kernel(
    groups,
    runs,
    order,
    me_ref,
    residue_ref,
    rate_ref,
    *refs,
):
    inputs = 1 + max(run[0] for run in runs)
    arrays, refs = refs[: 2 * inputs + 1], refs[2 * inputs + 1 :]
    hyena_ref, grad_ref = refs[:2]
    proj_refs, refs = refs[2 : 2 + len(order)], refs[2 + len(order) :]
    gated_s, slope_s, conv_s, back_s, feats_s, arrived = refs[:6]
    held = refs[6:]
    cot_ref, own, other = held[0], held[1 : 1 + inputs], held[1 + inputs :]
    copies = [
        pltpu.make_async_copy(array, here, arrived.at[k])
        for k, (array, here) in enumerate(zip(arrays, held))
    ]
    for copy in copies:
        copy.start()
    length, width = cot_ref.shape
    chunks = PLANE * groups
    span = length // chunks
    modes = rate_ref.shape[0]
    me = me_ref[0]

    def place(group, member):
        return lax.rem(me // PLANE + group, groups) * PLANE + (member ^ lax.rem(me, PLANE))

    def aligned(start, size):
        return pl.ds(pl.multiple_of(start, size), size)

    copies[0].wait()
    waited = set()
    for source, offset, group, base, members, count, first in sorted(runs):
        if source not in waited:
            waited.add(source)
            copies[1 + source].wait()
            copies[1 + inputs + source].wait()

        def before(step, _, source=source, offset=offset, group=group, base=base, count=count, first=first):
            member = base + step
            index = place(group, member)
            rows = pl.ds(pl.multiple_of(offset + step * count, 16), count)
            feats = own[source][rows, :] + other[source][rows, :].astype(jnp.float32)
            feats = rounded(feats)
            slot = (group * PLANE + member) * span + first
            feats_s[pl.ds(pl.multiple_of(slot, 16), count), :] = feats
            cot = cot_ref[pl.ds(pl.multiple_of(index * span + first, 16), count), :]
            query, key = feats[:, :width], feats[:, width : 2 * width]
            into = pl.ds(first * chunks + index, count, stride=chunks)
            gated_s[into, :] = rounded(key * feats[:, 2 * width :])
            slope_s[into, :] = rounded(cot.astype(jnp.float32) * query)
            return 0

        lax.fori_loop(0, members, before, 0)

    def at(step):
        return aligned(step * chunks, chunks)

    zero = jnp.zeros((chunks, width), jnp.float32)
    scale = 1.0 / math.sqrt(length)
    for first in range(0, modes, GROUP):
        count = min(GROUP, modes - first)
        rates = [
            jnp.broadcast_to(rate_ref[m : m + 1, :], (chunks, width))
            for m in range(first, first + count)
        ]
        decays = [jnp.exp(-rate) for rate in rates]
        norms = [jnp.sqrt(2.0 * rate) for rate in rates]
        gains = [
            residue_ref[first + n : first + n + 1, :] * norms[n] for n in range(count)
        ]

        def sums(step, state):
            ahead, behind = state
            gated = gated_s[at(step), :]
            slope = slope_s[at(span - 1 - step), :]
            return (
                tuple(decays[n] * ahead[n] + gated for n in range(count)),
                tuple(decays[n] * behind[n] + slope for n in range(count)),
            )

        ahead, behind = lax.fori_loop(0, span, sums, ((zero,) * count, (zero,) * count), unroll=8)
        ahead = tuple(earlier_sum(ahead[n], rates[n], span, False) for n in range(count))
        behind = tuple(earlier_sum(behind[n], rates[n], span, True) for n in range(count))

        def outs(step, state):
            ahead, behind, grads = state
            other = span - 1 - step
            gated = gated_s[at(step), :]
            slope = slope_s[at(step), :]
            slope_back = slope_s[at(other), :]
            ahead = tuple(decays[n] * ahead[n] + gated for n in range(count))
            behind = tuple(decays[n] * behind[n] + slope_back for n in range(count))
            grads = tuple(grads[n] + slope * ahead[n] for n in range(count))
            conv = sum(gains[n] * ahead[n] for n in range(count))
            back = sum(gains[n] * behind[n] for n in range(count))
            if first:
                conv = conv + conv_s[at(step), :]
                back = back + back_s[at(other), :]
            conv_s[at(step), :] = conv
            back_s[at(other), :] = back
            return ahead, behind, grads

        _, _, grads = lax.fori_loop(0, span, outs, (ahead, behind, (zero,) * count), unroll=4)
        for n in range(count):
            total = jnp.sum(grads[n] * norms[n], axis=0, keepdims=True) * scale
            grad_ref[first + n : first + n + 1, :] = total

    for proj_ref, pieces in zip(proj_refs, order):
        start = 0
        for group, base, members in pieces:

            def after(step, _, proj_ref=proj_ref, start=start, group=group, base=base):
                member = base + step
                index = place(group, member)
                feats = feats_s[aligned((group * PLANE + member) * span, span), :]
                query, key = feats[:, :width], feats[:, width : 2 * width]
                cot = cot_ref[aligned(index * span, span), :].astype(jnp.float32)
                conv = rounded(conv_s[pl.ds(index, span, stride=chunks), :])
                back = rounded(back_s[pl.ds(index, span, stride=chunks), :])
                hyena_ref[aligned(index * span, span), :] = narrowed(query * conv)
                rows = aligned(start + step * span, span)
                proj_ref[rows, :width] = narrowed(cot * conv)
                proj_ref[rows, width : 2 * width] = narrowed(back * feats[:, 2 * width :])
                proj_ref[rows, 2 * width :] = narrowed(back * key)
                return 0

            lax.fori_loop(0, members, after, 0)
            start += members * span


def scan_all(me, cot_cols, residue_rows, rate_rows, runs, order, own, other):
    length, width = cot_cols.shape
    span = length // (PLANE * PLANE)
    vmem = pl.BlockSpec(memory_space=pltpu.VMEM)
    arrays = (cot_cols, *own, *other)
    outs = pl.pallas_call(
        functools.partial(scan_kernel, PLANE, runs, order),
        out_shape=(
            jax.ShapeDtypeStruct((length, width), jnp.bfloat16),
            jax.ShapeDtypeStruct(rate_rows.shape, jnp.float32),
        )
        + tuple(
            jax.ShapeDtypeStruct((span * sum(piece[2] for piece in pieces), 3 * width), jnp.bfloat16)
            for pieces in order
        ),
        in_specs=[pl.BlockSpec(memory_space=pltpu.SMEM), vmem, vmem]
        + [pl.BlockSpec(memory_space=pl.ANY)] * len(arrays),
        out_specs=(vmem,) * (2 + len(order)),
        scratch_shapes=[pltpu.VMEM((length, width), jnp.float32)] * 4
        + [pltpu.VMEM((length, 3 * width), jnp.float32), pltpu.SemaphoreType.DMA((len(arrays),))]
        + [pltpu.VMEM(array.shape, array.dtype) for array in arrays],
        compiler_params=pltpu.CompilerParams(vmem_limit_bytes=40 * 2**20),
        name="modal_scan",
    )(me, residue_rows, rate_rows, *arrays)
    return outs[0], outs[1], outs[2:]


def swapped(value):
    return lax.ppermute(value, "tp", [(0, 1), (1, 0)])


def over_x(value):
    return lax.ppermute(value, "ctx", [(i, i ^ 1) for i in range(lax.axis_size("ctx"))])


def over_y(value):
    return lax.ppermute(value, "ctx", [(i, i ^ 2) for i in range(lax.axis_size("ctx"))])


def up(value):
    count = lax.axis_size("ctx")
    return lax.ppermute(value, "ctx", [(i, (i + PLANE) % count) for i in range(count)])


def down(value):
    count = lax.axis_size("ctx")
    return lax.ppermute(value, "ctx", [((i + PLANE) % count, i) for i in range(count)])


def stack(*parts):
    return jnp.concatenate(parts, axis=0)


def beside(*parts):
    return jnp.concatenate(parts, axis=1)


def narrowed(value):
    return value.astype(jnp.bfloat16)


def widened(value):
    return value.astype(jnp.float32)


def halves_kernel(plan, core_ref, *refs):
    arrays, outs, arrived = refs[: -1 - len(plan)], refs[-1 - len(plan) : -1], refs[-1]
    copies = []
    for k, (out, (index, count, mine)) in enumerate(zip(outs, plan)):
        half = out.shape[1]
        side = core_ref[0] if mine else 1 - core_ref[0]
        columns = pl.ds(pl.multiple_of(side * half, half), half)
        part = arrays[index].at[pl.ds(0, count), columns]
        copies.append(pltpu.make_async_copy(part, out, arrived.at[k]))
    for copy in copies:
        copy.start()
    for copy in copies:
        copy.wait()


def halves(arrays, *plan):
    core = lax.axis_index("tp").astype(jnp.int32).reshape(1)
    shapes = [(count, arrays[index].shape[1] // 2) for index, count, _ in plan]
    moved = sum(4 * rows * columns for rows, columns in shapes)
    return pl.pallas_call(
        functools.partial(halves_kernel, plan),
        out_shape=tuple(jax.ShapeDtypeStruct(shape, jnp.bfloat16) for shape in shapes),
        in_specs=[pl.BlockSpec(memory_space=pltpu.SMEM)]
        + [pl.BlockSpec(memory_space=pl.ANY)] * len(arrays),
        out_specs=(pl.BlockSpec(memory_space=pltpu.VMEM),) * len(plan),
        scratch_shapes=[pltpu.SemaphoreType.DMA((len(plan),))],
        compiler_params=pltpu.CompilerParams(vmem_limit_bytes=VMEM),
        cost_estimate=pl.CostEstimate(flops=0, bytes_accessed=moved, transcendentals=0),
        name="halves",
    )(core, *arrays)


def assemble_kernel(inputs, plans, *refs):
    arrays, refs = refs[:inputs], refs[inputs:]
    outs, refs = refs[: len(plans)], refs[len(plans) :]
    arrived, held = refs[0], refs[1:]
    started, k, slot = [], 0, 0
    pending = []
    for out, plan in zip(outs, plans):
        for row, col, height, width, sources in plan:
            here = out.at[pl.ds(row, height), pl.ds(col, width)]
            single = len(sources) == 1
            mine = []
            for index, from_row, from_col in sources:
                part = arrays[index].at[pl.ds(from_row, height), pl.ds(from_col, width)]
                into = here if single else held[slot]
                copy = pltpu.make_async_copy(part, into, arrived.at[k])
                copy.start()
                mine.append((copy, into))
                k += 1
                slot += 0 if single else 1
            if single:
                started.append(mine[0][0])
            else:
                pending.append((here, mine))
    for here, mine in pending:
        for copy, _ in mine:
            copy.wait()
        here[...] = narrowed(sum(widened(into[...]) for _, into in mine))
    for copy in started:
        copy.wait()


def assemble(arrays, *plans):
    sources = [(piece, source) for plan in plans for piece in plan for source in piece[4]]
    sums = [piece for piece, _ in sources if len(piece[4]) > 1]
    shapes = [
        (max(p[0] + p[2] for p in plan), max(p[1] + p[3] for p in plan)) for plan in plans
    ]
    moved = sum(2 * rows * cols for rows, cols in shapes)
    return pl.pallas_call(
        functools.partial(assemble_kernel, len(arrays), plans),
        out_shape=tuple(jax.ShapeDtypeStruct(shape, jnp.bfloat16) for shape in shapes),
        in_specs=[pl.BlockSpec(memory_space=pl.ANY)] * len(arrays),
        out_specs=(pl.BlockSpec(memory_space=pltpu.VMEM),) * len(plans),
        scratch_shapes=[pltpu.SemaphoreType.DMA((len(sources),))]
        + [pltpu.VMEM((piece[2], piece[3]), jnp.bfloat16) for piece in sums],
        compiler_params=pltpu.CompilerParams(vmem_limit_bytes=24 * 2**20),
        cost_estimate=pl.CostEstimate(flops=moved, bytes_accessed=4 * moved, transcendentals=0),
        name="assemble",
    )(*arrays)


def rows_of(*parts):
    plan, start = [], 0
    for index, first, count in parts:
        plan.append((start, count, [(index, first, 0)]))
        start += count
    return plan


def full_width(columns, plan):
    return [(row, 0, count, columns, sources) for row, count, sources in plan]


def columns_of(height, *parts):
    plan, start = [], 0
    for width, sources in parts:
        plan.append((0, start, height, width, sources))
        start += width
    return plan


def all_ways(for_x, for_y, for_above, for_below):
    return lax.optimization_barrier((over_x(for_x), over_y(for_y), up(for_above), down(for_below)))


def project(parts, kept, taken):
    rows = stack(*parts)
    own, given = (
        jnp.einsum("td,rd->tr", rows, matrix, preferred_element_type=jnp.float32)
        for matrix in (kept, taken)
    )
    return own, swapped(narrowed(given))


def columns_held(rows):
    return lax.all_to_all(rows.T, "ctx", split_axis=1, concat_axis=0, tiled=True)


def gather_groups(tokens, wide, matrices, later):
    span = tokens.shape[0]
    n, m = span * 3 // 4, span // 4
    nh, mh = n // 2, m // 2
    columns = tokens.shape[1]

    def put(arrays, *plans):
        return assemble(arrays, *[full_width(columns, rows_of(*plan)) for plan in plans])

    own_x, own_y, wide_3, wide_1 = all_ways(tokens, tokens, wide, wide)
    own_x, matrices = lax.optimization_barrier((own_x, matrices))
    first = (tokens, own_x, own_y, wide_3, wide_1)
    members = ((0, n, m), (1, n, m), (2, n, m))
    sent = put(
        first,
        ((2, 0, nh), (2, n, mh), (3, 0, n), (4, 0, n)),
        ((1, nh, nh), (1, n + mh, mh), (3, 0, n), (4, 0, n)),
        ((3, 0, nh), *members),
        ((4, nh, nh), *members),
    )
    sent, first = lax.optimization_barrier((sent, first))
    second = all_ways(*sent)
    start = nh + mh
    wide_2 = ((2, 0, nh), (3, 0, nh))
    across = ((0, nh, mh), (1, nh, mh))
    third = all_ways(
        *put(
            second,
            ((1, start, nh), (1, start + n, nh), *wide_2),
            ((0, start + nh, nh), (0, start + n + nh, nh), *wide_2),
            (*across, (2, nh, nh)),
            (*across, (3, 2 * nh, nh)),
        )
    )
    fourth = all_ways(
        *put(third, ((1, n, nh),), ((0, n + nh, nh),), ((2, 0, mh),), ((3, mh, mh),))
    )
    runs = [
        (0, 0, 0, 0, 3, span, 0),
        (0, 3 * span, 3, 0, 1, n, 0),
        (0, 3 * span + n, 1, 0, 1, n, 0),
    ]
    offset = 0
    for side in range(2):
        runs += [
            (1, offset, 0, 3, 1, nh, side * nh),
            (1, offset + nh, 0, 3, 1, mh, n + side * mh),
            (1, offset + start, 3, 1 + side, 1, n, 0),
            (1, offset + start + n, 1, 1 + side, 1, n, 0),
        ]
        offset += start + 2 * n
    for side in range(2):
        runs += [
            (1, offset, 2, 0, 1, nh, side * nh),
            (1, offset + nh, 3 - 2 * side, 0, 3, m, n),
        ]
        offset += nh + 3 * m
    offset = 0
    for side in range(2):
        runs += [
            (2, offset, 3, 3, 1, nh, side * nh),
            (2, offset + nh, 1, 3, 1, nh, side * nh),
            (2, offset + n, 2, 1 + side, 1, n, 0),
        ]
        offset += 2 * n
    runs += [
        (2, offset, 3, 3, 1, m, n),
        (2, offset + m, 2, 0, 1, m, n),
        (2, offset + 2 * m, 2, 1, 1, mh, n),
        (2, offset + 2 * m + mh, 1, 3, 1, m, n),
        (2, offset + 3 * m + mh, 2, 1, 1, mh, n + mh),
        (2, offset + 3 * m + 2 * mh, 2, 2, 1, m, n),
        (3, 0, 2, 3, 1, nh, 0),
        (3, nh, 2, 3, 1, nh, nh),
        (3, n, 2, 3, 1, mh, n),
        (3, n + mh, 2, 3, 1, mh, n + mh),
    ]
    parts = [project(part, *matrices) for part in (first, second, third, fourth)]
    later, first = lax.optimization_barrier((later, parts[0][1]))
    parts[0] = (parts[0][0], first)
    later = columns_held(later)
    return parts, tuple(runs), matrices, later


ORDER = (((2, 0, 4), (1, 3, 1), (3, 3, 1)), ((1, 0, 3), (3, 0, 3), (0, 3, 1), (0, 0, 3)))


def scatter_sum(early, later, matrix, hyena):
    span = early.shape[0] // 6
    columns = matrix.shape[1]
    wide, narrow = columns * 3 // 8, columns // 8
    places = {}
    for array, pieces in enumerate((ORDER[0], ORDER[1][:3], ORDER[1][3:])):
        row = 0
        for group, base, members in pieces:
            for member in range(base, base + members):
                places[group, member] = (array, row)
                row += span

    def product(part, other):
        both = beside(part, other)
        return narrowed(jnp.dot(both, matrix, preferred_element_type=jnp.float32))

    def term(group, member, side, *more):
        array, row = places[group, member]
        return (wide, [(array, row, side * wide), *more])

    def low(group, member, side, *more):
        array, row = places[group, member]
        return (narrow, [(array, row, 2 * wide + side * narrow), *more])

    def put(arrays, *plans):
        return assemble(arrays, *[columns_of(span, *plan) for plan in plans])

    early = product(early, swapped(early))
    other = swapped(later)
    first = all_ways(
        *put([early], [term(2, 3, 0)], [term(2, 3, 1)], [low(2, 3, 0)], [low(2, 3, 1)])
    )
    later, first = lax.optimization_barrier((later, first))
    x, y, below, above = range(1, 5)
    second = all_ways(
        *put(
            [early, *first],
            [term(2, 1, 0), term(2, 1, 1, (y, 0, 0)), term(1, 3, 0), term(3, 3, 0)],
            [term(2, 2, 0, (x, 0, 0)), term(2, 2, 1), term(1, 3, 1), term(3, 3, 1)],
            [low(1, 3, 0, (below, 0, 0)), low(1, 3, 1), *[low(2, k, 0) for k in range(3)]],
            [low(3, 3, 0), low(3, 3, 1, (above, 0, 0)), *[low(2, k, 1) for k in range(3)]],
        )
    )
    own = product(later[7 * span :], other[7 * span :])
    later = product(later[: 7 * span], other[: 7 * span])
    later, hyena, second = lax.optimization_barrier((later, hyena, second))
    hyena_out = lax.all_to_all(hyena, "ctx", split_axis=0, concat_axis=1, tiled=True).T
    x, y, below, above = range(2, 6)

    def low_3(side):
        return low(0, 3, side, (below, 0, side * narrow), (above, 0, side * narrow))

    def sum_2(side):
        return term(2, 0, side, (x, 0, side * wide), (y, 0, side * wide))

    for_above, for_below = [], []
    for k in range(3):
        start = (2 + k) * narrow
        for_above += [low(1, k, 0, (below, 0, start)), low(1, k, 1)]
        for_below += [low(3, k, 0), low(3, k, 1, (above, 0, start))]
    third = all_ways(
        *put(
            [early, later, *second],
            [
                term(1, 1, 0),
                term(1, 1, 1, (y, 0, 2 * wide)),
                term(3, 1, 0),
                term(3, 1, 1, (y, 0, 3 * wide)),
                term(0, 3, 0),
                low_3(0),
            ],
            [
                term(1, 2, 0, (x, 0, 2 * wide)),
                term(1, 2, 1),
                term(3, 2, 0, (x, 0, 3 * wide)),
                term(3, 2, 1),
                term(0, 3, 1),
                low_3(1),
            ],
            [sum_2(0), *for_above],
            [sum_2(1), *for_below],
        )
    )

    x, y, below, above = range(3, 7)

    def low_own(k, side, *more):
        start = wide + (2 * k + side) * narrow
        return low(0, k, side, (below, 0, start), (above, 0, start), *more)

    def own_sum(group, side, *more):
        start = (group - 1 + side) * wide
        return term(group, 0, side, (x, 0, start), (y, 0, start), *more)

    *sent, base = put(
            [early, later, own, *third],
            [
                term(0, 1, 0),
                term(0, 1, 1, (y, 0, 4 * wide)),
                low_own(1, 0),
                low_own(1, 1, (y, 0, 5 * wide)),
            ],
            [
                term(0, 2, 0, (x, 0, 4 * wide)),
                term(0, 2, 1),
                low_own(2, 0, (x, 0, 5 * wide)),
                low_own(2, 1),
            ],
            [own_sum(1, 0, (below, 0, 0)), own_sum(1, 1)],
            [own_sum(3, 0), own_sum(3, 1, (above, 0, 0))],
            [term(0, 0, 0), term(0, 0, 1), low_own(0, 0), low_own(0, 1)],
        )
    (grad_input,) = put(
        [base, *all_ways(*sent)],
        [
            (2 * wide, [(way, 0, 0) for way in range(5)]),
            (2 * narrow, [(way, 0, 2 * wide) for way in range(3)]),
        ],
    )
    return grad_input, hyena_out


def gather_tokens(tokens, weights, residues, decay_rates, cotangent):
    me = lax.axis_index("ctx").astype(jnp.int32).reshape(1)
    channels, span = weights.shape[1], tokens.shape[0]
    rows = weights[0].swapaxes(0, 1).reshape(3 * channels, weights.shape[3])
    *tokens_half, kept, given = halves(
        (tokens, rows),
        (0, span, True),
        (0, span * 3 // 4, True),
        (1, 3 * channels, True),
        (1, 3 * channels, False),
    )
    taken = swapped(given)
    parts, runs, (kept, taken), cot_cols = gather_groups(*tokens_half, (kept, taken), cotangent)
    own, other = zip(*parts)
    hyena, grads, (early, later) = scan_all(
        me, cot_cols, residues[0].T, decay_rates[0].T, runs, ORDER, own, other
    )
    grad_input, hyena_out = scatter_sum(early, later, stack(kept, taken), hyena)
    return (hyena_out, grad_input, grads.T[None])


def shards(tokens, weights, residues, decay_rates, cotangent):
    ctx, tp = lax.axis_size("ctx"), lax.axis_size("tp")
    if ctx == 4 * PLANE and tp == 2 and weights.size * tp > 2 * tokens.size:
        return gather_tokens(tokens, weights, residues, decay_rates, cotangent)
    return gather_weights(tokens, weights, residues, decay_rates, cotangent)


def solution(mesh):
    return jax.shard_map(
        shards,
        mesh=mesh,
        in_specs=(
            P("ctx", None),
            P("tp", "ctx", None, None),
            P("tp", "ctx", None),
            P("tp", "ctx", None),
            P("tp", "ctx"),
        ),
        out_specs=(P("tp", "ctx"), P("ctx", "tp"), P("tp", "ctx", None)),
        check_vma=False,
    )
```

```python
import functools
import math

import jax
import jax.numpy as jnp
from jax import lax
from jax.experimental import pallas as pl
from jax.experimental.pallas import tpu as pltpu
from jax.sharding import PartitionSpec as P


def precise(form, left, right):
    return jnp.einsum(
        form, left, right, precision=lax.Precision.HIGHEST, preferred_element_type=jnp.float32
    )


def tripled(form, left, right):
    return jnp.einsum(
        form, left, right, precision=lax.Precision.HIGH, preferred_element_type=jnp.float32
    )


def angle_table(row_count, col_count, period):
    product = (
        jnp.arange(row_count, dtype=jnp.int32)[:, None]
        * jnp.arange(col_count, dtype=jnp.int32)[None, :]
        % period
    )
    angles = product.astype(jnp.float32) * (2.0 * math.pi / period)
    return (jnp.cos(angles), jnp.sin(angles))


def make_tables(length):
    padded = 2 * length
    outer = math.gcd(padded, 1 << (padded.bit_length() - 1) // 2)
    inner = padded // outer
    cos_outer, sin_outer = angle_table(outer, outer, outer)
    cos_inner, sin_inner = angle_table(inner, inner, inner)
    twist_cos, twist_sin = angle_table(outer, inner, padded)
    return (outer, inner, cos_outer, sin_outer, cos_inner, sin_inner, twist_cos, twist_sin)


def spectrum(signal, tables, product):
    outer, inner, cos_outer, sin_outer, cos_inner, sin_inner, twist_cos, twist_sin = tables
    half_rows = outer // 2
    blocks = signal.reshape(signal.shape[0], half_rows, inner)
    first_re = product("kp,bpq->bkq", cos_outer[:, :half_rows], blocks)
    first_im = -product("kp,bpq->bkq", sin_outer[:, :half_rows], blocks)
    turned_re = first_re * twist_cos + first_im * twist_sin
    turned_im = first_im * twist_cos - first_re * twist_sin
    spec_re = product("bkq,qj->bkj", turned_re, cos_inner) + product(
        "bkq,qj->bkj", turned_im, sin_inner
    )
    spec_im = product("bkq,qj->bkj", turned_im, cos_inner) - product(
        "bkq,qj->bkj", turned_re, sin_inner
    )
    return (spec_re, spec_im)


def signal_of(spec_re, spec_im, tables):
    outer, inner, cos_outer, sin_outer, cos_inner, sin_inner, twist_cos, twist_sin = tables
    half_rows = outer // 2
    back_re = tripled("bkj,jq->bkq", spec_re, cos_inner) - tripled(
        "bkj,jq->bkq", spec_im, sin_inner
    )
    back_im = tripled("bkj,jq->bkq", spec_im, cos_inner) + tripled(
        "bkj,jq->bkq", spec_re, sin_inner
    )
    turned_re = back_re * twist_cos - back_im * twist_sin
    turned_im = back_im * twist_cos + back_re * twist_sin
    values = tripled("pk,bkq->bpq", cos_outer[:half_rows, :], turned_re) - tripled(
        "pk,bkq->bpq", sin_outer[:half_rows, :], turned_im
    )
    return values.reshape(values.shape[0], half_rows * inner) * (1.0 / (outer * inner))


def spec_product(left_re, left_im, right_re, right_im):
    return (left_re * right_re - left_im * right_im, left_re * right_im + left_im * right_re)


def conj_product(left_re, left_im, right_re, right_im):
    return (left_re * right_re + left_im * right_im, left_re * right_im - left_im * right_re)


def filter_basis(residue_loc, rate_loc, length):
    position = jnp.arange(length, dtype=jnp.float32)
    basis_all = jnp.sqrt(2.0 * rate_loc)[:, :, None] * jnp.exp(
        -rate_loc[:, :, None] * position[None, None, :]
    )
    return (basis_all, precise("cm,cmt->ct", residue_loc, basis_all))


def forward_cols(gated_cols, taps_re, taps_im, tables):
    gated_re, gated_im = spectrum(gated_cols.astype(jnp.float32), tables, tripled)
    conv_re, conv_im = spec_product(gated_re, gated_im, taps_re, taps_im)
    conv_cols = signal_of(conv_re, conv_im, tables).astype(jnp.bfloat16)
    return (conv_cols, gated_re, gated_im)


def backward_cols(slope_cols, gated_re, gated_im, taps_re, taps_im, basis_all, tables, length):
    slope_re, slope_im = spectrum(slope_cols.astype(jnp.float32), tables, tripled)
    grad_re, grad_im = conj_product(taps_re, taps_im, slope_re, slope_im)
    back_cols = signal_of(grad_re, grad_im, tables).astype(jnp.bfloat16)
    lag_re, lag_im = conj_product(gated_re, gated_im, slope_re, slope_im)
    taps_grad = signal_of(lag_re, lag_im, tables)
    grad_residue = precise("ct,cmt->cm", taps_grad, basis_all) * (1.0 / math.sqrt(length))
    return (back_cols, grad_residue)


def gather_weights(tokens, weights, residues, decay_rates, cotangent):
    gathered = lax.all_gather(weights, "ctx", axis=1, tiled=True)
    projected = jnp.einsum("xcpd,td->xcpt", gathered, tokens, preferred_element_type=jnp.float32)
    features = projected[0].astype(jnp.bfloat16)
    query_f = features[:, 0].astype(jnp.float32)
    key_part = features[:, 1].astype(jnp.float32)
    value_part = features[:, 2].astype(jnp.float32)
    gated_in = (key_part * value_part).astype(jnp.bfloat16)
    slope_in = (cotangent.astype(jnp.float32) * query_f).astype(jnp.bfloat16)
    length = tokens.shape[0] * lax.axis_size("ctx")
    tables = make_tables(length)
    basis_all, taps_full = filter_basis(residues[0], decay_rates[0], length)
    taps_re, taps_im = spectrum(taps_full, tables, precise)
    gated_cols = lax.all_to_all(gated_in, "ctx", split_axis=0, concat_axis=1, tiled=True)
    conv_cols, gated_re, gated_im = forward_cols(gated_cols, taps_re, taps_im, tables)
    conv_rows = lax.all_to_all(conv_cols, "ctx", split_axis=1, concat_axis=0, tiled=True)
    slope_cols = lax.all_to_all(slope_in, "ctx", split_axis=0, concat_axis=1, tiled=True)
    back_cols, grad_residue = backward_cols(
        slope_cols, gated_re, gated_im, taps_re, taps_im, basis_all, tables, length
    )
    back_rows = lax.all_to_all(back_cols, "ctx", split_axis=1, concat_axis=0, tiled=True)
    conv_f = conv_rows.astype(jnp.float32)
    back_f = back_rows.astype(jnp.float32)
    hyena_out = (query_f * conv_f).astype(jnp.bfloat16)
    grad_query = (cotangent.astype(jnp.float32) * conv_f).astype(jnp.bfloat16)
    grad_key = (back_f * value_part).astype(jnp.bfloat16)
    grad_value = (back_f * key_part).astype(jnp.bfloat16)
    grad_proj = jnp.stack([grad_query, grad_key, grad_value], axis=1)
    partial_value = jnp.einsum(
        "cpt,cpd->td", grad_proj, gathered[0], preferred_element_type=jnp.float32
    )
    grad_input = lax.psum_scatter(
        partial_value.astype(jnp.bfloat16), "tp", scatter_dimension=1, tiled=True
    )
    return (hyena_out, grad_input, grad_residue[None])


GROUP = 4
PLANE = 4
VMEM = 56 * 2**20


def rounded(value):
    return value.astype(jnp.bfloat16).astype(jnp.float32)


def earlier_sum(finals, rate, span, back):
    count = finals.shape[0]
    row = lax.broadcasted_iota(jnp.int32, finals.shape, 0)

    def shifted(value, by):
        if back:
            moved = pltpu.roll(value, count - by, 0)
            return jnp.where(row < count - by, moved, 0.0)
        moved = pltpu.roll(value, by, 0)
        return jnp.where(row >= by, moved, 0.0)

    total = shifted(finals, 1)
    by = 1
    while by < count:
        total = total + jnp.exp(rate * (-1.0 * span * by)) * shifted(total, by)
        by *= 2
    return total


def scan_kernel(
    groups,
    runs,
    order,
    me_ref,
    residue_ref,
    rate_ref,
    *refs,
):
    inputs = 1 + max(run[0] for run in runs)
    arrays, refs = refs[: 2 * inputs + 1], refs[2 * inputs + 1 :]
    hyena_ref, grad_ref = refs[:2]
    proj_refs, refs = refs[2 : 2 + len(order)], refs[2 + len(order) :]
    gated_s, slope_s, conv_s, back_s, feats_s, arrived = refs[:6]
    held = refs[6:]
    cot_ref, own, other = held[0], held[1 : 1 + inputs], held[1 + inputs :]
    copies = [
        pltpu.make_async_copy(array, here, arrived.at[k])
        for k, (array, here) in enumerate(zip(arrays, held))
    ]
    for copy in copies:
        copy.start()
    length, width = cot_ref.shape
    chunks = PLANE * groups
    span = length // chunks
    modes = rate_ref.shape[0]
    me = me_ref[0]

    def place(group, member):
        return lax.rem(me // PLANE + group, groups) * PLANE + (member ^ lax.rem(me, PLANE))

    def aligned(start, size):
        return pl.ds(pl.multiple_of(start, size), size)

    copies[0].wait()
    waited = set()
    for source, offset, group, base, members, count, first in sorted(runs):
        if source not in waited:
            waited.add(source)
            copies[1 + source].wait()
            copies[1 + inputs + source].wait()

        def before(step, _, source=source, offset=offset, group=group, base=base, count=count, first=first):
            member = base + step
            index = place(group, member)
            rows = pl.ds(pl.multiple_of(offset + step * count, 16), count)
            feats = own[source][rows, :] + other[source][rows, :].astype(jnp.float32)
            feats = rounded(feats)
            slot = (group * PLANE + member) * span + first
            feats_s[pl.ds(pl.multiple_of(slot, 16), count), :] = feats
            cot = cot_ref[pl.ds(pl.multiple_of(index * span + first, 16), count), :]
            query, key = feats[:, :width], feats[:, width : 2 * width]
            into = pl.ds(first * chunks + index, count, stride=chunks)
            gated_s[into, :] = rounded(key * feats[:, 2 * width :])
            slope_s[into, :] = rounded(cot.astype(jnp.float32) * query)
            return 0

        lax.fori_loop(0, members, before, 0)

    def at(step):
        return aligned(step * chunks, chunks)

    zero = jnp.zeros((chunks, width), jnp.float32)
    scale = 1.0 / math.sqrt(length)
    for first in range(0, modes, GROUP):
        count = min(GROUP, modes - first)
        rates = [
            jnp.broadcast_to(rate_ref[m : m + 1, :], (chunks, width))
            for m in range(first, first + count)
        ]
        decays = [jnp.exp(-rate) for rate in rates]
        norms = [jnp.sqrt(2.0 * rate) for rate in rates]
        gains = [
            residue_ref[first + n : first + n + 1, :] * norms[n] for n in range(count)
        ]

        def sums(step, state):
            ahead, behind = state
            gated = gated_s[at(step), :]
            slope = slope_s[at(span - 1 - step), :]
            return (
                tuple(decays[n] * ahead[n] + gated for n in range(count)),
                tuple(decays[n] * behind[n] + slope for n in range(count)),
            )

        ahead, behind = lax.fori_loop(0, span, sums, ((zero,) * count, (zero,) * count), unroll=8)
        ahead = tuple(earlier_sum(ahead[n], rates[n], span, False) for n in range(count))
        behind = tuple(earlier_sum(behind[n], rates[n], span, True) for n in range(count))

        def outs(step, state):
            ahead, behind, grads = state
            other = span - 1 - step
            gated = gated_s[at(step), :]
            slope = slope_s[at(step), :]
            slope_back = slope_s[at(other), :]
            ahead = tuple(decays[n] * ahead[n] + gated for n in range(count))
            behind = tuple(decays[n] * behind[n] + slope_back for n in range(count))
            grads = tuple(grads[n] + slope * ahead[n] for n in range(count))
            conv = sum(gains[n] * ahead[n] for n in range(count))
            back = sum(gains[n] * behind[n] for n in range(count))
            if first:
                conv = conv + conv_s[at(step), :]
                back = back + back_s[at(other), :]
            conv_s[at(step), :] = conv
            back_s[at(other), :] = back
            return ahead, behind, grads

        _, _, grads = lax.fori_loop(0, span, outs, (ahead, behind, (zero,) * count), unroll=4)
        for n in range(count):
            total = jnp.sum(grads[n] * norms[n], axis=0, keepdims=True) * scale
            grad_ref[first + n : first + n + 1, :] = total

    for proj_ref, pieces in zip(proj_refs, order):
        start = 0
        for group, base, members in pieces:

            def after(step, _, proj_ref=proj_ref, start=start, group=group, base=base):
                member = base + step
                index = place(group, member)
                feats = feats_s[aligned((group * PLANE + member) * span, span), :]
                query, key = feats[:, :width], feats[:, width : 2 * width]
                cot = cot_ref[aligned(index * span, span), :].astype(jnp.float32)
                conv = rounded(conv_s[pl.ds(index, span, stride=chunks), :])
                back = rounded(back_s[pl.ds(index, span, stride=chunks), :])
                hyena_ref[aligned(index * span, span), :] = narrowed(query * conv)
                rows = aligned(start + step * span, span)
                proj_ref[rows, :width] = narrowed(cot * conv)
                proj_ref[rows, width : 2 * width] = narrowed(back * feats[:, 2 * width :])
                proj_ref[rows, 2 * width :] = narrowed(back * key)
                return 0

            lax.fori_loop(0, members, after, 0)
            start += members * span


def scan_all(me, cot_cols, residue_rows, rate_rows, runs, order, own, other):
    length, width = cot_cols.shape
    span = length // (PLANE * PLANE)
    vmem = pl.BlockSpec(memory_space=pltpu.VMEM)
    arrays = (cot_cols, *own, *other)
    outs = pl.pallas_call(
        functools.partial(scan_kernel, PLANE, runs, order),
        out_shape=(
            jax.ShapeDtypeStruct((length, width), jnp.bfloat16),
            jax.ShapeDtypeStruct(rate_rows.shape, jnp.float32),
        )
        + tuple(
            jax.ShapeDtypeStruct((span * sum(piece[2] for piece in pieces), 3 * width), jnp.bfloat16)
            for pieces in order
        ),
        in_specs=[pl.BlockSpec(memory_space=pltpu.SMEM), vmem, vmem]
        + [pl.BlockSpec(memory_space=pl.ANY)] * len(arrays),
        out_specs=(vmem,) * (2 + len(order)),
        scratch_shapes=[pltpu.VMEM((length, width), jnp.float32)] * 4
        + [pltpu.VMEM((length, 3 * width), jnp.float32), pltpu.SemaphoreType.DMA((len(arrays),))]
        + [pltpu.VMEM(array.shape, array.dtype) for array in arrays],
        compiler_params=pltpu.CompilerParams(vmem_limit_bytes=40 * 2**20),
        name="modal_scan",
    )(me, residue_rows, rate_rows, *arrays)
    return outs[0], outs[1], outs[2:]


def swapped(value):
    return lax.ppermute(value, "tp", [(0, 1), (1, 0)])


def over_x(value):
    return lax.ppermute(value, "ctx", [(i, i ^ 1) for i in range(lax.axis_size("ctx"))])


def over_y(value):
    return lax.ppermute(value, "ctx", [(i, i ^ 2) for i in range(lax.axis_size("ctx"))])


def up(value):
    count = lax.axis_size("ctx")
    return lax.ppermute(value, "ctx", [(i, (i + PLANE) % count) for i in range(count)])


def down(value):
    count = lax.axis_size("ctx")
    return lax.ppermute(value, "ctx", [((i + PLANE) % count, i) for i in range(count)])


def stack(*parts):
    return jnp.concatenate(parts, axis=0)


def beside(*parts):
    return jnp.concatenate(parts, axis=1)


def narrowed(value):
    return value.astype(jnp.bfloat16)


def widened(value):
    return value.astype(jnp.float32)


def halves_kernel(plan, core_ref, *refs):
    arrays, outs, arrived = refs[: -1 - len(plan)], refs[-1 - len(plan) : -1], refs[-1]
    copies = []
    for k, (out, (index, count, mine)) in enumerate(zip(outs, plan)):
        half = out.shape[1]
        side = core_ref[0] if mine else 1 - core_ref[0]
        columns = pl.ds(pl.multiple_of(side * half, half), half)
        part = arrays[index].at[pl.ds(0, count), columns]
        copies.append(pltpu.make_async_copy(part, out, arrived.at[k]))
    for copy in copies:
        copy.start()
    for copy in copies:
        copy.wait()


def halves(arrays, *plan):
    core = lax.axis_index("tp").astype(jnp.int32).reshape(1)
    shapes = [(count, arrays[index].shape[1] // 2) for index, count, _ in plan]
    moved = sum(4 * rows * columns for rows, columns in shapes)
    return pl.pallas_call(
        functools.partial(halves_kernel, plan),
        out_shape=tuple(jax.ShapeDtypeStruct(shape, jnp.bfloat16) for shape in shapes),
        in_specs=[pl.BlockSpec(memory_space=pltpu.SMEM)]
        + [pl.BlockSpec(memory_space=pl.ANY)] * len(arrays),
        out_specs=(pl.BlockSpec(memory_space=pltpu.VMEM),) * len(plan),
        scratch_shapes=[pltpu.SemaphoreType.DMA((len(plan),))],
        compiler_params=pltpu.CompilerParams(vmem_limit_bytes=VMEM),
        cost_estimate=pl.CostEstimate(flops=0, bytes_accessed=moved, transcendentals=0),
        name="halves",
    )(core, *arrays)


def assemble_kernel(inputs, plans, *refs):
    arrays, outs = refs[:inputs], refs[inputs:]
    for out, plan in zip(outs, plans):
        for row, col, height, width, sources in plan:
            parts = [
                arrays[index][from_row : from_row + height, from_col : from_col + width]
                for index, from_row, from_col in sources
            ]
            if len(parts) > 1:
                parts = [narrowed(sum(widened(part) for part in parts))]
            out[row : row + height, col : col + width] = parts[0]


def assemble(arrays, *plans):
    shapes = [
        (max(p[0] + p[2] for p in plan), max(p[1] + p[3] for p in plan)) for plan in plans
    ]
    moved = sum(2 * rows * cols for rows, cols in shapes)
    vmem = pl.BlockSpec(memory_space=pltpu.VMEM)
    return pl.pallas_call(
        functools.partial(assemble_kernel, len(arrays), plans),
        out_shape=tuple(jax.ShapeDtypeStruct(shape, jnp.bfloat16) for shape in shapes),
        in_specs=[vmem] * len(arrays),
        out_specs=(vmem,) * len(plans),
        compiler_params=pltpu.CompilerParams(vmem_limit_bytes=32 * 2**20),
        cost_estimate=pl.CostEstimate(flops=moved, bytes_accessed=4 * moved, transcendentals=0),
        name="assemble",
    )(*arrays)


def rows_of(*parts):
    plan, start = [], 0
    for index, first, count in parts:
        plan.append((start, count, [(index, first, 0)]))
        start += count
    return plan


def full_width(columns, plan):
    return [(row, 0, count, columns, sources) for row, count, sources in plan]


def columns_of(height, *parts):
    plan, start = [], 0
    for width, sources in parts:
        plan.append((0, start, height, width, sources))
        start += width
    return plan


def all_ways(for_x, for_y, for_above, for_below):
    from_below, from_above = up(for_above), down(for_below)
    got_x, got_y = over_x(for_x), over_y(for_y)
    return lax.optimization_barrier((got_x, got_y, from_below, from_above))


def project(parts, kept, taken):
    rows = stack(*parts)
    own, given = (
        jnp.einsum("td,rd->tr", rows, matrix, preferred_element_type=jnp.float32)
        for matrix in (kept, taken)
    )
    return own, swapped(narrowed(given))


def columns_held(rows):
    return lax.all_to_all(rows.T, "ctx", split_axis=1, concat_axis=0, tiled=True)


def gather_groups(tokens, wide, matrices, later):
    span = tokens.shape[0]
    n, m = span * 3 // 4, span // 4
    nh, mh = n // 2, m // 2
    columns = tokens.shape[1]

    def put(arrays, *plans):
        return assemble(arrays, *[full_width(columns, rows_of(*plan)) for plan in plans])

    own_x, own_y, wide_3, wide_1 = all_ways(tokens, tokens, wide, wide)
    first = (tokens, own_x, own_y, wide_3, wide_1)
    members = ((0, n, m), (1, n, m), (2, n, m))
    sent = put(
        first,
        ((2, 0, nh), (2, n, mh), (3, 0, n), (4, 0, n)),
        ((1, nh, nh), (1, n + mh, mh), (3, 0, n), (4, 0, n)),
        ((3, 0, nh), *members),
        ((4, nh, nh), *members),
    )
    sent, first = lax.optimization_barrier((sent, first))
    second = all_ways(*sent)
    start = nh + mh
    wide_2 = ((2, 0, nh), (3, 0, nh))
    across = ((0, nh, mh), (1, nh, mh))
    third = all_ways(
        *put(
            second,
            ((1, start, nh), (1, start + n, nh), *wide_2),
            ((0, start + nh, nh), (0, start + n + nh, nh), *wide_2),
            (*across, (2, nh, nh)),
            (*across, (3, 2 * nh, nh)),
        )
    )
    fourth = all_ways(
        *put(third, ((1, n, nh),), ((0, n + nh, nh),), ((2, 0, mh),), ((3, mh, mh),))
    )
    runs = [
        (0, 0, 0, 0, 3, span, 0),
        (0, 3 * span, 3, 0, 1, n, 0),
        (0, 3 * span + n, 1, 0, 1, n, 0),
    ]
    offset = 0
    for side in range(2):
        runs += [
            (1, offset, 0, 3, 1, nh, side * nh),
            (1, offset + nh, 0, 3, 1, mh, n + side * mh),
            (1, offset + start, 3, 1 + side, 1, n, 0),
            (1, offset + start + n, 1, 1 + side, 1, n, 0),
        ]
        offset += start + 2 * n
    for side in range(2):
        runs += [
            (1, offset, 2, 0, 1, nh, side * nh),
            (1, offset + nh, 3 - 2 * side, 0, 3, m, n),
        ]
        offset += nh + 3 * m
    offset = 0
    for side in range(2):
        runs += [
            (2, offset, 3, 3, 1, nh, side * nh),
            (2, offset + nh, 1, 3, 1, nh, side * nh),
            (2, offset + n, 2, 1 + side, 1, n, 0),
        ]
        offset += 2 * n
    runs += [
        (2, offset, 3, 3, 1, m, n),
        (2, offset + m, 2, 0, 1, m, n),
        (2, offset + 2 * m, 2, 1, 1, mh, n),
        (2, offset + 2 * m + mh, 1, 3, 1, m, n),
        (2, offset + 3 * m + mh, 2, 1, 1, mh, n + mh),
        (2, offset + 3 * m + 2 * mh, 2, 2, 1, m, n),
        (3, 0, 2, 3, 1, nh, 0),
        (3, nh, 2, 3, 1, nh, nh),
        (3, n, 2, 3, 1, mh, n),
        (3, n + mh, 2, 3, 1, mh, n + mh),
    ]
    parts = [project(part, *matrices) for part in (first, second, third, fourth)]
    later, first = lax.optimization_barrier((later, parts[0][1]))
    parts[0] = (parts[0][0], first)
    later = columns_held(later)
    return parts, tuple(runs), matrices, later


ORDER = (((2, 0, 4), (1, 3, 1), (3, 3, 1)), ((1, 0, 3), (3, 0, 3), (0, 3, 1), (0, 0, 3)))


def scatter_sum(early, later, matrix, hyena):
    span = early.shape[0] // 6
    columns = matrix.shape[1]
    wide, narrow = columns * 3 // 8, columns // 8
    places = {}
    for array, pieces in enumerate((ORDER[0], ORDER[1][:3], ORDER[1][3:])):
        row = 0
        for group, base, members in pieces:
            for member in range(base, base + members):
                places[group, member] = (array, row)
                row += span

    def product(part, other):
        both = beside(part, other)
        return narrowed(jnp.dot(both, matrix, preferred_element_type=jnp.float32))

    def term(group, member, side, *more):
        array, row = places[group, member]
        return (wide, [(array, row, side * wide), *more])

    def low(group, member, side, *more):
        array, row = places[group, member]
        return (narrow, [(array, row, 2 * wide + side * narrow), *more])

    def put(arrays, *plans):
        return assemble(arrays, *[columns_of(span, *plan) for plan in plans])

    early = product(early, swapped(early))
    other = swapped(later)
    first = all_ways(
        *put([early], [term(2, 3, 0)], [term(2, 3, 1)], [low(2, 3, 0)], [low(2, 3, 1)])
    )
    later, first = lax.optimization_barrier((later, first))
    x, y, below, above = range(1, 5)
    second = all_ways(
        *put(
            [early, *first],
            [term(2, 1, 0), term(2, 1, 1, (y, 0, 0)), term(1, 3, 0), term(3, 3, 0)],
            [term(2, 2, 0, (x, 0, 0)), term(2, 2, 1), term(1, 3, 1), term(3, 3, 1)],
            [low(1, 3, 0, (below, 0, 0)), low(1, 3, 1), *[low(2, k, 0) for k in range(3)]],
            [low(3, 3, 0), low(3, 3, 1, (above, 0, 0)), *[low(2, k, 1) for k in range(3)]],
        )
    )
    own = product(later[7 * span :], other[7 * span :])
    later = product(later[: 7 * span], other[: 7 * span])
    later, hyena, second = lax.optimization_barrier((later, hyena, second))
    hyena_out = lax.all_to_all(hyena, "ctx", split_axis=0, concat_axis=1, tiled=True).T
    x, y, below, above = range(2, 6)

    def low_3(side):
        return low(0, 3, side, (below, 0, side * narrow), (above, 0, side * narrow))

    def sum_2(side):
        return term(2, 0, side, (x, 0, side * wide), (y, 0, side * wide))

    for_above, for_below = [], []
    for k in range(3):
        start = (2 + k) * narrow
        for_above += [low(1, k, 0, (below, 0, start)), low(1, k, 1)]
        for_below += [low(3, k, 0), low(3, k, 1, (above, 0, start))]
    third = all_ways(
        *put(
            [early, later, *second],
            [
                term(1, 1, 0),
                term(1, 1, 1, (y, 0, 2 * wide)),
                term(3, 1, 0),
                term(3, 1, 1, (y, 0, 3 * wide)),
                term(0, 3, 0),
                low_3(0),
            ],
            [
                term(1, 2, 0, (x, 0, 2 * wide)),
                term(1, 2, 1),
                term(3, 2, 0, (x, 0, 3 * wide)),
                term(3, 2, 1),
                term(0, 3, 1),
                low_3(1),
            ],
            [sum_2(0), *for_above],
            [sum_2(1), *for_below],
        )
    )

    x, y, below, above = range(3, 7)

    def low_own(k, side, *more):
        start = wide + (2 * k + side) * narrow
        return low(0, k, side, (below, 0, start), (above, 0, start), *more)

    def own_sum(group, side, *more):
        start = (group - 1 + side) * wide
        return term(group, 0, side, (x, 0, start), (y, 0, start), *more)

    *sent, base = put(
            [early, later, own, *third],
            [
                term(0, 1, 0),
                term(0, 1, 1, (y, 0, 4 * wide)),
                low_own(1, 0),
                low_own(1, 1, (y, 0, 5 * wide)),
            ],
            [
                term(0, 2, 0, (x, 0, 4 * wide)),
                term(0, 2, 1),
                low_own(2, 0, (x, 0, 5 * wide)),
                low_own(2, 1),
            ],
            [own_sum(1, 0, (below, 0, 0)), own_sum(1, 1)],
            [own_sum(3, 0), own_sum(3, 1, (above, 0, 0))],
            [term(0, 0, 0), term(0, 0, 1), low_own(0, 0), low_own(0, 1)],
        )
    (grad_input,) = put(
        [base, *all_ways(*sent)],
        [
            (2 * wide, [(way, 0, 0) for way in range(5)]),
            (2 * narrow, [(way, 0, 2 * wide) for way in range(3)]),
        ],
    )
    return grad_input, hyena_out


def gather_tokens(tokens, weights, residues, decay_rates, cotangent):
    me = lax.axis_index("ctx").astype(jnp.int32).reshape(1)
    channels, span = weights.shape[1], tokens.shape[0]
    rows = weights[0].swapaxes(0, 1).reshape(3 * channels, weights.shape[3])
    tokens_half = halves((tokens,), (0, span, True), (0, span * 3 // 4, True))
    kept, given = halves((rows,), (0, 3 * channels, True), (0, 3 * channels, False))
    taken = swapped(given)
    parts, runs, (kept, taken), cot_cols = gather_groups(*tokens_half, (kept, taken), cotangent)
    own, other = zip(*parts)
    hyena, grads, (early, later) = scan_all(
        me, cot_cols, residues[0].T, decay_rates[0].T, runs, ORDER, own, other
    )
    grad_input, hyena_out = scatter_sum(early, later, stack(kept, taken), hyena)
    return (hyena_out, grad_input, grads.T[None])


def shards(tokens, weights, residues, decay_rates, cotangent):
    ctx, tp = lax.axis_size("ctx"), lax.axis_size("tp")
    if ctx == 4 * PLANE and tp == 2 and weights.size * tp > 2 * tokens.size:
        return gather_tokens(tokens, weights, residues, decay_rates, cotangent)
    return gather_weights(tokens, weights, residues, decay_rates, cotangent)


def solution(mesh):
    return jax.shard_map(
        shards,
        mesh=mesh,
        in_specs=(
            P("ctx", None),
            P("tp", "ctx", None, None),
            P("tp", "ctx", None),
            P("tp", "ctx", None),
            P("tp", "ctx"),
        ),
        out_specs=(P("tp", "ctx"), P("ctx", "tp"), P("tp", "ctx", None)),
        check_vma=False,
    )
```

```python
import functools
import math
import operator

import jax
import jax.numpy as jnp
from jax import lax
from jax.experimental import pallas as pl
from jax.experimental.pallas import tpu as pltpu
from jax.sharding import PartitionSpec as P


def precise(form, left, right):
    return jnp.einsum(
        form, left, right, precision=lax.Precision.HIGHEST, preferred_element_type=jnp.float32
    )


def tripled(form, left, right):
    return jnp.einsum(
        form, left, right, precision=lax.Precision.HIGH, preferred_element_type=jnp.float32
    )


def angle_table(row_count, col_count, period):
    product = (
        jnp.arange(row_count, dtype=jnp.int32)[:, None]
        * jnp.arange(col_count, dtype=jnp.int32)[None, :]
        % period
    )
    angles = product.astype(jnp.float32) * (2.0 * math.pi / period)
    return (jnp.cos(angles), jnp.sin(angles))


def make_tables(length):
    padded = 2 * length
    outer = math.gcd(padded, 1 << (padded.bit_length() - 1) // 2)
    inner = padded // outer
    cos_outer, sin_outer = angle_table(outer, outer, outer)
    cos_inner, sin_inner = angle_table(inner, inner, inner)
    twist_cos, twist_sin = angle_table(outer, inner, padded)
    return (outer, inner, cos_outer, sin_outer, cos_inner, sin_inner, twist_cos, twist_sin)


def spectrum(signal, tables, product):
    outer, inner, cos_outer, sin_outer, cos_inner, sin_inner, twist_cos, twist_sin = tables
    half_rows = outer // 2
    blocks = signal.reshape(signal.shape[0], half_rows, inner)
    first_re = product("kp,bpq->bkq", cos_outer[:, :half_rows], blocks)
    first_im = -product("kp,bpq->bkq", sin_outer[:, :half_rows], blocks)
    turned_re = first_re * twist_cos + first_im * twist_sin
    turned_im = first_im * twist_cos - first_re * twist_sin
    spec_re = product("bkq,qj->bkj", turned_re, cos_inner) + product(
        "bkq,qj->bkj", turned_im, sin_inner
    )
    spec_im = product("bkq,qj->bkj", turned_im, cos_inner) - product(
        "bkq,qj->bkj", turned_re, sin_inner
    )
    return (spec_re, spec_im)


def signal_of(spec_re, spec_im, tables):
    outer, inner, cos_outer, sin_outer, cos_inner, sin_inner, twist_cos, twist_sin = tables
    half_rows = outer // 2
    back_re = tripled("bkj,jq->bkq", spec_re, cos_inner) - tripled(
        "bkj,jq->bkq", spec_im, sin_inner
    )
    back_im = tripled("bkj,jq->bkq", spec_im, cos_inner) + tripled(
        "bkj,jq->bkq", spec_re, sin_inner
    )
    turned_re = back_re * twist_cos - back_im * twist_sin
    turned_im = back_im * twist_cos + back_re * twist_sin
    values = tripled("pk,bkq->bpq", cos_outer[:half_rows, :], turned_re) - tripled(
        "pk,bkq->bpq", sin_outer[:half_rows, :], turned_im
    )
    return values.reshape(values.shape[0], half_rows * inner) * (1.0 / (outer * inner))


def spec_product(left_re, left_im, right_re, right_im):
    return (left_re * right_re - left_im * right_im, left_re * right_im + left_im * right_re)


def conj_product(left_re, left_im, right_re, right_im):
    return (left_re * right_re + left_im * right_im, left_re * right_im - left_im * right_re)


def filter_basis(residue_loc, rate_loc, length):
    position = jnp.arange(length, dtype=jnp.float32)
    basis_all = jnp.sqrt(2.0 * rate_loc)[:, :, None] * jnp.exp(
        -rate_loc[:, :, None] * position[None, None, :]
    )
    return (basis_all, precise("cm,cmt->ct", residue_loc, basis_all))


def forward_cols(gated_cols, taps_re, taps_im, tables):
    gated_re, gated_im = spectrum(gated_cols.astype(jnp.float32), tables, tripled)
    conv_re, conv_im = spec_product(gated_re, gated_im, taps_re, taps_im)
    conv_cols = signal_of(conv_re, conv_im, tables).astype(jnp.bfloat16)
    return (conv_cols, gated_re, gated_im)


def backward_cols(slope_cols, gated_re, gated_im, taps_re, taps_im, basis_all, tables, length):
    slope_re, slope_im = spectrum(slope_cols.astype(jnp.float32), tables, tripled)
    grad_re, grad_im = conj_product(taps_re, taps_im, slope_re, slope_im)
    back_cols = signal_of(grad_re, grad_im, tables).astype(jnp.bfloat16)
    lag_re, lag_im = conj_product(gated_re, gated_im, slope_re, slope_im)
    taps_grad = signal_of(lag_re, lag_im, tables)
    grad_residue = precise("ct,cmt->cm", taps_grad, basis_all) * (1.0 / math.sqrt(length))
    return (back_cols, grad_residue)


def gather_weights(tokens, weights, residues, decay_rates, cotangent):
    gathered = lax.all_gather(weights, "ctx", axis=1, tiled=True)
    projected = jnp.einsum("xcpd,td->xcpt", gathered, tokens, preferred_element_type=jnp.float32)
    features = projected[0].astype(jnp.bfloat16)
    query_f = features[:, 0].astype(jnp.float32)
    key_part = features[:, 1].astype(jnp.float32)
    value_part = features[:, 2].astype(jnp.float32)
    gated_in = (key_part * value_part).astype(jnp.bfloat16)
    slope_in = (cotangent.astype(jnp.float32) * query_f).astype(jnp.bfloat16)
    length = tokens.shape[0] * lax.axis_size("ctx")
    tables = make_tables(length)
    basis_all, taps_full = filter_basis(residues[0], decay_rates[0], length)
    taps_re, taps_im = spectrum(taps_full, tables, precise)
    gated_cols = lax.all_to_all(gated_in, "ctx", split_axis=0, concat_axis=1, tiled=True)
    conv_cols, gated_re, gated_im = forward_cols(gated_cols, taps_re, taps_im, tables)
    conv_rows = lax.all_to_all(conv_cols, "ctx", split_axis=1, concat_axis=0, tiled=True)
    slope_cols = lax.all_to_all(slope_in, "ctx", split_axis=0, concat_axis=1, tiled=True)
    back_cols, grad_residue = backward_cols(
        slope_cols, gated_re, gated_im, taps_re, taps_im, basis_all, tables, length
    )
    back_rows = lax.all_to_all(back_cols, "ctx", split_axis=1, concat_axis=0, tiled=True)
    conv_f = conv_rows.astype(jnp.float32)
    back_f = back_rows.astype(jnp.float32)
    hyena_out = (query_f * conv_f).astype(jnp.bfloat16)
    grad_query = (cotangent.astype(jnp.float32) * conv_f).astype(jnp.bfloat16)
    grad_key = (back_f * value_part).astype(jnp.bfloat16)
    grad_value = (back_f * key_part).astype(jnp.bfloat16)
    grad_proj = jnp.stack([grad_query, grad_key, grad_value], axis=1)
    partial_value = jnp.einsum(
        "cpt,cpd->td", grad_proj, gathered[0], preferred_element_type=jnp.float32
    )
    grad_input = lax.psum_scatter(
        partial_value.astype(jnp.bfloat16), "tp", scatter_dimension=1, tiled=True
    )
    return (hyena_out, grad_input, grad_residue[None])


GROUP = 4
PLANE = 4
VMEM = 56 * 2**20


def rounded(value):
    return value.astype(jnp.bfloat16).astype(jnp.float32)


def added_up(parts):
    return functools.reduce(operator.add, parts)


def earlier_sum(finals, rate, span, back):
    count = finals.shape[0]
    row = lax.broadcasted_iota(jnp.int32, finals.shape, 0)

    def shifted(value, by):
        if back:
            moved = pltpu.roll(value, count - by, 0)
            return jnp.where(row < count - by, moved, 0.0)
        moved = pltpu.roll(value, by, 0)
        return jnp.where(row >= by, moved, 0.0)

    total = shifted(finals, 1)
    by = 1
    while by < count:
        total = total + jnp.exp(rate * (-1.0 * span * by)) * shifted(total, by)
        by *= 2
    return total


def scan_kernel(
    groups,
    runs,
    order,
    me_ref,
    residue_ref,
    rate_ref,
    *refs,
):
    inputs = 1 + max(run[0] for run in runs)
    arrays, refs = refs[: 2 * inputs + 1], refs[2 * inputs + 1 :]
    hyena_ref, grad_ref = refs[:2]
    proj_refs, refs = refs[2 : 2 + len(order)], refs[2 + len(order) :]
    gated_s, slope_s, conv_s, back_s, feats_s = refs
    cot_ref, own, other = arrays[0], arrays[1 : 1 + inputs], arrays[1 + inputs :]
    length, width = cot_ref.shape
    chunks = PLANE * groups
    span = length // chunks
    modes = rate_ref.shape[0]
    me = me_ref[0]

    def place(group, member):
        return lax.rem(me // PLANE + group, groups) * PLANE + (member ^ lax.rem(me, PLANE))

    def aligned(start, size):
        return pl.ds(pl.multiple_of(start, size), size)

    for source, offset, group, base, members, count, first in runs:

        def before(step, _, source=source, offset=offset, group=group, base=base, count=count, first=first):
            member = base + step
            index = place(group, member)
            rows = pl.ds(pl.multiple_of(offset + step * count, 16), count)
            feats = own[source][rows, :] + other[source][rows, :].astype(jnp.float32)
            feats = rounded(feats)
            slot = (group * PLANE + member) * span + first
            feats_s[pl.ds(pl.multiple_of(slot, 16), count), :] = feats
            cot = cot_ref[pl.ds(pl.multiple_of(index * span + first, 16), count), :]
            query, key = feats[:, :width], feats[:, width : 2 * width]
            into = pl.ds(first * chunks + index, count, stride=chunks)
            gated_s[into, :] = rounded(key * feats[:, 2 * width :])
            slope_s[into, :] = rounded(cot.astype(jnp.float32) * query)
            return 0

        lax.fori_loop(0, members, before, 0)

    def at(step):
        return aligned(step * chunks, chunks)

    zero = jnp.zeros((chunks, width), jnp.float32)
    scale = 1.0 / math.sqrt(length)
    for first in range(0, modes, GROUP):
        count = min(GROUP, modes - first)
        rates = [
            jnp.broadcast_to(rate_ref[m : m + 1, :], (chunks, width))
            for m in range(first, first + count)
        ]
        decays = [jnp.exp(-rate) for rate in rates]
        norms = [jnp.sqrt(2.0 * rate) for rate in rates]
        gains = [
            residue_ref[first + n : first + n + 1, :] * norms[n] for n in range(count)
        ]

        def sums(step, state):
            ahead, behind = state
            gated = gated_s[at(step), :]
            slope = slope_s[at(span - 1 - step), :]
            return (
                tuple(decays[n] * ahead[n] + gated for n in range(count)),
                tuple(decays[n] * behind[n] + slope for n in range(count)),
            )

        ahead, behind = lax.fori_loop(0, span, sums, ((zero,) * count, (zero,) * count), unroll=16)
        ahead = tuple(earlier_sum(ahead[n], rates[n], span, False) for n in range(count))
        behind = tuple(earlier_sum(behind[n], rates[n], span, True) for n in range(count))

        def outs(step, state):
            ahead, behind, grads = state
            other = span - 1 - step
            gated = gated_s[at(step), :]
            slope = slope_s[at(step), :]
            slope_back = slope_s[at(other), :]
            ahead = tuple(decays[n] * ahead[n] + gated for n in range(count))
            behind = tuple(decays[n] * behind[n] + slope_back for n in range(count))
            grads = tuple(grads[n] + slope * ahead[n] for n in range(count))
            conv = added_up(gains[n] * ahead[n] for n in range(count))
            back = added_up(gains[n] * behind[n] for n in range(count))
            if first:
                conv = conv + conv_s[at(step), :]
                back = back + back_s[at(other), :]
            conv_s[at(step), :] = conv
            back_s[at(other), :] = back
            return ahead, behind, grads

        _, _, grads = lax.fori_loop(0, span, outs, (ahead, behind, (zero,) * count), unroll=8)
        for n in range(count):
            total = jnp.sum(grads[n] * norms[n], axis=0, keepdims=True) * scale
            grad_ref[first + n : first + n + 1, :] = total

    for proj_ref, pieces in zip(proj_refs, order):
        start = 0
        for group, base, members in pieces:

            def after(step, _, proj_ref=proj_ref, start=start, group=group, base=base):
                member = base + step
                index = place(group, member)
                feats = feats_s[aligned((group * PLANE + member) * span, span), :]
                query, key = feats[:, :width], feats[:, width : 2 * width]
                cot = cot_ref[aligned(index * span, span), :].astype(jnp.float32)
                conv = rounded(conv_s[pl.ds(index, span, stride=chunks), :])
                back = rounded(back_s[pl.ds(index, span, stride=chunks), :])
                hyena_ref[aligned(index * span, span), :] = narrowed(query * conv)
                rows = aligned(start + step * span, span)
                proj_ref[rows, :width] = narrowed(cot * conv)
                proj_ref[rows, width : 2 * width] = narrowed(back * feats[:, 2 * width :])
                proj_ref[rows, 2 * width :] = narrowed(back * key)
                return 0

            lax.fori_loop(0, members, after, 0)
            start += members * span


def scan_all(me, cot_cols, residue_rows, rate_rows, runs, order, own, other):
    length, width = cot_cols.shape
    span = length // (PLANE * PLANE)
    vmem = pl.BlockSpec(memory_space=pltpu.VMEM)
    arrays = (cot_cols, *own, *other)
    outs = pl.pallas_call(
        functools.partial(scan_kernel, PLANE, runs, order),
        out_shape=(
            jax.ShapeDtypeStruct((length, width), jnp.bfloat16),
            jax.ShapeDtypeStruct(rate_rows.shape, jnp.float32),
        )
        + tuple(
            jax.ShapeDtypeStruct((span * sum(piece[2] for piece in pieces), 3 * width), jnp.bfloat16)
            for pieces in order
        ),
        in_specs=[pl.BlockSpec(memory_space=pltpu.SMEM)] + [vmem] * (2 + len(arrays)),
        out_specs=(vmem,) * (2 + len(order)),
        scratch_shapes=[pltpu.VMEM((length, width), jnp.float32)] * 4
        + [pltpu.VMEM((length, 3 * width), jnp.float32)],
        compiler_params=pltpu.CompilerParams(vmem_limit_bytes=40 * 2**20),
        name="modal_scan",
    )(me, residue_rows, rate_rows, *arrays)
    return outs[0], outs[1], outs[2:]


def swapped(value):
    return lax.ppermute(value, "tp", [(0, 1), (1, 0)])


def over_x(value):
    return lax.ppermute(value, "ctx", [(i, i ^ 1) for i in range(lax.axis_size("ctx"))])


def over_y(value):
    return lax.ppermute(value, "ctx", [(i, i ^ 2) for i in range(lax.axis_size("ctx"))])


def up(value):
    count = lax.axis_size("ctx")
    return lax.ppermute(value, "ctx", [(i, (i + PLANE) % count) for i in range(count)])


def down(value):
    count = lax.axis_size("ctx")
    return lax.ppermute(value, "ctx", [((i + PLANE) % count, i) for i in range(count)])


def stack(*parts):
    return jnp.concatenate(parts, axis=0)


def beside(*parts):
    return jnp.concatenate(parts, axis=1)


def narrowed(value):
    return value.astype(jnp.bfloat16)


def widened(value):
    return value.astype(jnp.float32)


def halves_kernel(plan, core_ref, *refs):
    arrays, outs, arrived = refs[: -1 - len(plan)], refs[-1 - len(plan) : -1], refs[-1]
    copies = []
    for k, (out, (index, count, mine)) in enumerate(zip(outs, plan)):
        half = out.shape[1]
        side = core_ref[0] if mine else 1 - core_ref[0]
        columns = pl.ds(pl.multiple_of(side * half, half), half)
        part = arrays[index].at[pl.ds(0, count), columns]
        copies.append(pltpu.make_async_copy(part, out, arrived.at[k]))
    for copy in copies:
        copy.start()
    for copy in copies:
        copy.wait()


def halves(arrays, *plan):
    core = lax.axis_index("tp").astype(jnp.int32).reshape(1)
    shapes = [(count, arrays[index].shape[1] // 2) for index, count, _ in plan]
    moved = sum(4 * rows * columns for rows, columns in shapes)
    return pl.pallas_call(
        functools.partial(halves_kernel, plan),
        out_shape=tuple(jax.ShapeDtypeStruct(shape, jnp.bfloat16) for shape in shapes),
        in_specs=[pl.BlockSpec(memory_space=pltpu.SMEM)]
        + [pl.BlockSpec(memory_space=pl.ANY)] * len(arrays),
        out_specs=(pl.BlockSpec(memory_space=pltpu.VMEM),) * len(plan),
        scratch_shapes=[pltpu.SemaphoreType.DMA((len(plan),))],
        compiler_params=pltpu.CompilerParams(vmem_limit_bytes=VMEM),
        cost_estimate=pl.CostEstimate(flops=0, bytes_accessed=moved, transcendentals=0),
        name="halves",
    )(core, *arrays)


def assemble_kernel(inputs, plans, *refs):
    arrays, outs = refs[:inputs], refs[inputs:]
    for out, plan in zip(outs, plans):
        for row, col, height, width, sources in plan:
            parts = [
                arrays[index][from_row : from_row + height, from_col : from_col + width]
                for index, from_row, from_col in sources
            ]
            if len(parts) > 1:
                parts = [narrowed(added_up(widened(part) for part in parts))]
            out[row : row + height, col : col + width] = parts[0]


def assemble(arrays, *plans):
    shapes = [
        (max(p[0] + p[2] for p in plan), max(p[1] + p[3] for p in plan)) for plan in plans
    ]
    moved = sum(2 * rows * cols for rows, cols in shapes)
    vmem = pl.BlockSpec(memory_space=pltpu.VMEM)
    return pl.pallas_call(
        functools.partial(assemble_kernel, len(arrays), plans),
        out_shape=tuple(jax.ShapeDtypeStruct(shape, jnp.bfloat16) for shape in shapes),
        in_specs=[vmem] * len(arrays),
        out_specs=(vmem,) * len(plans),
        compiler_params=pltpu.CompilerParams(vmem_limit_bytes=32 * 2**20),
        cost_estimate=pl.CostEstimate(flops=moved, bytes_accessed=4 * moved, transcendentals=0),
        name="assemble",
    )(*arrays)


def rows_of(*parts):
    plan, start = [], 0
    for index, first, count in parts:
        plan.append((start, count, [(index, first, 0)]))
        start += count
    return plan


def full_width(columns, plan):
    return [(row, 0, count, columns, sources) for row, count, sources in plan]


def columns_of(height, *parts):
    plan, start = [], 0
    for width, sources in parts:
        plan.append((0, start, height, width, sources))
        start += width
    return plan


def all_ways(for_x, for_y, for_above, for_below):
    from_below, from_above = up(for_above), down(for_below)
    got_x, got_y = over_x(for_x), over_y(for_y)
    return lax.optimization_barrier((got_x, got_y, from_below, from_above))


def project(parts, kept, taken):
    rows = stack(*parts)
    own, given = (
        jnp.einsum("td,rd->tr", rows, matrix, preferred_element_type=jnp.float32)
        for matrix in (kept, taken)
    )
    return own, swapped(narrowed(given))


def columns_held(rows):
    return lax.all_to_all(rows.T, "ctx", split_axis=1, concat_axis=0, tiled=True)


def gather_groups(tokens, wide, matrices, later):
    span = tokens.shape[0]
    n, m = span * 3 // 4, span // 4
    nh, mh = n // 2, m // 2
    columns = tokens.shape[1]

    def put(arrays, *plans):
        return assemble(arrays, *[full_width(columns, rows_of(*plan)) for plan in plans])

    own_x, own_y, wide_3, wide_1 = all_ways(tokens, tokens, wide, wide)
    first = (tokens, own_x, own_y, wide_3, wide_1)
    members = ((0, n, m), (1, n, m), (2, n, m))
    sent = put(
        first,
        ((2, 0, nh), (2, n, mh), (3, 0, n), (4, 0, n)),
        ((1, nh, nh), (1, n + mh, mh), (3, 0, n), (4, 0, n)),
        ((3, 0, nh), *members),
        ((4, nh, nh), *members),
    )
    sent, first = lax.optimization_barrier((sent, first))
    second = all_ways(*sent)
    start = nh + mh
    wide_2 = ((2, 0, nh), (3, 0, nh))
    across = ((0, nh, mh), (1, nh, mh))
    third = all_ways(
        *put(
            second,
            ((1, start, nh), (1, start + n, nh), *wide_2),
            ((0, start + nh, nh), (0, start + n + nh, nh), *wide_2),
            (*across, (2, nh, nh)),
            (*across, (3, 2 * nh, nh)),
        )
    )
    fourth = all_ways(
        *put(third, ((1, n, nh),), ((0, n + nh, nh),), ((2, 0, mh),), ((3, mh, mh),))
    )
    runs = [
        (0, 0, 0, 0, 3, span, 0),
        (0, 3 * span, 3, 0, 1, n, 0),
        (0, 3 * span + n, 1, 0, 1, n, 0),
    ]
    offset = 0
    for side in range(2):
        runs += [
            (1, offset, 0, 3, 1, nh, side * nh),
            (1, offset + nh, 0, 3, 1, mh, n + side * mh),
            (1, offset + start, 3, 1 + side, 1, n, 0),
            (1, offset + start + n, 1, 1 + side, 1, n, 0),
        ]
        offset += start + 2 * n
    for side in range(2):
        runs += [
            (1, offset, 2, 0, 1, nh, side * nh),
            (1, offset + nh, 3 - 2 * side, 0, 3, m, n),
        ]
        offset += nh + 3 * m
    offset = 0
    for side in range(2):
        runs += [
            (2, offset, 3, 3, 1, nh, side * nh),
            (2, offset + nh, 1, 3, 1, nh, side * nh),
            (2, offset + n, 2, 1 + side, 1, n, 0),
        ]
        offset += 2 * n
    runs += [
        (2, offset, 3, 3, 1, m, n),
        (2, offset + m, 2, 0, 1, m, n),
        (2, offset + 2 * m, 2, 1, 1, mh, n),
        (2, offset + 2 * m + mh, 1, 3, 1, m, n),
        (2, offset + 3 * m + mh, 2, 1, 1, mh, n + mh),
        (2, offset + 3 * m + 2 * mh, 2, 2, 1, m, n),
        (3, 0, 2, 3, 1, nh, 0),
        (3, nh, 2, 3, 1, nh, nh),
        (3, n, 2, 3, 1, mh, n),
        (3, n + mh, 2, 3, 1, mh, n + mh),
    ]
    parts = [project(part, *matrices) for part in (first, second, third, fourth)]
    later, first = lax.optimization_barrier((later, parts[0][0]))
    parts[0] = (first, parts[0][1])
    later = columns_held(later)
    return parts, tuple(runs), matrices, later


ORDER = (((2, 0, 4), (1, 3, 1), (3, 3, 1)), ((1, 0, 3), (3, 0, 3), (0, 3, 1), (0, 0, 3)))


def scatter_sum(early, later, matrix, hyena):
    span = early.shape[0] // 6
    columns = matrix.shape[1]
    wide, narrow = columns * 3 // 8, columns // 8
    places = {}
    for array, pieces in enumerate((ORDER[0], ORDER[1][:3], ORDER[1][3:])):
        row = 0
        for group, base, members in pieces:
            for member in range(base, base + members):
                places[group, member] = (array, row)
                row += span

    def product(part, other):
        both = beside(part, other)
        return narrowed(jnp.dot(both, matrix, preferred_element_type=jnp.float32))

    def term(group, member, side, *more):
        array, row = places[group, member]
        return (wide, [(array, row, side * wide), *more])

    def low(group, member, side, *more):
        array, row = places[group, member]
        return (narrow, [(array, row, 2 * wide + side * narrow), *more])

    def put(arrays, *plans):
        return assemble(arrays, *[columns_of(span, *plan) for plan in plans])

    early = product(early, swapped(early))
    other = swapped(later)
    first = all_ways(
        *put([early], [term(2, 3, 0)], [term(2, 3, 1)], [low(2, 3, 0)], [low(2, 3, 1)])
    )
    later, hyena, first = lax.optimization_barrier((later, hyena, first))
    x, y, below, above = range(1, 5)
    second = all_ways(
        *put(
            [early, *first],
            [term(2, 1, 0), term(2, 1, 1, (y, 0, 0)), term(1, 3, 0), term(3, 3, 0)],
            [term(2, 2, 0, (x, 0, 0)), term(2, 2, 1), term(1, 3, 1), term(3, 3, 1)],
            [low(1, 3, 0, (below, 0, 0)), low(1, 3, 1), *[low(2, k, 0) for k in range(3)]],
            [low(3, 3, 0), low(3, 3, 1, (above, 0, 0)), *[low(2, k, 1) for k in range(3)]],
        )
    )
    own = product(later[7 * span :], other[7 * span :])
    later = product(later[: 7 * span], other[: 7 * span])
    later, second = lax.optimization_barrier((later, second))
    hyena_out = lax.all_to_all(hyena, "ctx", split_axis=0, concat_axis=1, tiled=True).T
    x, y, below, above = range(2, 6)

    def low_3(side):
        return low(0, 3, side, (below, 0, side * narrow), (above, 0, side * narrow))

    def sum_2(side):
        return term(2, 0, side, (x, 0, side * wide), (y, 0, side * wide))

    for_above, for_below = [], []
    for k in range(3):
        start = (2 + k) * narrow
        for_above += [low(1, k, 0, (below, 0, start)), low(1, k, 1)]
        for_below += [low(3, k, 0), low(3, k, 1, (above, 0, start))]
    third = all_ways(
        *put(
            [early, later, *second],
            [
                term(1, 1, 0),
                term(1, 1, 1, (y, 0, 2 * wide)),
                term(3, 1, 0),
                term(3, 1, 1, (y, 0, 3 * wide)),
                term(0, 3, 0),
                low_3(0),
            ],
            [
                term(1, 2, 0, (x, 0, 2 * wide)),
                term(1, 2, 1),
                term(3, 2, 0, (x, 0, 3 * wide)),
                term(3, 2, 1),
                term(0, 3, 1),
                low_3(1),
            ],
            [sum_2(0), *for_above],
            [sum_2(1), *for_below],
        )
    )

    x, y, below, above = range(3, 7)

    def low_own(k, side, *more):
        start = wide + (2 * k + side) * narrow
        return low(0, k, side, (below, 0, start), (above, 0, start), *more)

    def own_sum(group, side, *more):
        start = (group - 1 + side) * wide
        return term(group, 0, side, (x, 0, start), (y, 0, start), *more)

    *sent, base = put(
            [early, later, own, *third],
            [
                term(0, 1, 0),
                term(0, 1, 1, (y, 0, 4 * wide)),
                low_own(1, 0),
                low_own(1, 1, (y, 0, 5 * wide)),
            ],
            [
                term(0, 2, 0, (x, 0, 4 * wide)),
                term(0, 2, 1),
                low_own(2, 0, (x, 0, 5 * wide)),
                low_own(2, 1),
            ],
            [own_sum(1, 0, (below, 0, 0)), own_sum(1, 1)],
            [own_sum(3, 0), own_sum(3, 1, (above, 0, 0))],
            [term(0, 0, 0), term(0, 0, 1), low_own(0, 0), low_own(0, 1)],
        )
    (grad_input,) = put(
        [base, *all_ways(*sent)],
        [
            (2 * wide, [(way, 0, 0) for way in range(5)]),
            (2 * narrow, [(way, 0, 2 * wide) for way in range(3)]),
        ],
    )
    return grad_input, hyena_out


def gather_tokens(tokens, weights, residues, decay_rates, cotangent):
    me = lax.axis_index("ctx").astype(jnp.int32).reshape(1)
    channels, span = weights.shape[1], tokens.shape[0]
    rows = weights[0].swapaxes(0, 1).reshape(3 * channels, weights.shape[3])
    tokens_half = halves((tokens,), (0, span, True), (0, span * 3 // 4, True))
    kept, given = halves((rows,), (0, 3 * channels, True), (0, 3 * channels, False))
    taken = swapped(given)
    parts, runs, (kept, taken), cot_cols = gather_groups(*tokens_half, (kept, taken), cotangent)
    own, other = zip(*parts)
    hyena, grads, (early, later) = scan_all(
        me, cot_cols, residues[0].T, decay_rates[0].T, runs, ORDER, own, other
    )
    grad_input, hyena_out = scatter_sum(early, later, stack(kept, taken), hyena)
    return (hyena_out, grad_input, grads.T[None])


def shards(tokens, weights, residues, decay_rates, cotangent):
    ctx, tp = lax.axis_size("ctx"), lax.axis_size("tp")
    if ctx == 4 * PLANE and tp == 2 and weights.size * tp > 2 * tokens.size:
        return gather_tokens(tokens, weights, residues, decay_rates, cotangent)
    return gather_weights(tokens, weights, residues, decay_rates, cotangent)


def solution(mesh):
    return jax.shard_map(
        shards,
        mesh=mesh,
        in_specs=(
            P("ctx", None),
            P("tp", "ctx", None, None),
            P("tp", "ctx", None),
            P("tp", "ctx", None),
            P("tp", "ctx"),
        ),
        out_specs=(P("tp", "ctx"), P("ctx", "tp"), P("tp", "ctx", None)),
        check_vma=False,
    )
```

```python
import functools
import math
import operator

import jax
import jax.numpy as jnp
from jax import lax
from jax.experimental import pallas as pl
from jax.experimental.pallas import tpu as pltpu
from jax.sharding import PartitionSpec as P


def precise(form, left, right):
    return jnp.einsum(
        form, left, right, precision=lax.Precision.HIGHEST, preferred_element_type=jnp.float32
    )


def tripled(form, left, right):
    return jnp.einsum(
        form, left, right, precision=lax.Precision.HIGH, preferred_element_type=jnp.float32
    )


def angle_table(row_count, col_count, period):
    product = (
        jnp.arange(row_count, dtype=jnp.int32)[:, None]
        * jnp.arange(col_count, dtype=jnp.int32)[None, :]
        % period
    )
    angles = product.astype(jnp.float32) * (2.0 * math.pi / period)
    return (jnp.cos(angles), jnp.sin(angles))


def make_tables(length):
    padded = 2 * length
    outer = math.gcd(padded, 1 << (padded.bit_length() - 1) // 2)
    inner = padded // outer
    cos_outer, sin_outer = angle_table(outer, outer, outer)
    cos_inner, sin_inner = angle_table(inner, inner, inner)
    twist_cos, twist_sin = angle_table(outer, inner, padded)
    return (outer, inner, cos_outer, sin_outer, cos_inner, sin_inner, twist_cos, twist_sin)


def spectrum(signal, tables, product):
    outer, inner, cos_outer, sin_outer, cos_inner, sin_inner, twist_cos, twist_sin = tables
    half_rows = outer // 2
    blocks = signal.reshape(signal.shape[0], half_rows, inner)
    first_re = product("kp,bpq->bkq", cos_outer[:, :half_rows], blocks)
    first_im = -product("kp,bpq->bkq", sin_outer[:, :half_rows], blocks)
    turned_re = first_re * twist_cos + first_im * twist_sin
    turned_im = first_im * twist_cos - first_re * twist_sin
    spec_re = product("bkq,qj->bkj", turned_re, cos_inner) + product(
        "bkq,qj->bkj", turned_im, sin_inner
    )
    spec_im = product("bkq,qj->bkj", turned_im, cos_inner) - product(
        "bkq,qj->bkj", turned_re, sin_inner
    )
    return (spec_re, spec_im)


def signal_of(spec_re, spec_im, tables):
    outer, inner, cos_outer, sin_outer, cos_inner, sin_inner, twist_cos, twist_sin = tables
    half_rows = outer // 2
    back_re = tripled("bkj,jq->bkq", spec_re, cos_inner) - tripled(
        "bkj,jq->bkq", spec_im, sin_inner
    )
    back_im = tripled("bkj,jq->bkq", spec_im, cos_inner) + tripled(
        "bkj,jq->bkq", spec_re, sin_inner
    )
    turned_re = back_re * twist_cos - back_im * twist_sin
    turned_im = back_im * twist_cos + back_re * twist_sin
    values = tripled("pk,bkq->bpq", cos_outer[:half_rows, :], turned_re) - tripled(
        "pk,bkq->bpq", sin_outer[:half_rows, :], turned_im
    )
    return values.reshape(values.shape[0], half_rows * inner) * (1.0 / (outer * inner))


def spec_product(left_re, left_im, right_re, right_im):
    return (left_re * right_re - left_im * right_im, left_re * right_im + left_im * right_re)


def conj_product(left_re, left_im, right_re, right_im):
    return (left_re * right_re + left_im * right_im, left_re * right_im - left_im * right_re)


def filter_basis(residue_loc, rate_loc, length):
    position = jnp.arange(length, dtype=jnp.float32)
    basis_all = jnp.sqrt(2.0 * rate_loc)[:, :, None] * jnp.exp(
        -rate_loc[:, :, None] * position[None, None, :]
    )
    return (basis_all, precise("cm,cmt->ct", residue_loc, basis_all))


def forward_cols(gated_cols, taps_re, taps_im, tables):
    gated_re, gated_im = spectrum(gated_cols.astype(jnp.float32), tables, tripled)
    conv_re, conv_im = spec_product(gated_re, gated_im, taps_re, taps_im)
    conv_cols = signal_of(conv_re, conv_im, tables).astype(jnp.bfloat16)
    return (conv_cols, gated_re, gated_im)


def backward_cols(slope_cols, gated_re, gated_im, taps_re, taps_im, basis_all, tables, length):
    slope_re, slope_im = spectrum(slope_cols.astype(jnp.float32), tables, tripled)
    grad_re, grad_im = conj_product(taps_re, taps_im, slope_re, slope_im)
    back_cols = signal_of(grad_re, grad_im, tables).astype(jnp.bfloat16)
    lag_re, lag_im = conj_product(gated_re, gated_im, slope_re, slope_im)
    taps_grad = signal_of(lag_re, lag_im, tables)
    grad_residue = precise("ct,cmt->cm", taps_grad, basis_all) * (1.0 / math.sqrt(length))
    return (back_cols, grad_residue)


def gather_weights(tokens, weights, residues, decay_rates, cotangent):
    gathered = lax.all_gather(weights, "ctx", axis=1, tiled=True)
    projected = jnp.einsum("xcpd,td->xcpt", gathered, tokens, preferred_element_type=jnp.float32)
    features = projected[0].astype(jnp.bfloat16)
    query_f = features[:, 0].astype(jnp.float32)
    key_part = features[:, 1].astype(jnp.float32)
    value_part = features[:, 2].astype(jnp.float32)
    gated_in = (key_part * value_part).astype(jnp.bfloat16)
    slope_in = (cotangent.astype(jnp.float32) * query_f).astype(jnp.bfloat16)
    length = tokens.shape[0] * lax.axis_size("ctx")
    tables = make_tables(length)
    basis_all, taps_full = filter_basis(residues[0], decay_rates[0], length)
    taps_re, taps_im = spectrum(taps_full, tables, precise)
    gated_cols = lax.all_to_all(gated_in, "ctx", split_axis=0, concat_axis=1, tiled=True)
    conv_cols, gated_re, gated_im = forward_cols(gated_cols, taps_re, taps_im, tables)
    conv_rows = lax.all_to_all(conv_cols, "ctx", split_axis=1, concat_axis=0, tiled=True)
    slope_cols = lax.all_to_all(slope_in, "ctx", split_axis=0, concat_axis=1, tiled=True)
    back_cols, grad_residue = backward_cols(
        slope_cols, gated_re, gated_im, taps_re, taps_im, basis_all, tables, length
    )
    back_rows = lax.all_to_all(back_cols, "ctx", split_axis=1, concat_axis=0, tiled=True)
    conv_f = conv_rows.astype(jnp.float32)
    back_f = back_rows.astype(jnp.float32)
    hyena_out = (query_f * conv_f).astype(jnp.bfloat16)
    grad_query = (cotangent.astype(jnp.float32) * conv_f).astype(jnp.bfloat16)
    grad_key = (back_f * value_part).astype(jnp.bfloat16)
    grad_value = (back_f * key_part).astype(jnp.bfloat16)
    grad_proj = jnp.stack([grad_query, grad_key, grad_value], axis=1)
    partial_value = jnp.einsum(
        "cpt,cpd->td", grad_proj, gathered[0], preferred_element_type=jnp.float32
    )
    grad_input = lax.psum_scatter(
        partial_value.astype(jnp.bfloat16), "tp", scatter_dimension=1, tiled=True
    )
    return (hyena_out, grad_input, grad_residue[None])


GROUP = 4
PLANE = 4
VMEM = 56 * 2**20


def rounded(value):
    return value.astype(jnp.bfloat16).astype(jnp.float32)


def added_up(parts):
    return functools.reduce(operator.add, parts)


def earlier_sum(finals, rate, span, back):
    count = finals.shape[0]
    row = lax.broadcasted_iota(jnp.int32, finals.shape, 0)

    def shifted(value, by):
        if back:
            moved = pltpu.roll(value, count - by, 0)
            return jnp.where(row < count - by, moved, 0.0)
        moved = pltpu.roll(value, by, 0)
        return jnp.where(row >= by, moved, 0.0)

    total = shifted(finals, 1)
    by = 1
    while by < count:
        total = total + jnp.exp(rate * (-1.0 * span * by)) * shifted(total, by)
        by *= 2
    return total


def scan_kernel(
    groups,
    runs,
    order,
    me_ref,
    residue_ref,
    rate_ref,
    *refs,
):
    inputs = 1 + max(run[0] for run in runs)
    arrays, refs = refs[: 2 * inputs + 1], refs[2 * inputs + 1 :]
    hyena_ref, grad_ref = refs[:2]
    proj_refs, refs = refs[2 : 2 + len(order)], refs[2 + len(order) :]
    gated_s, slope_s, conv_s, back_s, feats_s = refs
    cot_ref, own, other = arrays[0], arrays[1 : 1 + inputs], arrays[1 + inputs :]
    length, width = cot_ref.shape
    chunks = PLANE * groups
    span = length // chunks
    modes = rate_ref.shape[0]
    me = me_ref[0]

    def place(group, member):
        return lax.rem(me // PLANE + group, groups) * PLANE + (member ^ lax.rem(me, PLANE))

    def aligned(start, size):
        return pl.ds(pl.multiple_of(start, size), size)

    for source, offset, group, base, members, count, first in runs:

        def before(step, _, source=source, offset=offset, group=group, base=base, count=count, first=first):
            member = base + step
            index = place(group, member)
            rows = pl.ds(pl.multiple_of(offset + step * count, 16), count)
            feats = own[source][rows, :] + other[source][rows, :].astype(jnp.float32)
            feats = rounded(feats)
            slot = (group * PLANE + member) * span + first
            feats_s[pl.ds(pl.multiple_of(slot, 16), count), :] = feats
            cot = cot_ref[pl.ds(pl.multiple_of(index * span + first, 16), count), :]
            query, key = feats[:, :width], feats[:, width : 2 * width]
            into = pl.ds(first * chunks + index, count, stride=chunks)
            gated_s[into, :] = rounded(key * feats[:, 2 * width :])
            slope_s[into, :] = rounded(cot.astype(jnp.float32) * query)
            return 0

        lax.fori_loop(0, members, before, 0)

    def at(step):
        return aligned(step * chunks, chunks)

    zero = jnp.zeros((chunks, width), jnp.float32)
    scale = 1.0 / math.sqrt(length)
    for first in range(0, modes, GROUP):
        count = min(GROUP, modes - first)
        rates = [
            jnp.broadcast_to(rate_ref[m : m + 1, :], (chunks, width))
            for m in range(first, first + count)
        ]
        decays = [jnp.exp(-rate) for rate in rates]
        norms = [jnp.sqrt(2.0 * rate) for rate in rates]
        gains = [
            residue_ref[first + n : first + n + 1, :] * norms[n] for n in range(count)
        ]

        def sums(step, state):
            ahead, behind = state
            gated = gated_s[at(step), :]
            slope = slope_s[at(span - 1 - step), :]
            return (
                tuple(decays[n] * ahead[n] + gated for n in range(count)),
                tuple(decays[n] * behind[n] + slope for n in range(count)),
            )

        ahead, behind = lax.fori_loop(0, span, sums, ((zero,) * count, (zero,) * count), unroll=16)
        ahead = tuple(earlier_sum(ahead[n], rates[n], span, False) for n in range(count))
        behind = tuple(earlier_sum(behind[n], rates[n], span, True) for n in range(count))

        def outs(step, state):
            ahead, behind, grads = state
            other = span - 1 - step
            gated = gated_s[at(step), :]
            slope = slope_s[at(step), :]
            slope_back = slope_s[at(other), :]
            ahead = tuple(decays[n] * ahead[n] + gated for n in range(count))
            behind = tuple(decays[n] * behind[n] + slope_back for n in range(count))
            grads = tuple(grads[n] + slope * ahead[n] for n in range(count))
            conv = added_up(gains[n] * ahead[n] for n in range(count))
            back = added_up(gains[n] * behind[n] for n in range(count))
            if first:
                conv = conv + conv_s[at(step), :]
                back = back + back_s[at(other), :]
            conv_s[at(step), :] = conv
            back_s[at(other), :] = back
            return ahead, behind, grads

        _, _, grads = lax.fori_loop(0, span, outs, (ahead, behind, (zero,) * count), unroll=8)
        for n in range(count):
            total = jnp.sum(grads[n] * norms[n], axis=0, keepdims=True) * scale
            grad_ref[first + n : first + n + 1, :] = total

    for proj_ref, pieces in zip(proj_refs, order):
        start = 0
        for group, base, members in pieces:

            def after(step, _, proj_ref=proj_ref, start=start, group=group, base=base):
                member = base + step
                index = place(group, member)
                feats = feats_s[aligned((group * PLANE + member) * span, span), :]
                query, key = feats[:, :width], feats[:, width : 2 * width]
                cot = cot_ref[aligned(index * span, span), :].astype(jnp.float32)
                conv = rounded(conv_s[pl.ds(index, span, stride=chunks), :])
                back = rounded(back_s[pl.ds(index, span, stride=chunks), :])
                hyena_ref[aligned(index * span, span), :] = narrowed(query * conv)
                rows = aligned(start + step * span, span)
                proj_ref[rows, :width] = narrowed(cot * conv)
                proj_ref[rows, width : 2 * width] = narrowed(back * feats[:, 2 * width :])
                proj_ref[rows, 2 * width :] = narrowed(back * key)
                return 0

            lax.fori_loop(0, members, after, 0)
            start += members * span


def scan_all(me, cot_cols, residue_rows, rate_rows, runs, order, own, other):
    length, width = cot_cols.shape
    span = length // (PLANE * PLANE)
    vmem = pl.BlockSpec(memory_space=pltpu.VMEM)
    arrays = (cot_cols, *own, *other)
    outs = pl.pallas_call(
        functools.partial(scan_kernel, PLANE, runs, order),
        out_shape=(
            jax.ShapeDtypeStruct((length, width), jnp.bfloat16),
            jax.ShapeDtypeStruct(rate_rows.shape, jnp.float32),
        )
        + tuple(
            jax.ShapeDtypeStruct((span * sum(piece[2] for piece in pieces), 3 * width), jnp.bfloat16)
            for pieces in order
        ),
        in_specs=[pl.BlockSpec(memory_space=pltpu.SMEM)] + [vmem] * (2 + len(arrays)),
        out_specs=(vmem,) * (2 + len(order)),
        scratch_shapes=[pltpu.VMEM((length, width), jnp.float32)] * 4
        + [pltpu.VMEM((length, 3 * width), jnp.float32)],
        compiler_params=pltpu.CompilerParams(vmem_limit_bytes=40 * 2**20),
        name="modal_scan",
    )(me, residue_rows, rate_rows, *arrays)
    return outs[0], outs[1], outs[2:]


def swapped(value):
    return lax.ppermute(value, "tp", [(0, 1), (1, 0)])


def over_x(value):
    return lax.ppermute(value, "ctx", [(i, i ^ 1) for i in range(lax.axis_size("ctx"))])


def over_y(value):
    return lax.ppermute(value, "ctx", [(i, i ^ 2) for i in range(lax.axis_size("ctx"))])


def up(value):
    count = lax.axis_size("ctx")
    return lax.ppermute(value, "ctx", [(i, (i + PLANE) % count) for i in range(count)])


def down(value):
    count = lax.axis_size("ctx")
    return lax.ppermute(value, "ctx", [((i + PLANE) % count, i) for i in range(count)])


def stack(*parts):
    return jnp.concatenate(parts, axis=0)


def beside(*parts):
    return jnp.concatenate(parts, axis=1)


def narrowed(value):
    return value.astype(jnp.bfloat16)


def widened(value):
    return value.astype(jnp.float32)


def halves_kernel(plan, core_ref, *refs):
    arrays, outs, arrived = refs[: -1 - len(plan)], refs[-1 - len(plan) : -1], refs[-1]
    copies = []
    for k, (out, (index, count, mine)) in enumerate(zip(outs, plan)):
        half = out.shape[1]
        side = core_ref[0] if mine else 1 - core_ref[0]
        columns = pl.ds(pl.multiple_of(side * half, half), half)
        part = arrays[index].at[pl.ds(0, count), columns]
        copies.append(pltpu.make_async_copy(part, out, arrived.at[k]))
    for copy in copies:
        copy.start()
    for copy in copies:
        copy.wait()


def halves(arrays, *plan):
    core = lax.axis_index("tp").astype(jnp.int32).reshape(1)
    shapes = [(count, arrays[index].shape[1] // 2) for index, count, _ in plan]
    moved = sum(4 * rows * columns for rows, columns in shapes)
    return pl.pallas_call(
        functools.partial(halves_kernel, plan),
        out_shape=tuple(jax.ShapeDtypeStruct(shape, jnp.bfloat16) for shape in shapes),
        in_specs=[pl.BlockSpec(memory_space=pltpu.SMEM)]
        + [pl.BlockSpec(memory_space=pl.ANY)] * len(arrays),
        out_specs=(pl.BlockSpec(memory_space=pltpu.VMEM),) * len(plan),
        scratch_shapes=[pltpu.SemaphoreType.DMA((len(plan),))],
        compiler_params=pltpu.CompilerParams(vmem_limit_bytes=VMEM),
        cost_estimate=pl.CostEstimate(flops=0, bytes_accessed=moved, transcendentals=0),
        name="halves",
    )(core, *arrays)


def assemble_kernel(inputs, plans, *refs):
    arrays, outs = refs[:inputs], refs[inputs:]
    for out, plan in zip(outs, plans):
        for row, col, height, width, sources in plan:
            parts = [
                arrays[index][from_row : from_row + height, from_col : from_col + width]
                for index, from_row, from_col in sources
            ]
            if len(parts) > 1:
                parts = [narrowed(added_up(widened(part) for part in parts))]
            out[row : row + height, col : col + width] = parts[0]


def assemble(arrays, *plans):
    used = sorted({source[0] for plan in plans for piece in plan for source in piece[4]})
    arrays = [arrays[index] for index in used]
    plans = [
        [(*piece[:4], [(used.index(source[0]), *source[1:]) for source in piece[4]]) for piece in plan]
        for plan in plans
    ]
    shapes = [
        (max(p[0] + p[2] for p in plan), max(p[1] + p[3] for p in plan)) for plan in plans
    ]
    moved = sum(2 * rows * cols for rows, cols in shapes)
    vmem = pl.BlockSpec(memory_space=pltpu.VMEM)
    return pl.pallas_call(
        functools.partial(assemble_kernel, len(arrays), plans),
        out_shape=tuple(jax.ShapeDtypeStruct(shape, jnp.bfloat16) for shape in shapes),
        in_specs=[vmem] * len(arrays),
        out_specs=(vmem,) * len(plans),
        compiler_params=pltpu.CompilerParams(vmem_limit_bytes=32 * 2**20),
        cost_estimate=pl.CostEstimate(flops=moved, bytes_accessed=4 * moved, transcendentals=0),
        name="assemble",
    )(*arrays)


def rows_of(*parts):
    plan, start = [], 0
    for index, first, count in parts:
        plan.append((start, count, [(index, first, 0)]))
        start += count
    return plan


def full_width(columns, plan):
    return [(row, 0, count, columns, sources) for row, count, sources in plan]


def columns_of(height, *parts):
    plan, start = [], 0
    for width, sources in parts:
        plan.append((0, start, height, width, sources))
        start += width
    return plan


def all_ways(for_x, for_y, for_above, for_below):
    from_below, from_above = up(for_above), down(for_below)
    got_x, got_y = over_x(for_x), over_y(for_y)
    return lax.optimization_barrier((got_x, got_y, from_below, from_above))


def project(parts, kept, taken):
    rows = stack(*parts)
    own, given = (
        jnp.einsum("td,rd->tr", rows, matrix, preferred_element_type=jnp.float32)
        for matrix in (kept, taken)
    )
    return own, swapped(narrowed(given))


def columns_held(rows):
    return lax.all_to_all(rows.T, "ctx", split_axis=1, concat_axis=0, tiled=True)


def gather_groups(tokens, wide, matrices, later):
    span = tokens.shape[0]
    n, m = span * 3 // 4, span // 4
    nh, mh = n // 2, m // 2
    columns = tokens.shape[1]

    def put(arrays, *plans):
        return assemble(arrays, *[full_width(columns, rows_of(*plan)) for plan in plans])

    own_x, own_y, wide_3, wide_1 = all_ways(tokens, tokens, wide, wide)
    first = (tokens, own_x, own_y, wide_3, wide_1)
    members = ((0, n, m), (1, n, m), (2, n, m))
    sent = put(
        first,
        ((2, 0, nh), (2, n, mh), (3, 0, n), (4, 0, n)),
        ((1, nh, nh), (1, n + mh, mh), (3, 0, n), (4, 0, n)),
        ((3, 0, nh), *members),
        ((4, nh, nh), *members),
    )
    sent, first = lax.optimization_barrier((sent, first))
    second = all_ways(*sent)
    start = nh + mh
    wide_2 = ((2, 0, nh), (3, 0, nh))
    across = ((0, nh, mh), (1, nh, mh))
    third = all_ways(
        *put(
            second,
            ((1, start, nh), (1, start + n, nh), *wide_2),
            ((0, start + nh, nh), (0, start + n + nh, nh), *wide_2),
            (*across, (2, nh, nh)),
            (*across, (3, 2 * nh, nh)),
        )
    )
    fourth = all_ways(
        *put(third, ((1, n, nh),), ((0, n + nh, nh),), ((2, 0, mh),), ((3, mh, mh),))
    )
    runs = [
        (0, 0, 0, 0, 3, span, 0),
        (0, 3 * span, 3, 0, 1, n, 0),
        (0, 3 * span + n, 1, 0, 1, n, 0),
    ]
    offset = 0
    for side in range(2):
        runs += [
            (1, offset, 0, 3, 1, nh, side * nh),
            (1, offset + nh, 0, 3, 1, mh, n + side * mh),
            (1, offset + start, 3, 1 + side, 1, n, 0),
            (1, offset + start + n, 1, 1 + side, 1, n, 0),
        ]
        offset += start + 2 * n
    for side in range(2):
        runs += [
            (1, offset, 2, 0, 1, nh, side * nh),
            (1, offset + nh, 3 - 2 * side, 0, 3, m, n),
        ]
        offset += nh + 3 * m
    offset = 0
    for side in range(2):
        runs += [
            (2, offset, 3, 3, 1, nh, side * nh),
            (2, offset + nh, 1, 3, 1, nh, side * nh),
            (2, offset + n, 2, 1 + side, 1, n, 0),
        ]
        offset += 2 * n
    runs += [
        (2, offset, 3, 3, 1, m, n),
        (2, offset + m, 2, 0, 1, m, n),
        (2, offset + 2 * m, 2, 1, 1, mh, n),
        (2, offset + 2 * m + mh, 1, 3, 1, m, n),
        (2, offset + 3 * m + mh, 2, 1, 1, mh, n + mh),
        (2, offset + 3 * m + 2 * mh, 2, 2, 1, m, n),
        (3, 0, 2, 3, 1, nh, 0),
        (3, nh, 2, 3, 1, nh, nh),
        (3, n, 2, 3, 1, mh, n),
        (3, n + mh, 2, 3, 1, mh, n + mh),
    ]
    parts = [project(part, *matrices) for part in (first, second, third, fourth)]
    later, first = lax.optimization_barrier((later, parts[0][0]))
    parts[0] = (first, parts[0][1])
    later = columns_held(later)
    return parts, tuple(runs), matrices, later


ORDER = (
    ((2, 3, 1),),
    ((2, 0, 3), (1, 3, 1), (3, 3, 1)),
    ((1, 0, 3), (3, 0, 3), (0, 3, 1), (0, 0, 3)),
)


def scatter_sum(first, early, later, matrix, hyena):
    span = first.shape[0]
    columns = matrix.shape[1]
    wide, narrow = columns * 3 // 8, columns // 8
    places = {}
    for array, pieces in enumerate((*ORDER[:2], ORDER[2][:3], ORDER[2][3:])):
        row = 0
        for group, base, members in pieces:
            for member in range(base, base + members):
                places[group, member] = (array, row)
                row += span

    def product(part, other):
        both = beside(part, other)
        return narrowed(jnp.dot(both, matrix, preferred_element_type=jnp.float32))

    def term(group, member, side, *more):
        array, row = places[group, member]
        return (wide, [(array, row, side * wide), *more])

    def low(group, member, side, *more):
        array, row = places[group, member]
        return (narrow, [(array, row, 2 * wide + side * narrow), *more])

    def put(arrays, *plans):
        return assemble(arrays, *[columns_of(span, *plan) for plan in plans])

    first = product(first, swapped(first))
    other_early = swapped(early)
    sent = put([first], [term(2, 3, 0)], [term(2, 3, 1)], [low(2, 3, 0)], [low(2, 3, 1)])
    early, sent = lax.optimization_barrier((early, sent))
    first = all_ways(*sent)
    early = product(early, other_early)
    later, hyena, first = lax.optimization_barrier((later, hyena, first))
    other = swapped(later)
    x, y, below, above = range(2, 6)
    second = all_ways(
        *put(
            [early, early, *first],
            [term(2, 1, 0), term(2, 1, 1, (y, 0, 0)), term(1, 3, 0), term(3, 3, 0)],
            [term(2, 2, 0, (x, 0, 0)), term(2, 2, 1), term(1, 3, 1), term(3, 3, 1)],
            [low(1, 3, 0, (below, 0, 0)), low(1, 3, 1), *[low(2, k, 0) for k in range(3)]],
            [low(3, 3, 0), low(3, 3, 1, (above, 0, 0)), *[low(2, k, 1) for k in range(3)]],
        )
    )
    own = product(later[7 * span :], other[7 * span :])
    later = product(later[: 7 * span], other[: 7 * span])
    later, second = lax.optimization_barrier((later, second))
    hyena_out = lax.all_to_all(hyena, "ctx", split_axis=0, concat_axis=1, tiled=True).T
    x, y, below, above = range(3, 7)

    def low_3(side):
        return low(0, 3, side, (below, 0, side * narrow), (above, 0, side * narrow))

    def sum_2(side):
        return term(2, 0, side, (x, 0, side * wide), (y, 0, side * wide))

    for_above, for_below = [], []
    for k in range(3):
        start = (2 + k) * narrow
        for_above += [low(1, k, 0, (below, 0, start)), low(1, k, 1)]
        for_below += [low(3, k, 0), low(3, k, 1, (above, 0, start))]
    third = all_ways(
        *put(
            [early, early, later, *second],
            [
                term(1, 1, 0),
                term(1, 1, 1, (y, 0, 2 * wide)),
                term(3, 1, 0),
                term(3, 1, 1, (y, 0, 3 * wide)),
                term(0, 3, 0),
                low_3(0),
            ],
            [
                term(1, 2, 0, (x, 0, 2 * wide)),
                term(1, 2, 1),
                term(3, 2, 0, (x, 0, 3 * wide)),
                term(3, 2, 1),
                term(0, 3, 1),
                low_3(1),
            ],
            [sum_2(0), *for_above],
            [sum_2(1), *for_below],
        )
    )

    x, y, below, above = range(4, 8)

    def low_own(k, side, *more):
        start = wide + (2 * k + side) * narrow
        return low(0, k, side, (below, 0, start), (above, 0, start), *more)

    def own_sum(group, side, *more):
        start = (group - 1 + side) * wide
        return term(group, 0, side, (x, 0, start), (y, 0, start), *more)

    sent = put(
        [early, early, later, own, *third],
            [
                term(0, 1, 0),
                term(0, 1, 1, (y, 0, 4 * wide)),
                low_own(1, 0),
                low_own(1, 1, (y, 0, 5 * wide)),
            ],
            [
                term(0, 2, 0, (x, 0, 4 * wide)),
                term(0, 2, 1),
                low_own(2, 0, (x, 0, 5 * wide)),
                low_own(2, 1),
            ],
            [own_sum(1, 0, (below, 0, 0)), own_sum(1, 1)],
            [own_sum(3, 0), own_sum(3, 1, (above, 0, 0))],
    )
    (base,) = put(
        [early, early, later, own, *third],
        [term(0, 0, 0), term(0, 0, 1), low_own(0, 0), low_own(0, 1)],
    )
    (grad_input,) = put(
        [base, *all_ways(*sent)],
        [
            (2 * wide, [(way, 0, 0) for way in range(5)]),
            (2 * narrow, [(way, 0, 2 * wide) for way in range(3)]),
        ],
    )
    return grad_input, hyena_out


def gather_tokens(tokens, weights, residues, decay_rates, cotangent):
    me = lax.axis_index("ctx").astype(jnp.int32).reshape(1)
    channels, span = weights.shape[1], tokens.shape[0]
    rows = weights[0].swapaxes(0, 1).reshape(3 * channels, weights.shape[3])
    tokens_half = halves((tokens,), (0, span, True), (0, span * 3 // 4, True))
    kept, given = halves((rows,), (0, 3 * channels, True), (0, 3 * channels, False))
    taken = swapped(given)
    parts, runs, (kept, taken), cot_cols = gather_groups(*tokens_half, (kept, taken), cotangent)
    own, other = zip(*parts)
    hyena, grads, proj = scan_all(
        me, cot_cols, residues[0].T, decay_rates[0].T, runs, ORDER, own, other
    )
    grad_input, hyena_out = scatter_sum(*proj, stack(kept, taken), hyena)
    return (hyena_out, grad_input, grads.T[None])


def shards(tokens, weights, residues, decay_rates, cotangent):
    ctx, tp = lax.axis_size("ctx"), lax.axis_size("tp")
    if ctx == 4 * PLANE and tp == 2 and weights.size * tp > 2 * tokens.size:
        return gather_tokens(tokens, weights, residues, decay_rates, cotangent)
    return gather_weights(tokens, weights, residues, decay_rates, cotangent)


def solution(mesh):
    return jax.shard_map(
        shards,
        mesh=mesh,
        in_specs=(
            P("ctx", None),
            P("tp", "ctx", None, None),
            P("tp", "ctx", None),
            P("tp", "ctx", None),
            P("tp", "ctx"),
        ),
        out_specs=(P("tp", "ctx"), P("ctx", "tp"), P("tp", "ctx", None)),
        check_vma=False,
    )
```

```python
import functools
import math
import operator

import jax
import jax.numpy as jnp
from jax import lax
from jax.experimental import pallas as pl
from jax.experimental.pallas import tpu as pltpu
from jax.sharding import PartitionSpec as P


def precise(form, left, right):
    return jnp.einsum(
        form, left, right, precision=lax.Precision.HIGHEST, preferred_element_type=jnp.float32
    )


def tripled(form, left, right):
    return jnp.einsum(
        form, left, right, precision=lax.Precision.HIGH, preferred_element_type=jnp.float32
    )


def angle_table(row_count, col_count, period):
    product = (
        jnp.arange(row_count, dtype=jnp.int32)[:, None]
        * jnp.arange(col_count, dtype=jnp.int32)[None, :]
        % period
    )
    angles = product.astype(jnp.float32) * (2.0 * math.pi / period)
    return (jnp.cos(angles), jnp.sin(angles))


def make_tables(length):
    padded = 2 * length
    outer = math.gcd(padded, 1 << (padded.bit_length() - 1) // 2)
    inner = padded // outer
    cos_outer, sin_outer = angle_table(outer, outer, outer)
    cos_inner, sin_inner = angle_table(inner, inner, inner)
    twist_cos, twist_sin = angle_table(outer, inner, padded)
    return (outer, inner, cos_outer, sin_outer, cos_inner, sin_inner, twist_cos, twist_sin)


def spectrum(signal, tables, product):
    outer, inner, cos_outer, sin_outer, cos_inner, sin_inner, twist_cos, twist_sin = tables
    half_rows = outer // 2
    blocks = signal.reshape(signal.shape[0], half_rows, inner)
    first_re = product("kp,bpq->bkq", cos_outer[:, :half_rows], blocks)
    first_im = -product("kp,bpq->bkq", sin_outer[:, :half_rows], blocks)
    turned_re = first_re * twist_cos + first_im * twist_sin
    turned_im = first_im * twist_cos - first_re * twist_sin
    spec_re = product("bkq,qj->bkj", turned_re, cos_inner) + product(
        "bkq,qj->bkj", turned_im, sin_inner
    )
    spec_im = product("bkq,qj->bkj", turned_im, cos_inner) - product(
        "bkq,qj->bkj", turned_re, sin_inner
    )
    return (spec_re, spec_im)


def signal_of(spec_re, spec_im, tables):
    outer, inner, cos_outer, sin_outer, cos_inner, sin_inner, twist_cos, twist_sin = tables
    half_rows = outer // 2
    back_re = tripled("bkj,jq->bkq", spec_re, cos_inner) - tripled(
        "bkj,jq->bkq", spec_im, sin_inner
    )
    back_im = tripled("bkj,jq->bkq", spec_im, cos_inner) + tripled(
        "bkj,jq->bkq", spec_re, sin_inner
    )
    turned_re = back_re * twist_cos - back_im * twist_sin
    turned_im = back_im * twist_cos + back_re * twist_sin
    values = tripled("pk,bkq->bpq", cos_outer[:half_rows, :], turned_re) - tripled(
        "pk,bkq->bpq", sin_outer[:half_rows, :], turned_im
    )
    return values.reshape(values.shape[0], half_rows * inner) * (1.0 / (outer * inner))


def spec_product(left_re, left_im, right_re, right_im):
    return (left_re * right_re - left_im * right_im, left_re * right_im + left_im * right_re)


def conj_product(left_re, left_im, right_re, right_im):
    return (left_re * right_re + left_im * right_im, left_re * right_im - left_im * right_re)


def filter_basis(residue_loc, rate_loc, length):
    position = jnp.arange(length, dtype=jnp.float32)
    basis_all = jnp.sqrt(2.0 * rate_loc)[:, :, None] * jnp.exp(
        -rate_loc[:, :, None] * position[None, None, :]
    )
    return (basis_all, precise("cm,cmt->ct", residue_loc, basis_all))


def forward_cols(gated_cols, taps_re, taps_im, tables):
    gated_re, gated_im = spectrum(gated_cols.astype(jnp.float32), tables, tripled)
    conv_re, conv_im = spec_product(gated_re, gated_im, taps_re, taps_im)
    conv_cols = signal_of(conv_re, conv_im, tables).astype(jnp.bfloat16)
    return (conv_cols, gated_re, gated_im)


def backward_cols(slope_cols, gated_re, gated_im, taps_re, taps_im, basis_all, tables, length):
    slope_re, slope_im = spectrum(slope_cols.astype(jnp.float32), tables, tripled)
    grad_re, grad_im = conj_product(taps_re, taps_im, slope_re, slope_im)
    back_cols = signal_of(grad_re, grad_im, tables).astype(jnp.bfloat16)
    lag_re, lag_im = conj_product(gated_re, gated_im, slope_re, slope_im)
    taps_grad = signal_of(lag_re, lag_im, tables)
    grad_residue = precise("ct,cmt->cm", taps_grad, basis_all) * (1.0 / math.sqrt(length))
    return (back_cols, grad_residue)


def gather_weights(tokens, weights, residues, decay_rates, cotangent):
    gathered = lax.all_gather(weights, "ctx", axis=1, tiled=True)
    projected = jnp.einsum("xcpd,td->xcpt", gathered, tokens, preferred_element_type=jnp.float32)
    features = projected[0].astype(jnp.bfloat16)
    query_f = features[:, 0].astype(jnp.float32)
    key_part = features[:, 1].astype(jnp.float32)
    value_part = features[:, 2].astype(jnp.float32)
    gated_in = (key_part * value_part).astype(jnp.bfloat16)
    slope_in = (cotangent.astype(jnp.float32) * query_f).astype(jnp.bfloat16)
    length = tokens.shape[0] * lax.axis_size("ctx")
    tables = make_tables(length)
    basis_all, taps_full = filter_basis(residues[0], decay_rates[0], length)
    taps_re, taps_im = spectrum(taps_full, tables, precise)
    gated_cols = lax.all_to_all(gated_in, "ctx", split_axis=0, concat_axis=1, tiled=True)
    conv_cols, gated_re, gated_im = forward_cols(gated_cols, taps_re, taps_im, tables)
    conv_rows = lax.all_to_all(conv_cols, "ctx", split_axis=1, concat_axis=0, tiled=True)
    slope_cols = lax.all_to_all(slope_in, "ctx", split_axis=0, concat_axis=1, tiled=True)
    back_cols, grad_residue = backward_cols(
        slope_cols, gated_re, gated_im, taps_re, taps_im, basis_all, tables, length
    )
    back_rows = lax.all_to_all(back_cols, "ctx", split_axis=1, concat_axis=0, tiled=True)
    conv_f = conv_rows.astype(jnp.float32)
    back_f = back_rows.astype(jnp.float32)
    hyena_out = (query_f * conv_f).astype(jnp.bfloat16)
    grad_query = (cotangent.astype(jnp.float32) * conv_f).astype(jnp.bfloat16)
    grad_key = (back_f * value_part).astype(jnp.bfloat16)
    grad_value = (back_f * key_part).astype(jnp.bfloat16)
    grad_proj = jnp.stack([grad_query, grad_key, grad_value], axis=1)
    partial_value = jnp.einsum(
        "cpt,cpd->td", grad_proj, gathered[0], preferred_element_type=jnp.float32
    )
    grad_input = lax.psum_scatter(
        partial_value.astype(jnp.bfloat16), "tp", scatter_dimension=1, tiled=True
    )
    return (hyena_out, grad_input, grad_residue[None])


GROUP = 4
ROWS = 8
PLANE = 4
VMEM = 56 * 2**20


def rounded(value):
    return value.astype(jnp.bfloat16).astype(jnp.float32)


def added_up(parts):
    return functools.reduce(operator.add, parts)


def earlier_sum(finals, rate, span, back):
    count = finals.shape[0]
    row = lax.broadcasted_iota(jnp.int32, finals.shape, 0)

    def shifted(value, by):
        if back:
            moved = pltpu.roll(value, count - by, 0)
            return jnp.where(row < count - by, moved, 0.0)
        moved = pltpu.roll(value, by, 0)
        return jnp.where(row >= by, moved, 0.0)

    total = shifted(finals, 1)
    by = 1
    while by < count:
        total = total + jnp.exp(rate * (-1.0 * span * by)) * shifted(total, by)
        by *= 2
    return total


def scan_kernel(
    groups,
    runs,
    order,
    me_ref,
    residue_ref,
    rate_ref,
    *refs,
):
    inputs = 1 + max(run[0] for run in runs)
    arrays, refs = refs[: 2 * inputs + 1], refs[2 * inputs + 1 :]
    hyena_ref, grad_ref = refs[:2]
    proj_refs, refs = refs[2 : 2 + len(order)], refs[2 + len(order) :]
    gated_s, slope_s, conv_s, back_s, feats_s = refs
    cot_ref, own, other = arrays[0], arrays[1 : 1 + inputs], arrays[1 + inputs :]
    length, width = cot_ref.shape
    chunks = PLANE * groups
    span = length // chunks
    modes = rate_ref.shape[0]
    me = me_ref[0]

    def place(group, member):
        return lax.rem(me // PLANE + group, groups) * PLANE + (member ^ lax.rem(me, PLANE))

    def aligned(start, size):
        return pl.ds(pl.multiple_of(start, size), size)

    for source, offset, group, base, members, count, first in runs:

        def before(step, _, source=source, offset=offset, group=group, base=base, count=count, first=first):
            member = base + step
            index = place(group, member)
            rows = pl.ds(pl.multiple_of(offset + step * count, 16), count)
            feats = own[source][rows, :] + other[source][rows, :].astype(jnp.float32)
            feats = rounded(feats)
            slot = (group * PLANE + member) * span + first
            feats_s[pl.ds(pl.multiple_of(slot, 16), count), :] = feats
            cot = cot_ref[pl.ds(pl.multiple_of(index * span + first, 16), count), :]
            query, key = feats[:, :width], feats[:, width : 2 * width]
            into = pl.ds(first * chunks + index, count, stride=chunks)
            gated_s[into, :] = rounded(key * feats[:, 2 * width :])
            slope_s[into, :] = rounded(cot.astype(jnp.float32) * query)
            return 0

        lax.fori_loop(0, members, before, 0)

    sides = range(chunks // ROWS)
    scale = 1.0 / math.sqrt(length)

    def rows_at(step, side):
        return pl.ds(pl.multiple_of(step * chunks + side * ROWS, ROWS), ROWS)

    def zeros(count):
        zero = jnp.zeros((ROWS, width), jnp.float32)
        return tuple((zero,) * len(sides) for _ in range(count))

    def moved_on(states, decays, inputs):
        return tuple(
            tuple(decay * state[side] + inputs[side] for side in sides)
            for decay, state in zip(decays, states)
        )

    def entered(states, rates, back):
        whole = [
            earlier_sum(
                jnp.concatenate(state, axis=0),
                jnp.concatenate([rate] * len(sides), axis=0),
                span,
                back,
            )
            for state, rate in zip(states, rates)
        ]
        return tuple(
            tuple(state[side * ROWS : (side + 1) * ROWS, :] for side in sides) for state in whole
        )

    for first in range(0, modes, GROUP):
        count = min(GROUP, modes - first)
        rates = [
            jnp.broadcast_to(rate_ref[m : m + 1, :], (ROWS, width))
            for m in range(first, first + count)
        ]
        decays = [jnp.exp(-rate) for rate in rates]
        norms = [jnp.sqrt(2.0 * rate) for rate in rates]
        gains = [residue_ref[first + n : first + n + 1, :] * norms[n] for n in range(count)]

        def sums(step, state):
            ahead, behind = state
            gated = [gated_s[rows_at(step, side), :] for side in sides]
            slope = [slope_s[rows_at(span - 1 - step, side), :] for side in sides]
            return moved_on(ahead, decays, gated), moved_on(behind, decays, slope)

        ahead, behind = lax.fori_loop(0, span, sums, (zeros(count), zeros(count)), unroll=16)
        ahead, behind = entered(ahead, rates, False), entered(behind, rates, True)

        def outs(step, state):
            ahead, behind, grads = state
            other = span - 1 - step
            gated = [gated_s[rows_at(step, side), :] for side in sides]
            slope = [slope_s[rows_at(step, side), :] for side in sides]
            slope_back = [slope_s[rows_at(other, side), :] for side in sides]
            ahead = moved_on(ahead, decays, gated)
            behind = moved_on(behind, decays, slope_back)
            grads = tuple(
                tuple(grad[side] + slope[side] * state[side] for side in sides)
                for grad, state in zip(grads, ahead)
            )
            for side in sides:
                conv = added_up(gains[n] * ahead[n][side] for n in range(count))
                back = added_up(gains[n] * behind[n][side] for n in range(count))
                if first:
                    conv = conv + conv_s[rows_at(step, side), :]
                    back = back + back_s[rows_at(other, side), :]
                conv_s[rows_at(step, side), :] = conv
                back_s[rows_at(other, side), :] = back
            return ahead, behind, grads

        _, _, grads = lax.fori_loop(0, span, outs, (ahead, behind, zeros(count)), unroll=8)
        for n in range(count):
            total = jnp.sum(added_up(grads[n]) * norms[n], axis=0, keepdims=True) * scale
            grad_ref[first + n : first + n + 1, :] = total

    for proj_ref, pieces in zip(proj_refs, order):
        start = 0
        for group, base, members in pieces:

            def after(step, _, proj_ref=proj_ref, start=start, group=group, base=base):
                member = base + step
                index = place(group, member)
                feats = feats_s[aligned((group * PLANE + member) * span, span), :]
                query, key = feats[:, :width], feats[:, width : 2 * width]
                cot = cot_ref[aligned(index * span, span), :].astype(jnp.float32)
                conv = rounded(conv_s[pl.ds(index, span, stride=chunks), :])
                back = rounded(back_s[pl.ds(index, span, stride=chunks), :])
                hyena_ref[aligned(index * span, span), :] = narrowed(query * conv)
                rows = aligned(start + step * span, span)
                proj_ref[rows, :width] = narrowed(cot * conv)
                proj_ref[rows, width : 2 * width] = narrowed(back * feats[:, 2 * width :])
                proj_ref[rows, 2 * width :] = narrowed(back * key)
                return 0

            lax.fori_loop(0, members, after, 0)
            start += members * span


def scan_all(me, cot_cols, residue_rows, rate_rows, runs, order, own, other):
    length, width = cot_cols.shape
    span = length // (PLANE * PLANE)
    vmem = pl.BlockSpec(memory_space=pltpu.VMEM)
    arrays = (cot_cols, *own, *other)
    outs = pl.pallas_call(
        functools.partial(scan_kernel, PLANE, runs, order),
        out_shape=(
            jax.ShapeDtypeStruct((length, width), jnp.bfloat16),
            jax.ShapeDtypeStruct(rate_rows.shape, jnp.float32),
        )
        + tuple(
            jax.ShapeDtypeStruct((span * sum(piece[2] for piece in pieces), 3 * width), jnp.bfloat16)
            for pieces in order
        ),
        in_specs=[pl.BlockSpec(memory_space=pltpu.SMEM)] + [vmem] * (2 + len(arrays)),
        out_specs=(vmem,) * (2 + len(order)),
        scratch_shapes=[pltpu.VMEM((length, width), jnp.float32)] * 4
        + [pltpu.VMEM((length, 3 * width), jnp.float32)],
        compiler_params=pltpu.CompilerParams(vmem_limit_bytes=40 * 2**20),
        name="modal_scan",
    )(me, residue_rows, rate_rows, *arrays)
    return outs[0], outs[1], outs[2:]


def swapped(value):
    return lax.ppermute(value, "tp", [(0, 1), (1, 0)])


def over_x(value):
    return lax.ppermute(value, "ctx", [(i, i ^ 1) for i in range(lax.axis_size("ctx"))])


def over_y(value):
    return lax.ppermute(value, "ctx", [(i, i ^ 2) for i in range(lax.axis_size("ctx"))])


def up(value):
    count = lax.axis_size("ctx")
    return lax.ppermute(value, "ctx", [(i, (i + PLANE) % count) for i in range(count)])


def down(value):
    count = lax.axis_size("ctx")
    return lax.ppermute(value, "ctx", [((i + PLANE) % count, i) for i in range(count)])


def stack(*parts):
    return jnp.concatenate(parts, axis=0)


def beside(*parts):
    return jnp.concatenate(parts, axis=1)


def narrowed(value):
    return value.astype(jnp.bfloat16)


def widened(value):
    return value.astype(jnp.float32)


def halves_kernel(plan, core_ref, *refs):
    arrays, outs, arrived = refs[: -1 - len(plan)], refs[-1 - len(plan) : -1], refs[-1]
    copies = []
    for k, (out, (index, count, mine)) in enumerate(zip(outs, plan)):
        half = out.shape[1]
        side = core_ref[0] if mine else 1 - core_ref[0]
        columns = pl.ds(pl.multiple_of(side * half, half), half)
        part = arrays[index].at[pl.ds(0, count), columns]
        copies.append(pltpu.make_async_copy(part, out, arrived.at[k]))
    for copy in copies:
        copy.start()
    for copy in copies:
        copy.wait()


def halves(arrays, *plan):
    core = lax.axis_index("tp").astype(jnp.int32).reshape(1)
    shapes = [(count, arrays[index].shape[1] // 2) for index, count, _ in plan]
    moved = sum(4 * rows * columns for rows, columns in shapes)
    return pl.pallas_call(
        functools.partial(halves_kernel, plan),
        out_shape=tuple(jax.ShapeDtypeStruct(shape, jnp.bfloat16) for shape in shapes),
        in_specs=[pl.BlockSpec(memory_space=pltpu.SMEM)]
        + [pl.BlockSpec(memory_space=pl.ANY)] * len(arrays),
        out_specs=(pl.BlockSpec(memory_space=pltpu.VMEM),) * len(plan),
        scratch_shapes=[pltpu.SemaphoreType.DMA((len(plan),))],
        compiler_params=pltpu.CompilerParams(vmem_limit_bytes=VMEM),
        cost_estimate=pl.CostEstimate(flops=0, bytes_accessed=moved, transcendentals=0),
        name="halves",
    )(core, *arrays)


def assemble_kernel(inputs, plans, *refs):
    arrays, outs = refs[:inputs], refs[inputs:]
    for out, plan in zip(outs, plans):
        for row, col, height, width, sources in plan:
            parts = [
                arrays[index][from_row : from_row + height, from_col : from_col + width]
                for index, from_row, from_col in sources
            ]
            if len(parts) > 1:
                parts = [narrowed(added_up(widened(part) for part in parts))]
            out[row : row + height, col : col + width] = parts[0]


def assemble(arrays, *plans):
    used = sorted({source[0] for plan in plans for piece in plan for source in piece[4]})
    arrays = [arrays[index] for index in used]
    plans = [
        [(*piece[:4], [(used.index(source[0]), *source[1:]) for source in piece[4]]) for piece in plan]
        for plan in plans
    ]
    shapes = [
        (max(p[0] + p[2] for p in plan), max(p[1] + p[3] for p in plan)) for plan in plans
    ]
    moved = sum(2 * rows * cols for rows, cols in shapes)
    vmem = pl.BlockSpec(memory_space=pltpu.VMEM)
    return pl.pallas_call(
        functools.partial(assemble_kernel, len(arrays), plans),
        out_shape=tuple(jax.ShapeDtypeStruct(shape, jnp.bfloat16) for shape in shapes),
        in_specs=[vmem] * len(arrays),
        out_specs=(vmem,) * len(plans),
        compiler_params=pltpu.CompilerParams(vmem_limit_bytes=32 * 2**20),
        cost_estimate=pl.CostEstimate(flops=moved, bytes_accessed=4 * moved, transcendentals=0),
        name="assemble",
    )(*arrays)


def rows_of(*parts):
    plan, start = [], 0
    for index, first, count in parts:
        plan.append((start, count, [(index, first, 0)]))
        start += count
    return plan


def full_width(columns, plan):
    return [(row, 0, count, columns, sources) for row, count, sources in plan]


def columns_of(height, *parts):
    plan, start = [], 0
    for width, sources in parts:
        plan.append((0, start, height, width, sources))
        start += width
    return plan


def all_ways(for_x, for_y, for_above, for_below):
    from_below, from_above = up(for_above), down(for_below)
    got_x, got_y = over_x(for_x), over_y(for_y)
    return lax.optimization_barrier((got_x, got_y, from_below, from_above))


def project(parts, kept, taken):
    rows = stack(*parts)
    own, given = (
        jnp.einsum("td,rd->tr", rows, matrix, preferred_element_type=jnp.float32)
        for matrix in (kept, taken)
    )
    return own, swapped(narrowed(given))


def columns_held(rows):
    return lax.all_to_all(rows.T, "ctx", split_axis=1, concat_axis=0, tiled=True)


def gather_groups(tokens, wide, matrices, later):
    span = tokens.shape[0]
    n, m = span * 3 // 4, span // 4
    nh, mh = n // 2, m // 2
    columns = tokens.shape[1]

    def put(arrays, *plans):
        return assemble(arrays, *[full_width(columns, rows_of(*plan)) for plan in plans])

    own_x, own_y, wide_3, wide_1 = all_ways(tokens, tokens, wide, wide)
    first = (tokens, own_x, own_y, wide_3, wide_1)
    members = ((0, n, m), (1, n, m), (2, n, m))
    sent = put(
        first,
        ((2, 0, nh), (2, n, mh), (3, 0, n), (4, 0, n)),
        ((1, nh, nh), (1, n + mh, mh), (3, 0, n), (4, 0, n)),
        ((3, 0, nh), *members),
        ((4, nh, nh), *members),
    )
    sent, first = lax.optimization_barrier((sent, first))
    second = all_ways(*sent)
    start = nh + mh
    wide_2 = ((2, 0, nh), (3, 0, nh))
    across = ((0, nh, mh), (1, nh, mh))
    third = all_ways(
        *put(
            second,
            ((1, start, nh), (1, start + n, nh), *wide_2),
            ((0, start + nh, nh), (0, start + n + nh, nh), *wide_2),
            (*across, (2, nh, nh)),
            (*across, (3, 2 * nh, nh)),
        )
    )
    fourth = all_ways(
        *put(third, ((1, n, nh),), ((0, n + nh, nh),), ((2, 0, mh),), ((3, mh, mh),))
    )
    runs = [
        (0, 0, 0, 0, 3, span, 0),
        (0, 3 * span, 3, 0, 1, n, 0),
        (0, 3 * span + n, 1, 0, 1, n, 0),
    ]
    offset = 0
    for side in range(2):
        runs += [
            (1, offset, 0, 3, 1, nh, side * nh),
            (1, offset + nh, 0, 3, 1, mh, n + side * mh),
            (1, offset + start, 3, 1 + side, 1, n, 0),
            (1, offset + start + n, 1, 1 + side, 1, n, 0),
        ]
        offset += start + 2 * n
    for side in range(2):
        runs += [
            (1, offset, 2, 0, 1, nh, side * nh),
            (1, offset + nh, 3 - 2 * side, 0, 3, m, n),
        ]
        offset += nh + 3 * m
    offset = 0
    for side in range(2):
        runs += [
            (2, offset, 3, 3, 1, nh, side * nh),
            (2, offset + nh, 1, 3, 1, nh, side * nh),
            (2, offset + n, 2, 1 + side, 1, n, 0),
        ]
        offset += 2 * n
    runs += [
        (2, offset, 3, 3, 1, m, n),
        (2, offset + m, 2, 0, 1, m, n),
        (2, offset + 2 * m, 2, 1, 1, mh, n),
        (2, offset + 2 * m + mh, 1, 3, 1, m, n),
        (2, offset + 3 * m + mh, 2, 1, 1, mh, n + mh),
        (2, offset + 3 * m + 2 * mh, 2, 2, 1, m, n),
        (3, 0, 2, 3, 1, nh, 0),
        (3, nh, 2, 3, 1, nh, nh),
        (3, n, 2, 3, 1, mh, n),
        (3, n + mh, 2, 3, 1, mh, n + mh),
    ]
    parts = [project(part, *matrices) for part in (first, second, third, fourth)]
    later, first = lax.optimization_barrier((later, parts[0][0]))
    parts[0] = (first, parts[0][1])
    later = columns_held(later)
    return parts, tuple(runs), matrices, later


ORDER = (((2, 0, 4), (1, 3, 1), (3, 3, 1)), ((1, 0, 3), (3, 0, 3), (0, 3, 1), (0, 0, 3)))


def scatter_sum(early, later, matrix, hyena):
    span = early.shape[0] // 6
    columns = matrix.shape[1]
    wide, narrow = columns * 3 // 8, columns // 8
    places = {}
    for array, pieces in enumerate((ORDER[0], ORDER[1][:3], ORDER[1][3:])):
        row = 0
        for group, base, members in pieces:
            for member in range(base, base + members):
                places[group, member] = (array, row)
                row += span

    def product(part, other):
        both = beside(part, other)
        return narrowed(jnp.dot(both, matrix, preferred_element_type=jnp.float32))

    def term(group, member, side, *more):
        array, row = places[group, member]
        return (wide, [(array, row, side * wide), *more])

    def low(group, member, side, *more):
        array, row = places[group, member]
        return (narrow, [(array, row, 2 * wide + side * narrow), *more])

    def put(arrays, *plans):
        return assemble(arrays, *[columns_of(span, *plan) for plan in plans])

    early = product(early, swapped(early))
    other = swapped(later)
    first = all_ways(
        *put([early], [term(2, 3, 0)], [term(2, 3, 1)], [low(2, 3, 0)], [low(2, 3, 1)])
    )
    later, hyena, first = lax.optimization_barrier((later, hyena, first))
    x, y, below, above = range(1, 5)
    second = all_ways(
        *put(
            [early, *first],
            [term(2, 1, 0), term(2, 1, 1, (y, 0, 0)), term(1, 3, 0), term(3, 3, 0)],
            [term(2, 2, 0, (x, 0, 0)), term(2, 2, 1), term(1, 3, 1), term(3, 3, 1)],
            [low(1, 3, 0, (below, 0, 0)), low(1, 3, 1), *[low(2, k, 0) for k in range(3)]],
            [low(3, 3, 0), low(3, 3, 1, (above, 0, 0)), *[low(2, k, 1) for k in range(3)]],
        )
    )
    own = product(later[7 * span :], other[7 * span :])
    later = product(later[: 7 * span], other[: 7 * span])
    later, second = lax.optimization_barrier((later, second))
    hyena_out = lax.all_to_all(hyena, "ctx", split_axis=0, concat_axis=1, tiled=True).T
    x, y, below, above = range(2, 6)

    def low_3(side):
        return low(0, 3, side, (below, 0, side * narrow), (above, 0, side * narrow))

    def sum_2(side):
        return term(2, 0, side, (x, 0, side * wide), (y, 0, side * wide))

    for_above, for_below = [], []
    for k in range(3):
        start = (2 + k) * narrow
        for_above += [low(1, k, 0, (below, 0, start)), low(1, k, 1)]
        for_below += [low(3, k, 0), low(3, k, 1, (above, 0, start))]
    third = all_ways(
        *put(
            [early, later, *second],
            [
                term(1, 1, 0),
                term(1, 1, 1, (y, 0, 2 * wide)),
                term(3, 1, 0),
                term(3, 1, 1, (y, 0, 3 * wide)),
                term(0, 3, 0),
                low_3(0),
            ],
            [
                term(1, 2, 0, (x, 0, 2 * wide)),
                term(1, 2, 1),
                term(3, 2, 0, (x, 0, 3 * wide)),
                term(3, 2, 1),
                term(0, 3, 1),
                low_3(1),
            ],
            [sum_2(0), *for_above],
            [sum_2(1), *for_below],
        )
    )

    x, y, below, above = range(3, 7)

    def low_own(k, side, *more):
        start = wide + (2 * k + side) * narrow
        return low(0, k, side, (below, 0, start), (above, 0, start), *more)

    def own_sum(group, side, *more):
        start = (group - 1 + side) * wide
        return term(group, 0, side, (x, 0, start), (y, 0, start), *more)

    sent = put(
        [early, later, own, *third],
            [
                term(0, 1, 0),
                term(0, 1, 1, (y, 0, 4 * wide)),
                low_own(1, 0),
                low_own(1, 1, (y, 0, 5 * wide)),
            ],
            [
                term(0, 2, 0, (x, 0, 4 * wide)),
                term(0, 2, 1),
                low_own(2, 0, (x, 0, 5 * wide)),
                low_own(2, 1),
            ],
            [own_sum(1, 0, (below, 0, 0)), own_sum(1, 1)],
            [own_sum(3, 0), own_sum(3, 1, (above, 0, 0))],
    )
    (base,) = put(
        [early, later, own, *third],
        [term(0, 0, 0), term(0, 0, 1), low_own(0, 0), low_own(0, 1)],
    )
    (grad_input,) = put(
        [base, *all_ways(*sent)],
        [
            (2 * wide, [(way, 0, 0) for way in range(5)]),
            (2 * narrow, [(way, 0, 2 * wide) for way in range(3)]),
        ],
    )
    return grad_input, hyena_out


def gather_tokens(tokens, weights, residues, decay_rates, cotangent):
    me = lax.axis_index("ctx").astype(jnp.int32).reshape(1)
    channels, span = weights.shape[1], tokens.shape[0]
    rows = weights[0].swapaxes(0, 1).reshape(3 * channels, weights.shape[3])
    tokens_half = halves((tokens,), (0, span, True), (0, span * 3 // 4, True))
    kept, given = halves((rows,), (0, 3 * channels, True), (0, 3 * channels, False))
    count, columns = given.shape
    (taken,) = assemble([swapped(given)], [(0, 0, count, columns, [(0, 0, 0)])])
    parts, runs, (kept, taken), cot_cols = gather_groups(*tokens_half, (kept, taken), cotangent)
    own, other = zip(*parts)
    hyena, grads, (early, later) = scan_all(
        me, cot_cols, residues[0].T, decay_rates[0].T, runs, ORDER, own, other
    )
    grad_input, hyena_out = scatter_sum(early, later, stack(kept, taken), hyena)
    return (hyena_out, grad_input, grads.T[None])


def shards(tokens, weights, residues, decay_rates, cotangent):
    ctx, tp = lax.axis_size("ctx"), lax.axis_size("tp")
    if ctx == 4 * PLANE and tp == 2 and weights.size * tp > 2 * tokens.size:
        return gather_tokens(tokens, weights, residues, decay_rates, cotangent)
    return gather_weights(tokens, weights, residues, decay_rates, cotangent)


def solution(mesh):
    return jax.shard_map(
        shards,
        mesh=mesh,
        in_specs=(
            P("ctx", None),
            P("tp", "ctx", None, None),
            P("tp", "ctx", None),
            P("tp", "ctx", None),
            P("tp", "ctx"),
        ),
        out_specs=(P("tp", "ctx"), P("ctx", "tp"), P("tp", "ctx", None)),
        check_vma=False,
    )
```

```python
import functools
import math
import operator

import jax
import jax.numpy as jnp
from jax import lax
from jax.experimental import pallas as pl
from jax.experimental.pallas import tpu as pltpu
from jax.sharding import PartitionSpec as P


def precise(form, left, right):
    return jnp.einsum(
        form, left, right, precision=lax.Precision.HIGHEST, preferred_element_type=jnp.float32
    )


def tripled(form, left, right):
    return jnp.einsum(
        form, left, right, precision=lax.Precision.HIGH, preferred_element_type=jnp.float32
    )


def angle_table(row_count, col_count, period):
    product = (
        jnp.arange(row_count, dtype=jnp.int32)[:, None]
        * jnp.arange(col_count, dtype=jnp.int32)[None, :]
        % period
    )
    angles = product.astype(jnp.float32) * (2.0 * math.pi / period)
    return (jnp.cos(angles), jnp.sin(angles))


def make_tables(length):
    padded = 2 * length
    outer = math.gcd(padded, 1 << (padded.bit_length() - 1) // 2)
    inner = padded // outer
    cos_outer, sin_outer = angle_table(outer, outer, outer)
    cos_inner, sin_inner = angle_table(inner, inner, inner)
    twist_cos, twist_sin = angle_table(outer, inner, padded)
    return (outer, inner, cos_outer, sin_outer, cos_inner, sin_inner, twist_cos, twist_sin)


def spectrum(signal, tables, product):
    outer, inner, cos_outer, sin_outer, cos_inner, sin_inner, twist_cos, twist_sin = tables
    half_rows = outer // 2
    blocks = signal.reshape(signal.shape[0], half_rows, inner)
    first_re = product("kp,bpq->bkq", cos_outer[:, :half_rows], blocks)
    first_im = -product("kp,bpq->bkq", sin_outer[:, :half_rows], blocks)
    turned_re = first_re * twist_cos + first_im * twist_sin
    turned_im = first_im * twist_cos - first_re * twist_sin
    spec_re = product("bkq,qj->bkj", turned_re, cos_inner) + product(
        "bkq,qj->bkj", turned_im, sin_inner
    )
    spec_im = product("bkq,qj->bkj", turned_im, cos_inner) - product(
        "bkq,qj->bkj", turned_re, sin_inner
    )
    return (spec_re, spec_im)


def signal_of(spec_re, spec_im, tables):
    outer, inner, cos_outer, sin_outer, cos_inner, sin_inner, twist_cos, twist_sin = tables
    half_rows = outer // 2
    back_re = tripled("bkj,jq->bkq", spec_re, cos_inner) - tripled(
        "bkj,jq->bkq", spec_im, sin_inner
    )
    back_im = tripled("bkj,jq->bkq", spec_im, cos_inner) + tripled(
        "bkj,jq->bkq", spec_re, sin_inner
    )
    turned_re = back_re * twist_cos - back_im * twist_sin
    turned_im = back_im * twist_cos + back_re * twist_sin
    values = tripled("pk,bkq->bpq", cos_outer[:half_rows, :], turned_re) - tripled(
        "pk,bkq->bpq", sin_outer[:half_rows, :], turned_im
    )
    return values.reshape(values.shape[0], half_rows * inner) * (1.0 / (outer * inner))


def spec_product(left_re, left_im, right_re, right_im):
    return (left_re * right_re - left_im * right_im, left_re * right_im + left_im * right_re)


def conj_product(left_re, left_im, right_re, right_im):
    return (left_re * right_re + left_im * right_im, left_re * right_im - left_im * right_re)


def filter_basis(residue_loc, rate_loc, length):
    position = jnp.arange(length, dtype=jnp.float32)
    basis_all = jnp.sqrt(2.0 * rate_loc)[:, :, None] * jnp.exp(
        -rate_loc[:, :, None] * position[None, None, :]
    )
    return (basis_all, precise("cm,cmt->ct", residue_loc, basis_all))


def forward_cols(gated_cols, taps_re, taps_im, tables):
    gated_re, gated_im = spectrum(gated_cols.astype(jnp.float32), tables, tripled)
    conv_re, conv_im = spec_product(gated_re, gated_im, taps_re, taps_im)
    conv_cols = signal_of(conv_re, conv_im, tables).astype(jnp.bfloat16)
    return (conv_cols, gated_re, gated_im)


def backward_cols(slope_cols, gated_re, gated_im, taps_re, taps_im, basis_all, tables, length):
    slope_re, slope_im = spectrum(slope_cols.astype(jnp.float32), tables, tripled)
    grad_re, grad_im = conj_product(taps_re, taps_im, slope_re, slope_im)
    back_cols = signal_of(grad_re, grad_im, tables).astype(jnp.bfloat16)
    lag_re, lag_im = conj_product(gated_re, gated_im, slope_re, slope_im)
    taps_grad = signal_of(lag_re, lag_im, tables)
    grad_residue = precise("ct,cmt->cm", taps_grad, basis_all) * (1.0 / math.sqrt(length))
    return (back_cols, grad_residue)


def gather_weights(tokens, weights, residues, decay_rates, cotangent):
    gathered = lax.all_gather(weights, "ctx", axis=1, tiled=True)
    projected = jnp.einsum("xcpd,td->xcpt", gathered, tokens, preferred_element_type=jnp.float32)
    features = projected[0].astype(jnp.bfloat16)
    query_f = features[:, 0].astype(jnp.float32)
    key_part = features[:, 1].astype(jnp.float32)
    value_part = features[:, 2].astype(jnp.float32)
    gated_in = (key_part * value_part).astype(jnp.bfloat16)
    slope_in = (cotangent.astype(jnp.float32) * query_f).astype(jnp.bfloat16)
    length = tokens.shape[0] * lax.axis_size("ctx")
    tables = make_tables(length)
    basis_all, taps_full = filter_basis(residues[0], decay_rates[0], length)
    taps_re, taps_im = spectrum(taps_full, tables, precise)
    gated_cols = lax.all_to_all(gated_in, "ctx", split_axis=0, concat_axis=1, tiled=True)
    conv_cols, gated_re, gated_im = forward_cols(gated_cols, taps_re, taps_im, tables)
    conv_rows = lax.all_to_all(conv_cols, "ctx", split_axis=1, concat_axis=0, tiled=True)
    slope_cols = lax.all_to_all(slope_in, "ctx", split_axis=0, concat_axis=1, tiled=True)
    back_cols, grad_residue = backward_cols(
        slope_cols, gated_re, gated_im, taps_re, taps_im, basis_all, tables, length
    )
    back_rows = lax.all_to_all(back_cols, "ctx", split_axis=1, concat_axis=0, tiled=True)
    conv_f = conv_rows.astype(jnp.float32)
    back_f = back_rows.astype(jnp.float32)
    hyena_out = (query_f * conv_f).astype(jnp.bfloat16)
    grad_query = (cotangent.astype(jnp.float32) * conv_f).astype(jnp.bfloat16)
    grad_key = (back_f * value_part).astype(jnp.bfloat16)
    grad_value = (back_f * key_part).astype(jnp.bfloat16)
    grad_proj = jnp.stack([grad_query, grad_key, grad_value], axis=1)
    partial_value = jnp.einsum(
        "cpt,cpd->td", grad_proj, gathered[0], preferred_element_type=jnp.float32
    )
    grad_input = lax.psum_scatter(
        partial_value.astype(jnp.bfloat16), "tp", scatter_dimension=1, tiled=True
    )
    return (hyena_out, grad_input, grad_residue[None])


GROUP = 4
ROWS = 8
PLANE = 4
VMEM = 56 * 2**20


def rounded(value):
    return value.astype(jnp.bfloat16).astype(jnp.float32)


def added_up(parts):
    return functools.reduce(operator.add, parts)


def earlier_sum(finals, rate, span, back):
    count = finals.shape[0]
    row = lax.broadcasted_iota(jnp.int32, finals.shape, 0)

    def shifted(value, by):
        if back:
            moved = pltpu.roll(value, count - by, 0)
            return jnp.where(row < count - by, moved, 0.0)
        moved = pltpu.roll(value, by, 0)
        return jnp.where(row >= by, moved, 0.0)

    total = shifted(finals, 1)
    by = 1
    while by < count:
        total = total + jnp.exp(rate * (-1.0 * span * by)) * shifted(total, by)
        by *= 2
    return total


def scan_kernel(
    groups,
    runs,
    order,
    me_ref,
    residue_ref,
    rate_ref,
    *refs,
):
    inputs = 1 + max(run[0] for run in runs)
    arrays, refs = refs[: 2 * inputs + 1], refs[2 * inputs + 1 :]
    hyena_ref, grad_ref = refs[:2]
    proj_refs, refs = refs[2 : 2 + len(order)], refs[2 + len(order) :]
    gated_s, slope_s, conv_s, back_s, feats_s = refs
    cot_ref, own, other = arrays[0], arrays[1 : 1 + inputs], arrays[1 + inputs :]
    length, width = cot_ref.shape
    chunks = PLANE * groups
    span = length // chunks
    modes = rate_ref.shape[0]
    me = me_ref[0]

    def place(group, member):
        return lax.rem(me // PLANE + group, groups) * PLANE + (member ^ lax.rem(me, PLANE))

    def aligned(start, size):
        return pl.ds(pl.multiple_of(start, size), size)

    for source, offset, group, base, members, count, first in runs:

        def before(step, _, source=source, offset=offset, group=group, base=base, count=count, first=first):
            member = base + step
            index = place(group, member)
            rows = pl.ds(pl.multiple_of(offset + step * count, 16), count)
            feats = own[source][rows, :] + other[source][rows, :].astype(jnp.float32)
            feats = rounded(feats)
            slot = (group * PLANE + member) * span + first
            feats_s[pl.ds(pl.multiple_of(slot, 16), count), :] = feats
            cot = cot_ref[pl.ds(pl.multiple_of(index * span + first, 16), count), :]
            query, key = feats[:, :width], feats[:, width : 2 * width]
            into = pl.ds(first * chunks + index, count, stride=chunks)
            gated_s[into, :] = rounded(key * feats[:, 2 * width :])
            slope_s[into, :] = rounded(cot.astype(jnp.float32) * query)
            return 0

        lax.fori_loop(0, members, before, 0)

    sides = range(chunks // ROWS)
    scale = 1.0 / math.sqrt(length)

    def rows_at(step, side):
        return pl.ds(pl.multiple_of(step * chunks + side * ROWS, ROWS), ROWS)

    def zeros(count):
        zero = jnp.zeros((ROWS, width), jnp.float32)
        return tuple((zero,) * len(sides) for _ in range(count))

    def moved_on(states, decays, inputs):
        return tuple(
            tuple(decay * state[side] + inputs[side] for side in sides)
            for decay, state in zip(decays, states)
        )

    def entered(states, rates, back):
        whole = [
            earlier_sum(
                jnp.concatenate(state, axis=0),
                jnp.concatenate([rate] * len(sides), axis=0),
                span,
                back,
            )
            for state, rate in zip(states, rates)
        ]
        return tuple(
            tuple(state[side * ROWS : (side + 1) * ROWS, :] for side in sides) for state in whole
        )

    for first in range(0, modes, GROUP):
        count = min(GROUP, modes - first)
        rates = [
            jnp.broadcast_to(rate_ref[m : m + 1, :], (ROWS, width))
            for m in range(first, first + count)
        ]
        decays = [jnp.exp(-rate) for rate in rates]
        norms = [jnp.sqrt(2.0 * rate) for rate in rates]
        gains = [residue_ref[first + n : first + n + 1, :] * norms[n] for n in range(count)]

        def sums(step, state):
            ahead, behind = state
            gated = [gated_s[rows_at(step, side), :] for side in sides]
            slope = [slope_s[rows_at(span - 1 - step, side), :] for side in sides]
            return moved_on(ahead, decays, gated), moved_on(behind, decays, slope)

        ahead, behind = lax.fori_loop(0, span, sums, (zeros(count), zeros(count)), unroll=16)
        ahead, behind = entered(ahead, rates, False), entered(behind, rates, True)

        def outs(step, state):
            ahead, behind, grads = state
            other = span - 1 - step
            gated = [gated_s[rows_at(step, side), :] for side in sides]
            slope = [slope_s[rows_at(step, side), :] for side in sides]
            slope_back = [slope_s[rows_at(other, side), :] for side in sides]
            ahead = moved_on(ahead, decays, gated)
            behind = moved_on(behind, decays, slope_back)
            grads = tuple(
                tuple(grad[side] + slope[side] * state[side] for side in sides)
                for grad, state in zip(grads, ahead)
            )
            for side in sides:
                conv = added_up(gains[n] * ahead[n][side] for n in range(count))
                back = added_up(gains[n] * behind[n][side] for n in range(count))
                if first:
                    conv = conv + conv_s[rows_at(step, side), :]
                    back = back + back_s[rows_at(other, side), :]
                conv_s[rows_at(step, side), :] = conv
                back_s[rows_at(other, side), :] = back
            return ahead, behind, grads

        _, _, grads = lax.fori_loop(0, span, outs, (ahead, behind, zeros(count)), unroll=8)
        for n in range(count):
            total = jnp.sum(added_up(grads[n]) * norms[n], axis=0, keepdims=True) * scale
            grad_ref[first + n : first + n + 1, :] = total

    for proj_ref, pieces in zip(proj_refs, order):
        start = 0
        for group, base, members in pieces:

            def after(step, _, proj_ref=proj_ref, start=start, group=group, base=base):
                member = base + step
                index = place(group, member)
                feats = feats_s[aligned((group * PLANE + member) * span, span), :]
                query, key = feats[:, :width], feats[:, width : 2 * width]
                cot = cot_ref[aligned(index * span, span), :].astype(jnp.float32)
                conv = rounded(conv_s[pl.ds(index, span, stride=chunks), :])
                back = rounded(back_s[pl.ds(index, span, stride=chunks), :])
                hyena_ref[aligned(index * span, span), :] = narrowed(query * conv)
                rows = aligned(start + step * span, span)
                proj_ref[rows, :width] = narrowed(cot * conv)
                proj_ref[rows, width : 2 * width] = narrowed(back * feats[:, 2 * width :])
                proj_ref[rows, 2 * width :] = narrowed(back * key)
                return 0

            lax.fori_loop(0, members, after, 0)
            start += members * span


def scan_all(me, cot_cols, residue_rows, rate_rows, runs, order, own, other):
    length, width = cot_cols.shape
    span = length // (PLANE * PLANE)
    vmem = pl.BlockSpec(memory_space=pltpu.VMEM)
    arrays = (cot_cols, *own, *other)
    outs = pl.pallas_call(
        functools.partial(scan_kernel, PLANE, runs, order),
        out_shape=(
            jax.ShapeDtypeStruct((length, width), jnp.bfloat16),
            jax.ShapeDtypeStruct(rate_rows.shape, jnp.float32),
        )
        + tuple(
            jax.ShapeDtypeStruct((span * sum(piece[2] for piece in pieces), 3 * width), jnp.bfloat16)
            for pieces in order
        ),
        in_specs=[pl.BlockSpec(memory_space=pltpu.SMEM)] + [vmem] * (2 + len(arrays)),
        out_specs=(vmem,) * (2 + len(order)),
        scratch_shapes=[pltpu.VMEM((length, width), jnp.float32)] * 4
        + [pltpu.VMEM((length, 3 * width), jnp.float32)],
        compiler_params=pltpu.CompilerParams(vmem_limit_bytes=40 * 2**20),
        name="modal_scan",
    )(me, residue_rows, rate_rows, *arrays)
    return outs[0], outs[1], outs[2:]


def swapped(value):
    return lax.ppermute(value, "tp", [(0, 1), (1, 0)])


def over_x(value):
    return lax.ppermute(value, "ctx", [(i, i ^ 1) for i in range(lax.axis_size("ctx"))])


def over_y(value):
    return lax.ppermute(value, "ctx", [(i, i ^ 2) for i in range(lax.axis_size("ctx"))])


def up(value):
    count = lax.axis_size("ctx")
    return lax.ppermute(value, "ctx", [(i, (i + PLANE) % count) for i in range(count)])


def down(value):
    count = lax.axis_size("ctx")
    return lax.ppermute(value, "ctx", [((i + PLANE) % count, i) for i in range(count)])


def stack(*parts):
    return jnp.concatenate(parts, axis=0)


def beside(*parts):
    return jnp.concatenate(parts, axis=1)


def narrowed(value):
    return value.astype(jnp.bfloat16)


def widened(value):
    return value.astype(jnp.float32)


def halves_kernel(plan, core_ref, *refs):
    arrays, outs, arrived = refs[: -1 - len(plan)], refs[-1 - len(plan) : -1], refs[-1]
    copies = []
    for k, (out, (index, count, mine)) in enumerate(zip(outs, plan)):
        half = out.shape[1]
        side = core_ref[0] if mine else 1 - core_ref[0]
        columns = pl.ds(pl.multiple_of(side * half, half), half)
        part = arrays[index].at[pl.ds(0, count), columns]
        copies.append(pltpu.make_async_copy(part, out, arrived.at[k]))
    for copy in copies:
        copy.start()
    for copy in copies:
        copy.wait()


def halves(arrays, *plan):
    core = lax.axis_index("tp").astype(jnp.int32).reshape(1)
    shapes = [(count, arrays[index].shape[1] // 2) for index, count, _ in plan]
    moved = sum(4 * rows * columns for rows, columns in shapes)
    return pl.pallas_call(
        functools.partial(halves_kernel, plan),
        out_shape=tuple(jax.ShapeDtypeStruct(shape, jnp.bfloat16) for shape in shapes),
        in_specs=[pl.BlockSpec(memory_space=pltpu.SMEM)]
        + [pl.BlockSpec(memory_space=pl.ANY)] * len(arrays),
        out_specs=(pl.BlockSpec(memory_space=pltpu.VMEM),) * len(plan),
        scratch_shapes=[pltpu.SemaphoreType.DMA((len(plan),))],
        compiler_params=pltpu.CompilerParams(vmem_limit_bytes=VMEM),
        cost_estimate=pl.CostEstimate(flops=0, bytes_accessed=moved, transcendentals=0),
        name="halves",
    )(core, *arrays)


def assemble_kernel(inputs, plans, *refs):
    arrays, outs = refs[:inputs], refs[inputs:]
    for out, plan in zip(outs, plans):
        for row, col, height, width, sources in plan:
            parts = [
                arrays[index][from_row : from_row + height, from_col : from_col + width]
                for index, from_row, from_col in sources
            ]
            if len(parts) > 1:
                parts = [narrowed(added_up(widened(part) for part in parts))]
            out[row : row + height, col : col + width] = parts[0]


def assemble(arrays, *plans):
    used = sorted({source[0] for plan in plans for piece in plan for source in piece[4]})
    arrays = [arrays[index] for index in used]
    plans = [
        [(*piece[:4], [(used.index(source[0]), *source[1:]) for source in piece[4]]) for piece in plan]
        for plan in plans
    ]
    shapes = [
        (max(p[0] + p[2] for p in plan), max(p[1] + p[3] for p in plan)) for plan in plans
    ]
    moved = sum(2 * rows * cols for rows, cols in shapes)
    vmem = pl.BlockSpec(memory_space=pltpu.VMEM)
    return pl.pallas_call(
        functools.partial(assemble_kernel, len(arrays), plans),
        out_shape=tuple(jax.ShapeDtypeStruct(shape, jnp.bfloat16) for shape in shapes),
        in_specs=[vmem] * len(arrays),
        out_specs=(vmem,) * len(plans),
        compiler_params=pltpu.CompilerParams(vmem_limit_bytes=32 * 2**20),
        cost_estimate=pl.CostEstimate(flops=moved, bytes_accessed=4 * moved, transcendentals=0),
        name="assemble",
    )(*arrays)


def rows_of(*parts):
    plan, start = [], 0
    for index, first, count in parts:
        plan.append((start, count, [(index, first, 0)]))
        start += count
    return plan


def full_width(columns, plan):
    return [(row, 0, count, columns, sources) for row, count, sources in plan]


def columns_of(height, *parts):
    plan, start = [], 0
    for width, sources in parts:
        plan.append((0, start, height, width, sources))
        start += width
    return plan


def all_ways(for_x, for_y, for_above, for_below):
    from_below, from_above = up(for_above), down(for_below)
    got_x, got_y = over_x(for_x), over_y(for_y)
    return lax.optimization_barrier((got_x, got_y, from_below, from_above))


def project(parts, kept, taken):
    rows = stack(*parts)
    own, given = (
        jnp.einsum("td,rd->tr", rows, matrix, preferred_element_type=jnp.float32)
        for matrix in (kept, taken)
    )
    return own, swapped(narrowed(given))


def columns_held(rows):
    return lax.all_to_all(rows.T, "ctx", split_axis=1, concat_axis=0, tiled=True)


def gather_groups(tokens, wide, matrices, later):
    span = tokens.shape[0]
    n, m = span * 3 // 4, span // 4
    nh, mh = n // 2, m // 2
    columns = tokens.shape[1]

    def put(arrays, *plans):
        return assemble(arrays, *[full_width(columns, rows_of(*plan)) for plan in plans])

    own_x, own_y, wide_3, wide_1 = all_ways(tokens, tokens, wide, wide)
    first = (tokens, own_x, own_y, wide_3, wide_1)
    members = ((0, n, m), (1, n, m))
    sent = put(
        first,
        ((2, 0, nh), (2, n, mh), (3, 0, n), (4, 0, n)),
        ((1, nh, nh), (1, n + mh, mh), (3, 0, n), (4, 0, n)),
        ((3, 0, nh), *members),
        ((4, nh, nh), *members),
    )
    sent, first = lax.optimization_barrier((sent, first))
    second = all_ways(*sent)
    start = nh + mh
    wide_2 = ((2, 0, nh), (3, 0, nh))
    across = ((0, nh, mh), (1, nh, mh))
    third = all_ways(
        *put(
            (*second, own_y),
            ((1, start, nh), (1, start + n, nh), *wide_2),
            ((0, start + nh, nh), (0, start + n + nh, nh), *wide_2),
            (*across, (4, n, m), (2, nh, m)),
            (*across, (4, n, m), (3, nh + m, m)),
        )
    )
    fourth = all_ways(
        *put(third, ((1, n, nh),), ((0, n + nh, nh),), ((2, 0, m),), ((3, m, m),))
    )
    runs = [
        (0, 0, 0, 0, 3, span, 0),
        (0, 3 * span, 3, 0, 1, n, 0),
        (0, 3 * span + n, 1, 0, 1, n, 0),
    ]
    offset = 0
    for side in range(2):
        runs += [
            (1, offset, 0, 3, 1, nh, side * nh),
            (1, offset + nh, 0, 3, 1, mh, n + side * mh),
            (1, offset + start, 3, 1 + side, 1, n, 0),
            (1, offset + start + n, 1, 1 + side, 1, n, 0),
        ]
        offset += start + 2 * n
    for side in range(2):
        runs += [
            (1, offset, 2, 0, 1, nh, side * nh),
            (1, offset + nh, 3 - 2 * side, 0, 2, m, n),
        ]
        offset += nh + 2 * m
    offset = 0
    for side in range(2):
        runs += [
            (2, offset, 3, 3, 1, nh, side * nh),
            (2, offset + nh, 1, 3, 1, nh, side * nh),
            (2, offset + n, 2, 1 + side, 1, n, 0),
        ]
        offset += 2 * n
    runs += [
        (2, offset, 3, 3, 1, m, n),
        (2, offset + m, 3, 2, 1, m, n),
        (2, offset + 2 * m, 2, 0, 1, m, n),
        (2, offset + 3 * m, 1, 3, 1, m, n),
        (2, offset + 4 * m, 1, 2, 1, m, n),
        (2, offset + 5 * m, 2, 1, 1, m, n),
        (3, 0, 2, 3, 1, nh, 0),
        (3, nh, 2, 3, 1, nh, nh),
        (3, n, 2, 3, 1, m, n),
        (3, n + m, 2, 2, 1, m, n),
    ]
    parts = [project(part, *matrices) for part in (first, second, third, fourth)]
    later, first = lax.optimization_barrier((later, parts[0][0]))
    parts[0] = (first, parts[0][1])
    later = columns_held(later)
    return parts, tuple(runs), matrices, later


ORDER = (((2, 0, 4), (1, 2, 2), (3, 2, 2)), ((1, 0, 2), (3, 0, 2), (0, 3, 1), (0, 0, 3)))


def scatter_sum(early, later, matrix, hyena):
    span = early.shape[0] // 8
    columns = matrix.shape[1]
    wide, narrow = columns * 3 // 8, columns // 8
    places = {}
    for array, pieces in enumerate((ORDER[0], ORDER[1][:3], ORDER[1][3:])):
        row = 0
        for group, base, members in pieces:
            for member in range(base, base + members):
                places[group, member] = (array, row)
                row += span

    def product(part, other):
        both = beside(part, other)
        return narrowed(jnp.dot(both, matrix, preferred_element_type=jnp.float32))

    def term(group, member, side, *more):
        array, row = places[group, member]
        return (wide, [(array, row, side * wide), *more])

    def low(group, member, side, *more):
        array, row = places[group, member]
        return (narrow, [(array, row, 2 * wide + side * narrow), *more])

    def put(arrays, *plans):
        return assemble(arrays, *[columns_of(span, *plan) for plan in plans])

    early = product(early, swapped(early))
    other = swapped(later)
    first = all_ways(
        *put(
            [early],
            [term(2, 3, 0)],
            [term(2, 3, 1)],
            [low(2, 3, 0), low(2, 2, 0)],
            [low(2, 3, 1), low(2, 2, 1)],
        )
    )
    later, hyena, first = lax.optimization_barrier((later, hyena, first))
    x, y, below, above = range(1, 5)
    second = all_ways(
        *put(
            [early, *first],
            [term(2, 1, 0), term(2, 1, 1, (y, 0, 0)), term(1, 3, 0), term(3, 3, 0)],
            [term(2, 2, 0, (x, 0, 0)), term(2, 2, 1), term(1, 3, 1), term(3, 3, 1)],
            [
                low(1, 3, 0, (below, 0, 0)),
                low(1, 3, 1),
                low(1, 2, 0, (below, 0, narrow)),
                low(1, 2, 1),
                low(2, 0, 0),
                low(2, 1, 0),
            ],
            [
                low(3, 3, 0),
                low(3, 3, 1, (above, 0, 0)),
                low(3, 2, 0),
                low(3, 2, 1, (above, 0, narrow)),
                low(2, 0, 1),
                low(2, 1, 1),
            ],
        )
    )
    own = product(later[5 * span :], other[5 * span :])
    later = product(later[: 5 * span], other[: 5 * span])
    later, second = lax.optimization_barrier((later, second))
    hyena_out = lax.all_to_all(hyena, "ctx", split_axis=0, concat_axis=1, tiled=True).T
    x, y, below, above = range(2, 6)

    def low_3(side):
        return low(0, 3, side, (below, 0, side * narrow), (above, 0, side * narrow))

    def sum_2(side):
        return term(2, 0, side, (x, 0, side * wide), (y, 0, side * wide))

    for_above, for_below = [], []
    for k in range(2):
        start = (4 + k) * narrow
        for_above += [low(1, k, 0, (below, 0, start)), low(1, k, 1)]
        for_below += [low(3, k, 0), low(3, k, 1, (above, 0, start))]
    third = all_ways(
        *put(
            [early, later, *second],
            [
                term(1, 1, 0),
                term(1, 1, 1, (y, 0, 2 * wide)),
                term(3, 1, 0),
                term(3, 1, 1, (y, 0, 3 * wide)),
                term(0, 3, 0),
                low_3(0),
            ],
            [
                term(1, 2, 0, (x, 0, 2 * wide)),
                term(1, 2, 1),
                term(3, 2, 0, (x, 0, 3 * wide)),
                term(3, 2, 1),
                term(0, 3, 1),
                low_3(1),
            ],
            [sum_2(0), *for_above],
            [sum_2(1), *for_below],
        )
    )

    (low_2,) = put(
        [early, later, own, *second],
        [
            low(0, 2, side, *[(way, 0, (2 + side) * narrow) for way in (5, 6)])
            for side in (0, 1)
        ],
    )
    x, y, below, above = range(3, 7)

    def low_own(k, side, *more):
        if k == 2:
            return (narrow, [(7, 0, side * narrow), *more])
        start = wide + (2 * k + side) * narrow
        return low(0, k, side, (below, 0, start), (above, 0, start), *more)

    def own_sum(group, side, *more):
        start = (group - 1 + side) * wide
        return term(group, 0, side, (x, 0, start), (y, 0, start), *more)

    sent = put(
        [early, later, own, *third, low_2],
            [
                term(0, 1, 0),
                term(0, 1, 1, (y, 0, 4 * wide)),
                low_own(1, 0),
                low_own(1, 1, (y, 0, 5 * wide)),
            ],
            [
                term(0, 2, 0, (x, 0, 4 * wide)),
                term(0, 2, 1),
                low_own(2, 0, (x, 0, 5 * wide)),
                low_own(2, 1),
            ],
            [own_sum(1, 0, (below, 0, 0)), own_sum(1, 1)],
            [own_sum(3, 0), own_sum(3, 1, (above, 0, 0))],
    )
    (base,) = put(
        [early, later, own, *third],
        [term(0, 0, 0), term(0, 0, 1), low_own(0, 0), low_own(0, 1)],
    )
    (grad_input,) = put(
        [base, *all_ways(*sent)],
        [
            (2 * wide, [(way, 0, 0) for way in range(5)]),
            (2 * narrow, [(way, 0, 2 * wide) for way in range(3)]),
        ],
    )
    return grad_input, hyena_out


def gather_tokens(tokens, weights, residues, decay_rates, cotangent):
    me = lax.axis_index("ctx").astype(jnp.int32).reshape(1)
    channels, span = weights.shape[1], tokens.shape[0]
    rows = weights[0].swapaxes(0, 1).reshape(3 * channels, weights.shape[3])
    tokens_half = halves((tokens,), (0, span, True), (0, span * 3 // 4, True))
    kept, given = halves((rows,), (0, 3 * channels, True), (0, 3 * channels, False))
    count, columns = given.shape
    (taken,) = assemble([swapped(given)], [(0, 0, count, columns, [(0, 0, 0)])])
    parts, runs, (kept, taken), cot_cols = gather_groups(*tokens_half, (kept, taken), cotangent)
    own, other = zip(*parts)
    hyena, grads, (early, later) = scan_all(
        me, cot_cols, residues[0].T, decay_rates[0].T, runs, ORDER, own, other
    )
    grad_input, hyena_out = scatter_sum(early, later, stack(kept, taken), hyena)
    return (hyena_out, grad_input, grads.T[None])


def shards(tokens, weights, residues, decay_rates, cotangent):
    ctx, tp = lax.axis_size("ctx"), lax.axis_size("tp")
    if ctx == 4 * PLANE and tp == 2 and weights.size * tp > 2 * tokens.size:
        return gather_tokens(tokens, weights, residues, decay_rates, cotangent)
    return gather_weights(tokens, weights, residues, decay_rates, cotangent)


def solution(mesh):
    return jax.shard_map(
        shards,
        mesh=mesh,
        in_specs=(
            P("ctx", None),
            P("tp", "ctx", None, None),
            P("tp", "ctx", None),
            P("tp", "ctx", None),
            P("tp", "ctx"),
        ),
        out_specs=(P("tp", "ctx"), P("ctx", "tp"), P("tp", "ctx", None)),
        check_vma=False,
    )
```

```python
import functools
import math
import operator

import jax
import jax.numpy as jnp
from jax import lax
from jax.experimental import pallas as pl
from jax.experimental.pallas import tpu as pltpu
from jax.sharding import PartitionSpec as P


def precise(form, left, right):
    return jnp.einsum(
        form, left, right, precision=lax.Precision.HIGHEST, preferred_element_type=jnp.float32
    )


def tripled(form, left, right):
    return jnp.einsum(
        form, left, right, precision=lax.Precision.HIGH, preferred_element_type=jnp.float32
    )


def angle_table(row_count, col_count, period):
    product = (
        jnp.arange(row_count, dtype=jnp.int32)[:, None]
        * jnp.arange(col_count, dtype=jnp.int32)[None, :]
        % period
    )
    angles = product.astype(jnp.float32) * (2.0 * math.pi / period)
    return (jnp.cos(angles), jnp.sin(angles))


def make_tables(length):
    padded = 2 * length
    outer = math.gcd(padded, 1 << (padded.bit_length() - 1) // 2)
    inner = padded // outer
    cos_outer, sin_outer = angle_table(outer, outer, outer)
    cos_inner, sin_inner = angle_table(inner, inner, inner)
    twist_cos, twist_sin = angle_table(outer, inner, padded)
    return (outer, inner, cos_outer, sin_outer, cos_inner, sin_inner, twist_cos, twist_sin)


def spectrum(signal, tables, product):
    outer, inner, cos_outer, sin_outer, cos_inner, sin_inner, twist_cos, twist_sin = tables
    half_rows = outer // 2
    blocks = signal.reshape(signal.shape[0], half_rows, inner)
    first_re = product("kp,bpq->bkq", cos_outer[:, :half_rows], blocks)
    first_im = -product("kp,bpq->bkq", sin_outer[:, :half_rows], blocks)
    turned_re = first_re * twist_cos + first_im * twist_sin
    turned_im = first_im * twist_cos - first_re * twist_sin
    spec_re = product("bkq,qj->bkj", turned_re, cos_inner) + product(
        "bkq,qj->bkj", turned_im, sin_inner
    )
    spec_im = product("bkq,qj->bkj", turned_im, cos_inner) - product(
        "bkq,qj->bkj", turned_re, sin_inner
    )
    return (spec_re, spec_im)


def signal_of(spec_re, spec_im, tables):
    outer, inner, cos_outer, sin_outer, cos_inner, sin_inner, twist_cos, twist_sin = tables
    half_rows = outer // 2
    back_re = tripled("bkj,jq->bkq", spec_re, cos_inner) - tripled(
        "bkj,jq->bkq", spec_im, sin_inner
    )
    back_im = tripled("bkj,jq->bkq", spec_im, cos_inner) + tripled(
        "bkj,jq->bkq", spec_re, sin_inner
    )
    turned_re = back_re * twist_cos - back_im * twist_sin
    turned_im = back_im * twist_cos + back_re * twist_sin
    values = tripled("pk,bkq->bpq", cos_outer[:half_rows, :], turned_re) - tripled(
        "pk,bkq->bpq", sin_outer[:half_rows, :], turned_im
    )
    return values.reshape(values.shape[0], half_rows * inner) * (1.0 / (outer * inner))


def spec_product(left_re, left_im, right_re, right_im):
    return (left_re * right_re - left_im * right_im, left_re * right_im + left_im * right_re)


def conj_product(left_re, left_im, right_re, right_im):
    return (left_re * right_re + left_im * right_im, left_re * right_im - left_im * right_re)


def filter_basis(residue_loc, rate_loc, length):
    position = jnp.arange(length, dtype=jnp.float32)
    basis_all = jnp.sqrt(2.0 * rate_loc)[:, :, None] * jnp.exp(
        -rate_loc[:, :, None] * position[None, None, :]
    )
    return (basis_all, precise("cm,cmt->ct", residue_loc, basis_all))


def forward_cols(gated_cols, taps_re, taps_im, tables):
    gated_re, gated_im = spectrum(gated_cols.astype(jnp.float32), tables, tripled)
    conv_re, conv_im = spec_product(gated_re, gated_im, taps_re, taps_im)
    conv_cols = signal_of(conv_re, conv_im, tables).astype(jnp.bfloat16)
    return (conv_cols, gated_re, gated_im)


def backward_cols(slope_cols, gated_re, gated_im, taps_re, taps_im, basis_all, tables, length):
    slope_re, slope_im = spectrum(slope_cols.astype(jnp.float32), tables, tripled)
    grad_re, grad_im = conj_product(taps_re, taps_im, slope_re, slope_im)
    back_cols = signal_of(grad_re, grad_im, tables).astype(jnp.bfloat16)
    lag_re, lag_im = conj_product(gated_re, gated_im, slope_re, slope_im)
    taps_grad = signal_of(lag_re, lag_im, tables)
    grad_residue = precise("ct,cmt->cm", taps_grad, basis_all) * (1.0 / math.sqrt(length))
    return (back_cols, grad_residue)


def gather_weights(tokens, weights, residues, decay_rates, cotangent):
    gathered = lax.all_gather(weights, "ctx", axis=1, tiled=True)
    projected = jnp.einsum("xcpd,td->xcpt", gathered, tokens, preferred_element_type=jnp.float32)
    features = projected[0].astype(jnp.bfloat16)
    query_f = features[:, 0].astype(jnp.float32)
    key_part = features[:, 1].astype(jnp.float32)
    value_part = features[:, 2].astype(jnp.float32)
    gated_in = (key_part * value_part).astype(jnp.bfloat16)
    slope_in = (cotangent.astype(jnp.float32) * query_f).astype(jnp.bfloat16)
    length = tokens.shape[0] * lax.axis_size("ctx")
    tables = make_tables(length)
    basis_all, taps_full = filter_basis(residues[0], decay_rates[0], length)
    taps_re, taps_im = spectrum(taps_full, tables, precise)
    gated_cols = lax.all_to_all(gated_in, "ctx", split_axis=0, concat_axis=1, tiled=True)
    conv_cols, gated_re, gated_im = forward_cols(gated_cols, taps_re, taps_im, tables)
    conv_rows = lax.all_to_all(conv_cols, "ctx", split_axis=1, concat_axis=0, tiled=True)
    slope_cols = lax.all_to_all(slope_in, "ctx", split_axis=0, concat_axis=1, tiled=True)
    back_cols, grad_residue = backward_cols(
        slope_cols, gated_re, gated_im, taps_re, taps_im, basis_all, tables, length
    )
    back_rows = lax.all_to_all(back_cols, "ctx", split_axis=1, concat_axis=0, tiled=True)
    conv_f = conv_rows.astype(jnp.float32)
    back_f = back_rows.astype(jnp.float32)
    hyena_out = (query_f * conv_f).astype(jnp.bfloat16)
    grad_query = (cotangent.astype(jnp.float32) * conv_f).astype(jnp.bfloat16)
    grad_key = (back_f * value_part).astype(jnp.bfloat16)
    grad_value = (back_f * key_part).astype(jnp.bfloat16)
    grad_proj = jnp.stack([grad_query, grad_key, grad_value], axis=1)
    partial_value = jnp.einsum(
        "cpt,cpd->td", grad_proj, gathered[0], preferred_element_type=jnp.float32
    )
    grad_input = lax.psum_scatter(
        partial_value.astype(jnp.bfloat16), "tp", scatter_dimension=1, tiled=True
    )
    return (hyena_out, grad_input, grad_residue[None])


GROUP = 4
ROWS = 8
PLANE = 4
VMEM = 56 * 2**20


def rounded(value):
    return value.astype(jnp.bfloat16).astype(jnp.float32)


def added_up(parts):
    return functools.reduce(operator.add, parts)


def earlier_sum(finals, rate, span, back):
    count = finals.shape[0]
    row = lax.broadcasted_iota(jnp.int32, finals.shape, 0)

    def shifted(value, by):
        if back:
            moved = pltpu.roll(value, count - by, 0)
            return jnp.where(row < count - by, moved, 0.0)
        moved = pltpu.roll(value, by, 0)
        return jnp.where(row >= by, moved, 0.0)

    total = shifted(finals, 1)
    by = 1
    while by < count:
        total = total + jnp.exp(rate * (-1.0 * span * by)) * shifted(total, by)
        by *= 2
    return total


def scan_kernel(
    groups,
    runs,
    order,
    me_ref,
    residue_ref,
    rate_ref,
    *refs,
):
    inputs = 1 + max(run[0] for run in runs)
    arrays, refs = refs[: 2 * inputs + 1], refs[2 * inputs + 1 :]
    hyena_ref, grad_ref = refs[:2]
    proj_refs, refs = refs[2 : 2 + len(order)], refs[2 + len(order) :]
    gated_s, slope_s, conv_s, back_s, feats_s = refs
    cot_ref, own, other = arrays[0], arrays[1 : 1 + inputs], arrays[1 + inputs :]
    length, width = cot_ref.shape
    chunks = PLANE * groups
    span = length // chunks
    modes = rate_ref.shape[0]
    me = me_ref[0]

    def place(group, member):
        return lax.rem(me // PLANE + group, groups) * PLANE + (member ^ lax.rem(me, PLANE))

    def aligned(start, size):
        return pl.ds(pl.multiple_of(start, size), size)

    for source, offset, group, base, members, count, first in runs:

        def before(step, _, source=source, offset=offset, group=group, base=base, count=count, first=first):
            member = base + step
            index = place(group, member)
            rows = pl.ds(pl.multiple_of(offset + step * count, 16), count)
            feats = widened(own[source][rows, :]) + widened(other[source][rows, :])
            feats = rounded(feats)
            slot = (group * PLANE + member) * span + first
            feats_s[pl.ds(pl.multiple_of(slot, 16), count), :] = feats
            cot = cot_ref[pl.ds(pl.multiple_of(index * span + first, 16), count), :]
            query, key = feats[:, :width], feats[:, width : 2 * width]
            into = pl.ds(first * chunks + index, count, stride=chunks)
            gated_s[into, :] = rounded(key * feats[:, 2 * width :])
            slope_s[into, :] = rounded(cot.astype(jnp.float32) * query)
            return 0

        lax.fori_loop(0, members, before, 0)

    sides = range(chunks // ROWS)
    scale = 1.0 / math.sqrt(length)

    def rows_at(step, side):
        return pl.ds(pl.multiple_of(step * chunks + side * ROWS, ROWS), ROWS)

    def zeros(count):
        zero = jnp.zeros((ROWS, width), jnp.float32)
        return tuple((zero,) * len(sides) for _ in range(count))

    def moved_on(states, decays, inputs):
        return tuple(
            tuple(decay * state[side] + inputs[side] for side in sides)
            for decay, state in zip(decays, states)
        )

    def entered(states, rates, back):
        whole = [
            earlier_sum(
                jnp.concatenate(state, axis=0),
                jnp.concatenate([rate] * len(sides), axis=0),
                span,
                back,
            )
            for state, rate in zip(states, rates)
        ]
        return tuple(
            tuple(state[side * ROWS : (side + 1) * ROWS, :] for side in sides) for state in whole
        )

    for first in range(0, modes, GROUP):
        count = min(GROUP, modes - first)
        rates = [
            jnp.broadcast_to(rate_ref[m : m + 1, :], (ROWS, width))
            for m in range(first, first + count)
        ]
        decays = [jnp.exp(-rate) for rate in rates]
        norms = [jnp.sqrt(2.0 * rate) for rate in rates]
        gains = [residue_ref[first + n : first + n + 1, :] * norms[n] for n in range(count)]

        def sums(step, state):
            ahead, behind = state
            gated = [gated_s[rows_at(step, side), :] for side in sides]
            slope = [slope_s[rows_at(span - 1 - step, side), :] for side in sides]
            return moved_on(ahead, decays, gated), moved_on(behind, decays, slope)

        ahead, behind = lax.fori_loop(0, span, sums, (zeros(count), zeros(count)), unroll=16)
        ahead, behind = entered(ahead, rates, False), entered(behind, rates, True)

        def outs(step, state):
            ahead, behind, grads = state
            other = span - 1 - step
            gated = [gated_s[rows_at(step, side), :] for side in sides]
            slope = [slope_s[rows_at(step, side), :] for side in sides]
            slope_back = [slope_s[rows_at(other, side), :] for side in sides]
            ahead = moved_on(ahead, decays, gated)
            behind = moved_on(behind, decays, slope_back)
            grads = tuple(
                tuple(grad[side] + slope[side] * state[side] for side in sides)
                for grad, state in zip(grads, ahead)
            )
            for side in sides:
                conv = added_up(gains[n] * ahead[n][side] for n in range(count))
                back = added_up(gains[n] * behind[n][side] for n in range(count))
                if first:
                    conv = conv + conv_s[rows_at(step, side), :]
                    back = back + back_s[rows_at(other, side), :]
                conv_s[rows_at(step, side), :] = conv
                back_s[rows_at(other, side), :] = back
            return ahead, behind, grads

        _, _, grads = lax.fori_loop(0, span, outs, (ahead, behind, zeros(count)), unroll=8)
        for n in range(count):
            total = jnp.sum(added_up(grads[n]) * norms[n], axis=0, keepdims=True) * scale
            grad_ref[first + n : first + n + 1, :] = total

    for proj_ref, pieces in zip(proj_refs, order):
        start = 0
        for group, base, members in pieces:

            def after(step, _, proj_ref=proj_ref, start=start, group=group, base=base):
                member = base + step
                index = place(group, member)
                feats = feats_s[aligned((group * PLANE + member) * span, span), :]
                query, key = feats[:, :width], feats[:, width : 2 * width]
                cot = cot_ref[aligned(index * span, span), :].astype(jnp.float32)
                conv = rounded(conv_s[pl.ds(index, span, stride=chunks), :])
                back = rounded(back_s[pl.ds(index, span, stride=chunks), :])
                hyena_ref[aligned(index * span, span), :] = narrowed(query * conv)
                rows = aligned(start + step * span, span)
                proj_ref[rows, :width] = narrowed(cot * conv)
                proj_ref[rows, width : 2 * width] = narrowed(back * feats[:, 2 * width :])
                proj_ref[rows, 2 * width :] = narrowed(back * key)
                return 0

            lax.fori_loop(0, members, after, 0)
            start += members * span


def scan_all(me, cot_cols, residue_rows, rate_rows, runs, order, own, other):
    length, width = cot_cols.shape
    span = length // (PLANE * PLANE)
    vmem = pl.BlockSpec(memory_space=pltpu.VMEM)
    arrays = (cot_cols, *own, *other)
    outs = pl.pallas_call(
        functools.partial(scan_kernel, PLANE, runs, order),
        out_shape=(
            jax.ShapeDtypeStruct((length, width), jnp.bfloat16),
            jax.ShapeDtypeStruct(rate_rows.shape, jnp.float32),
        )
        + tuple(
            jax.ShapeDtypeStruct((span * sum(piece[2] for piece in pieces), 3 * width), jnp.bfloat16)
            for pieces in order
        ),
        in_specs=[pl.BlockSpec(memory_space=pltpu.SMEM)] + [vmem] * (2 + len(arrays)),
        out_specs=(vmem,) * (2 + len(order)),
        scratch_shapes=[pltpu.VMEM((length, width), jnp.float32)] * 4
        + [pltpu.VMEM((length, 3 * width), jnp.float32)],
        compiler_params=pltpu.CompilerParams(vmem_limit_bytes=40 * 2**20),
        name="modal_scan",
    )(me, residue_rows, rate_rows, *arrays)
    return outs[0], outs[1], outs[2:]


def swapped(value):
    return lax.ppermute(value, "tp", [(0, 1), (1, 0)])


def over_x(value):
    return lax.ppermute(value, "ctx", [(i, i ^ 1) for i in range(lax.axis_size("ctx"))])


def over_y(value):
    return lax.ppermute(value, "ctx", [(i, i ^ 2) for i in range(lax.axis_size("ctx"))])


def up(value):
    count = lax.axis_size("ctx")
    return lax.ppermute(value, "ctx", [(i, (i + PLANE) % count) for i in range(count)])


def down(value):
    count = lax.axis_size("ctx")
    return lax.ppermute(value, "ctx", [((i + PLANE) % count, i) for i in range(count)])


def stack(*parts):
    return jnp.concatenate(parts, axis=0)


def beside(*parts):
    return jnp.concatenate(parts, axis=1)


def narrowed(value):
    return value.astype(jnp.bfloat16)


def widened(value):
    return value.astype(jnp.float32)


def halves_kernel(plan, core_ref, *refs):
    arrays, outs, arrived = refs[: -1 - len(plan)], refs[-1 - len(plan) : -1], refs[-1]
    copies = []
    for k, (out, (index, count, mine)) in enumerate(zip(outs, plan)):
        half = out.shape[1]
        side = core_ref[0] if mine else 1 - core_ref[0]
        columns = pl.ds(pl.multiple_of(side * half, half), half)
        part = arrays[index].at[pl.ds(0, count), columns]
        copies.append(pltpu.make_async_copy(part, out, arrived.at[k]))
    for copy in copies:
        copy.start()
    for copy in copies:
        copy.wait()


def halves(arrays, *plan):
    core = lax.axis_index("tp").astype(jnp.int32).reshape(1)
    shapes = [(count, arrays[index].shape[1] // 2) for index, count, _ in plan]
    moved = sum(4 * rows * columns for rows, columns in shapes)
    return pl.pallas_call(
        functools.partial(halves_kernel, plan),
        out_shape=tuple(jax.ShapeDtypeStruct(shape, jnp.bfloat16) for shape in shapes),
        in_specs=[pl.BlockSpec(memory_space=pltpu.SMEM)]
        + [pl.BlockSpec(memory_space=pl.ANY)] * len(arrays),
        out_specs=(pl.BlockSpec(memory_space=pltpu.VMEM),) * len(plan),
        scratch_shapes=[pltpu.SemaphoreType.DMA((len(plan),))],
        compiler_params=pltpu.CompilerParams(vmem_limit_bytes=VMEM),
        cost_estimate=pl.CostEstimate(flops=0, bytes_accessed=moved, transcendentals=0),
        name="halves",
    )(core, *arrays)


def assemble_kernel(inputs, plans, *refs):
    arrays, outs = refs[:inputs], refs[inputs:]
    for out, plan in zip(outs, plans):
        for row, col, height, width, sources in plan:
            parts = [
                arrays[index][from_row : from_row + height, from_col : from_col + width]
                for index, from_row, from_col in sources
            ]
            if len(parts) > 1:
                parts = [narrowed(added_up(widened(part) for part in parts))]
            out[row : row + height, col : col + width] = parts[0]


def assemble(arrays, *plans):
    used = sorted({source[0] for plan in plans for piece in plan for source in piece[4]})
    arrays = [arrays[index] for index in used]
    plans = [
        [(*piece[:4], [(used.index(source[0]), *source[1:]) for source in piece[4]]) for piece in plan]
        for plan in plans
    ]
    shapes = [
        (max(p[0] + p[2] for p in plan), max(p[1] + p[3] for p in plan)) for plan in plans
    ]
    moved = sum(2 * rows * cols for rows, cols in shapes)
    vmem = pl.BlockSpec(memory_space=pltpu.VMEM)
    return pl.pallas_call(
        functools.partial(assemble_kernel, len(arrays), plans),
        out_shape=tuple(jax.ShapeDtypeStruct(shape, jnp.bfloat16) for shape in shapes),
        in_specs=[vmem] * len(arrays),
        out_specs=(vmem,) * len(plans),
        compiler_params=pltpu.CompilerParams(vmem_limit_bytes=32 * 2**20),
        cost_estimate=pl.CostEstimate(flops=moved, bytes_accessed=4 * moved, transcendentals=0),
        name="assemble",
    )(*arrays)


def rows_of(*parts):
    plan, start = [], 0
    for index, first, count in parts:
        plan.append((start, count, [(index, first, 0)]))
        start += count
    return plan


def full_width(columns, plan):
    return [(row, 0, count, columns, sources) for row, count, sources in plan]


def columns_of(height, *parts):
    plan, start = [], 0
    for width, sources in parts:
        plan.append((0, start, height, width, sources))
        start += width
    return plan


def all_ways(for_x, for_y, for_above, for_below):
    from_below, from_above = up(for_above), down(for_below)
    got_x, got_y = over_x(for_x), over_y(for_y)
    return lax.optimization_barrier((got_x, got_y, from_below, from_above))


def project(parts, kept, taken):
    rows = stack(*parts)
    own, given = (
        jnp.einsum("td,rd->tr", rows, matrix, preferred_element_type=jnp.float32)
        for matrix in (kept, taken)
    )
    return narrowed(own), swapped(narrowed(given))


def columns_held(rows):
    return lax.all_to_all(rows.T, "ctx", split_axis=1, concat_axis=0, tiled=True)


def gather_groups(tokens, wide, matrices, later):
    span = tokens.shape[0]
    n, m = span * 3 // 4, span // 4
    nh, mh = n // 2, m // 2
    columns = tokens.shape[1]

    def put(arrays, *plans):
        return assemble(arrays, *[full_width(columns, rows_of(*plan)) for plan in plans])

    own_x, own_y, wide_3, wide_1 = all_ways(tokens, tokens, wide, wide)
    first = (tokens, own_x, own_y, wide_3, wide_1)
    members = ((0, n, m), (1, n, m))
    sent = put(
        first,
        ((2, 0, nh), (2, n, mh), (3, 0, n), (4, 0, n)),
        ((1, nh, nh), (1, n + mh, mh), (3, 0, n), (4, 0, n)),
        ((3, 0, nh), *members),
        ((4, nh, nh), *members),
    )
    sent, first = lax.optimization_barrier((sent, first))
    second = all_ways(*sent)
    start = nh + mh
    wide_2 = ((2, 0, nh), (3, 0, nh))
    across = ((0, nh, mh), (1, nh, mh))
    third = all_ways(
        *put(
            (*second, own_y),
            ((1, start, nh), (1, start + n, nh), *wide_2),
            ((0, start + nh, nh), (0, start + n + nh, nh), *wide_2),
            (*across, (4, n, m), (2, nh, m)),
            (*across, (4, n, m), (3, nh + m, m)),
        )
    )
    fourth = all_ways(
        *put(third, ((1, n, nh),), ((0, n + nh, nh),), ((2, 0, m),), ((3, m, m),))
    )
    runs = [
        (0, 0, 0, 0, 3, span, 0),
        (0, 3 * span, 3, 0, 1, n, 0),
        (0, 3 * span + n, 1, 0, 1, n, 0),
    ]
    offset = 0
    for side in range(2):
        runs += [
            (1, offset, 0, 3, 1, nh, side * nh),
            (1, offset + nh, 0, 3, 1, mh, n + side * mh),
            (1, offset + start, 3, 1 + side, 1, n, 0),
            (1, offset + start + n, 1, 1 + side, 1, n, 0),
        ]
        offset += start + 2 * n
    for side in range(2):
        runs += [
            (1, offset, 2, 0, 1, nh, side * nh),
            (1, offset + nh, 3 - 2 * side, 0, 2, m, n),
        ]
        offset += nh + 2 * m
    offset = 0
    for side in range(2):
        runs += [
            (2, offset, 3, 3, 1, nh, side * nh),
            (2, offset + nh, 1, 3, 1, nh, side * nh),
            (2, offset + n, 2, 1 + side, 1, n, 0),
        ]
        offset += 2 * n
    runs += [
        (2, offset, 3, 3, 1, m, n),
        (2, offset + m, 3, 2, 1, m, n),
        (2, offset + 2 * m, 2, 0, 1, m, n),
        (2, offset + 3 * m, 1, 3, 1, m, n),
        (2, offset + 4 * m, 1, 2, 1, m, n),
        (2, offset + 5 * m, 2, 1, 1, m, n),
        (3, 0, 2, 3, 1, nh, 0),
        (3, nh, 2, 3, 1, nh, nh),
        (3, n, 2, 3, 1, m, n),
        (3, n + m, 2, 2, 1, m, n),
    ]
    parts = [project(part, *matrices) for part in (first, second, third, fourth)]
    later, first = lax.optimization_barrier((later, parts[0][0]))
    parts[0] = (first, parts[0][1])
    later = columns_held(later)
    return parts, tuple(runs), matrices, later


ORDER = (((2, 0, 4), (1, 3, 1), (3, 3, 1)), ((1, 0, 3), (3, 0, 3), (0, 3, 1), (0, 0, 3)))


def scatter_sum(early, later, matrix, hyena):
    span = early.shape[0] // 6
    columns = matrix.shape[1]
    wide, narrow = columns * 3 // 8, columns // 8
    places = {}
    for array, pieces in enumerate((ORDER[0], ORDER[1][:3], ORDER[1][3:])):
        row = 0
        for group, base, members in pieces:
            for member in range(base, base + members):
                places[group, member] = (array, row)
                row += span

    def product(part, other):
        both = beside(part, other)
        return narrowed(jnp.dot(both, matrix, preferred_element_type=jnp.float32))

    def term(group, member, side, *more):
        array, row = places[group, member]
        return (wide, [(array, row, side * wide), *more])

    def low(group, member, side, *more):
        array, row = places[group, member]
        return (narrow, [(array, row, 2 * wide + side * narrow), *more])

    def put(arrays, *plans):
        return assemble(arrays, *[columns_of(span, *plan) for plan in plans])

    early = product(early, swapped(early))
    other = swapped(later)
    first = all_ways(
        *put([early], [term(2, 3, 0)], [term(2, 3, 1)], [low(2, 3, 0)], [low(2, 3, 1)])
    )
    later, hyena, first = lax.optimization_barrier((later, hyena, first))
    x, y, below, above = range(1, 5)
    second = all_ways(
        *put(
            [early, *first],
            [term(2, 1, 0), term(2, 1, 1, (y, 0, 0)), term(1, 3, 0), term(3, 3, 0)],
            [term(2, 2, 0, (x, 0, 0)), term(2, 2, 1), term(1, 3, 1), term(3, 3, 1)],
            [low(1, 3, 0, (below, 0, 0)), low(1, 3, 1), *[low(2, k, 0) for k in range(3)]],
            [low(3, 3, 0), low(3, 3, 1, (above, 0, 0)), *[low(2, k, 1) for k in range(3)]],
        )
    )
    own = product(later[7 * span :], other[7 * span :])
    later = product(later[: 7 * span], other[: 7 * span])
    later, second = lax.optimization_barrier((later, second))
    hyena_out = lax.all_to_all(hyena, "ctx", split_axis=0, concat_axis=1, tiled=True).T
    x, y, below, above = range(2, 6)

    def low_3(side):
        return low(0, 3, side, (below, 0, side * narrow), (above, 0, side * narrow))

    def sum_2(side):
        return term(2, 0, side, (x, 0, side * wide), (y, 0, side * wide))

    for_above, for_below = [], []
    for k in range(3):
        start = (2 + k) * narrow
        for_above += [low(1, k, 0, (below, 0, start)), low(1, k, 1)]
        for_below += [low(3, k, 0), low(3, k, 1, (above, 0, start))]
    third = all_ways(
        *put(
            [early, later, *second],
            [
                term(1, 1, 0),
                term(1, 1, 1, (y, 0, 2 * wide)),
                term(3, 1, 0),
                term(3, 1, 1, (y, 0, 3 * wide)),
                term(0, 3, 0),
                low_3(0),
            ],
            [
                term(1, 2, 0, (x, 0, 2 * wide)),
                term(1, 2, 1),
                term(3, 2, 0, (x, 0, 3 * wide)),
                term(3, 2, 1),
                term(0, 3, 1),
                low_3(1),
            ],
            [sum_2(0), *for_above],
            [sum_2(1), *for_below],
        )
    )

    x, y, below, above = range(3, 7)

    def low_own(k, side, *more):
        start = wide + (2 * k + side) * narrow
        return low(0, k, side, (below, 0, start), (above, 0, start), *more)

    def own_sum(group, side, *more):
        start = (group - 1 + side) * wide
        return term(group, 0, side, (x, 0, start), (y, 0, start), *more)

    sent = put(
        [early, later, own, *third],
            [
                term(0, 1, 0),
                term(0, 1, 1, (y, 0, 4 * wide)),
                low_own(1, 0),
                low_own(1, 1, (y, 0, 5 * wide)),
            ],
            [
                term(0, 2, 0, (x, 0, 4 * wide)),
                term(0, 2, 1),
                low_own(2, 0, (x, 0, 5 * wide)),
                low_own(2, 1),
            ],
            [own_sum(1, 0, (below, 0, 0)), own_sum(1, 1)],
            [own_sum(3, 0), own_sum(3, 1, (above, 0, 0))],
    )
    (base,) = put(
        [early, later, own, *third],
        [term(0, 0, 0), term(0, 0, 1), low_own(0, 0), low_own(0, 1)],
    )
    (grad_input,) = put(
        [base, *all_ways(*sent)],
        [
            (2 * wide, [(way, 0, 0) for way in range(5)]),
            (2 * narrow, [(way, 0, 2 * wide) for way in range(3)]),
        ],
    )
    return grad_input, hyena_out


def gather_tokens(tokens, weights, residues, decay_rates, cotangent):
    me = lax.axis_index("ctx").astype(jnp.int32).reshape(1)
    channels, span = weights.shape[1], tokens.shape[0]
    rows = weights[0].swapaxes(0, 1).reshape(3 * channels, weights.shape[3])
    tokens_half = halves((tokens,), (0, span, True), (0, span * 3 // 4, True))
    kept, given = halves((rows,), (0, 3 * channels, True), (0, 3 * channels, False))
    count, columns = given.shape
    (taken,) = assemble([swapped(given)], [(0, 0, count, columns, [(0, 0, 0)])])
    parts, runs, (kept, taken), cot_cols = gather_groups(*tokens_half, (kept, taken), cotangent)
    own, other = zip(*parts)
    hyena, grads, (early, later) = scan_all(
        me, cot_cols, residues[0].T, decay_rates[0].T, runs, ORDER, own, other
    )
    grad_input, hyena_out = scatter_sum(early, later, stack(kept, taken), hyena)
    return (hyena_out, grad_input, grads.T[None])


def shards(tokens, weights, residues, decay_rates, cotangent):
    ctx, tp = lax.axis_size("ctx"), lax.axis_size("tp")
    if ctx == 4 * PLANE and tp == 2 and weights.size * tp > 2 * tokens.size:
        return gather_tokens(tokens, weights, residues, decay_rates, cotangent)
    return gather_weights(tokens, weights, residues, decay_rates, cotangent)


def solution(mesh):
    return jax.shard_map(
        shards,
        mesh=mesh,
        in_specs=(
            P("ctx", None),
            P("tp", "ctx", None, None),
            P("tp", "ctx", None),
            P("tp", "ctx", None),
            P("tp", "ctx"),
        ),
        out_specs=(P("tp", "ctx"), P("ctx", "tp"), P("tp", "ctx", None)),
        check_vma=False,
    )
```

```python
import functools
import math
import operator

import jax
import jax.numpy as jnp
from jax import lax
from jax.experimental import pallas as pl
from jax.experimental.pallas import tpu as pltpu
from jax.sharding import PartitionSpec as P


def precise(form, left, right):
    return jnp.einsum(
        form, left, right, precision=lax.Precision.HIGHEST, preferred_element_type=jnp.float32
    )


def tripled(form, left, right):
    return jnp.einsum(
        form, left, right, precision=lax.Precision.HIGH, preferred_element_type=jnp.float32
    )


def angle_table(row_count, col_count, period):
    product = (
        jnp.arange(row_count, dtype=jnp.int32)[:, None]
        * jnp.arange(col_count, dtype=jnp.int32)[None, :]
        % period
    )
    angles = product.astype(jnp.float32) * (2.0 * math.pi / period)
    return (jnp.cos(angles), jnp.sin(angles))


def make_tables(length):
    padded = 2 * length
    outer = math.gcd(padded, 1 << (padded.bit_length() - 1) // 2)
    inner = padded // outer
    cos_outer, sin_outer = angle_table(outer, outer, outer)
    cos_inner, sin_inner = angle_table(inner, inner, inner)
    twist_cos, twist_sin = angle_table(outer, inner, padded)
    return (outer, inner, cos_outer, sin_outer, cos_inner, sin_inner, twist_cos, twist_sin)


def spectrum(signal, tables, product):
    outer, inner, cos_outer, sin_outer, cos_inner, sin_inner, twist_cos, twist_sin = tables
    half_rows = outer // 2
    blocks = signal.reshape(signal.shape[0], half_rows, inner)
    first_re = product("kp,bpq->bkq", cos_outer[:, :half_rows], blocks)
    first_im = -product("kp,bpq->bkq", sin_outer[:, :half_rows], blocks)
    turned_re = first_re * twist_cos + first_im * twist_sin
    turned_im = first_im * twist_cos - first_re * twist_sin
    spec_re = product("bkq,qj->bkj", turned_re, cos_inner) + product(
        "bkq,qj->bkj", turned_im, sin_inner
    )
    spec_im = product("bkq,qj->bkj", turned_im, cos_inner) - product(
        "bkq,qj->bkj", turned_re, sin_inner
    )
    return (spec_re, spec_im)


def signal_of(spec_re, spec_im, tables):
    outer, inner, cos_outer, sin_outer, cos_inner, sin_inner, twist_cos, twist_sin = tables
    half_rows = outer // 2
    back_re = tripled("bkj,jq->bkq", spec_re, cos_inner) - tripled(
        "bkj,jq->bkq", spec_im, sin_inner
    )
    back_im = tripled("bkj,jq->bkq", spec_im, cos_inner) + tripled(
        "bkj,jq->bkq", spec_re, sin_inner
    )
    turned_re = back_re * twist_cos - back_im * twist_sin
    turned_im = back_im * twist_cos + back_re * twist_sin
    values = tripled("pk,bkq->bpq", cos_outer[:half_rows, :], turned_re) - tripled(
        "pk,bkq->bpq", sin_outer[:half_rows, :], turned_im
    )
    return values.reshape(values.shape[0], half_rows * inner) * (1.0 / (outer * inner))


def spec_product(left_re, left_im, right_re, right_im):
    return (left_re * right_re - left_im * right_im, left_re * right_im + left_im * right_re)


def conj_product(left_re, left_im, right_re, right_im):
    return (left_re * right_re + left_im * right_im, left_re * right_im - left_im * right_re)


def filter_basis(residue_loc, rate_loc, length):
    position = jnp.arange(length, dtype=jnp.float32)
    basis_all = jnp.sqrt(2.0 * rate_loc)[:, :, None] * jnp.exp(
        -rate_loc[:, :, None] * position[None, None, :]
    )
    return (basis_all, precise("cm,cmt->ct", residue_loc, basis_all))


def forward_cols(gated_cols, taps_re, taps_im, tables):
    gated_re, gated_im = spectrum(gated_cols.astype(jnp.float32), tables, tripled)
    conv_re, conv_im = spec_product(gated_re, gated_im, taps_re, taps_im)
    conv_cols = signal_of(conv_re, conv_im, tables).astype(jnp.bfloat16)
    return (conv_cols, gated_re, gated_im)


def backward_cols(slope_cols, gated_re, gated_im, taps_re, taps_im, basis_all, tables, length):
    slope_re, slope_im = spectrum(slope_cols.astype(jnp.float32), tables, tripled)
    grad_re, grad_im = conj_product(taps_re, taps_im, slope_re, slope_im)
    back_cols = signal_of(grad_re, grad_im, tables).astype(jnp.bfloat16)
    lag_re, lag_im = conj_product(gated_re, gated_im, slope_re, slope_im)
    taps_grad = signal_of(lag_re, lag_im, tables)
    grad_residue = precise("ct,cmt->cm", taps_grad, basis_all) * (1.0 / math.sqrt(length))
    return (back_cols, grad_residue)


def gather_weights(tokens, weights, residues, decay_rates, cotangent):
    gathered = lax.all_gather(weights, "ctx", axis=1, tiled=True)
    projected = jnp.einsum("xcpd,td->xcpt", gathered, tokens, preferred_element_type=jnp.float32)
    features = projected[0].astype(jnp.bfloat16)
    query_f = features[:, 0].astype(jnp.float32)
    key_part = features[:, 1].astype(jnp.float32)
    value_part = features[:, 2].astype(jnp.float32)
    gated_in = (key_part * value_part).astype(jnp.bfloat16)
    slope_in = (cotangent.astype(jnp.float32) * query_f).astype(jnp.bfloat16)
    length = tokens.shape[0] * lax.axis_size("ctx")
    tables = make_tables(length)
    basis_all, taps_full = filter_basis(residues[0], decay_rates[0], length)
    taps_re, taps_im = spectrum(taps_full, tables, precise)
    gated_cols = lax.all_to_all(gated_in, "ctx", split_axis=0, concat_axis=1, tiled=True)
    conv_cols, gated_re, gated_im = forward_cols(gated_cols, taps_re, taps_im, tables)
    conv_rows = lax.all_to_all(conv_cols, "ctx", split_axis=1, concat_axis=0, tiled=True)
    slope_cols = lax.all_to_all(slope_in, "ctx", split_axis=0, concat_axis=1, tiled=True)
    back_cols, grad_residue = backward_cols(
        slope_cols, gated_re, gated_im, taps_re, taps_im, basis_all, tables, length
    )
    back_rows = lax.all_to_all(back_cols, "ctx", split_axis=1, concat_axis=0, tiled=True)
    conv_f = conv_rows.astype(jnp.float32)
    back_f = back_rows.astype(jnp.float32)
    hyena_out = (query_f * conv_f).astype(jnp.bfloat16)
    grad_query = (cotangent.astype(jnp.float32) * conv_f).astype(jnp.bfloat16)
    grad_key = (back_f * value_part).astype(jnp.bfloat16)
    grad_value = (back_f * key_part).astype(jnp.bfloat16)
    grad_proj = jnp.stack([grad_query, grad_key, grad_value], axis=1)
    partial_value = jnp.einsum(
        "cpt,cpd->td", grad_proj, gathered[0], preferred_element_type=jnp.float32
    )
    grad_input = lax.psum_scatter(
        partial_value.astype(jnp.bfloat16), "tp", scatter_dimension=1, tiled=True
    )
    return (hyena_out, grad_input, grad_residue[None])


GROUP = 4
ROWS = 8
PLANE = 4
VMEM = 56 * 2**20


def rounded(value):
    return value.astype(jnp.bfloat16).astype(jnp.float32)


def added_up(parts):
    return functools.reduce(operator.add, parts)


def earlier_sum(finals, rate, span, back):
    count = finals.shape[0]
    row = lax.broadcasted_iota(jnp.int32, finals.shape, 0)

    def shifted(value, by):
        if back:
            moved = pltpu.roll(value, count - by, 0)
            return jnp.where(row < count - by, moved, 0.0)
        moved = pltpu.roll(value, by, 0)
        return jnp.where(row >= by, moved, 0.0)

    total = shifted(finals, 1)
    by = 1
    while by < count:
        total = total + jnp.exp(rate * (-1.0 * span * by)) * shifted(total, by)
        by *= 2
    return total


def scan_kernel(
    groups,
    runs,
    order,
    me_ref,
    residue_ref,
    rate_ref,
    *refs,
):
    inputs = 1 + max(run[0] for run in runs)
    arrays, refs = refs[: 2 * inputs + 1], refs[2 * inputs + 1 :]
    hyena_ref, grad_ref = refs[:2]
    proj_refs, refs = refs[2 : 2 + len(order)], refs[2 + len(order) :]
    gated_s, slope_s, conv_s, back_s, feats_s = refs
    cot_ref, own, other = arrays[0], arrays[1 : 1 + inputs], arrays[1 + inputs :]
    length, width = cot_ref.shape
    chunks = PLANE * groups
    span = length // chunks
    modes = rate_ref.shape[0]
    me = me_ref[0]

    def place(group, member):
        return lax.rem(me // PLANE + group, groups) * PLANE + (member ^ lax.rem(me, PLANE))

    def aligned(start, size):
        return pl.ds(pl.multiple_of(start, size), size)

    for source, offset, group, base, members, count, first in runs:

        def before(step, _, source=source, offset=offset, group=group, base=base, count=count, first=first):
            member = base + step
            index = place(group, member)
            rows = pl.ds(pl.multiple_of(offset + step * count, 16), count)
            feats = own[source][rows, :] + other[source][rows, :].astype(jnp.float32)
            feats = rounded(feats)
            slot = (group * PLANE + member) * span + first
            feats_s[pl.ds(pl.multiple_of(slot, 16), count), :] = feats
            cot = cot_ref[pl.ds(pl.multiple_of(index * span + first, 16), count), :]
            query, key = feats[:, :width], feats[:, width : 2 * width]
            into = pl.ds(first * chunks + index, count, stride=chunks)
            gated_s[into, :] = rounded(key * feats[:, 2 * width :])
            slope_s[into, :] = rounded(cot.astype(jnp.float32) * query)
            return 0

        lax.fori_loop(0, members, before, 0)

    sides = range(chunks // ROWS)
    scale = 1.0 / math.sqrt(length)

    def rows_at(step, side):
        return pl.ds(pl.multiple_of(step * chunks + side * ROWS, ROWS), ROWS)

    def zeros(count):
        zero = jnp.zeros((ROWS, width), jnp.float32)
        return tuple((zero,) * len(sides) for _ in range(count))

    def moved_on(states, decays, inputs):
        return tuple(
            tuple(decay * state[side] + inputs[side] for side in sides)
            for decay, state in zip(decays, states)
        )

    def entered(states, rates, back):
        whole = [
            earlier_sum(
                jnp.concatenate(state, axis=0),
                jnp.concatenate([rate] * len(sides), axis=0),
                span,
                back,
            )
            for state, rate in zip(states, rates)
        ]
        return tuple(
            tuple(state[side * ROWS : (side + 1) * ROWS, :] for side in sides) for state in whole
        )

    for first in range(0, modes, GROUP):
        count = min(GROUP, modes - first)
        rates = [
            jnp.broadcast_to(rate_ref[m : m + 1, :], (ROWS, width))
            for m in range(first, first + count)
        ]
        decays = [jnp.exp(-rate) for rate in rates]
        norms = [jnp.sqrt(2.0 * rate) for rate in rates]
        gains = [residue_ref[first + n : first + n + 1, :] * norms[n] for n in range(count)]

        def sums(step, state):
            ahead, behind = state
            gated = [gated_s[rows_at(step, side), :] for side in sides]
            slope = [slope_s[rows_at(span - 1 - step, side), :] for side in sides]
            return moved_on(ahead, decays, gated), moved_on(behind, decays, slope)

        ahead, behind = lax.fori_loop(0, span, sums, (zeros(count), zeros(count)), unroll=16)
        ahead, behind = entered(ahead, rates, False), entered(behind, rates, True)

        def outs(step, state):
            ahead, behind, grads = state
            other = span - 1 - step
            gated = [gated_s[rows_at(step, side), :] for side in sides]
            slope = [slope_s[rows_at(step, side), :] for side in sides]
            slope_back = [slope_s[rows_at(other, side), :] for side in sides]
            ahead = moved_on(ahead, decays, gated)
            behind = moved_on(behind, decays, slope_back)
            grads = tuple(
                tuple(grad[side] + slope[side] * state[side] for side in sides)
                for grad, state in zip(grads, ahead)
            )
            for side in sides:
                conv = added_up(gains[n] * ahead[n][side] for n in range(count))
                back = added_up(gains[n] * behind[n][side] for n in range(count))
                if first:
                    conv = conv + conv_s[rows_at(step, side), :]
                    back = back + back_s[rows_at(other, side), :]
                conv_s[rows_at(step, side), :] = conv
                back_s[rows_at(other, side), :] = back
            return ahead, behind, grads

        _, _, grads = lax.fori_loop(0, span, outs, (ahead, behind, zeros(count)), unroll=8)
        for n in range(count):
            total = jnp.sum(added_up(grads[n]) * norms[n], axis=0, keepdims=True) * scale
            grad_ref[first + n : first + n + 1, :] = total

    for proj_ref, pieces in zip(proj_refs, order):
        start = 0
        for group, base, members in pieces:

            def after(step, _, proj_ref=proj_ref, start=start, group=group, base=base):
                member = base + step
                index = place(group, member)
                feats = feats_s[aligned((group * PLANE + member) * span, span), :]
                query, key = feats[:, :width], feats[:, width : 2 * width]
                cot = cot_ref[aligned(index * span, span), :].astype(jnp.float32)
                conv = rounded(conv_s[pl.ds(index, span, stride=chunks), :])
                back = rounded(back_s[pl.ds(index, span, stride=chunks), :])
                hyena_ref[aligned(index * span, span), :] = narrowed(query * conv)
                rows = aligned(start + step * span, span)
                proj_ref[rows, :width] = narrowed(cot * conv)
                proj_ref[rows, width : 2 * width] = narrowed(back * feats[:, 2 * width :])
                proj_ref[rows, 2 * width :] = narrowed(back * key)
                return 0

            lax.fori_loop(0, members, after, 0)
            start += members * span


def scan_all(me, cot_cols, residue_rows, rate_rows, runs, order, own, other):
    length, width = cot_cols.shape
    span = length // (PLANE * PLANE)
    vmem = pl.BlockSpec(memory_space=pltpu.VMEM)
    arrays = (cot_cols, *own, *other)
    outs = pl.pallas_call(
        functools.partial(scan_kernel, PLANE, runs, order),
        out_shape=(
            jax.ShapeDtypeStruct((length, width), jnp.bfloat16),
            jax.ShapeDtypeStruct(rate_rows.shape, jnp.float32),
        )
        + tuple(
            jax.ShapeDtypeStruct((span * sum(piece[2] for piece in pieces), 3 * width), jnp.bfloat16)
            for pieces in order
        ),
        in_specs=[pl.BlockSpec(memory_space=pltpu.SMEM)] + [vmem] * (2 + len(arrays)),
        out_specs=(vmem,) * (2 + len(order)),
        scratch_shapes=[pltpu.VMEM((length, width), jnp.float32)] * 4
        + [pltpu.VMEM((length, 3 * width), jnp.float32)],
        compiler_params=pltpu.CompilerParams(vmem_limit_bytes=24 * 2**20),
        name="modal_scan",
    )(me, residue_rows, rate_rows, *arrays)
    return outs[0], outs[1], outs[2:]


def swapped(value):
    return lax.ppermute(value, "tp", [(0, 1), (1, 0)])


def over_x(value):
    return lax.ppermute(value, "ctx", [(i, i ^ 1) for i in range(lax.axis_size("ctx"))])


def over_y(value):
    return lax.ppermute(value, "ctx", [(i, i ^ 2) for i in range(lax.axis_size("ctx"))])


def up(value):
    count = lax.axis_size("ctx")
    return lax.ppermute(value, "ctx", [(i, (i + PLANE) % count) for i in range(count)])


def down(value):
    count = lax.axis_size("ctx")
    return lax.ppermute(value, "ctx", [((i + PLANE) % count, i) for i in range(count)])


def stack(*parts):
    return jnp.concatenate(parts, axis=0)


def beside(*parts):
    return jnp.concatenate(parts, axis=1)


def narrowed(value):
    return value.astype(jnp.bfloat16)


def widened(value):
    return value.astype(jnp.float32)


def halves_kernel(plan, core_ref, *refs):
    arrays, outs, arrived = refs[: -1 - len(plan)], refs[-1 - len(plan) : -1], refs[-1]
    copies = []
    for k, (out, (index, count, mine)) in enumerate(zip(outs, plan)):
        half = out.shape[1]
        side = core_ref[0] if mine else 1 - core_ref[0]
        columns = pl.ds(pl.multiple_of(side * half, half), half)
        part = arrays[index].at[pl.ds(0, count), columns]
        copies.append(pltpu.make_async_copy(part, out, arrived.at[k]))
    for copy in copies:
        copy.start()
    for copy in copies:
        copy.wait()


def halves(arrays, *plan):
    core = lax.axis_index("tp").astype(jnp.int32).reshape(1)
    shapes = [(count, arrays[index].shape[1] // 2) for index, count, _ in plan]
    moved = sum(4 * rows * columns for rows, columns in shapes)
    return pl.pallas_call(
        functools.partial(halves_kernel, plan),
        out_shape=tuple(jax.ShapeDtypeStruct(shape, jnp.bfloat16) for shape in shapes),
        in_specs=[pl.BlockSpec(memory_space=pltpu.SMEM)]
        + [pl.BlockSpec(memory_space=pl.ANY)] * len(arrays),
        out_specs=(pl.BlockSpec(memory_space=pltpu.VMEM),) * len(plan),
        scratch_shapes=[pltpu.SemaphoreType.DMA((len(plan),))],
        compiler_params=pltpu.CompilerParams(vmem_limit_bytes=VMEM),
        cost_estimate=pl.CostEstimate(flops=0, bytes_accessed=moved, transcendentals=0),
        name="halves",
    )(core, *arrays)


def assemble_kernel(inputs, plans, *refs):
    arrays, outs = refs[:inputs], refs[inputs:]
    for out, plan in zip(outs, plans):
        for row, col, height, width, sources in plan:
            parts = [
                arrays[index][from_row : from_row + height, from_col : from_col + width]
                for index, from_row, from_col in sources
            ]
            if len(parts) > 1:
                parts = [narrowed(added_up(widened(part) for part in parts))]
            out[row : row + height, col : col + width] = parts[0]


def assemble(arrays, *plans):
    used = sorted({source[0] for plan in plans for piece in plan for source in piece[4]})
    arrays = [arrays[index] for index in used]
    plans = [
        [(*piece[:4], [(used.index(source[0]), *source[1:]) for source in piece[4]]) for piece in plan]
        for plan in plans
    ]
    shapes = [
        (max(p[0] + p[2] for p in plan), max(p[1] + p[3] for p in plan)) for plan in plans
    ]
    moved = sum(2 * rows * cols for rows, cols in shapes)
    vmem = pl.BlockSpec(memory_space=pltpu.VMEM)
    return pl.pallas_call(
        functools.partial(assemble_kernel, len(arrays), plans),
        out_shape=tuple(jax.ShapeDtypeStruct(shape, jnp.bfloat16) for shape in shapes),
        in_specs=[vmem] * len(arrays),
        out_specs=(vmem,) * len(plans),
        compiler_params=pltpu.CompilerParams(vmem_limit_bytes=32 * 2**20),
        cost_estimate=pl.CostEstimate(flops=moved, bytes_accessed=4 * moved, transcendentals=0),
        name="assemble",
    )(*arrays)


def rows_of(*parts):
    plan, start = [], 0
    for index, first, count in parts:
        plan.append((start, count, [(index, first, 0)]))
        start += count
    return plan


def full_width(columns, plan):
    return [(row, 0, count, columns, sources) for row, count, sources in plan]


def columns_of(height, *parts):
    plan, start = [], 0
    for width, sources in parts:
        plan.append((0, start, height, width, sources))
        start += width
    return plan


def all_ways(for_x, for_y, for_above, for_below):
    from_below, from_above = up(for_above), down(for_below)
    got_x, got_y = over_x(for_x), over_y(for_y)
    return lax.optimization_barrier((got_x, got_y, from_below, from_above))


def project(parts, kept, taken):
    rows = stack(*parts)
    own, given = (
        jnp.einsum("td,rd->tr", rows, matrix, preferred_element_type=jnp.float32)
        for matrix in (kept, taken)
    )
    return own, swapped(narrowed(given))


def columns_held(rows):
    return lax.all_to_all(rows.T, "ctx", split_axis=1, concat_axis=0, tiled=True)


def gather_groups(tokens, wide, matrices, later):
    span = tokens.shape[0]
    n, m = span * 3 // 4, span // 4
    nh, mh = n // 2, m // 2
    columns = tokens.shape[1]

    def put(arrays, *plans):
        return assemble(arrays, *[full_width(columns, rows_of(*plan)) for plan in plans])

    own_x, own_y, wide_3, wide_1 = all_ways(tokens, tokens, wide, wide)
    first = (tokens, own_x, own_y, wide_3, wide_1)
    members = ((0, n, m), (1, n, m))
    sent = put(
        first,
        ((2, 0, nh), (2, n, mh), (3, 0, n), (4, 0, n)),
        ((1, nh, nh), (1, n + mh, mh), (3, 0, n), (4, 0, n)),
        ((3, 0, nh), *members),
        ((4, nh, nh), *members),
    )
    sent, first = lax.optimization_barrier((sent, first))
    second = all_ways(*sent)
    start = nh + mh
    wide_2 = ((2, 0, nh), (3, 0, nh))
    across = ((0, nh, mh), (1, nh, mh))
    third = all_ways(
        *put(
            (*second, own_y),
            ((1, start, nh), (1, start + n, nh), *wide_2),
            ((0, start + nh, nh), (0, start + n + nh, nh), *wide_2),
            (*across, (4, n, m), (2, nh, m)),
            (*across, (4, n, m), (3, nh + m, m)),
        )
    )
    fourth = all_ways(
        *put(third, ((1, n, nh),), ((0, n + nh, nh),), ((2, 0, m),), ((3, m, m),))
    )
    runs = [
        (0, 0, 0, 0, 3, span, 0),
        (0, 3 * span, 3, 0, 1, n, 0),
        (0, 3 * span + n, 1, 0, 1, n, 0),
    ]
    offset = 0
    for side in range(2):
        runs += [
            (1, offset, 0, 3, 1, nh, side * nh),
            (1, offset + nh, 0, 3, 1, mh, n + side * mh),
            (1, offset + start, 3, 1 + side, 1, n, 0),
            (1, offset + start + n, 1, 1 + side, 1, n, 0),
        ]
        offset += start + 2 * n
    for side in range(2):
        runs += [
            (1, offset, 2, 0, 1, nh, side * nh),
            (1, offset + nh, 3 - 2 * side, 0, 2, m, n),
        ]
        offset += nh + 2 * m
    offset = 0
    for side in range(2):
        runs += [
            (2, offset, 3, 3, 1, nh, side * nh),
            (2, offset + nh, 1, 3, 1, nh, side * nh),
            (2, offset + n, 2, 1 + side, 1, n, 0),
        ]
        offset += 2 * n
    runs += [
        (2, offset, 3, 3, 1, m, n),
        (2, offset + m, 3, 2, 1, m, n),
        (2, offset + 2 * m, 2, 0, 1, m, n),
        (2, offset + 3 * m, 1, 3, 1, m, n),
        (2, offset + 4 * m, 1, 2, 1, m, n),
        (2, offset + 5 * m, 2, 1, 1, m, n),
        (3, 0, 2, 3, 1, nh, 0),
        (3, nh, 2, 3, 1, nh, nh),
        (3, n, 2, 3, 1, m, n),
        (3, n + m, 2, 2, 1, m, n),
    ]
    parts = [project(part, *matrices) for part in (first, second, third, fourth)]
    later, first = lax.optimization_barrier((later, parts[0][0]))
    parts[0] = (first, parts[0][1])
    later = columns_held(later)
    return parts, tuple(runs), matrices, later


ORDER = (((2, 0, 4), (1, 3, 1), (3, 3, 1)), ((1, 0, 3), (3, 0, 3), (0, 3, 1), (0, 0, 3)))


def scatter_sum(early, later, matrix, hyena):
    span = early.shape[0] // 6
    columns = matrix.shape[1]
    wide, narrow = columns * 3 // 8, columns // 8
    places = {}
    for array, pieces in enumerate((ORDER[0], ORDER[1][:3], ORDER[1][3:])):
        row = 0
        for group, base, members in pieces:
            for member in range(base, base + members):
                places[group, member] = (array, row)
                row += span

    def product(part, other):
        both = beside(part, other)
        return narrowed(jnp.dot(both, matrix, preferred_element_type=jnp.float32))

    def term(group, member, side, *more):
        array, row = places[group, member]
        return (wide, [(array, row, side * wide), *more])

    def low(group, member, side, *more):
        array, row = places[group, member]
        return (narrow, [(array, row, 2 * wide + side * narrow), *more])

    def put(arrays, *plans):
        return assemble(arrays, *[columns_of(span, *plan) for plan in plans])

    early = product(early, swapped(early))
    other = swapped(later)
    first = all_ways(
        *put([early], [term(2, 3, 0)], [term(2, 3, 1)], [low(2, 3, 0)], [low(2, 3, 1)])
    )
    later, hyena, first = lax.optimization_barrier((later, hyena, first))
    x, y, below, above = range(1, 5)
    second = all_ways(
        *put(
            [early, *first],
            [term(2, 1, 0), term(2, 1, 1, (y, 0, 0)), term(1, 3, 0), term(3, 3, 0)],
            [term(2, 2, 0, (x, 0, 0)), term(2, 2, 1), term(1, 3, 1), term(3, 3, 1)],
            [low(1, 3, 0, (below, 0, 0)), low(1, 3, 1), *[low(2, k, 0) for k in range(3)]],
            [low(3, 3, 0), low(3, 3, 1, (above, 0, 0)), *[low(2, k, 1) for k in range(3)]],
        )
    )
    own = product(later[7 * span :], other[7 * span :])
    later = product(later[: 7 * span], other[: 7 * span])
    later, second = lax.optimization_barrier((later, second))
    hyena_out = lax.all_to_all(hyena, "ctx", split_axis=0, concat_axis=1, tiled=True).T
    x, y, below, above = range(2, 6)

    def low_3(side):
        return low(0, 3, side, (below, 0, side * narrow), (above, 0, side * narrow))

    def sum_2(side):
        return term(2, 0, side, (x, 0, side * wide), (y, 0, side * wide))

    for_above, for_below = [], []
    for k in range(3):
        start = (2 + k) * narrow
        for_above += [low(1, k, 0, (below, 0, start)), low(1, k, 1)]
        for_below += [low(3, k, 0), low(3, k, 1, (above, 0, start))]
    third = all_ways(
        *put(
            [early, later, *second],
            [
                term(1, 1, 0),
                term(1, 1, 1, (y, 0, 2 * wide)),
                term(3, 1, 0),
                term(3, 1, 1, (y, 0, 3 * wide)),
                term(0, 3, 0),
                low_3(0),
            ],
            [
                term(1, 2, 0, (x, 0, 2 * wide)),
                term(1, 2, 1),
                term(3, 2, 0, (x, 0, 3 * wide)),
                term(3, 2, 1),
                term(0, 3, 1),
                low_3(1),
            ],
            [sum_2(0), *for_above],
            [sum_2(1), *for_below],
        )
    )

    x, y, below, above = range(3, 7)

    def low_own(k, side, *more):
        start = wide + (2 * k + side) * narrow
        return low(0, k, side, (below, 0, start), (above, 0, start), *more)

    def own_sum(group, side, *more):
        start = (group - 1 + side) * wide
        return term(group, 0, side, (x, 0, start), (y, 0, start), *more)

    sent = put(
        [early, later, own, *third],
            [
                term(0, 1, 0),
                term(0, 1, 1, (y, 0, 4 * wide)),
                low_own(1, 0),
                low_own(1, 1, (y, 0, 5 * wide)),
            ],
            [
                term(0, 2, 0, (x, 0, 4 * wide)),
                term(0, 2, 1),
                low_own(2, 0, (x, 0, 5 * wide)),
                low_own(2, 1),
            ],
            [own_sum(1, 0, (below, 0, 0)), own_sum(1, 1)],
            [own_sum(3, 0), own_sum(3, 1, (above, 0, 0))],
    )
    (base,) = put(
        [early, later, own, *third],
        [term(0, 0, 0), term(0, 0, 1), low_own(0, 0), low_own(0, 1)],
    )
    (grad_input,) = put(
        [base, *all_ways(*sent)],
        [
            (2 * wide, [(way, 0, 0) for way in range(5)]),
            (2 * narrow, [(way, 0, 2 * wide) for way in range(3)]),
        ],
    )
    return grad_input, hyena_out


def gather_tokens(tokens, weights, residues, decay_rates, cotangent):
    me = lax.axis_index("ctx").astype(jnp.int32).reshape(1)
    channels, span = weights.shape[1], tokens.shape[0]
    rows = weights[0].swapaxes(0, 1).reshape(3 * channels, weights.shape[3])
    tokens_half = halves((tokens,), (0, span, True), (0, span * 3 // 4, True))
    kept, given = halves((rows,), (0, 3 * channels, True), (0, 3 * channels, False))
    count, columns = given.shape
    (taken,) = assemble([swapped(given)], [(0, 0, count, columns, [(0, 0, 0)])])
    parts, runs, (kept, taken), cot_cols = gather_groups(*tokens_half, (kept, taken), cotangent)
    own, other = zip(*parts)
    hyena, grads, (early, later) = scan_all(
        me, cot_cols, residues[0].T, decay_rates[0].T, runs, ORDER, own, other
    )
    grad_input, hyena_out = scatter_sum(early, later, stack(kept, taken), hyena)
    return (hyena_out, grad_input, grads.T[None])


def shards(tokens, weights, residues, decay_rates, cotangent):
    ctx, tp = lax.axis_size("ctx"), lax.axis_size("tp")
    if ctx == 4 * PLANE and tp == 2 and weights.size * tp > 2 * tokens.size:
        return gather_tokens(tokens, weights, residues, decay_rates, cotangent)
    return gather_weights(tokens, weights, residues, decay_rates, cotangent)


def solution(mesh):
    return jax.shard_map(
        shards,
        mesh=mesh,
        in_specs=(
            P("ctx", None),
            P("tp", "ctx", None, None),
            P("tp", "ctx", None),
            P("tp", "ctx", None),
            P("tp", "ctx"),
        ),
        out_specs=(P("tp", "ctx"), P("ctx", "tp"), P("tp", "ctx", None)),
        check_vma=False,
    )
```

```python
import functools
import math
import operator

import jax
import jax.numpy as jnp
from jax import lax
from jax.experimental import pallas as pl
from jax.experimental.pallas import tpu as pltpu
from jax.sharding import PartitionSpec as P


def precise(form, left, right):
    return jnp.einsum(
        form, left, right, precision=lax.Precision.HIGHEST, preferred_element_type=jnp.float32
    )


def tripled(form, left, right):
    return jnp.einsum(
        form, left, right, precision=lax.Precision.HIGH, preferred_element_type=jnp.float32
    )


def angle_table(row_count, col_count, period):
    product = (
        jnp.arange(row_count, dtype=jnp.int32)[:, None]
        * jnp.arange(col_count, dtype=jnp.int32)[None, :]
        % period
    )
    angles = product.astype(jnp.float32) * (2.0 * math.pi / period)
    return (jnp.cos(angles), jnp.sin(angles))


def make_tables(length):
    padded = 2 * length
    outer = math.gcd(padded, 1 << (padded.bit_length() - 1) // 2)
    inner = padded // outer
    cos_outer, sin_outer = angle_table(outer, outer, outer)
    cos_inner, sin_inner = angle_table(inner, inner, inner)
    twist_cos, twist_sin = angle_table(outer, inner, padded)
    return (outer, inner, cos_outer, sin_outer, cos_inner, sin_inner, twist_cos, twist_sin)


def spectrum(signal, tables, product):
    outer, inner, cos_outer, sin_outer, cos_inner, sin_inner, twist_cos, twist_sin = tables
    half_rows = outer // 2
    blocks = signal.reshape(signal.shape[0], half_rows, inner)
    first_re = product("kp,bpq->bkq", cos_outer[:, :half_rows], blocks)
    first_im = -product("kp,bpq->bkq", sin_outer[:, :half_rows], blocks)
    turned_re = first_re * twist_cos + first_im * twist_sin
    turned_im = first_im * twist_cos - first_re * twist_sin
    spec_re = product("bkq,qj->bkj", turned_re, cos_inner) + product(
        "bkq,qj->bkj", turned_im, sin_inner
    )
    spec_im = product("bkq,qj->bkj", turned_im, cos_inner) - product(
        "bkq,qj->bkj", turned_re, sin_inner
    )
    return (spec_re, spec_im)


def signal_of(spec_re, spec_im, tables):
    outer, inner, cos_outer, sin_outer, cos_inner, sin_inner, twist_cos, twist_sin = tables
    half_rows = outer // 2
    back_re = tripled("bkj,jq->bkq", spec_re, cos_inner) - tripled(
        "bkj,jq->bkq", spec_im, sin_inner
    )
    back_im = tripled("bkj,jq->bkq", spec_im, cos_inner) + tripled(
        "bkj,jq->bkq", spec_re, sin_inner
    )
    turned_re = back_re * twist_cos - back_im * twist_sin
    turned_im = back_im * twist_cos + back_re * twist_sin
    values = tripled("pk,bkq->bpq", cos_outer[:half_rows, :], turned_re) - tripled(
        "pk,bkq->bpq", sin_outer[:half_rows, :], turned_im
    )
    return values.reshape(values.shape[0], half_rows * inner) * (1.0 / (outer * inner))


def spec_product(left_re, left_im, right_re, right_im):
    return (left_re * right_re - left_im * right_im, left_re * right_im + left_im * right_re)


def conj_product(left_re, left_im, right_re, right_im):
    return (left_re * right_re + left_im * right_im, left_re * right_im - left_im * right_re)


def filter_basis(residue_loc, rate_loc, length):
    position = jnp.arange(length, dtype=jnp.float32)
    basis_all = jnp.sqrt(2.0 * rate_loc)[:, :, None] * jnp.exp(
        -rate_loc[:, :, None] * position[None, None, :]
    )
    return (basis_all, precise("cm,cmt->ct", residue_loc, basis_all))


def forward_cols(gated_cols, taps_re, taps_im, tables):
    gated_re, gated_im = spectrum(gated_cols.astype(jnp.float32), tables, tripled)
    conv_re, conv_im = spec_product(gated_re, gated_im, taps_re, taps_im)
    conv_cols = signal_of(conv_re, conv_im, tables).astype(jnp.bfloat16)
    return (conv_cols, gated_re, gated_im)


def backward_cols(slope_cols, gated_re, gated_im, taps_re, taps_im, basis_all, tables, length):
    slope_re, slope_im = spectrum(slope_cols.astype(jnp.float32), tables, tripled)
    grad_re, grad_im = conj_product(taps_re, taps_im, slope_re, slope_im)
    back_cols = signal_of(grad_re, grad_im, tables).astype(jnp.bfloat16)
    lag_re, lag_im = conj_product(gated_re, gated_im, slope_re, slope_im)
    taps_grad = signal_of(lag_re, lag_im, tables)
    grad_residue = precise("ct,cmt->cm", taps_grad, basis_all) * (1.0 / math.sqrt(length))
    return (back_cols, grad_residue)


def gather_weights(tokens, weights, residues, decay_rates, cotangent):
    gathered = lax.all_gather(weights, "ctx", axis=1, tiled=True)
    projected = jnp.einsum("xcpd,td->xcpt", gathered, tokens, preferred_element_type=jnp.float32)
    features = projected[0].astype(jnp.bfloat16)
    query_f = features[:, 0].astype(jnp.float32)
    key_part = features[:, 1].astype(jnp.float32)
    value_part = features[:, 2].astype(jnp.float32)
    gated_in = (key_part * value_part).astype(jnp.bfloat16)
    slope_in = (cotangent.astype(jnp.float32) * query_f).astype(jnp.bfloat16)
    length = tokens.shape[0] * lax.axis_size("ctx")
    tables = make_tables(length)
    basis_all, taps_full = filter_basis(residues[0], decay_rates[0], length)
    taps_re, taps_im = spectrum(taps_full, tables, precise)
    gated_cols = lax.all_to_all(gated_in, "ctx", split_axis=0, concat_axis=1, tiled=True)
    conv_cols, gated_re, gated_im = forward_cols(gated_cols, taps_re, taps_im, tables)
    conv_rows = lax.all_to_all(conv_cols, "ctx", split_axis=1, concat_axis=0, tiled=True)
    slope_cols = lax.all_to_all(slope_in, "ctx", split_axis=0, concat_axis=1, tiled=True)
    back_cols, grad_residue = backward_cols(
        slope_cols, gated_re, gated_im, taps_re, taps_im, basis_all, tables, length
    )
    back_rows = lax.all_to_all(back_cols, "ctx", split_axis=1, concat_axis=0, tiled=True)
    conv_f = conv_rows.astype(jnp.float32)
    back_f = back_rows.astype(jnp.float32)
    hyena_out = (query_f * conv_f).astype(jnp.bfloat16)
    grad_query = (cotangent.astype(jnp.float32) * conv_f).astype(jnp.bfloat16)
    grad_key = (back_f * value_part).astype(jnp.bfloat16)
    grad_value = (back_f * key_part).astype(jnp.bfloat16)
    grad_proj = jnp.stack([grad_query, grad_key, grad_value], axis=1)
    partial_value = jnp.einsum(
        "cpt,cpd->td", grad_proj, gathered[0], preferred_element_type=jnp.float32
    )
    grad_input = lax.psum_scatter(
        partial_value.astype(jnp.bfloat16), "tp", scatter_dimension=1, tiled=True
    )
    return (hyena_out, grad_input, grad_residue[None])


GROUP = 4
ROWS = 8
PLANE = 4
VMEM = 56 * 2**20


def rounded(value):
    return value.astype(jnp.bfloat16).astype(jnp.float32)


def added_up(parts):
    return functools.reduce(operator.add, parts)


def earlier_sum(finals, rate, span, back):
    count = finals.shape[0]
    row = lax.broadcasted_iota(jnp.int32, finals.shape, 0)

    def shifted(value, by):
        if back:
            moved = pltpu.roll(value, count - by, 0)
            return jnp.where(row < count - by, moved, 0.0)
        moved = pltpu.roll(value, by, 0)
        return jnp.where(row >= by, moved, 0.0)

    total = shifted(finals, 1)
    by = 1
    while by < count:
        total = total + jnp.exp(rate * (-1.0 * span * by)) * shifted(total, by)
        by *= 2
    return total


def scan_kernel(
    groups,
    runs,
    order,
    me_ref,
    residue_ref,
    rate_ref,
    *refs,
):
    inputs = 1 + max(run[0] for run in runs)
    arrays, refs = refs[: 2 * inputs + 1], refs[2 * inputs + 1 :]
    hyena_ref, grad_ref = refs[:2]
    proj_refs, refs = refs[2 : 2 + len(order)], refs[2 + len(order) :]
    gated_s, slope_s, conv_s, back_s, feats_s = refs
    cot_ref, own, other = arrays[0], arrays[1 : 1 + inputs], arrays[1 + inputs :]
    length, width = cot_ref.shape
    chunks = PLANE * groups
    span = length // chunks
    modes = rate_ref.shape[0]
    me = me_ref[0]

    def place(group, member):
        return lax.rem(me // PLANE + group, groups) * PLANE + (member ^ lax.rem(me, PLANE))

    def aligned(start, size):
        return pl.ds(pl.multiple_of(start, size), size)

    for source, offset, group, base, members, count, first in runs:

        def before(step, _, source=source, offset=offset, group=group, base=base, count=count, first=first):
            member = base + step
            index = place(group, member)
            rows = pl.ds(pl.multiple_of(offset + step * count, 16), count)
            feats = own[source][rows, :] + other[source][rows, :].astype(jnp.float32)
            feats = rounded(feats)
            slot = (group * PLANE + member) * span + first
            feats_s[pl.ds(pl.multiple_of(slot, 16), count), :] = feats
            cot = cot_ref[pl.ds(pl.multiple_of(index * span + first, 16), count), :]
            query, key = feats[:, :width], feats[:, width : 2 * width]
            into = pl.ds(first * chunks + index, count, stride=chunks)
            gated_s[into, :] = rounded(key * feats[:, 2 * width :])
            slope_s[into, :] = rounded(cot.astype(jnp.float32) * query)
            return 0

        lax.fori_loop(0, members, before, 0)

    sides = range(chunks // ROWS)
    scale = 1.0 / math.sqrt(length)

    def rows_at(step, side):
        return pl.ds(pl.multiple_of(step * chunks + side * ROWS, ROWS), ROWS)

    def zeros(count):
        zero = jnp.zeros((ROWS, width), jnp.float32)
        return tuple((zero,) * len(sides) for _ in range(count))

    def moved_on(states, decays, inputs):
        return tuple(
            tuple(decay * state[side] + inputs[side] for side in sides)
            for decay, state in zip(decays, states)
        )

    def entered(states, rates, back):
        whole = [
            earlier_sum(
                jnp.concatenate(state, axis=0),
                jnp.concatenate([rate] * len(sides), axis=0),
                span,
                back,
            )
            for state, rate in zip(states, rates)
        ]
        return tuple(
            tuple(state[side * ROWS : (side + 1) * ROWS, :] for side in sides) for state in whole
        )

    for first in range(0, modes, GROUP):
        count = min(GROUP, modes - first)
        rates = [
            jnp.broadcast_to(rate_ref[m : m + 1, :], (ROWS, width))
            for m in range(first, first + count)
        ]
        decays = [jnp.exp(-rate) for rate in rates]
        norms = [jnp.sqrt(2.0 * rate) for rate in rates]
        gains = [residue_ref[first + n : first + n + 1, :] * norms[n] for n in range(count)]

        def sums(step, state):
            ahead, behind = state
            gated = [gated_s[rows_at(step, side), :] for side in sides]
            slope = [slope_s[rows_at(span - 1 - step, side), :] for side in sides]
            return moved_on(ahead, decays, gated), moved_on(behind, decays, slope)

        ahead, behind = lax.fori_loop(0, span, sums, (zeros(count), zeros(count)), unroll=16)
        ahead, behind = entered(ahead, rates, False), entered(behind, rates, True)

        def outs(step, state):
            ahead, behind, grads = state
            other = span - 1 - step
            gated = [gated_s[rows_at(step, side), :] for side in sides]
            slope = [slope_s[rows_at(step, side), :] for side in sides]
            slope_back = [slope_s[rows_at(other, side), :] for side in sides]
            ahead = moved_on(ahead, decays, gated)
            behind = moved_on(behind, decays, slope_back)
            grads = tuple(
                tuple(grad[side] + slope[side] * state[side] for side in sides)
                for grad, state in zip(grads, ahead)
            )
            for side in sides:
                conv = added_up(gains[n] * ahead[n][side] for n in range(count))
                back = added_up(gains[n] * behind[n][side] for n in range(count))
                if first:
                    conv = conv + conv_s[rows_at(step, side), :]
                    back = back + back_s[rows_at(other, side), :]
                conv_s[rows_at(step, side), :] = conv
                back_s[rows_at(other, side), :] = back
            return ahead, behind, grads

        _, _, grads = lax.fori_loop(0, span, outs, (ahead, behind, zeros(count)), unroll=8)
        for n in range(count):
            total = jnp.sum(added_up(grads[n]) * norms[n], axis=0, keepdims=True) * scale
            grad_ref[first + n : first + n + 1, :] = total

    for proj_ref, pieces in zip(proj_refs, order):
        start = 0
        for group, base, members in pieces:

            def after(step, _, proj_ref=proj_ref, start=start, group=group, base=base):
                member = base + step
                index = place(group, member)
                feats = feats_s[aligned((group * PLANE + member) * span, span), :]
                query, key = feats[:, :width], feats[:, width : 2 * width]
                cot = cot_ref[aligned(index * span, span), :].astype(jnp.float32)
                conv = rounded(conv_s[pl.ds(index, span, stride=chunks), :])
                back = rounded(back_s[pl.ds(index, span, stride=chunks), :])
                hyena_ref[aligned(index * span, span), :] = narrowed(query * conv)
                rows = aligned(start + step * span, span)
                proj_ref[rows, :width] = narrowed(cot * conv)
                proj_ref[rows, width : 2 * width] = narrowed(back * feats[:, 2 * width :])
                proj_ref[rows, 2 * width :] = narrowed(back * key)
                return 0

            lax.fori_loop(0, members, after, 0)
            start += members * span


def scan_all(me, cot_cols, residue_rows, rate_rows, runs, order, own, other):
    length, width = cot_cols.shape
    span = length // (PLANE * PLANE)
    vmem = pl.BlockSpec(memory_space=pltpu.VMEM)
    arrays = (cot_cols, *own, *other)
    outs = pl.pallas_call(
        functools.partial(scan_kernel, PLANE, runs, order),
        out_shape=(
            jax.ShapeDtypeStruct((length, width), jnp.bfloat16),
            jax.ShapeDtypeStruct(rate_rows.shape, jnp.float32),
        )
        + tuple(
            jax.ShapeDtypeStruct((span * sum(piece[2] for piece in pieces), 3 * width), jnp.bfloat16)
            for pieces in order
        ),
        in_specs=[pl.BlockSpec(memory_space=pltpu.SMEM)] + [vmem] * (2 + len(arrays)),
        out_specs=(vmem,) * (2 + len(order)),
        scratch_shapes=[pltpu.VMEM((length, width), jnp.float32)] * 4
        + [pltpu.VMEM((length, 3 * width), jnp.float32)],
        compiler_params=pltpu.CompilerParams(vmem_limit_bytes=40 * 2**20),
        name="modal_scan",
    )(me, residue_rows, rate_rows, *arrays)
    return outs[0], outs[1], outs[2:]


def swapped(value):
    return lax.ppermute(value, "tp", [(0, 1), (1, 0)])


def over_x(value):
    return lax.ppermute(value, "ctx", [(i, i ^ 1) for i in range(lax.axis_size("ctx"))])


def over_y(value):
    return lax.ppermute(value, "ctx", [(i, i ^ 2) for i in range(lax.axis_size("ctx"))])


def up(value):
    count = lax.axis_size("ctx")
    return lax.ppermute(value, "ctx", [(i, (i + PLANE) % count) for i in range(count)])


def down(value):
    count = lax.axis_size("ctx")
    return lax.ppermute(value, "ctx", [((i + PLANE) % count, i) for i in range(count)])


def stack(*parts):
    return jnp.concatenate(parts, axis=0)


def beside(*parts):
    return jnp.concatenate(parts, axis=1)


def narrowed(value):
    return value.astype(jnp.bfloat16)


def widened(value):
    return value.astype(jnp.float32)


def halves_kernel(plan, core_ref, *refs):
    arrays, outs, arrived = refs[: -1 - len(plan)], refs[-1 - len(plan) : -1], refs[-1]
    copies = []
    for k, (out, (index, count, mine)) in enumerate(zip(outs, plan)):
        half = out.shape[1]
        side = core_ref[0] if mine else 1 - core_ref[0]
        columns = pl.ds(pl.multiple_of(side * half, half), half)
        part = arrays[index].at[pl.ds(0, count), columns]
        copies.append(pltpu.make_async_copy(part, out, arrived.at[k]))
    for copy in copies:
        copy.start()
    for copy in copies:
        copy.wait()


def halves(arrays, *plan):
    core = lax.axis_index("tp").astype(jnp.int32).reshape(1)
    shapes = [(count, arrays[index].shape[1] // 2) for index, count, _ in plan]
    moved = sum(4 * rows * columns for rows, columns in shapes)
    return pl.pallas_call(
        functools.partial(halves_kernel, plan),
        out_shape=tuple(jax.ShapeDtypeStruct(shape, jnp.bfloat16) for shape in shapes),
        in_specs=[pl.BlockSpec(memory_space=pltpu.SMEM)]
        + [pl.BlockSpec(memory_space=pl.ANY)] * len(arrays),
        out_specs=(pl.BlockSpec(memory_space=pltpu.VMEM),) * len(plan),
        scratch_shapes=[pltpu.SemaphoreType.DMA((len(plan),))],
        compiler_params=pltpu.CompilerParams(vmem_limit_bytes=VMEM),
        cost_estimate=pl.CostEstimate(flops=0, bytes_accessed=moved, transcendentals=0),
        name="halves",
    )(core, *arrays)


def assemble_kernel(inputs, plans, *refs):
    arrays, outs = refs[:inputs], refs[inputs:]
    for out, plan in zip(outs, plans):
        for row, col, height, width, sources in plan:
            parts = [
                arrays[index][from_row : from_row + height, from_col : from_col + width]
                for index, from_row, from_col in sources
            ]
            if len(parts) > 1:
                parts = [narrowed(added_up(widened(part) for part in parts))]
            out[row : row + height, col : col + width] = parts[0]


def assemble(arrays, *plans):
    used = sorted({source[0] for plan in plans for piece in plan for source in piece[4]})
    arrays = [arrays[index] for index in used]
    plans = [
        [(*piece[:4], [(used.index(source[0]), *source[1:]) for source in piece[4]]) for piece in plan]
        for plan in plans
    ]
    shapes = [
        (max(p[0] + p[2] for p in plan), max(p[1] + p[3] for p in plan)) for plan in plans
    ]
    moved = sum(2 * rows * cols for rows, cols in shapes)
    vmem = pl.BlockSpec(memory_space=pltpu.VMEM)
    return pl.pallas_call(
        functools.partial(assemble_kernel, len(arrays), plans),
        out_shape=tuple(jax.ShapeDtypeStruct(shape, jnp.bfloat16) for shape in shapes),
        in_specs=[vmem] * len(arrays),
        out_specs=(vmem,) * len(plans),
        compiler_params=pltpu.CompilerParams(vmem_limit_bytes=32 * 2**20),
        cost_estimate=pl.CostEstimate(flops=moved, bytes_accessed=4 * moved, transcendentals=0),
        name="assemble",
    )(*arrays)


def rows_of(*parts):
    plan, start = [], 0
    for index, first, count in parts:
        plan.append((start, count, [(index, first, 0)]))
        start += count
    return plan


def full_width(columns, plan):
    return [(row, 0, count, columns, sources) for row, count, sources in plan]


def columns_of(height, *parts):
    plan, start = [], 0
    for width, sources in parts:
        plan.append((0, start, height, width, sources))
        start += width
    return plan


def all_ways(for_x, for_y, for_above, for_below):
    got_x, got_y = over_x(for_x), over_y(for_y)
    from_below, from_above = up(for_above), down(for_below)
    return lax.optimization_barrier((got_x, got_y, from_below, from_above))


def project(parts, kept, taken):
    rows = stack(*parts)
    own, given = (
        jnp.einsum("td,rd->tr", rows, matrix, preferred_element_type=jnp.float32)
        for matrix in (kept, taken)
    )
    return own, swapped(narrowed(given))


def columns_held(rows):
    return lax.all_to_all(rows.T, "ctx", split_axis=1, concat_axis=0, tiled=True)


def gather_groups(tokens, wide, matrices, later):
    span = tokens.shape[0]
    n, m = span * 3 // 4, span // 4
    nh, mh = n // 2, m // 2
    columns = tokens.shape[1]

    def put(arrays, *plans):
        return assemble(arrays, *[full_width(columns, rows_of(*plan)) for plan in plans])

    own_x, own_y, wide_3, wide_1 = all_ways(tokens, tokens, wide, wide)
    first = (tokens, own_x, own_y, wide_3, wide_1)
    members = ((0, n, m), (1, n, m), (2, n, m))
    sent = put(
        first,
        ((2, 0, nh), (2, n, mh), (3, 0, n), (4, 0, n)),
        ((1, nh, nh), (1, n + mh, mh), (3, 0, n), (4, 0, n)),
        ((3, 0, nh), *members),
        ((4, nh, nh), *members),
    )
    sent, first = lax.optimization_barrier((sent, first))
    second = all_ways(*sent)
    start = nh + mh
    wide_2 = ((2, 0, nh), (3, 0, nh))
    across = ((0, nh, mh), (1, nh, mh))
    third = all_ways(
        *put(
            second,
            ((1, start, nh), (1, start + n, nh), *wide_2),
            ((0, start + nh, nh), (0, start + n + nh, nh), *wide_2),
            (*across, (2, nh, nh)),
            (*across, (3, 2 * nh, nh)),
        )
    )
    fourth = all_ways(
        *put(third, ((1, n, nh),), ((0, n + nh, nh),), ((2, 0, mh),), ((3, mh, mh),))
    )
    runs = [
        (0, 0, 0, 0, 3, span, 0),
        (0, 3 * span, 3, 0, 1, n, 0),
        (0, 3 * span + n, 1, 0, 1, n, 0),
    ]
    offset = 0
    for side in range(2):
        runs += [
            (1, offset, 0, 3, 1, nh, side * nh),
            (1, offset + nh, 0, 3, 1, mh, n + side * mh),
            (1, offset + start, 3, 1 + side, 1, n, 0),
            (1, offset + start + n, 1, 1 + side, 1, n, 0),
        ]
        offset += start + 2 * n
    for side in range(2):
        runs += [
            (1, offset, 2, 0, 1, nh, side * nh),
            (1, offset + nh, 3 - 2 * side, 0, 3, m, n),
        ]
        offset += nh + 3 * m
    offset = 0
    for side in range(2):
        runs += [
            (2, offset, 3, 3, 1, nh, side * nh),
            (2, offset + nh, 1, 3, 1, nh, side * nh),
            (2, offset + n, 2, 1 + side, 1, n, 0),
        ]
        offset += 2 * n
    runs += [
        (2, offset, 3, 3, 1, m, n),
        (2, offset + m, 2, 0, 1, m, n),
        (2, offset + 2 * m, 2, 1, 1, mh, n),
        (2, offset + 2 * m + mh, 1, 3, 1, m, n),
        (2, offset + 3 * m + mh, 2, 1, 1, mh, n + mh),
        (2, offset + 3 * m + 2 * mh, 2, 2, 1, m, n),
        (3, 0, 2, 3, 1, nh, 0),
        (3, nh, 2, 3, 1, nh, nh),
        (3, n, 2, 3, 1, mh, n),
        (3, n + mh, 2, 3, 1, mh, n + mh),
    ]
    parts = [project(part, *matrices) for part in (first, second, third, fourth)]
    later, first = lax.optimization_barrier((later, parts[0][0]))
    parts[0] = (first, parts[0][1])
    later = columns_held(later)
    return parts, tuple(runs), matrices, later


ORDER = (((2, 0, 4), (1, 3, 1), (3, 3, 1)), ((1, 0, 3), (3, 0, 3), (0, 3, 1), (0, 0, 3)))


def scatter_sum(early, later, matrix, hyena):
    span = early.shape[0] // 6
    columns = matrix.shape[1]
    wide, narrow = columns * 3 // 8, columns // 8
    places = {}
    for array, pieces in enumerate((ORDER[0], ORDER[1][:3], ORDER[1][3:])):
        row = 0
        for group, base, members in pieces:
            for member in range(base, base + members):
                places[group, member] = (array, row)
                row += span

    def product(part, other):
        both = beside(part, other)
        return narrowed(jnp.dot(both, matrix, preferred_element_type=jnp.float32))

    def term(group, member, side, *more):
        array, row = places[group, member]
        return (wide, [(array, row, side * wide), *more])

    def low(group, member, side, *more):
        array, row = places[group, member]
        return (narrow, [(array, row, 2 * wide + side * narrow), *more])

    def put(arrays, *plans):
        return assemble(arrays, *[columns_of(span, *plan) for plan in plans])

    early = product(early, swapped(early))
    other = swapped(later)
    first = all_ways(
        *put([early], [term(2, 3, 0)], [term(2, 3, 1)], [low(2, 3, 0)], [low(2, 3, 1)])
    )
    later, hyena, first = lax.optimization_barrier((later, hyena, first))
    x, y, below, above = range(1, 5)
    second = all_ways(
        *put(
            [early, *first],
            [term(2, 1, 0), term(2, 1, 1, (y, 0, 0)), term(1, 3, 0), term(3, 3, 0)],
            [term(2, 2, 0, (x, 0, 0)), term(2, 2, 1), term(1, 3, 1), term(3, 3, 1)],
            [low(1, 3, 0, (below, 0, 0)), low(1, 3, 1), *[low(2, k, 0) for k in range(3)]],
            [low(3, 3, 0), low(3, 3, 1, (above, 0, 0)), *[low(2, k, 1) for k in range(3)]],
        )
    )
    own = product(later[7 * span :], other[7 * span :])
    later = product(later[: 7 * span], other[: 7 * span])
    later, second = lax.optimization_barrier((later, second))
    hyena_out = lax.all_to_all(hyena, "ctx", split_axis=0, concat_axis=1, tiled=True).T
    x, y, below, above = range(2, 6)

    def low_3(side):
        return low(0, 3, side, (below, 0, side * narrow), (above, 0, side * narrow))

    def sum_2(side):
        return term(2, 0, side, (x, 0, side * wide), (y, 0, side * wide))

    for_above, for_below = [], []
    for k in range(3):
        start = (2 + k) * narrow
        for_above += [low(1, k, 0, (below, 0, start)), low(1, k, 1)]
        for_below += [low(3, k, 0), low(3, k, 1, (above, 0, start))]
    third = all_ways(
        *put(
            [early, later, *second],
            [
                term(1, 1, 0),
                term(1, 1, 1, (y, 0, 2 * wide)),
                term(3, 1, 0),
                term(3, 1, 1, (y, 0, 3 * wide)),
                term(0, 3, 0),
                low_3(0),
            ],
            [
                term(1, 2, 0, (x, 0, 2 * wide)),
                term(1, 2, 1),
                term(3, 2, 0, (x, 0, 3 * wide)),
                term(3, 2, 1),
                term(0, 3, 1),
                low_3(1),
            ],
            [sum_2(0), *for_above],
            [sum_2(1), *for_below],
        )
    )

    x, y, below, above = range(3, 7)

    def low_own(k, side, *more):
        start = wide + (2 * k + side) * narrow
        return low(0, k, side, (below, 0, start), (above, 0, start), *more)

    def own_sum(group, side, *more):
        start = (group - 1 + side) * wide
        return term(group, 0, side, (x, 0, start), (y, 0, start), *more)

    sent = put(
        [early, later, own, *third],
            [
                term(0, 1, 0),
                term(0, 1, 1, (y, 0, 4 * wide)),
                low_own(1, 0),
                low_own(1, 1, (y, 0, 5 * wide)),
            ],
            [
                term(0, 2, 0, (x, 0, 4 * wide)),
                term(0, 2, 1),
                low_own(2, 0, (x, 0, 5 * wide)),
                low_own(2, 1),
            ],
            [own_sum(1, 0, (below, 0, 0)), own_sum(1, 1)],
            [own_sum(3, 0), own_sum(3, 1, (above, 0, 0))],
    )
    (base,) = put(
        [early, later, own, *third],
        [term(0, 0, 0), term(0, 0, 1), low_own(0, 0), low_own(0, 1)],
    )
    (grad_input,) = put(
        [base, *all_ways(*sent)],
        [
            (2 * wide, [(way, 0, 0) for way in range(5)]),
            (2 * narrow, [(way, 0, 2 * wide) for way in range(3)]),
        ],
    )
    return grad_input, hyena_out


def gather_tokens(tokens, weights, residues, decay_rates, cotangent):
    me = lax.axis_index("ctx").astype(jnp.int32).reshape(1)
    channels, span = weights.shape[1], tokens.shape[0]
    rows = weights[0].swapaxes(0, 1).reshape(3 * channels, weights.shape[3])
    tokens_half = halves((tokens,), (0, span, True), (0, span * 3 // 4, True))
    kept, given = halves((rows,), (0, 3 * channels, True), (0, 3 * channels, False))
    count, columns = given.shape
    (taken,) = assemble([swapped(given)], [(0, 0, count, columns, [(0, 0, 0)])])
    parts, runs, (kept, taken), cot_cols = gather_groups(*tokens_half, (kept, taken), cotangent)
    own, other = zip(*parts)
    hyena, grads, (early, later) = scan_all(
        me, cot_cols, residues[0].T, decay_rates[0].T, runs, ORDER, own, other
    )
    grad_input, hyena_out = scatter_sum(early, later, stack(kept, taken), hyena)
    return (hyena_out, grad_input, grads.T[None])


def shards(tokens, weights, residues, decay_rates, cotangent):
    ctx, tp = lax.axis_size("ctx"), lax.axis_size("tp")
    if ctx == 4 * PLANE and tp == 2 and weights.size * tp > 2 * tokens.size:
        return gather_tokens(tokens, weights, residues, decay_rates, cotangent)
    return gather_weights(tokens, weights, residues, decay_rates, cotangent)


def solution(mesh):
    return jax.shard_map(
        shards,
        mesh=mesh,
        in_specs=(
            P("ctx", None),
            P("tp", "ctx", None, None),
            P("tp", "ctx", None),
            P("tp", "ctx", None),
            P("tp", "ctx"),
        ),
        out_specs=(P("tp", "ctx"), P("ctx", "tp"), P("tp", "ctx", None)),
        check_vma=False,
    )
```
